32 devices in a mesh: dp: 8 (over z, y), blk: 4 (over x, core).
Axes of the slice: x: 2, y: 2, z: 4, core: 2. Of those that a mesh axis runs over, the one named last changes fastest.
Arguments:
- patches: bfloat16 [5632, 768], P(('dp', 'blk')), may hold values from -6 to 6
- special: bfloat16 [160, 768], P('dp'), may hold values from -6 to 6
- image_ids: int32 [5632], P('dp'), may hold values from 0 to 2, as said below
- w_qkv: bfloat16 [768, 2304], P(('dp', 'blk')), may hold values from -0.21875 to 0.21875
- w_out: bfloat16 [768, 768], P(('dp', 'blk')), may hold values from -2.5 to 2.5
- w_up: bfloat16 [768, 3072], P(('dp', 'blk')), may hold values from -0.21875 to 0.21875
- w_down: bfloat16 [3072, 768], P(('dp', 'blk')), may hold values from -0.109375 to 0.109375
- gains: bfloat16 [4, 768], P(None, ('dp', 'blk')), may hold values from 0.5 to 1.5
- cot_patches: bfloat16 [5632, 768], P(('dp', 'blk')), may hold values from -6 to 6
- cot_special: bfloat16 [160, 768], P('dp'), may hold values from -6 to 6
Outputs:
- out_patches: bfloat16 [5632, 768], P(('dp', 'blk'))
- out_special: bfloat16 [160, 768], P('dp')
- grad_patches: float32 [5632, 768], P(('dp', 'blk'))
- grad_special: float32 [160, 768], P('dp')
- grad_qkv: float32 [768, 2304], P(('dp', 'blk'))
- grad_out: float32 [768, 768], P(('dp', 'blk'))
- grad_up: float32 [768, 3072], P(('dp', 'blk'))
- grad_down: float32 [3072, 768], P(('dp', 'blk'))
- grad_gains: float32 [4, 768], P(None, ('dp', 'blk'))
The draws below stay inside these ranges and needn't reach their ends.
Inputs may be any that keep to these rules, and one draw needn't show every extreme that they name: `image_ids`: along a group's slots in band order the ids never fall. A group holds either one 518px image of 348 slots followed by padding, or 2 224px images of 176 slots each followed by padding (possibly none); image places without slots have only their special rows. Some group of every draw holds a 518px image.
All inputs are finite; a program needn't handle non-finite values.
Results may differ from the reference program's by a relative error of at most 0.015.
Values may be sent and summed in bfloat16 or wider, within the bound.
No kernel may reach another device: no remote copies, remote signals or barrier semaphores. Data moves between devices by JAX's collectives and lax.ppermute only.
A program may use at most 192 MiB of HBM per device.

```python
import jax
import jax.numpy as jnp
from jax import lax

D = 768
FF = 3072
HEADS = 12
HEAD_DIM = 64
SPECIAL = 5
MICRO = 2
TOK_MB = 88
IMAGES = 2
LONG_LEN = 348
SHORT_LEN = 176
TOKENS = 5632
SPECIAL_ROWS = 160
N_DP = 8
N_BLK = 4


def draw_image_ids(key, part):
    key = jax.random.fold_in(key, 11)
    key_class, key_pick = jax.random.split(key)
    group_count = N_DP * MICRO
    tall = jax.random.randint(key_class, (group_count,), 0, 4) == 0
    chosen = jax.random.randint(key_pick, (), 0, group_count)
    tall = jnp.logical_or(tall, jnp.arange(group_count, dtype=jnp.int32) == chosen)
    places = jnp.arange(IMAGES, dtype=jnp.int32)
    long_lengths = jnp.where(places == 0, LONG_LEN, 0).astype(jnp.int32)
    short_lengths = jnp.full((IMAGES,), SHORT_LEN, jnp.int32)
    lengths = jnp.where(tall[:, None], long_lengths[None, :], short_lengths[None, :]).astype(jnp.int32)
    bounds = jnp.cumsum(lengths, -1)
    slots = jnp.arange(N_BLK * TOK_MB, dtype=jnp.int32)
    labels = jnp.sum((slots[None, :, None] >= bounds[:, None, :]).astype(jnp.int32), -1)
    labels = labels.reshape(N_DP, MICRO, N_BLK, TOK_MB).transpose(0, 2, 1, 3)
    return labels.reshape(-1).astype(jnp.int32)


def shard_levels(rng, extent, pieces, low, largest):
    def one(dim, parts):
        steps = jax.random.uniform(jax.random.fold_in(jax.random.fold_in(rng, 6), dim), (parts,), jnp.float32, low / len(pieces), largest / len(pieces))
        return jnp.repeat(jnp.exp(steps), extent[dim] // parts).reshape((-1,) + (1,) * (len(extent) - dim - 1))

    level = one(*pieces[0])
    for cut in pieces[1:]:
        level = level * one(*cut)
    return level


def normal_values(stream_key, extent, deviation, reach, cuts=(), kind=jnp.bfloat16):
    drawn = deviation * jax.random.normal(stream_key, extent, jnp.float32)
    if cuts:
        drawn = drawn * shard_levels(stream_key, extent, cuts, -0.22, 0.18)
    return jnp.clip(drawn, -reach, reach).astype(kind)


def setup_inputs(seed: int = 0) -> dict:
    splits = jax.random.split(jax.random.key(seed), 11)
    patches = normal_values(splits[0], (TOKENS, D), 1.0, 6.0, ((0, 32),))
    special = normal_values(splits[1], (SPECIAL_ROWS, D), 1.0, 6.0, ((0, 8),))
    image_ids = draw_image_ids(jax.random.fold_in(splits[10], 71), 0)
    w_qkv = normal_values(splits[3], (D, 3 * D), D ** -0.5, 0.21875, ((0, 32),))
    w_out = normal_values(splits[4], (D, D), (D // 128) ** -0.5, 2.5, ((0, 32),))
    w_up = normal_values(splits[5], (D, FF), D ** -0.5, 0.21875, ((0, 32),))
    w_down = normal_values(splits[6], (FF, D), FF ** -0.5, 0.109375, ((0, 32),))
    gains = jnp.clip(1.0 + 0.1 * jax.random.normal(splits[7], (4, D), jnp.float32), 0.5, 1.5).astype(jnp.bfloat16)
    cot_patches = normal_values(splits[8], (TOKENS, D), 1.0, 6.0, ((0, 32),))
    cot_special = normal_values(splits[9], (SPECIAL_ROWS, D), 1.0, 6.0, ((0, 8),))
    return dict(patches=patches, special=special, image_ids=image_ids, w_qkv=w_qkv, w_out=w_out, w_up=w_up, w_down=w_down, gains=gains, cot_patches=cot_patches, cot_special=cot_special)


SCORE_SCALE = 0.125
MASKED = -1e+30
EPSILON = 1e-06

@jax.custom_vjp
def low(v):
    return lax.optimization_barrier(v.astype(jnp.bfloat16)).astype(jnp.float32)

@jax.custom_vjp
def low_back(v):
    return v

def low_keep(v):
    return (low(v), None)

def low_pass(kept, grad):
    return (grad,)

def back_keep(v):
    return (v, None)

def back_low(kept, grad):
    return (low(grad),)
low.defvjp(low_keep, low_pass)
low_back.defvjp(back_keep, back_low)

def layer_norm(values, gain_row):
    centre = values - lax.optimization_barrier(jnp.mean(values, -1, keepdims=True))
    spread = lax.optimization_barrier(jnp.mean(centre * centre, -1, keepdims=True))
    return centre * lax.rsqrt(spread + EPSILON) * gain_row

@jax.checkpoint
def attend(queries, key_heads, value_heads, query_ids, key_ids):
    scores = jnp.einsum('qhd,khd->hqk', queries, key_heads, precision=lax.Precision.HIGHEST) * SCORE_SCALE
    scores = low_back(scores)
    scores = jnp.where((query_ids[:, None] == key_ids[None, :])[None], scores, MASKED)
    probabilities = low(jax.nn.softmax(scores, axis=-1))
    mixture = jnp.einsum('hqk,khd->qhd', probabilities, value_heads, precision=lax.Precision.HIGHEST)
    return mixture.reshape(queries.shape[0], -1)

def group_layer(patch_rows, special_rows, patch_ids, w_qkv, w_out, w_up, w_down, gains):
    tokens = jnp.concatenate([patch_rows, special_rows], 0)
    normed = low(layer_norm(tokens, gains[0]))
    projected = low(low_back(jnp.dot(normed, w_qkv, precision=lax.Precision.HIGHEST)))
    split_qkv = projected.reshape(projected.shape[0], 3, HEADS, HEAD_DIM)
    queries = split_qkv[:, 0]
    key_heads = split_qkv[:, 1]
    value_heads = split_qkv[:, 2]
    spec_ids = jnp.arange(special_rows.shape[0], dtype=jnp.int32) // SPECIAL
    key_ids = jnp.concatenate([patch_ids, spec_ids])
    patch_count = patch_rows.shape[0]
    query_blocks = queries[:patch_count].reshape(N_BLK, TOK_MB, HEADS, HEAD_DIM)
    id_blocks = patch_ids.reshape(N_BLK, TOK_MB)
    patch_out = lax.map(lambda block_pair: attend(block_pair[0], key_heads, value_heads, block_pair[1], key_ids), (query_blocks, id_blocks))
    patch_out = patch_out.reshape(patch_count, D)
    special_out = attend(queries[patch_count:], key_heads, value_heads, spec_ids, key_ids)
    attended = low(low_back(jnp.concatenate([patch_out, special_out], 0)))
    branch = low_back(jnp.dot(attended, w_out, precision=lax.Precision.HIGHEST))
    middle = tokens + gains[1] * branch
    normed_mlp = low(layer_norm(middle, gains[2]))
    hidden = low_back(jnp.dot(normed_mlp, w_up, precision=lax.Precision.HIGHEST))
    active = low(jax.nn.gelu(hidden, approximate=False))
    mlp_out = low_back(jnp.dot(active, w_down, precision=lax.Precision.HIGHEST))
    final = middle + gains[3] * mlp_out
    return (final[:patch_count], final[patch_count:])

def reference(patches, special, image_ids, w_qkv, w_out, w_up, w_down, gains, cot_patches, cot_special):
    groups = N_DP * MICRO
    spec_rows = IMAGES * SPECIAL

    def to_groups(matrix):
        return matrix.reshape(N_DP, N_BLK, MICRO, TOK_MB, D).transpose(0, 2, 1, 3, 4).reshape(groups, N_BLK * TOK_MB, D)

    def from_groups(matrix):
        return matrix.reshape(N_DP, MICRO, N_BLK, TOK_MB, D).transpose(0, 2, 1, 3, 4).reshape(N_DP * N_BLK * MICRO * TOK_MB, D)
    group_ids = image_ids.reshape(N_DP, N_BLK, MICRO, TOK_MB).transpose(0, 2, 1, 3).reshape(groups, N_BLK * TOK_MB)

    def forward(patch_all, special_all, qkv_full, out_full, up_full, down_full, gains_full):

        def one_group(group_item):
            return group_layer(group_item[0], group_item[1], group_item[2], qkv_full, out_full, up_full, down_full, gains_full)
        return lax.map(one_group, (patch_all, special_all, group_ids))
    outputs, pullback = jax.vjp(forward, to_groups(patches).astype(jnp.float32), special.reshape(groups, spec_rows, D).astype(jnp.float32), w_qkv.astype(jnp.float32), w_out.astype(jnp.float32), w_up.astype(jnp.float32), w_down.astype(jnp.float32), gains.astype(jnp.float32))
    grads = pullback((to_groups(cot_patches).astype(jnp.float32), cot_special.reshape(groups, spec_rows, D).astype(jnp.float32)))
    return (from_groups(outputs[0]).astype(jnp.bfloat16), outputs[1].reshape(-1, D).astype(jnp.bfloat16), from_groups(grads[0]), grads[1].reshape(-1, D), grads[2], grads[3], grads[4], grads[5], grads[6])
```

```python
import jax
import jax.numpy as jnp
from jax import lax
from jax.experimental import pallas as pl
from jax.experimental.pallas import tpu as pltpu
from jax.sharding import PartitionSpec as P

HEAD_DIM = 64
SPECIAL = 5
MICRO = 2
TOK_MB = 88

SCORE_SCALE = 0.125
MASKED = -1e30
EPSILON = 1e-06

BF16 = jnp.bfloat16
F32 = jnp.float32


def merged(shard, axis, combine):
    everything = jax.tree.map(
        lambda part, kind: lax.all_gather(part.astype(kind), axis),
        shard,
        (jnp.bfloat16, jnp.bfloat16, jnp.bfloat16),
    )

    def take(k):
        return jax.tree.map(lambda part, own: part[k].astype(own.dtype), everything, shard)

    return lax.fori_loop(
        1, lax.axis_size(axis), lambda k, so_far: combine(so_far, take(k)), take(0)
    )


def from_behind(shard, axis, by):
    peers = lax.axis_size(axis)
    return lax.ppermute(shard, axis, [(i, (i + by) % peers) for i in range(peers)])


def norm_rows(values, gain_row):
    centre = values - jnp.mean(values, -1, keepdims=True)
    spread = jnp.mean(centre * centre, -1, keepdims=True)
    return centre * lax.rsqrt(spread + EPSILON) * gain_row


def split_heads(matrix):
    return matrix.reshape(matrix.shape[0], -1, HEAD_DIM)


def widen(per_head):
    return jnp.repeat(per_head.T, HEAD_DIM, axis=1)


def empty_state(length, head_count, feature_width):
    return (
        jnp.full((head_count, length), MASKED, jnp.float32),
        jnp.zeros((head_count, length), jnp.float32),
        jnp.zeros((length, feature_width), jnp.float32),
    )


def online(carried, queries, query_ids, key_rows, value_rows, key_ids):
    top_score, totals, accumulated = carried
    same_image = (query_ids[:, None] == key_ids[None, :])[None]
    scores = (
        jnp.einsum(
            "qhd,khd->hqk",
            split_heads(queries),
            split_heads(key_rows),
            preferred_element_type=jnp.float32,
        )
        * SCORE_SCALE
    )
    scores = jnp.where(same_image, scores, MASKED)
    new_top = jnp.maximum(top_score, jnp.max(scores, -1))
    weights = jnp.where(same_image, jnp.exp(scores - new_top[..., None]), 0.0)
    factor = jnp.exp(top_score - new_top)
    totals = totals * factor + jnp.sum(weights, -1)
    mixture = jnp.einsum(
        "hqk,khd->qhd",
        weights.astype(jnp.bfloat16),
        split_heads(value_rows),
        preferred_element_type=jnp.float32,
    )
    accumulated = accumulated * widen(factor) + mixture.reshape(accumulated.shape)
    return (new_top, totals, accumulated)


def combine(former, latter):
    highest = jnp.maximum(former[0], latter[0])
    scale_former = jnp.exp(former[0] - highest)
    scale_latter = jnp.exp(latter[0] - highest)
    return (
        highest,
        former[1] * scale_former + latter[1] * scale_latter,
        former[2] * widen(scale_former) + latter[2] * widen(scale_latter),
    )


def finish(carried):
    top_score, totals, accumulated = carried
    return (accumulated / widen(totals), top_score + jnp.log(totals))


def block_grads(queries, grad_attn, log_total, row_delta, query_ids, key_rows, value_rows, key_ids):
    same_image = (query_ids[:, None] == key_ids[None, :])[None]
    q_heads = split_heads(queries)
    g_heads = split_heads(grad_attn)
    scores = (
        jnp.einsum(
            "qhd,khd->hqk", q_heads, split_heads(key_rows), preferred_element_type=jnp.float32
        )
        * SCORE_SCALE
    )
    probabilities = jnp.where(same_image, jnp.exp(scores - log_total[..., None]), 0.0)
    grad_prob = jnp.einsum(
        "qhd,khd->hqk", g_heads, split_heads(value_rows), preferred_element_type=jnp.float32
    )
    dscore = (probabilities * (grad_prob - row_delta[..., None])).astype(jnp.bfloat16)
    grad_query = (
        jnp.einsum(
            "hqk,khd->qhd", dscore, split_heads(key_rows), preferred_element_type=jnp.float32
        ).reshape(queries.shape[0], -1)
        * SCORE_SCALE
    )
    grad_key = (
        jnp.einsum("hqk,qhd->khd", dscore, q_heads, preferred_element_type=jnp.float32).reshape(
            key_rows.shape[0], -1
        )
        * SCORE_SCALE
    )
    grad_value = jnp.einsum(
        "hqk,qhd->khd",
        probabilities.astype(jnp.bfloat16),
        g_heads,
        preferred_element_type=jnp.float32,
    ).reshape(key_rows.shape[0], -1)
    return (grad_query, grad_key, grad_value)


def fetch_weights(w_qkv, w_out, w_up, w_down, gains):
    return (
        lax.all_gather(w_qkv, ("dp", "blk"), axis=0, tiled=True),
        lax.all_gather(w_out, ("dp", "blk"), axis=0, tiled=True),
        lax.all_gather(w_up, ("dp", "blk"), axis=0, tiled=True),
        lax.all_gather(w_down, ("dp", "blk"), axis=0, tiled=True),
        lax.all_gather(gains, ("dp", "blk"), axis=1, tiled=True),
    )


def reduce_grads(grad_terms):
    g_qkv, g_out, g_up, g_down, g_gains = grad_terms
    return (
        lax.psum_scatter(g_qkv, ("dp", "blk"), scatter_dimension=0, tiled=True),
        lax.psum_scatter(g_out, ("dp", "blk"), scatter_dimension=0, tiled=True),
        lax.psum_scatter(g_up, ("dp", "blk"), scatter_dimension=0, tiled=True),
        lax.psum_scatter(g_down, ("dp", "blk"), scatter_dimension=0, tiled=True),
        lax.psum_scatter(g_gains, ("dp", "blk"), scatter_dimension=1, tiled=True),
    )


def contract_rows(left_rows, right_rows):
    return jnp.einsum("ra,rb->ab", left_rows, right_rows, preferred_element_type=jnp.float32)


def row_delta_of(grad_attn, attended):
    product = grad_attn.astype(jnp.float32) * attended
    return product.reshape(product.shape[0], -1, HEAD_DIM).sum(-1).T


def on_device(
    patches, special, image_ids, w_qkv, w_out, w_up, w_down, gains, cot_patches, cot_special
):
    cycle_size = lax.axis_size("blk")
    cycle_index = lax.axis_index("blk")
    width = w_out.shape[1]
    head_count = width // HEAD_DIM
    tok_rows = TOK_MB
    spec_rows = special.shape[0] // MICRO
    ids_group = image_ids.reshape(cycle_size, MICRO, tok_rows)
    spec_ids = jnp.arange(spec_rows, dtype=jnp.int32) // SPECIAL
    row_weight = jnp.concatenate(
        [jnp.ones((tok_rows,), jnp.float32), jnp.full((spec_rows,), 1.0 / cycle_size, jnp.float32)]
    )
    row_weight_low = row_weight.astype(jnp.bfloat16)[:, None]
    summed_terms = None
    shard_terms = None
    out_parts = []
    spec_parts = []
    grad_parts = []
    grad_spec_parts = []
    for micro_index in range(MICRO):
        full_weights = fetch_weights(w_qkv, w_out, w_up, w_down, gains)
        qkv_full, out_full, up_full, down_full, gains_full = full_weights
        gain_rows = gains_full.astype(jnp.float32)
        tokens = jnp.concatenate(
            [
                patches[micro_index * tok_rows : (micro_index + 1) * tok_rows],
                special[micro_index * spec_rows : (micro_index + 1) * spec_rows],
            ],
            0,
        ).astype(jnp.float32)
        ids_flat = ids_group[:, micro_index].reshape(-1)
        patch_ids = lax.dynamic_slice_in_dim(ids_flat, cycle_index * tok_rows, tok_rows)
        normed = norm_rows(tokens, gain_rows[0]).astype(jnp.bfloat16)
        projected = jnp.dot(normed, qkv_full, preferred_element_type=jnp.float32).astype(
            jnp.bfloat16
        )
        patch_q = projected[:tok_rows, :width]
        patch_k = projected[:tok_rows, width : 2 * width]
        patch_v = projected[:tok_rows, 2 * width :]
        spec_q = projected[tok_rows:, :width]
        spec_k = projected[tok_rows:, width : 2 * width]
        spec_v = projected[tok_rows:, 2 * width :]
        start_state = online(
            empty_state(tok_rows, head_count, width), patch_q, patch_ids, spec_k, spec_v, spec_ids
        )
        partial_value = start_state
        key_rows = lax.all_gather(patch_k, "blk", axis=0, tiled=True)
        value_rows = lax.all_gather(patch_v, "blk", axis=0, tiled=True)
        length = key_rows.shape[0]
        key_ids = ids_flat
        blocks = length // tok_rows

        def visit_block(running, block_item):
            return (
                online(running, patch_q, patch_ids, block_item[0], block_item[1], block_item[2]),
                None,
            )

        partial_value, unused = lax.scan(
            visit_block,
            partial_value,
            (
                key_rows.reshape(blocks, tok_rows, -1),
                value_rows.reshape(blocks, tok_rows, -1),
                key_ids.reshape(blocks, tok_rows),
            ),
        )
        spec_top, spec_total, spec_accum = online(
            empty_state(spec_rows, head_count, width), spec_q, spec_ids, patch_k, patch_v, patch_ids
        )
        spec_state = merged((spec_top, spec_total, spec_accum), "blk", combine)
        spec_state = online(spec_state, spec_q, spec_ids, spec_k, spec_v, spec_ids)
        patch_attn, patch_lse = finish(partial_value)
        spec_attn, spec_lse = finish(spec_state)
        attended = jnp.concatenate([patch_attn, spec_attn], 0)
        attended_low = attended.astype(jnp.bfloat16)
        branch = jnp.dot(attended_low, out_full, preferred_element_type=jnp.float32)
        middle = tokens + gain_rows[1] * branch
        normed_mlp = norm_rows(middle, gain_rows[2]).astype(jnp.bfloat16)
        hidden = jnp.dot(normed_mlp, up_full, preferred_element_type=jnp.float32)
        active = jax.nn.gelu(hidden, approximate=False).astype(jnp.bfloat16)
        mlp_out = jnp.dot(active, down_full, preferred_element_type=jnp.float32)
        final = middle + gain_rows[3] * mlp_out
        out_parts.append(final[:tok_rows].astype(jnp.bfloat16))
        spec_parts.append(final[tok_rows:].astype(jnp.bfloat16))
        upstream = jnp.concatenate(
            [
                cot_patches[micro_index * tok_rows : (micro_index + 1) * tok_rows],
                cot_special[micro_index * spec_rows : (micro_index + 1) * spec_rows],
            ],
            0,
        ).astype(jnp.float32)
        grad_mlp = (gain_rows[3] * upstream).astype(jnp.bfloat16)
        g_down = contract_rows(active, grad_mlp * row_weight_low)
        grad_active = jnp.einsum(
            "rd,fd->rf", grad_mlp, down_full, preferred_element_type=jnp.float32
        )
        unused_value, gelu_pull = jax.vjp(
            lambda pre_act: jax.nn.gelu(pre_act, approximate=False), hidden
        )
        grad_hidden = gelu_pull(grad_active)[0].astype(jnp.bfloat16)
        g_up = contract_rows(normed_mlp, grad_hidden * row_weight_low)
        grad_normed_mlp = jnp.einsum(
            "rf,df->rd", grad_hidden, up_full, preferred_element_type=jnp.float32
        )
        unused_value, norm_pull_mlp = jax.vjp(
            lambda rows_in: norm_rows(rows_in, gain_rows[2]), middle
        )
        grad_middle = upstream + norm_pull_mlp(grad_normed_mlp)[0]
        g_ln2 = jnp.sum(row_weight[:, None] * grad_normed_mlp * norm_rows(middle, 1.0), 0)
        g_ls2 = jnp.sum(row_weight[:, None] * upstream * mlp_out, 0)
        g_ls1 = jnp.sum(row_weight[:, None] * grad_middle * branch, 0)
        grad_branch = (gain_rows[1] * grad_middle).astype(jnp.bfloat16)
        g_out = contract_rows(attended_low, grad_branch * row_weight_low)
        grad_attended = jnp.einsum(
            "re,de->rd", grad_branch, out_full, preferred_element_type=jnp.float32
        ).astype(jnp.bfloat16)
        all_delta = row_delta_of(grad_attended, attended)
        patch_delta = all_delta[:, :tok_rows]
        spec_delta = all_delta[:, tok_rows:]
        patch_grad_attn = grad_attended[:tok_rows]
        spec_grad_attn = grad_attended[tok_rows:]
        grad_pq_first, grad_sk_part, grad_sv_part = block_grads(
            patch_q, patch_grad_attn, patch_lse, patch_delta, patch_ids, spec_k, spec_v, spec_ids
        )
        grad_sq_part, grad_pk_local, grad_pv_local = block_grads(
            spec_q, spec_grad_attn, spec_lse, spec_delta, spec_ids, patch_k, patch_v, patch_ids
        )
        sum_sq, sum_sk, sum_sv = (
            lax.psum(grad_sq_part.astype(jnp.bfloat16), "blk").astype(jnp.float32),
            lax.psum(grad_sk_part.astype(jnp.bfloat16), "blk").astype(jnp.float32),
            lax.psum(grad_sv_part.astype(jnp.bfloat16), "blk").astype(jnp.float32),
        )
        grad_sq_own, grad_sk_own, grad_sv_own = block_grads(
            spec_q, spec_grad_attn, spec_lse, spec_delta, spec_ids, spec_k, spec_v, spec_ids
        )

        def cycle_step(hop_index, carried):
            keys_now, values_now, grad_keys, grad_values, grad_queries = carried
            source = (cycle_index - hop_index) % cycle_size
            key_ids = lax.dynamic_slice_in_dim(ids_flat, source * tok_rows, tok_rows)
            term_q, term_k, term_v = block_grads(
                patch_q,
                patch_grad_attn,
                patch_lse,
                patch_delta,
                patch_ids,
                keys_now,
                values_now,
                key_ids,
            )
            keys_now, values_now = from_behind((keys_now, values_now), "blk", 1)
            grad_keys, grad_values = (
                from_behind((grad_keys + term_k).astype(jnp.bfloat16), "blk", 1).astype(
                    jnp.float32
                ),
                from_behind((grad_values + term_v).astype(jnp.bfloat16), "blk", 1).astype(
                    jnp.float32
                ),
            )
            return (keys_now, values_now, grad_keys, grad_values, grad_queries + term_q)

        zero_rows = jnp.zeros((tok_rows, width), jnp.float32)
        unused_keys, unused_values, grad_pk, grad_pv, grad_pq = lax.fori_loop(
            0, cycle_size, cycle_step, (patch_k, patch_v, zero_rows, zero_rows, grad_pq_first)
        )
        grad_pk = grad_pk + grad_pk_local
        grad_pv = grad_pv + grad_pv_local
        grad_patch_qkv = jnp.concatenate([grad_pq, grad_pk, grad_pv], 1)
        grad_spec_qkv = jnp.concatenate(
            [sum_sq + grad_sq_own, sum_sk + grad_sk_own, sum_sv + grad_sv_own], 1
        )
        grad_projected = jnp.concatenate([grad_patch_qkv, grad_spec_qkv], 0).astype(jnp.bfloat16)
        g_qkv = contract_rows(normed, grad_projected * row_weight_low)
        grad_normed = jnp.einsum(
            "re,de->rd", grad_projected, qkv_full, preferred_element_type=jnp.float32
        )
        unused_value, norm_pull_attn = jax.vjp(
            lambda rows_in: norm_rows(rows_in, gain_rows[0]), tokens
        )
        grad_tokens = grad_middle + norm_pull_attn(grad_normed)[0]
        g_ln1 = jnp.sum(row_weight[:, None] * grad_normed * norm_rows(tokens, 1.0), 0)
        grad_parts.append(grad_tokens[:tok_rows])
        grad_spec_parts.append(grad_tokens[tok_rows:])
        grad_terms = (g_qkv, g_out, g_up, g_down, jnp.stack([g_ln1, g_ls1, g_ln2, g_ls2], 0))
        summed_terms = (
            grad_terms
            if summed_terms is None
            else tuple((held + extra for held, extra in zip(summed_terms, grad_terms)))
        )
    shard_terms = reduce_grads(summed_terms)
    return (
        jnp.concatenate(out_parts, 0),
        jnp.concatenate(spec_parts, 0),
        jnp.concatenate(grad_parts, 0),
        jnp.concatenate(grad_spec_parts, 0),
        shard_terms[0],
        shard_terms[1],
        shard_terms[2],
        shard_terms[3],
        shard_terms[4],
    )


PAD_ID = 99


def mm(a, b):
    return jnp.dot(a, b, preferred_element_type=F32)


def mm_nt(a, b):
    return lax.dot_general(a, b, (((1,), (1,)), ((), ())), preferred_element_type=F32)


def mm_tn(a, b):
    return lax.dot_general(a, b, (((0,), (0,)), ((), ())), preferred_element_type=F32)


def here():
    place = lax.axis_index("blk")
    group = lax.axis_index("dp")
    return place, place // 2, place % 2, group // 2, group % 2


def chunk_index(slot, z, y):
    hops, crossed = slot % 4, slot // 4
    source_z = lax.rem(z + 4 - hops, 4)
    source_y = y if not crossed else 1 - y
    return source_z * 2 + source_y


def loop_rows(count, block, body):
    def step(i, carry):
        body(pl.ds(pl.multiple_of(i * block, block), block))
        return carry

    lax.fori_loop(0, count // block, step, 0)


def call(kernel, outs, ins, scratch=(), flops=0, limit=48):
    moved = sum(o.size * o.dtype.itemsize for o in outs) + sum(i.size * i.dtype.itemsize for i in ins)
    return pl.pallas_call(
        kernel,
        out_shape=tuple(outs),
        in_specs=[pl.BlockSpec(memory_space=pltpu.VMEM)] * len(ins),
        out_specs=tuple(pl.BlockSpec(memory_space=pltpu.VMEM) for _ in outs),
        scratch_shapes=list(scratch),
        compiler_params=pltpu.CompilerParams(vmem_limit_bytes=limit * 2**20),
        cost_estimate=pl.CostEstimate(flops=flops, bytes_accessed=moved, transcendentals=0),
        name=kernel.__name__,
    )(*ins)


def sds(*shape, dtype=BF16):
    return jax.ShapeDtypeStruct(shape, dtype)


def pick_pieces(w_qkv, w_up, gains, patches, cots, own, near, far, rows, held):
    place = here()[0]
    held[...] = jnp.zeros_like(held)
    up = w_up[...].astype(F32)
    qkv = w_qkv[...].astype(F32)
    gain = gains[...].astype(F32)
    for b in range(4):
        for d in range(8):
            held[b, 0:24, d * 96 : d * 96 + 96] = up[:, d * 384 + b * 96 : d * 384 + b * 96 + 96]
        for part in range(3):
            held[b, 24:48, part * 192 : part * 192 + 192] = qkv[
                :, part * 768 + b * 192 : part * 768 + b * 192 + 192
            ]
        held[b, 24:28, 576:600] = gain
    own[...] = held[place].astype(BF16)
    near[...] = held[place ^ 1].astype(BF16)
    far[0:48, :] = held[place ^ 2].astype(BF16)
    far[48:96, :] = held[place ^ 3].astype(BF16)
    rows[0:176, :] = patches[...]
    rows[176:352, :] = cots[...]


def join_pieces(own, near, far, near_far, w_out, pack, up_chunk, pack_f, up_f):
    place = here()[0]
    pieces = (
        own[...].astype(F32),
        near[...].astype(F32),
        far[0:48, :].astype(F32),
        near_far[48:96, :].astype(F32),
    )
    for k, piece in enumerate(pieces):
        source = place ^ k
        at = pl.ds(pl.multiple_of(source * 24, 8), 24)
        up_f[at, :] = piece[0:24]
        pack_f[at, 0:576] = piece[24:48, 0:576]
        pack_f[pl.ds(pl.multiple_of(96 + source * 8, 8), 8), 0:576] = jnp.zeros((8, 576), F32)
        pack_f[pl.ds(pl.multiple_of(96 + source * 8, 8), 8), 576:768] = piece[24:32, 576:768]
    out = w_out[...].astype(F32)
    for i in range(4):
        pack_f[i * 24 : i * 24 + 24, 576:768] = out[:, i * 192 : i * 192 + 192]
    pack[...] = pack_f[...].astype(BF16)
    up_chunk[...] = up_f[...].astype(BF16)


def open_pack(*refs):
    chunks, (w_qkv, w_out, gain_rows, out_f, gain_f) = refs[:8], refs[8:]
    _, _, _, z, y = here()
    for slot, chunk in enumerate(chunks):
        d = chunk_index(slot, z, y)
        w_qkv[pl.ds(pl.multiple_of(d * 96, 96), 96), :] = chunk[0:96, 0:576]
        tail = chunk[0:128, 576:768].astype(F32)
        for i in range(4):
            out_f[pl.ds(pl.multiple_of(d * 24, 8), 24), i * 192 : i * 192 + 192] = tail[
                i * 24 : i * 24 + 24
            ]
        gain_f[d] = tail[96:128, :]
    w_out[...] = out_f[...].astype(BF16)
    gain_rows[...] = jnp.zeros_like(gain_rows)
    for d in range(8):
        for b in range(4):
            at = (d * 4 + b) * 24
            gain_rows[0:4, at : at + 24] = gain_f[d, b * 8 : b * 8 + 4, 0:24]


def normalise(rows):
    centre = rows - jnp.mean(rows, -1, keepdims=True)
    spread = jnp.mean(centre * centre, -1, keepdims=True)
    scale = lax.rsqrt(spread + EPSILON)
    return centre * scale, scale


def place_rows(scratch, blocks, tail, first):
    place = here()[0]
    for k, block in enumerate(blocks):
        rows = block[first : first + 176, :].astype(F32)
        source = place ^ k
        for m in range(MICRO):
            scratch[pl.ds(pl.multiple_of(m * 368 + source * 88, 8), 88), :] = rows[m * 88 : m * 88 + 88]
    rows = tail[...].astype(F32)
    for m in range(MICRO):
        scratch[m * 368 + 352 : m * 368 + 368, :] = rows[m * 16 : m * 16 + 16]


def attend(
    rows_0, rows_1, rows_2, rows_3, tail, cot_tail, ids_col, ids_row, w_qkv, gain_rows,
    tokens, cots, normed, projected, probs, attended, rows_f,
):
    place_rows(rows_f, (rows_0, rows_1, rows_2, rows_3), cot_tail, 176)
    cots[...] = rows_f[...].astype(BF16)
    place_rows(rows_f, (rows_0, rows_1, rows_2, rows_3), tail, 0)
    gain = gain_rows[0:1, :]

    def norm_block(at):
        rows = rows_f[at, :]
        tokens[at, :] = rows.astype(BF16)
        normed[at, :] = (normalise(rows)[0] * gain).astype(BF16)

    loop_rows(736, 16, norm_block)
    for m in range(MICRO):
        at = slice(m * 368, m * 368 + 368)
        qkv = mm(normed[at, :], w_qkv[...]).astype(BF16)
        projected[at, :] = qkv
        same = ids_col[at, :] == ids_row[m : m + 1, :]
        heads = []
        for h in range(3):
            q = qkv[:, h * 64 : h * 64 + 64]
            k = qkv[:, 192 + h * 64 : 192 + h * 64 + 64]
            v = qkv[:, 384 + h * 64 : 384 + h * 64 + 64]
            scores = jnp.where(same, mm_nt(q, k) * SCORE_SCALE, MASKED)
            weights = jnp.exp(scores - jnp.max(scores, -1, keepdims=True))
            weights = weights * (1.0 / jnp.sum(weights, -1, keepdims=True))
            weights = weights.astype(BF16)
            probs[m * 3 + h] = weights
            heads.append(mm(weights, v))
        attended[at, :] = jnp.concatenate(heads, -1).astype(BF16)


def order_out(out_0, out_1, out_2, out_3, ordered, mine, out_f):
    place = here()[0]
    for k, part in enumerate((out_0, out_1, out_2, out_3)):
        source = place ^ k
        rows = part[...].astype(F32)
        for d in range(8):
            at = pl.multiple_of((d * 4 + source) * 24, 8)
            out_f[pl.ds(at, 24), :] = rows[d * 24 : d * 24 + 24]
    ordered[...] = out_f[...].astype(BF16)
    mine[...] = out_f[pl.ds(pl.multiple_of(place * 192, 8), 192), :].astype(BF16)


def raise_rows(*refs):
    heads, (w_out, tokens, gain_rows), chunks = refs[0:4], refs[4:7], refs[7:15]
    branch, middle, normed, active, slope, w_up, up_f = refs[15:]
    place, _, _, z, y = here()
    for slot, chunk in enumerate(chunks):
        d = chunk_index(slot, z, y)
        w_up[pl.ds(pl.multiple_of(d * 96, 96), 96), :] = chunk[...]
    for m in range(MICRO):
        at = slice(m * 368, m * 368 + 368)
        total = None
        for k, part in enumerate(heads):
            source = place ^ k
            rows = w_out[pl.ds(pl.multiple_of(source * 192, 16), 192), :]
            term = mm(part[at, :], rows)
            total = term if total is None else total + term
        up_f[at, :] = total
    gain_s, gain_n = gain_rows[1:2, :], gain_rows[2:3, :]

    def norm_block(at):
        a = up_f[at, :]
        branch[at, :] = a.astype(BF16)
        rows = tokens[at, :].astype(F32) + gain_s * a
        middle[at, :] = rows
        normed[at, :] = (normalise(rows)[0] * gain_n).astype(BF16)

    loop_rows(736, 16, norm_block)
    for m in range(MICRO):
        at = slice(m * 368, m * 368 + 368)
        up_f[at, :] = mm(normed[at, :], w_up[...])

    def gelu_block(at):
        u = up_f[at, :]
        half = 0.5 + 0.5 * lax.erf(u * 0.7071067811865476)
        active[at, :] = (u * half).astype(BF16)
        slope[at, :] = half + u * (0.3989422804014327 * jnp.exp(-0.5 * u * u))

    loop_rows(736, 16, gelu_block)


def lower_rows(*refs):
    (active, slope, cots, gain_rows, w_up), chunks = refs[:5], refs[5:13]
    w_down, grad_mlp, grad_hidden, away, kept, work = refs[13:]
    _, _, core, z, y = here()
    for slot, chunk in enumerate(chunks):
        d = chunk_index(slot, z, y)
        w_down[pl.ds(pl.multiple_of(d * 96, 96), 96), :] = chunk[...]
    gain = gain_rows[3:4, :]

    def scale_block(at):
        grad_mlp[at, :] = (gain * cots[at, :].astype(F32)).astype(BF16)

    loop_rows(736, 16, scale_block)
    for m in range(MICRO):
        at = slice(m * 368, m * 368 + 368)
        grad = mm_nt(grad_mlp[at, :], w_down[...])
        grad_hidden[at, :] = (slope[at, :] * grad).astype(BF16)
        work[m] = mm_nt(grad_hidden[at, :], w_up[...])
    away[...] = work[1 - core].astype(BF16)
    kept[...] = work[core]


def split_rows(pieces, place, away, kept):
    away[0:208, :] = pieces[place ^ 1].astype(BF16)
    away[208:416, :] = pieces[place ^ 3].astype(BF16)
    kept[0:208, :] = pieces[place]
    kept[208:416, :] = pieces[place ^ 2]


def cut_rows(rows_f, pieces):
    for b in range(4):
        for m in range(MICRO):
            pieces[b, m * 104 : m * 104 + 88, :] = rows_f[m * 368 + b * 88 : m * 368 + b * 88 + 88, :]
            pieces[b, m * 104 + 88 : m * 104 + 104, :] = rows_f[m * 368 + 352 : m * 368 + 368, :]


def halve(grad_f, y, away, kept, rows):
    for zz in range(4):
        other = pl.ds(pl.multiple_of((zz * 2 + 1 - y) * rows, 8), rows)
        ours = pl.ds(pl.multiple_of((zz * 2 + y) * rows, 8), rows)
        away[zz] = grad_f[other, :].astype(BF16)
        kept[zz] = grad_f[ours, :]


def mlp_grads(
    active, normed, grad_mlp, grad_hidden, w_down, cots,
    down_away, down_kept, up_away, up_kept, rows_away, rows_kept, scale_grad, work, pieces,
):
    place, _, _, _, y = here()
    work[0:768, :] = mm_tn(active[...], grad_mlp[...])
    halve(work, y, down_away, down_kept, 96)
    work[0:768, :] = mm_tn(normed[...], grad_hidden[...])
    halve(work, y, up_away, up_kept, 96)
    for m in range(MICRO):
        at = slice(m * 368, m * 368 + 368)
        work[at, :] = mm(active[at, :], w_down[...])
    scale_grad[...] = jnp.zeros_like(scale_grad)

    def sum_block(at):
        scale_grad[...] += (cots[at, :].astype(F32) * work[at, :]).reshape(2, 8, 768).sum(0)

    loop_rows(736, 16, sum_block)
    cut_rows(work, pieces)
    split_rows(pieces, place, rows_away, rows_kept)


def add_rows(kept, came, total):
    total[...] = (kept[...] + came[...].astype(F32)).astype(BF16)


def add_pair(here_rows, came, total):
    total[...] = (here_rows[...].astype(F32) + came[...].astype(F32)).astype(BF16)


def attend_back(
    sum_own, sum_near, middle, cots, branch, tokens, gain_rows, w_mine, w_qkv, projected, probs,
    head_0, head_1, head_2, head_3, normed, targets, scale_grad_mlp,
    grad_rows, away, kept, rows_away, rows_kept,
    work, grad_branch, grad_heads, grad_qkv, grad_mid, extra, pieces, scale_grad,
):
    place, _, core, _, y = here()
    for m in range(MICRO):
        at = slice(m * 368, m * 368 + 368)

        @pl.when(core == m)
        def _():
            work[at, :] = sum_own[...].astype(F32)

        @pl.when(core != m)
        def _():
            work[at, :] = sum_near[...].astype(F32)

    scale_grad[...] = jnp.zeros_like(scale_grad)
    gain_s, gain_n = gain_rows[1:2, :], gain_rows[2:3, :]

    def norm_block(at):
        unit, scale = normalise(middle[at, :])
        grad = work[at, :]
        pulled = grad * gain_n
        pulled = pulled - jnp.mean(pulled, -1, keepdims=True) - unit * jnp.mean(
            pulled * unit, -1, keepdims=True
        )
        through = cots[at, :].astype(F32) + scale * pulled
        grad_mid[at, :] = through
        grad_branch[at, :] = (gain_s * through).astype(BF16)
        scale_grad[1] += (through * branch[at, :].astype(F32)).reshape(2, 8, 768).sum(0)
        scale_grad[2] += (grad * unit).reshape(2, 8, 768).sum(0)

    loop_rows(736, 16, norm_block)
    for m in range(MICRO):
        for part, first in ((0, place * 88), (88, 352)):
            rows = 88 if part == 0 else 16
            grad_rows[m * 104 + part : m * 104 + part + rows, :] = grad_mid[
                pl.ds(pl.multiple_of(m * 368 + first, 8), rows), :
            ]
    for m in range(MICRO):
        at = slice(m * 368, m * 368 + 368)
        grad_heads[at, :] = mm_nt(grad_branch[at, :], w_mine[...]).astype(BF16)
        qkv = projected[at, :]
        g_heads = grad_heads[at, :]
        grads = [[], [], []]
        for h in range(3):
            q = qkv[:, h * 64 : h * 64 + 64]
            k = qkv[:, 192 + h * 64 : 192 + h * 64 + 64]
            v = qkv[:, 384 + h * 64 : 384 + h * 64 + 64]
            g = g_heads[:, h * 64 : h * 64 + 64]
            weights = probs[m * 3 + h]
            grad_prob = mm_nt(g, v)
            wide = weights.astype(F32)
            moved = wide * grad_prob
            delta = jnp.sum(moved, -1, keepdims=True)
            grad_score = (moved - wide * delta).astype(BF16)
            grads[0].append(mm(grad_score, k) * SCORE_SCALE)
            grads[1].append(mm_tn(grad_score, q) * SCORE_SCALE)
            grads[2].append(mm_tn(weights, g))
        grad_qkv[at, :] = jnp.concatenate(grads[0] + grads[1] + grads[2], -1).astype(BF16)
    for m in range(MICRO):
        at = slice(m * 368, m * 368 + 368)
        work[at, :] = mm_nt(grad_qkv[at, :], w_qkv[...])

    def sum_block(at):
        unit, _ = normalise(tokens[at, :].astype(F32))
        scale_grad[0] += (work[at, :] * unit).reshape(2, 8, 768).sum(0)

    loop_rows(736, 16, sum_block)
    cut_rows(work, pieces)
    split_rows(pieces, place, rows_away, rows_kept)
    grad_mid[0:768, 0:576] = mm_tn(normed[...], grad_qkv[...])
    chosen = None
    for k, part in enumerate((head_0, head_1, head_2, head_3)):
        source = place ^ k
        index = lax.broadcasted_iota(jnp.int32, (192, 192), 0) + source * 192
        pick = jnp.where(index == targets[...], 1.0, 0.0).astype(BF16)
        term = mm(part[...], pick)
        chosen = term if chosen is None else chosen + term
    extra[...] = mm_tn(chosen.astype(BF16), grad_branch[...])
    rows = [
        jnp.sum(scale_grad[0], 0, keepdims=True),
        0.25 * jnp.sum(scale_grad[1], 0, keepdims=True),
        0.25 * jnp.sum(scale_grad[2], 0, keepdims=True),
        jnp.sum(scale_grad_mlp[...], 0, keepdims=True),
    ]
    for d in range(8):
        base = d * 112
        work[base : base + 96, 0:576] = grad_mid[d * 96 : d * 96 + 96, 0:576]
        for i in range(4):
            work[base + i * 24 : base + i * 24 + 24, 576:768] = extra[
                d * 24 : d * 24 + 24, i * 192 : i * 192 + 192
            ]
        work[base + 96 : base + 112, :] = jnp.zeros((16, 768), F32)
        for i in range(4):
            work[base + 96 + i : base + 97 + i, 0:96] = rows[i][:, d * 96 : d * 96 + 96]
    halve(work, y, away, kept, 112)


def sum_y(kept, came, own, send_1, send_2, send_3):
    _, _, _, z, _ = here()
    own[...] = kept[z] + came[z].astype(F32)
    for k, send in ((1, send_1), (2, send_2), (3, send_3)):
        there = lax.rem(z + k, 4)
        send[...] = (kept[there] + came[there].astype(F32)).astype(BF16)


def sum_z(own, came_1, came_2, came_3, total):
    total[...] = (
        own[...]
        + came_1[...].astype(F32)
        + came_2[...].astype(F32)
        + came_3[...].astype(F32)
    )


def add_pieces(kept_m, came_m, kept_h, came_h, stay, go):
    for i, (kept, came) in enumerate(((kept_m, came_m), (kept_h, came_h))):
        stay[i * 208 : i * 208 + 208, :] = kept[0:208, :] + came[0:208, :].astype(F32)
        go[i * 208 : i * 208 + 208, :] = (kept[208:416, :] + came[208:416, :].astype(F32)).astype(BF16)


def finish_rows(
    stay, came, middle, grad_rows, patches, tail, gain_rows,
    out_patches, out_special, grad_patches, grad_special,
):
    place = here()[0]
    own = patches[...].astype(F32)
    rest = tail[...].astype(F32)
    outs, out_tails = [], []
    for m in range(MICRO):
        for part, first in ((0, place * 88), (88, 352)):
            count = 88 if part == 0 else 16
            at = slice(m * 104 + part, m * 104 + part + count)
            far_at = slice(208 + m * 104 + part, 208 + m * 104 + part + count)
            mid = middle[pl.ds(pl.multiple_of(m * 368 + first, 8), count), :]
            final = mid + gain_rows[3:4, :] * (stay[at, :] + came[at, :].astype(F32))
            (outs if part == 0 else out_tails).append(final)
            rows = own[m * 88 : m * 88 + 88] if part == 0 else rest[m * 16 : m * 16 + 16]
            unit, scale = normalise(rows)
            pulled = gain_rows[0:1, :] * (stay[far_at, :] + came[far_at, :].astype(F32))
            pulled = pulled - jnp.mean(pulled, -1, keepdims=True) - unit * jnp.mean(
                pulled * unit, -1, keepdims=True
            )
            grad = grad_rows[at, :] + scale * pulled
            if part == 0:
                grad_patches[m * 88 : m * 88 + 88, :] = grad
            else:
                grad_special[m * 10 : m * 10 + 10, :] = grad[0:10]
    out_patches[...] = jnp.concatenate(outs, 0).astype(BF16)
    out_special[...] = jnp.concatenate([part[0:10] for part in out_tails], 0).astype(BF16)


def pick_grads(up, pack, own, near, far, grad_out, held):
    place = here()[0]
    for b in range(4):
        held[b, 0:24, :] = up[b * 24 : b * 24 + 24, :]
        held[b, 24:48, 0:576] = pack[b * 24 : b * 24 + 24, 0:576]
        held[b, 24:48, 576:768] = jnp.zeros((24, 192), F32)
        held[b, 24:28, 576:600] = pack[96:100, b * 24 : b * 24 + 24]
        grad_out[:, b * 192 : b * 192 + 192] = pack[b * 24 : b * 24 + 24, 576:768]
    own[...] = held[place]
    near[...] = held[place ^ 1].astype(BF16)
    far[0:48, :] = held[place ^ 2].astype(BF16)
    far[48:96, :] = held[place ^ 3].astype(BF16)


def join_grads(own, near, far, near_far, grad_qkv, grad_up, grad_gains, held):
    place = here()[0]
    held[place] = own[...]
    held[place ^ 1] = near[...].astype(F32)
    held[place ^ 2] = far[0:48, :].astype(F32)
    held[place ^ 3] = near_far[48:96, :].astype(F32)
    gains = None
    for b in range(4):
        for d in range(8):
            at = d * 384 + b * 96
            grad_up[:, at : at + 96] = held[b, 0:24, d * 96 : d * 96 + 96]
        for part in range(3):
            at = part * 768 + b * 192
            grad_qkv[:, at : at + 192] = held[b, 24:48, part * 192 : part * 192 + 192]
        term = held[b, 24:28, 576:600]
        gains = term if gains is None else gains + term
    grad_gains[...] = gains


def send(rows, axis, step):
    pairs = []
    for group in range(8):
        z, y = group // 2, group % 2
        for place in range(4):
            target = {
                "core": (group, place ^ 1),
                "x": (group, place ^ 2),
                "y": (z * 2 + 1 - y, place),
                "z": ((z + step) % 4 * 2 + y, place),
            }[axis]
            pairs.append((group * 4 + place, target[0] * 4 + target[1]))
    return lax.ppermute(rows, ("dp", "blk"), pairs)


def gather_dp(chunk):
    along_z = [chunk] + [send(chunk, "z", k) for k in (1, 2, 3)]
    return along_z + [send(part, "y", 1) for part in along_z]


def gather_blk(rows):
    near = send(rows, "core", 1)
    far = send(rows, "x", 1)
    return [rows, near, far, send(far, "core", 1)]


def scatter_dp(away, kept, rows):
    came = send(away, "y", 1)
    own, *parts = call(sum_y, [sds(rows, 768, dtype=F32)] + [sds(rows, 768)] * 3, [kept, came])
    came = [send(part, "z", k) for k, part in zip((1, 2, 3), parts)]
    return call(sum_z, [sds(rows, 768, dtype=F32)], [own, *came])[0]


def pad_tail(rows):
    return jnp.pad(rows.reshape(2, 10, 768), ((0, 0), (0, 6), (0, 0))).reshape(32, 768)


def on_device_split(
    patches, special, image_ids, w_qkv, w_out, w_up, w_down, gains, cot_patches, cot_special
):
    place = lax.axis_index("blk")
    tail, cot_tail = pad_tail(special), pad_tail(cot_special)
    spec_ids = jnp.concatenate(
        [jnp.arange(10, dtype=jnp.int32) // SPECIAL, jnp.full((6,), PAD_ID, jnp.int32)]
    )
    ids = image_ids.reshape(4, 2, 88).transpose(1, 0, 2).reshape(2, 352)
    ids_row = jnp.concatenate([ids, jnp.broadcast_to(spec_ids, (2, 16))], 1)
    ids_col = ids_row.reshape(736, 1)
    column = jnp.arange(192, dtype=jnp.int32)
    targets = (column + column // 24 * 72 + place * 24).reshape(1, 192)

    own, near, far, rows = call(
        pick_pieces,
        [sds(48, 768), sds(48, 768), sds(96, 768), sds(352, 768)],
        [w_qkv, w_up, gains, patches, cot_patches],
        [pltpu.VMEM((4, 48, 768), F32)],
    )
    came_far = send(far, "x", 1)
    came_near, came_near_far = send(near, "core", 1), send(came_far, "core", 1)
    row_parts = gather_blk(rows)
    down_chunks = gather_dp(w_down)
    pack, up_chunk = call(
        join_pieces,
        [sds(128, 768), sds(96, 768)],
        [own, came_near, came_far, came_near_far, w_out],
        [pltpu.VMEM((128, 768), F32), pltpu.VMEM((96, 768), F32)],
    )
    pack_chunks = gather_dp(pack)
    up_chunks = gather_dp(up_chunk)
    qkv_full, out_part, gain_rows = call(
        open_pack,
        [sds(768, 576), sds(192, 768), sds(8, 768, dtype=F32)],
        pack_chunks,
        [pltpu.VMEM((192, 768), F32), pltpu.VMEM((8, 32, 192), F32)],
    )
    out_parts = gather_blk(out_part)
    tokens, cots, normed, projected, probs, attended = call(
        attend,
        [
            sds(736, 768), sds(736, 768), sds(736, 768), sds(736, 576),
            sds(6, 368, 368), sds(736, 192),
        ],
        [*row_parts, tail, cot_tail, ids_col, ids_row, qkv_full, gain_rows],
        [pltpu.VMEM((736, 768), F32)],
        flops=2 * 736 * 768 * 576 + 4 * 6 * 368 * 368 * 64,
    )
    heads = gather_blk(attended)
    out_full, out_mine = call(
        order_out, [sds(768, 768), sds(192, 768)], out_parts, [pltpu.VMEM((768, 768), F32)]
    )
    branch, middle, normed_mlp, active, slope, up_full = call(
        raise_rows,
        [
            sds(736, 768), sds(736, 768, dtype=F32), sds(736, 768), sds(736, 768),
            sds(736, 768, dtype=F32), sds(768, 768),
        ],
        [*heads, out_full, tokens, gain_rows, *up_chunks],
        [pltpu.VMEM((736, 768), F32)],
        flops=4 * 736 * 768 * 768,
    )
    down_full, grad_mlp, grad_hidden, sum_away, sum_kept = call(
        lower_rows,
        [sds(768, 768), sds(736, 768), sds(736, 768), sds(368, 768), sds(368, 768, dtype=F32)],
        [active, slope, cots, gain_rows, up_full, *down_chunks],
        [pltpu.VMEM((2, 368, 768), F32)],
        flops=4 * 736 * 768 * 768,
    )
    sum_came = send(sum_away, "core", 1)
    chip_sum = call(add_rows, [sds(368, 768)], [sum_kept, sum_came])[0]
    chip_came = send(chip_sum, "x", 1)
    half = [sds(4, 96, 768), sds(4, 96, 768, dtype=F32)]
    rows_split = [sds(416, 768), sds(416, 768, dtype=F32)]
    down_away, down_kept, up_away, up_kept, m_away, m_kept, scale_mlp = call(
        mlp_grads,
        [*half, *half, *rows_split, sds(8, 768, dtype=F32)],
        [active, normed_mlp, grad_mlp, grad_hidden, down_full, cots],
        [pltpu.VMEM((768, 768), F32), pltpu.VMEM((4, 208, 768), F32)],
        flops=6 * 736 * 768 * 768,
    )
    grad_down = scatter_dp(down_away, down_kept, 96)
    grad_up_rows = scatter_dp(up_away, up_kept, 96)
    sum_own = call(add_pair, [sds(368, 768)], [chip_sum, chip_came])[0]
    sum_near = send(sum_own, "core", 1)
    m_came = send(m_away, "core", 1)
    grad_rows, q_away, q_kept, h_away, h_kept = call(
        attend_back,
        [
            sds(208, 768, dtype=F32), sds(4, 112, 768), sds(4, 112, 768, dtype=F32), *rows_split,
        ],
        [
            sum_own, sum_near, middle, cots, branch, tokens, gain_rows, out_mine, qkv_full,
            projected, probs, *heads, normed, targets, scale_mlp,
        ],
        [
            pltpu.VMEM((896, 768), F32), pltpu.VMEM((736, 768), BF16), pltpu.VMEM((736, 192), BF16),
            pltpu.VMEM((736, 576), BF16), pltpu.VMEM((768, 768), F32), pltpu.VMEM((192, 768), F32),
            pltpu.VMEM((4, 208, 768), F32), pltpu.VMEM((3, 8, 768), F32),
        ],
        flops=4 * 736 * 768 * 576 + 4 * 736 * 768 * 192 + 10 * 6 * 368 * 368 * 64,
    )
    h_came = send(h_away, "core", 1)
    stay, go = call(
        add_pieces, [sds(416, 768, dtype=F32), sds(416, 768)], [m_kept, m_came, h_kept, h_came]
    )
    far_rows = send(go, "x", 1)
    pack_rows = scatter_dp(q_away, q_kept, 112)
    own, near, far, grad_out = call(
        pick_grads,
        [sds(48, 768, dtype=F32), sds(48, 768), sds(96, 768), sds(24, 768, dtype=F32)],
        [grad_up_rows, pack_rows],
        [pltpu.VMEM((4, 48, 768), F32)],
    )
    came_far = send(far, "x", 1)
    came_near, came_near_far = send(near, "core", 1), send(came_far, "core", 1)
    out_patches, out_special, grad_patches, grad_special = call(
        finish_rows,
        [
            sds(176, 768), sds(20, 768), sds(176, 768, dtype=F32), sds(20, 768, dtype=F32),
        ],
        [stay, far_rows, middle, grad_rows, patches, tail, gain_rows],
    )
    grad_qkv, grad_up, grad_gains = call(
        join_grads,
        [sds(24, 2304, dtype=F32), sds(24, 3072, dtype=F32), sds(4, 24, dtype=F32)],
        [own, came_near, came_far, came_near_far],
        [pltpu.VMEM((4, 48, 768), F32)],
    )
    return (
        out_patches, out_special, grad_patches, grad_special,
        grad_qkv, grad_out, grad_up, grad_down, grad_gains,
    )


def solution(mesh):
    placed = (
        P(("dp", "blk"), None),
        P("dp", None),
        P("dp"),
        P(("dp", "blk"), None),
        P(("dp", "blk"), None),
        P(("dp", "blk"), None),
        P(("dp", "blk"), None),
        P(None, ("dp", "blk")),
        P(("dp", "blk"), None),
        P("dp", None),
    )
    whole = dict(mesh.shape) != {"dp": 8, "blk": 4}
    return jax.shard_map(
        on_device if whole else on_device_split,
        mesh=mesh,
        in_specs=placed,
        out_specs=(
            P(("dp", "blk"), None),
            P("dp", None),
            P(("dp", "blk"), None),
            P("dp", None),
            P(("dp", "blk"), None),
            P(("dp", "blk"), None),
            P(("dp", "blk"), None),
            P(("dp", "blk"), None),
            P(None, ("dp", "blk")),
        ),
        check_vma=False,
    )
```

```python
import jax
import jax.numpy as jnp
from jax import lax
from jax.experimental import pallas as pl
from jax.experimental.pallas import tpu as pltpu
from jax.sharding import PartitionSpec as P

HEAD_DIM = 64
SPECIAL = 5
MICRO = 2
TOK_MB = 88

SCORE_SCALE = 0.125
MASKED = -1e30
EPSILON = 1e-06

BF16 = jnp.bfloat16
F32 = jnp.float32


def merged(shard, axis, combine):
    everything = jax.tree.map(
        lambda part, kind: lax.all_gather(part.astype(kind), axis),
        shard,
        (jnp.bfloat16, jnp.bfloat16, jnp.bfloat16),
    )

    def take(k):
        return jax.tree.map(lambda part, own: part[k].astype(own.dtype), everything, shard)

    return lax.fori_loop(
        1, lax.axis_size(axis), lambda k, so_far: combine(so_far, take(k)), take(0)
    )


def from_behind(shard, axis, by):
    peers = lax.axis_size(axis)
    return lax.ppermute(shard, axis, [(i, (i + by) % peers) for i in range(peers)])


def norm_rows(values, gain_row):
    centre = values - jnp.mean(values, -1, keepdims=True)
    spread = jnp.mean(centre * centre, -1, keepdims=True)
    return centre * lax.rsqrt(spread + EPSILON) * gain_row


def split_heads(matrix):
    return matrix.reshape(matrix.shape[0], -1, HEAD_DIM)


def widen(per_head):
    return jnp.repeat(per_head.T, HEAD_DIM, axis=1)


def empty_state(length, head_count, feature_width):
    return (
        jnp.full((head_count, length), MASKED, jnp.float32),
        jnp.zeros((head_count, length), jnp.float32),
        jnp.zeros((length, feature_width), jnp.float32),
    )


def online(carried, queries, query_ids, key_rows, value_rows, key_ids):
    top_score, totals, accumulated = carried
    same_image = (query_ids[:, None] == key_ids[None, :])[None]
    scores = (
        jnp.einsum(
            "qhd,khd->hqk",
            split_heads(queries),
            split_heads(key_rows),
            preferred_element_type=jnp.float32,
        )
        * SCORE_SCALE
    )
    scores = jnp.where(same_image, scores, MASKED)
    new_top = jnp.maximum(top_score, jnp.max(scores, -1))
    weights = jnp.where(same_image, jnp.exp(scores - new_top[..., None]), 0.0)
    factor = jnp.exp(top_score - new_top)
    totals = totals * factor + jnp.sum(weights, -1)
    mixture = jnp.einsum(
        "hqk,khd->qhd",
        weights.astype(jnp.bfloat16),
        split_heads(value_rows),
        preferred_element_type=jnp.float32,
    )
    accumulated = accumulated * widen(factor) + mixture.reshape(accumulated.shape)
    return (new_top, totals, accumulated)


def combine(former, latter):
    highest = jnp.maximum(former[0], latter[0])
    scale_former = jnp.exp(former[0] - highest)
    scale_latter = jnp.exp(latter[0] - highest)
    return (
        highest,
        former[1] * scale_former + latter[1] * scale_latter,
        former[2] * widen(scale_former) + latter[2] * widen(scale_latter),
    )


def finish(carried):
    top_score, totals, accumulated = carried
    return (accumulated / widen(totals), top_score + jnp.log(totals))


def block_grads(queries, grad_attn, log_total, row_delta, query_ids, key_rows, value_rows, key_ids):
    same_image = (query_ids[:, None] == key_ids[None, :])[None]
    q_heads = split_heads(queries)
    g_heads = split_heads(grad_attn)
    scores = (
        jnp.einsum(
            "qhd,khd->hqk", q_heads, split_heads(key_rows), preferred_element_type=jnp.float32
        )
        * SCORE_SCALE
    )
    probabilities = jnp.where(same_image, jnp.exp(scores - log_total[..., None]), 0.0)
    grad_prob = jnp.einsum(
        "qhd,khd->hqk", g_heads, split_heads(value_rows), preferred_element_type=jnp.float32
    )
    dscore = (probabilities * (grad_prob - row_delta[..., None])).astype(jnp.bfloat16)
    grad_query = (
        jnp.einsum(
            "hqk,khd->qhd", dscore, split_heads(key_rows), preferred_element_type=jnp.float32
        ).reshape(queries.shape[0], -1)
        * SCORE_SCALE
    )
    grad_key = (
        jnp.einsum("hqk,qhd->khd", dscore, q_heads, preferred_element_type=jnp.float32).reshape(
            key_rows.shape[0], -1
        )
        * SCORE_SCALE
    )
    grad_value = jnp.einsum(
        "hqk,qhd->khd",
        probabilities.astype(jnp.bfloat16),
        g_heads,
        preferred_element_type=jnp.float32,
    ).reshape(key_rows.shape[0], -1)
    return (grad_query, grad_key, grad_value)


def fetch_weights(w_qkv, w_out, w_up, w_down, gains):
    return (
        lax.all_gather(w_qkv, ("dp", "blk"), axis=0, tiled=True),
        lax.all_gather(w_out, ("dp", "blk"), axis=0, tiled=True),
        lax.all_gather(w_up, ("dp", "blk"), axis=0, tiled=True),
        lax.all_gather(w_down, ("dp", "blk"), axis=0, tiled=True),
        lax.all_gather(gains, ("dp", "blk"), axis=1, tiled=True),
    )


def reduce_grads(grad_terms):
    g_qkv, g_out, g_up, g_down, g_gains = grad_terms
    return (
        lax.psum_scatter(g_qkv, ("dp", "blk"), scatter_dimension=0, tiled=True),
        lax.psum_scatter(g_out, ("dp", "blk"), scatter_dimension=0, tiled=True),
        lax.psum_scatter(g_up, ("dp", "blk"), scatter_dimension=0, tiled=True),
        lax.psum_scatter(g_down, ("dp", "blk"), scatter_dimension=0, tiled=True),
        lax.psum_scatter(g_gains, ("dp", "blk"), scatter_dimension=1, tiled=True),
    )


def contract_rows(left_rows, right_rows):
    return jnp.einsum("ra,rb->ab", left_rows, right_rows, preferred_element_type=jnp.float32)


def row_delta_of(grad_attn, attended):
    product = grad_attn.astype(jnp.float32) * attended
    return product.reshape(product.shape[0], -1, HEAD_DIM).sum(-1).T


def on_device(
    patches, special, image_ids, w_qkv, w_out, w_up, w_down, gains, cot_patches, cot_special
):
    cycle_size = lax.axis_size("blk")
    cycle_index = lax.axis_index("blk")
    width = w_out.shape[1]
    head_count = width // HEAD_DIM
    tok_rows = TOK_MB
    spec_rows = special.shape[0] // MICRO
    ids_group = image_ids.reshape(cycle_size, MICRO, tok_rows)
    spec_ids = jnp.arange(spec_rows, dtype=jnp.int32) // SPECIAL
    row_weight = jnp.concatenate(
        [jnp.ones((tok_rows,), jnp.float32), jnp.full((spec_rows,), 1.0 / cycle_size, jnp.float32)]
    )
    row_weight_low = row_weight.astype(jnp.bfloat16)[:, None]
    summed_terms = None
    shard_terms = None
    out_parts = []
    spec_parts = []
    grad_parts = []
    grad_spec_parts = []
    for micro_index in range(MICRO):
        full_weights = fetch_weights(w_qkv, w_out, w_up, w_down, gains)
        qkv_full, out_full, up_full, down_full, gains_full = full_weights
        gain_rows = gains_full.astype(jnp.float32)
        tokens = jnp.concatenate(
            [
                patches[micro_index * tok_rows : (micro_index + 1) * tok_rows],
                special[micro_index * spec_rows : (micro_index + 1) * spec_rows],
            ],
            0,
        ).astype(jnp.float32)
        ids_flat = ids_group[:, micro_index].reshape(-1)
        patch_ids = lax.dynamic_slice_in_dim(ids_flat, cycle_index * tok_rows, tok_rows)
        normed = norm_rows(tokens, gain_rows[0]).astype(jnp.bfloat16)
        projected = jnp.dot(normed, qkv_full, preferred_element_type=jnp.float32).astype(
            jnp.bfloat16
        )
        patch_q = projected[:tok_rows, :width]
        patch_k = projected[:tok_rows, width : 2 * width]
        patch_v = projected[:tok_rows, 2 * width :]
        spec_q = projected[tok_rows:, :width]
        spec_k = projected[tok_rows:, width : 2 * width]
        spec_v = projected[tok_rows:, 2 * width :]
        start_state = online(
            empty_state(tok_rows, head_count, width), patch_q, patch_ids, spec_k, spec_v, spec_ids
        )
        partial_value = start_state
        key_rows = lax.all_gather(patch_k, "blk", axis=0, tiled=True)
        value_rows = lax.all_gather(patch_v, "blk", axis=0, tiled=True)
        length = key_rows.shape[0]
        key_ids = ids_flat
        blocks = length // tok_rows

        def visit_block(running, block_item):
            return (
                online(running, patch_q, patch_ids, block_item[0], block_item[1], block_item[2]),
                None,
            )

        partial_value, unused = lax.scan(
            visit_block,
            partial_value,
            (
                key_rows.reshape(blocks, tok_rows, -1),
                value_rows.reshape(blocks, tok_rows, -1),
                key_ids.reshape(blocks, tok_rows),
            ),
        )
        spec_top, spec_total, spec_accum = online(
            empty_state(spec_rows, head_count, width), spec_q, spec_ids, patch_k, patch_v, patch_ids
        )
        spec_state = merged((spec_top, spec_total, spec_accum), "blk", combine)
        spec_state = online(spec_state, spec_q, spec_ids, spec_k, spec_v, spec_ids)
        patch_attn, patch_lse = finish(partial_value)
        spec_attn, spec_lse = finish(spec_state)
        attended = jnp.concatenate([patch_attn, spec_attn], 0)
        attended_low = attended.astype(jnp.bfloat16)
        branch = jnp.dot(attended_low, out_full, preferred_element_type=jnp.float32)
        middle = tokens + gain_rows[1] * branch
        normed_mlp = norm_rows(middle, gain_rows[2]).astype(jnp.bfloat16)
        hidden = jnp.dot(normed_mlp, up_full, preferred_element_type=jnp.float32)
        active = jax.nn.gelu(hidden, approximate=False).astype(jnp.bfloat16)
        mlp_out = jnp.dot(active, down_full, preferred_element_type=jnp.float32)
        final = middle + gain_rows[3] * mlp_out
        out_parts.append(final[:tok_rows].astype(jnp.bfloat16))
        spec_parts.append(final[tok_rows:].astype(jnp.bfloat16))
        upstream = jnp.concatenate(
            [
                cot_patches[micro_index * tok_rows : (micro_index + 1) * tok_rows],
                cot_special[micro_index * spec_rows : (micro_index + 1) * spec_rows],
            ],
            0,
        ).astype(jnp.float32)
        grad_mlp = (gain_rows[3] * upstream).astype(jnp.bfloat16)
        g_down = contract_rows(active, grad_mlp * row_weight_low)
        grad_active = jnp.einsum(
            "rd,fd->rf", grad_mlp, down_full, preferred_element_type=jnp.float32
        )
        unused_value, gelu_pull = jax.vjp(
            lambda pre_act: jax.nn.gelu(pre_act, approximate=False), hidden
        )
        grad_hidden = gelu_pull(grad_active)[0].astype(jnp.bfloat16)
        g_up = contract_rows(normed_mlp, grad_hidden * row_weight_low)
        grad_normed_mlp = jnp.einsum(
            "rf,df->rd", grad_hidden, up_full, preferred_element_type=jnp.float32
        )
        unused_value, norm_pull_mlp = jax.vjp(
            lambda rows_in: norm_rows(rows_in, gain_rows[2]), middle
        )
        grad_middle = upstream + norm_pull_mlp(grad_normed_mlp)[0]
        g_ln2 = jnp.sum(row_weight[:, None] * grad_normed_mlp * norm_rows(middle, 1.0), 0)
        g_ls2 = jnp.sum(row_weight[:, None] * upstream * mlp_out, 0)
        g_ls1 = jnp.sum(row_weight[:, None] * grad_middle * branch, 0)
        grad_branch = (gain_rows[1] * grad_middle).astype(jnp.bfloat16)
        g_out = contract_rows(attended_low, grad_branch * row_weight_low)
        grad_attended = jnp.einsum(
            "re,de->rd", grad_branch, out_full, preferred_element_type=jnp.float32
        ).astype(jnp.bfloat16)
        all_delta = row_delta_of(grad_attended, attended)
        patch_delta = all_delta[:, :tok_rows]
        spec_delta = all_delta[:, tok_rows:]
        patch_grad_attn = grad_attended[:tok_rows]
        spec_grad_attn = grad_attended[tok_rows:]
        grad_pq_first, grad_sk_part, grad_sv_part = block_grads(
            patch_q, patch_grad_attn, patch_lse, patch_delta, patch_ids, spec_k, spec_v, spec_ids
        )
        grad_sq_part, grad_pk_local, grad_pv_local = block_grads(
            spec_q, spec_grad_attn, spec_lse, spec_delta, spec_ids, patch_k, patch_v, patch_ids
        )
        sum_sq, sum_sk, sum_sv = (
            lax.psum(grad_sq_part.astype(jnp.bfloat16), "blk").astype(jnp.float32),
            lax.psum(grad_sk_part.astype(jnp.bfloat16), "blk").astype(jnp.float32),
            lax.psum(grad_sv_part.astype(jnp.bfloat16), "blk").astype(jnp.float32),
        )
        grad_sq_own, grad_sk_own, grad_sv_own = block_grads(
            spec_q, spec_grad_attn, spec_lse, spec_delta, spec_ids, spec_k, spec_v, spec_ids
        )

        def cycle_step(hop_index, carried):
            keys_now, values_now, grad_keys, grad_values, grad_queries = carried
            source = (cycle_index - hop_index) % cycle_size
            key_ids = lax.dynamic_slice_in_dim(ids_flat, source * tok_rows, tok_rows)
            term_q, term_k, term_v = block_grads(
                patch_q,
                patch_grad_attn,
                patch_lse,
                patch_delta,
                patch_ids,
                keys_now,
                values_now,
                key_ids,
            )
            keys_now, values_now = from_behind((keys_now, values_now), "blk", 1)
            grad_keys, grad_values = (
                from_behind((grad_keys + term_k).astype(jnp.bfloat16), "blk", 1).astype(
                    jnp.float32
                ),
                from_behind((grad_values + term_v).astype(jnp.bfloat16), "blk", 1).astype(
                    jnp.float32
                ),
            )
            return (keys_now, values_now, grad_keys, grad_values, grad_queries + term_q)

        zero_rows = jnp.zeros((tok_rows, width), jnp.float32)
        unused_keys, unused_values, grad_pk, grad_pv, grad_pq = lax.fori_loop(
            0, cycle_size, cycle_step, (patch_k, patch_v, zero_rows, zero_rows, grad_pq_first)
        )
        grad_pk = grad_pk + grad_pk_local
        grad_pv = grad_pv + grad_pv_local
        grad_patch_qkv = jnp.concatenate([grad_pq, grad_pk, grad_pv], 1)
        grad_spec_qkv = jnp.concatenate(
            [sum_sq + grad_sq_own, sum_sk + grad_sk_own, sum_sv + grad_sv_own], 1
        )
        grad_projected = jnp.concatenate([grad_patch_qkv, grad_spec_qkv], 0).astype(jnp.bfloat16)
        g_qkv = contract_rows(normed, grad_projected * row_weight_low)
        grad_normed = jnp.einsum(
            "re,de->rd", grad_projected, qkv_full, preferred_element_type=jnp.float32
        )
        unused_value, norm_pull_attn = jax.vjp(
            lambda rows_in: norm_rows(rows_in, gain_rows[0]), tokens
        )
        grad_tokens = grad_middle + norm_pull_attn(grad_normed)[0]
        g_ln1 = jnp.sum(row_weight[:, None] * grad_normed * norm_rows(tokens, 1.0), 0)
        grad_parts.append(grad_tokens[:tok_rows])
        grad_spec_parts.append(grad_tokens[tok_rows:])
        grad_terms = (g_qkv, g_out, g_up, g_down, jnp.stack([g_ln1, g_ls1, g_ln2, g_ls2], 0))
        summed_terms = (
            grad_terms
            if summed_terms is None
            else tuple((held + extra for held, extra in zip(summed_terms, grad_terms)))
        )
    shard_terms = reduce_grads(summed_terms)
    return (
        jnp.concatenate(out_parts, 0),
        jnp.concatenate(spec_parts, 0),
        jnp.concatenate(grad_parts, 0),
        jnp.concatenate(grad_spec_parts, 0),
        shard_terms[0],
        shard_terms[1],
        shard_terms[2],
        shard_terms[3],
        shard_terms[4],
    )


PAD_ID = 99


def mm(a, b):
    return jnp.dot(a, b, preferred_element_type=F32)


def mm_nt(a, b):
    return lax.dot_general(a, b, (((1,), (1,)), ((), ())), preferred_element_type=F32)


def mm_tn(a, b):
    return lax.dot_general(a, b, (((0,), (0,)), ((), ())), preferred_element_type=F32)


def here():
    place = lax.axis_index("blk")
    group = lax.axis_index("dp")
    return place, place // 2, place % 2, group // 2, group % 2


def chunk_index(slot, z, y):
    hops, crossed = slot % 4, slot // 4
    source_z = lax.rem(z + 4 - hops, 4)
    source_y = y if not crossed else 1 - y
    return source_z * 2 + source_y


def row_blocks(block):
    return [slice(first, first + block) for first in range(0, 736, block)]


def fold(rows):
    return rows.reshape(rows.shape[0] // 8, 8, rows.shape[1]).sum(0)


def call(kernel, outs, ins, scratch=(), us=1, limit=28):
    moved = sum(o.size * o.dtype.itemsize for o in outs) + sum(i.size * i.dtype.itemsize for i in ins)
    return pl.pallas_call(
        kernel,
        out_shape=tuple(outs),
        in_specs=[pl.BlockSpec(memory_space=pltpu.VMEM)] * len(ins),
        out_specs=tuple(pl.BlockSpec(memory_space=pltpu.VMEM) for _ in outs),
        scratch_shapes=list(scratch),
        compiler_params=pltpu.CompilerParams(vmem_limit_bytes=limit * 2**20),
        cost_estimate=pl.CostEstimate(flops=us * 10**9, bytes_accessed=moved, transcendentals=0),
        name=kernel.__name__,
    )(*ins)


def sds(*shape, dtype=BF16):
    return jax.ShapeDtypeStruct(shape, dtype)


def pick_pieces(w_qkv, w_up, gains, patches, cots, own, near, far, rows, held):
    place = here()[0]
    held[...] = jnp.zeros_like(held)
    up = w_up[...].astype(F32)
    qkv = w_qkv[...].astype(F32)
    gain = gains[...].astype(F32)
    for b in range(4):
        for d in range(8):
            held[b, 0:24, d * 96 : d * 96 + 96] = up[:, d * 384 + b * 96 : d * 384 + b * 96 + 96]
        for part in range(3):
            held[b, 24:48, part * 192 : part * 192 + 192] = qkv[
                :, part * 768 + b * 192 : part * 768 + b * 192 + 192
            ]
        held[b, 24:28, 576:600] = gain
    own[...] = held[place].astype(BF16)
    near[...] = held[place ^ 1].astype(BF16)
    far[0:48, :] = held[place ^ 2].astype(BF16)
    far[48:96, :] = held[place ^ 3].astype(BF16)
    rows[0:176, :] = patches[...]
    rows[176:352, :] = cots[...]


def join_pieces(own, near, far, near_far, w_out, pack, up_chunk, pack_f, up_f):
    place = here()[0]
    pack_f[96:112, :] = jnp.zeros((16, 768), F32)
    pieces = (
        own[...].astype(F32),
        near[...].astype(F32),
        far[0:48, :].astype(F32),
        near_far[48:96, :].astype(F32),
    )
    for k, piece in enumerate(pieces):
        source = place ^ k
        at = pl.ds(pl.multiple_of(source * 24, 8), 24)
        up_f[at, :] = piece[0:24]
        pack_f[at, 0:576] = piece[24:48, 0:576]
        lanes = pl.ds(pl.multiple_of(source * 128, 128), 128)
        pack_f[96:104, lanes] = piece[24:32, 576:704]
    out = w_out[...].astype(F32)
    for i in range(4):
        pack_f[i * 24 : i * 24 + 24, 576:768] = out[:, i * 192 : i * 192 + 192]
    pack[...] = pack_f[...].astype(BF16)
    up_chunk[...] = up_f[...].astype(BF16)


def open_pack(*refs):
    chunks, (w_qkv, w_out, gain_rows, out_f, gain_f) = refs[:8], refs[8:]
    _, _, _, z, y = here()
    for slot, chunk in enumerate(chunks):
        d = chunk_index(slot, z, y)
        w_qkv[pl.ds(pl.multiple_of(d * 96, 96), 96), :] = chunk[0:96, 0:576]
        tail = chunk[0:96, 576:768].astype(F32)
        for i in range(4):
            out_f[pl.ds(pl.multiple_of(d * 24, 8), 24), i * 192 : i * 192 + 192] = tail[
                i * 24 : i * 24 + 24
            ]
        gain_f[d] = chunk[96:112, :].astype(F32)
    w_out[...] = out_f[...].astype(BF16)
    gain_rows[...] = jnp.zeros_like(gain_rows)
    for d in range(8):
        for b in range(4):
            at = (d * 4 + b) * 24
            gain_rows[0:4, at : at + 24] = gain_f[d, 0:4, b * 128 : b * 128 + 24]


def normalise(rows):
    centre = rows - jnp.mean(rows, -1, keepdims=True)
    spread = jnp.mean(centre * centre, -1, keepdims=True)
    scale = lax.rsqrt(spread + EPSILON)
    return centre * scale, scale


def place_rows(scratch, blocks, tail, first):
    place = here()[0]
    for k, block in enumerate(blocks):
        rows = block[first : first + 176, :].astype(F32)
        source = place ^ k
        for m in range(MICRO):
            scratch[pl.ds(pl.multiple_of(m * 368 + source * 88, 8), 88), :] = rows[m * 88 : m * 88 + 88]
    rows = tail[...].astype(F32)
    for m in range(MICRO):
        scratch[m * 368 + 352 : m * 368 + 368, :] = rows[m * 16 : m * 16 + 16]


def attend(
    rows_0, rows_1, rows_2, rows_3, tail, ids_col, ids_row, w_qkv, gain_rows,
    tokens, normed, projected, probs, attended, rows_f,
):
    place_rows(rows_f, (rows_0, rows_1, rows_2, rows_3), tail, 0)
    gain = gain_rows[0:1, :]

    for at in row_blocks(32):
        rows = rows_f[at, :]
        tokens[at, :] = rows.astype(BF16)
        normed[at, :] = (normalise(rows)[0] * gain).astype(BF16)
    for m in range(MICRO):
        at = slice(m * 368, m * 368 + 368)
        qkv = mm(normed[at, :], w_qkv[...])
        qkv = jnp.concatenate([qkv[:, 0:192] * SCORE_SCALE, qkv[:, 192:576]], -1).astype(BF16)
        projected[at, :] = qkv
        same = ids_col[at, :] == ids_row[m : m + 1, :]
        bias = jnp.where(same, 0.0, MASKED)
        heads = []
        for h in range(3):
            q = qkv[:, h * 64 : h * 64 + 64]
            k = qkv[:, 192 + h * 64 : 192 + h * 64 + 64]
            v = qkv[:, 384 + h * 64 : 384 + h * 64 + 64]
            scores = mm_nt(q, k) + bias
            weights = jnp.exp(scores - jnp.max(scores, -1, keepdims=True))
            weights = weights * (1.0 / jnp.sum(weights, -1, keepdims=True))
            weights = weights.astype(BF16)
            probs[m * 3 + h] = weights
            heads.append(mm(weights, v))
        attended[at, :] = jnp.concatenate(heads, -1).astype(BF16)


def order_out(
    out_0, out_1, out_2, out_3, rows_0, rows_1, rows_2, rows_3, cot_tail, gain_rows,
    ordered, mine, cots, grad_mlp, out_f,
):
    place = here()[0]
    for k, part in enumerate((out_0, out_1, out_2, out_3)):
        source = place ^ k
        rows = part[...].astype(F32)
        for d in range(8):
            at = pl.multiple_of((d * 4 + source) * 24, 8)
            out_f[pl.ds(at, 24), :] = rows[d * 24 : d * 24 + 24]
    ordered[...] = out_f[...].astype(BF16)
    mine[...] = out_f[pl.ds(pl.multiple_of(place * 192, 8), 192), :].astype(BF16)
    place_rows(out_f, (rows_0, rows_1, rows_2, rows_3), cot_tail, 176)
    gain = gain_rows[3:4, :]
    for at in row_blocks(32):
        rows = out_f[at, :]
        cots[at, :] = rows.astype(BF16)
        grad_mlp[at, :] = (gain * rows).astype(BF16)


def raise_rows(*refs):
    heads, (w_out, tokens, gain_rows), chunks = refs[0:4], refs[4:7], refs[7:15]
    branch, middle, normed, active, slope, w_up, up_f = refs[15:]
    place, _, _, z, y = here()
    for slot, chunk in enumerate(chunks):
        d = chunk_index(slot, z, y)
        w_up[pl.ds(pl.multiple_of(d * 96, 96), 96), :] = chunk[...]
    for m in range(MICRO):
        at = slice(m * 368, m * 368 + 368)
        total = None
        for k, part in enumerate(heads):
            source = place ^ k
            rows = w_out[pl.ds(pl.multiple_of(source * 192, 16), 192), :]
            term = mm(part[at, :], rows)
            total = term if total is None else total + term
        up_f[at, :] = total
    gain_s, gain_n = gain_rows[1:2, :], gain_rows[2:3, :]

    for at in row_blocks(32):
        a = up_f[at, :]
        branch[at, :] = a.astype(BF16)
        rows = tokens[at, :].astype(F32) + gain_s * a
        middle[at, :] = rows
        normed[at, :] = (normalise(rows)[0] * gain_n).astype(BF16)
    for m in range(MICRO):
        at = slice(m * 368, m * 368 + 368)
        up_f[at, :] = mm(normed[at, :], w_up[...])

    for at in row_blocks(32):
        u = up_f[at, :]
        half = 0.5 + 0.5 * lax.erf(u * 0.7071067811865476)
        active[at, :] = (u * half).astype(BF16)
        slope[at, :] = half + u * (0.3989422804014327 * jnp.exp(-0.5 * u * u))


def lower_rows(*refs):
    (slope, grad_mlp, w_up), chunks = refs[:3], refs[3:11]
    w_down, grad_hidden, away, kept, work = refs[11:]
    _, _, core, z, y = here()
    for slot, chunk in enumerate(chunks):
        d = chunk_index(slot, z, y)
        w_down[pl.ds(pl.multiple_of(d * 96, 96), 96), :] = chunk[...]
    for m in range(MICRO):
        at = slice(m * 368, m * 368 + 368)
        grad = mm_nt(grad_mlp[at, :], w_down[...])
        grad_hidden[at, :] = (slope[at, :] * grad).astype(BF16)
        work[m] = mm_nt(grad_hidden[at, :], w_up[...])
    away[...] = work[1 - core].astype(BF16)
    kept[...] = work[core]


def split_rows(pieces, place, away, kept):
    away[0:208, :] = pieces[place ^ 1].astype(BF16)
    away[208:416, :] = pieces[place ^ 3].astype(BF16)
    kept[0:208, :] = pieces[place]
    kept[208:416, :] = pieces[place ^ 2]


def cut_rows(rows_f, pieces):
    for b in range(4):
        for m in range(MICRO):
            pieces[b, m * 104 : m * 104 + 88, :] = rows_f[m * 368 + b * 88 : m * 368 + b * 88 + 88, :]
            pieces[b, m * 104 + 88 : m * 104 + 104, :] = rows_f[m * 368 + 352 : m * 368 + 368, :]


def halve(grad_f, y, away, kept, rows):
    for zz in range(4):
        other = pl.ds(pl.multiple_of((zz * 2 + 1 - y) * rows, 8), rows)
        ours = pl.ds(pl.multiple_of((zz * 2 + y) * rows, 8), rows)
        away[zz] = grad_f[other, 0 : away.shape[2]].astype(BF16)
        kept[zz] = grad_f[ours, 0 : away.shape[2]]


def mlp_grads(
    active, normed, grad_mlp, grad_hidden, w_down, cots,
    down_away, down_kept, up_away, up_kept, rows_away, rows_kept, scale_grad, work, pieces,
):
    place, _, _, _, y = here()
    work[0:768, :] = mm_tn(active[...], grad_mlp[...])
    halve(work, y, down_away, down_kept, 96)
    work[0:768, :] = mm_tn(normed[...], grad_hidden[...])
    halve(work, y, up_away, up_kept, 96)
    for m in range(MICRO):
        at = slice(m * 368, m * 368 + 368)
        work[at, :] = mm(active[at, :], w_down[...])
    total = jnp.zeros((8, 768), F32)
    for at in row_blocks(32):
        total = total + fold(cots[at, :].astype(F32) * work[at, :])
    scale_grad[...] = total
    cut_rows(work, pieces)
    split_rows(pieces, place, rows_away, rows_kept)


def add_rows(kept, came, total):
    total[...] = (kept[...] + came[...].astype(F32)).astype(BF16)


def add_pair(here_rows, came, total):
    total[...] = (here_rows[...].astype(F32) + came[...].astype(F32)).astype(BF16)


def branch_back(
    sum_own, sum_near, middle, cots, branch, gain_rows, w_mine, probs, normed, targets,
    scale_grad_mlp, head_0, head_1, head_2, head_3,
    grad_rows, grad_heads, grad_v, away, kept,
    work, grad_branch, grad_mid, extra,
):
    place, _, core, _, y = here()
    for m in range(MICRO):
        at = slice(m * 368, m * 368 + 368)

        @pl.when(core == m)
        def _():
            work[at, :] = sum_own[...].astype(F32)

        @pl.when(core != m)
        def _():
            work[at, :] = sum_near[...].astype(F32)

    gain_s, gain_n = gain_rows[1:2, :], gain_rows[2:3, :]
    scale_sum = jnp.zeros((8, 768), F32)
    for at in row_blocks(32):
        unit, scale = normalise(middle[at, :])
        pulled = work[at, :] * gain_n
        pulled = pulled - jnp.mean(pulled, -1, keepdims=True) - unit * jnp.mean(
            pulled * unit, -1, keepdims=True
        )
        through = cots[at, :].astype(F32) + scale * pulled
        grad_mid[at, :] = through
        grad_branch[at, :] = (gain_s * through).astype(BF16)
        scale_sum = scale_sum + fold(through * branch[at, :].astype(F32))
    for m in range(MICRO):
        for part, first in ((0, place * 88), (88, 352)):
            rows = 88 if part == 0 else 16
            grad_rows[m * 104 + part : m * 104 + part + rows, :] = grad_mid[
                pl.ds(pl.multiple_of(m * 368 + first, 8), rows), :
            ]
    for m in range(MICRO):
        at = slice(m * 368, m * 368 + 368)
        heads = mm_nt(grad_branch[at, :], w_mine[...]).astype(BF16)
        grad_heads[at, :] = heads
        terms = [mm_tn(probs[m * 3 + h], heads[:, h * 64 : h * 64 + 64]) for h in range(3)]
        grad_v[at, :] = jnp.concatenate(terms, -1).astype(BF16)
    grad_mid[0:768, 0:192] = mm_tn(normed[...], grad_v[...])
    chosen = None
    for k, part in enumerate((head_0, head_1, head_2, head_3)):
        source = place ^ k
        index = lax.broadcasted_iota(jnp.int32, (192, 192), 0) + source * 192
        pick = jnp.where(index == targets[...], 1.0, 0.0).astype(BF16)
        term = mm(part[...], pick)
        chosen = term if chosen is None else chosen + term
    extra[...] = mm_tn(chosen.astype(BF16), grad_branch[...])
    scale_rows = (
        0.25 * jnp.sum(scale_sum, 0, keepdims=True),
        jnp.sum(scale_grad_mlp[...], 0, keepdims=True),
    )
    for d in range(8):
        base = d * 112
        work[base : base + 96, 0:192] = grad_mid[d * 96 : d * 96 + 96, 0:192]
        for i in range(4):
            work[base + i * 24 : base + i * 24 + 24, 192:384] = extra[
                d * 24 : d * 24 + 24, i * 192 : i * 192 + 192
            ]
        work[base + 96 : base + 112, 0:384] = jnp.zeros((16, 384), F32)
        for i in range(2):
            work[base + 96 + i : base + 97 + i, 0:96] = scale_rows[i][:, d * 96 : d * 96 + 96]
    halve(work, y, away, kept, 112)


def score_back(probs, projected, grad_heads, normed, grad_qk, away, kept, work):
    _, _, _, _, y = here()
    for m in range(MICRO):
        at = slice(m * 368, m * 368 + 368)
        qkv = projected[at, :]
        g_heads = grad_heads[at, :]
        grads = [[], []]
        for h in range(3):
            q = qkv[:, h * 64 : h * 64 + 64]
            k = qkv[:, 192 + h * 64 : 192 + h * 64 + 64]
            v = qkv[:, 384 + h * 64 : 384 + h * 64 + 64]
            grad_prob = mm_nt(g_heads[:, h * 64 : h * 64 + 64], v)
            wide = probs[m * 3 + h].astype(F32)
            moved = wide * grad_prob
            delta = jnp.sum(moved, -1, keepdims=True)
            grad_score = (moved - wide * delta).astype(BF16)
            grads[0].append(mm(grad_score, k) * SCORE_SCALE)
            grads[1].append(mm_tn(grad_score, q))
        grad_qk[at, :] = jnp.concatenate(grads[0] + grads[1], -1).astype(BF16)
    work[...] = mm_tn(normed[...], grad_qk[...])
    halve(work, y, away, kept, 96)


def project_back(grad_qk, grad_v, w_qkv, rows_away, rows_kept, work, pieces):
    place = here()[0]
    for m in range(MICRO):
        at = slice(m * 368, m * 368 + 368)
        work[at, :] = mm_nt(grad_qk[at, :], w_qkv[:, 0:384]) + mm_nt(grad_v[at, :], w_qkv[:, 384:576])
    cut_rows(work, pieces)
    split_rows(pieces, place, rows_away, rows_kept)


def sum_y(kept, came, own, send_1, send_2, send_3):
    _, _, _, z, _ = here()
    own[...] = kept[z] + came[z].astype(F32)
    for k, send in ((1, send_1), (2, send_2), (3, send_3)):
        there = lax.rem(z + k, 4)
        send[...] = (kept[there] + came[there].astype(F32)).astype(BF16)


def sum_z(own, came_1, came_2, came_3, total):
    total[...] = (
        own[...]
        + came_1[...].astype(F32)
        + came_2[...].astype(F32)
        + came_3[...].astype(F32)
    )


def add_pieces(kept_m, came_m, kept_h, came_h, stay, go):
    for i, (kept, came) in enumerate(((kept_m, came_m), (kept_h, came_h))):
        stay[i * 208 : i * 208 + 208, :] = kept[0:208, :] + came[0:208, :].astype(F32)
        go[i * 208 : i * 208 + 208, :] = (kept[208:416, :] + came[208:416, :].astype(F32)).astype(BF16)


def finish_rows(
    stay, came, middle, grad_rows, patches, tail, gain_rows,
    out_patches, out_special, grad_patches, grad_special,
):
    place = here()[0]
    own = patches[...].astype(F32)
    rest = tail[...].astype(F32)
    outs, out_tails = [], []
    for m in range(MICRO):
        for part, first in ((0, place * 88), (88, 352)):
            count = 88 if part == 0 else 16
            at = slice(m * 104 + part, m * 104 + part + count)
            far_at = slice(208 + m * 104 + part, 208 + m * 104 + part + count)
            mid = middle[pl.ds(pl.multiple_of(m * 368 + first, 8), count), :]
            final = mid + gain_rows[3:4, :] * (stay[at, :] + came[at, :].astype(F32))
            (outs if part == 0 else out_tails).append(final)
            rows = own[m * 88 : m * 88 + 88] if part == 0 else rest[m * 16 : m * 16 + 16]
            unit, scale = normalise(rows)
            pulled = gain_rows[0:1, :] * (stay[far_at, :] + came[far_at, :].astype(F32))
            pulled = pulled - jnp.mean(pulled, -1, keepdims=True) - unit * jnp.mean(
                pulled * unit, -1, keepdims=True
            )
            grad = grad_rows[at, :] + scale * pulled
            if part == 0:
                grad_patches[m * 88 : m * 88 + 88, :] = grad
            else:
                grad_special[m * 10 : m * 10 + 10, :] = grad[0:10]
    out_patches[...] = jnp.concatenate(outs, 0).astype(BF16)
    out_special[...] = jnp.concatenate([part[0:10] for part in out_tails], 0).astype(BF16)


def pick_grads(up, first, second, own, near, far, grad_out, held):
    place = here()[0]
    for b in range(4):
        at = slice(b * 24, b * 24 + 24)
        held[b, 0:24, :] = up[at, :]
        held[b, 24:48, 0:384] = second[at, :]
        held[b, 24:48, 384:576] = first[at, 0:192]
        held[b, 24:48, 576:768] = jnp.zeros((24, 192), F32)
        held[b, 24:26, 576:600] = first[96:98, at]
        grad_out[:, b * 192 : b * 192 + 192] = first[at, 192:384]
    own[...] = held[place]
    near[...] = held[place ^ 1].astype(BF16)
    far[0:48, :] = held[place ^ 2].astype(BF16)
    far[48:96, :] = held[place ^ 3].astype(BF16)


def as_row(column):
    count = column.shape[0]
    square = lax.broadcasted_iota(jnp.int32, (count, count), 0)
    across = lax.broadcasted_iota(jnp.int32, (count, count), 1)
    return jnp.sum(jnp.where(square == across, column, 0.0), 0, keepdims=True)


def join_grads(
    own, near, far, near_far, w_qkv, w_up, gains, grad_qkv, grad_up, grad_gains, held
):
    place = here()[0]
    held[place] = own[...]
    held[place ^ 1] = near[...].astype(F32)
    held[place ^ 2] = far[0:48, :].astype(F32)
    held[place ^ 3] = near_far[48:96, :].astype(F32)
    scales = None
    for b in range(4):
        for d in range(8):
            at = d * 384 + b * 96
            grad_up[:, at : at + 96] = held[b, 0:24, d * 96 : d * 96 + 96]
        for part in range(3):
            at = part * 768 + b * 192
            grad_qkv[:, at : at + 192] = held[b, 24:48, part * 192 : part * 192 + 192]
        term = held[b, 24:26, 576:600]
        scales = term if scales is None else scales + term
    norm_1 = as_row(jnp.sum(w_qkv[...].astype(F32) * grad_qkv[...], -1, keepdims=True))
    norm_2 = as_row(jnp.sum(w_up[...].astype(F32) * grad_up[...], -1, keepdims=True))
    gain = gains[...].astype(F32)
    grad_gains[0:1, :] = norm_1 / gain[0:1, :]
    grad_gains[1:2, :] = scales[0:1, :]
    grad_gains[2:3, :] = norm_2 / gain[2:3, :]
    grad_gains[3:4, :] = scales[1:2, :]


def send(rows, axis, step):
    pairs = []
    for group in range(8):
        z, y = group // 2, group % 2
        for place in range(4):
            target = {
                "core": (group, place ^ 1),
                "x": (group, place ^ 2),
                "y": (z * 2 + 1 - y, place),
                "z": ((z + step) % 4 * 2 + y, place),
            }[axis]
            pairs.append((group * 4 + place, target[0] * 4 + target[1]))
    return lax.ppermute(rows, ("dp", "blk"), pairs)


def gather_dp(chunk):
    along_z = [chunk] + [send(chunk, "z", k) for k in (1, 2, 3)]
    return along_z + [send(part, "y", 1) for part in along_z]


def gather_blk(rows):
    near = send(rows, "core", 1)
    far = send(rows, "x", 1)
    return [rows, near, far, send(far, "core", 1)]


def scatter_dp(away, kept):
    rows, width = away.shape[1:]
    came = send(away, "y", 1)
    own, *parts = call(
        sum_y, [sds(rows, width, dtype=F32)] + [sds(rows, width)] * 3, [kept, came]
    )
    came = [send(part, "z", k) for k, part in zip((1, 2, 3), parts)]
    return call(sum_z, [sds(rows, width, dtype=F32)], [own, *came])[0]


def pad_tail(rows):
    return jnp.pad(rows.reshape(2, 10, 768), ((0, 0), (0, 6), (0, 0))).reshape(32, 768)


def on_device_split(
    patches, special, image_ids, w_qkv, w_out, w_up, w_down, gains, cot_patches, cot_special
):
    place = lax.axis_index("blk")
    tail, cot_tail = pad_tail(special), pad_tail(cot_special)
    spec_ids = jnp.concatenate(
        [jnp.arange(10, dtype=jnp.int32) // SPECIAL, jnp.full((6,), PAD_ID, jnp.int32)]
    )
    ids = image_ids.reshape(4, 2, 88).transpose(1, 0, 2).reshape(2, 352)
    ids_row = jnp.concatenate([ids, jnp.broadcast_to(spec_ids, (2, 16))], 1)
    ids_col = ids_row.reshape(736, 1)
    column = jnp.arange(192, dtype=jnp.int32)
    targets = (column + column // 24 * 72 + place * 24).reshape(1, 192)

    own, near, far, rows = call(
        pick_pieces,
        [sds(48, 768), sds(48, 768), sds(96, 768), sds(352, 768)],
        [w_qkv, w_up, gains, patches, cot_patches],
        [pltpu.VMEM((4, 48, 768), F32)],
    )
    came_far = send(far, "x", 1)
    came_near, came_near_far = send(near, "core", 1), send(came_far, "core", 1)
    rows, _ = lax.optimization_barrier((rows, came_far))
    row_parts = gather_blk(rows)
    down_chunks = gather_dp(w_down)
    pack, up_chunk = call(
        join_pieces,
        [sds(112, 768), sds(96, 768)],
        [own, came_near, came_far, came_near_far, w_out],
        [pltpu.VMEM((112, 768), F32), pltpu.VMEM((96, 768), F32)],
    )
    pack_chunks = gather_dp(pack)
    up_chunks = gather_dp(up_chunk)
    qkv_full, out_part, gain_rows = call(
        open_pack,
        [sds(768, 576), sds(192, 768), sds(8, 768, dtype=F32)],
        pack_chunks,
        [pltpu.VMEM((192, 768), F32), pltpu.VMEM((8, 16, 768), F32)],
    )
    out_parts = gather_blk(out_part)
    tokens, normed, projected, probs, attended = call(
        attend,
        [sds(736, 768), sds(736, 768), sds(736, 576), sds(6, 368, 368), sds(736, 192)],
        [*row_parts, tail, ids_col, ids_row, qkv_full, gain_rows],
        [pltpu.VMEM((736, 768), F32)],
        us=10,
    )
    heads = gather_blk(attended)
    out_full, out_mine, cots, grad_mlp = call(
        order_out,
        [sds(768, 768), sds(192, 768), sds(736, 768), sds(736, 768)],
        [*out_parts, *row_parts, cot_tail, gain_rows],
        [pltpu.VMEM((768, 768), F32)],
        us=3,
    )
    branch, middle, normed_mlp, active, slope, up_full = call(
        raise_rows,
        [
            sds(736, 768), sds(736, 768, dtype=F32), sds(736, 768), sds(736, 768),
            sds(736, 768, dtype=F32), sds(768, 768),
        ],
        [*heads, out_full, tokens, gain_rows, *up_chunks],
        [pltpu.VMEM((736, 768), F32)],
        us=10,
    )
    down_full, grad_hidden, sum_away, sum_kept = call(
        lower_rows,
        [sds(768, 768), sds(736, 768), sds(368, 768), sds(368, 768, dtype=F32)],
        [slope, grad_mlp, up_full, *down_chunks],
        [pltpu.VMEM((2, 368, 768), F32)],
        us=4,
    )
    sum_came = send(sum_away, "core", 1)
    chip_sum = call(add_rows, [sds(368, 768)], [sum_kept, sum_came])[0]
    chip_came = send(chip_sum, "x", 1)
    half = [sds(4, 96, 768), sds(4, 96, 768, dtype=F32)]
    rows_split = [sds(416, 768), sds(416, 768, dtype=F32)]
    down_away, down_kept, up_away, up_kept, m_away, m_kept, scale_mlp = call(
        mlp_grads,
        [*half, *half, *rows_split, sds(8, 768, dtype=F32)],
        [active, normed_mlp, grad_mlp, grad_hidden, down_full, cots],
        [pltpu.VMEM((768, 768), F32), pltpu.VMEM((4, 208, 768), F32)],
        us=5,
    )
    grad_down = scatter_dp(down_away, down_kept)
    grad_up_rows = scatter_dp(up_away, up_kept)
    sum_own = call(add_pair, [sds(368, 768)], [chip_sum, chip_came])[0]
    sum_near = send(sum_own, "core", 1)
    m_came = send(m_away, "core", 1)
    grad_rows, grad_heads, grad_v, a_away, a_kept = call(
        branch_back,
        [
            sds(208, 768, dtype=F32), sds(736, 192), sds(736, 192),
            sds(4, 112, 384), sds(4, 112, 384, dtype=F32),
        ],
        [
            sum_own, sum_near, middle, cots, branch, gain_rows, out_mine, probs, normed, targets,
            scale_mlp, *heads,
        ],
        [
            pltpu.VMEM((896, 768), F32), pltpu.VMEM((736, 768), BF16),
            pltpu.VMEM((768, 768), F32), pltpu.VMEM((192, 768), F32),
        ],
        us=10,
    )
    first_rows = scatter_dp(a_away, a_kept)
    grad_qk, b_away, b_kept = call(
        score_back,
        [sds(736, 384), sds(4, 96, 384), sds(4, 96, 384, dtype=F32)],
        [probs, projected, grad_heads, normed],
        [pltpu.VMEM((768, 384), F32)],
        us=10,
    )
    second_rows = scatter_dp(b_away, b_kept)
    h_away, h_kept = call(
        project_back,
        rows_split,
        [grad_qk, grad_v, qkv_full],
        [pltpu.VMEM((736, 768), F32), pltpu.VMEM((4, 208, 768), F32)],
        us=3,
    )
    h_came = send(h_away, "core", 1)
    stay, go = call(
        add_pieces, [sds(416, 768, dtype=F32), sds(416, 768)], [m_kept, m_came, h_kept, h_came]
    )
    far_rows = send(go, "x", 1)
    own, near, far, grad_out = call(
        pick_grads,
        [sds(48, 768, dtype=F32), sds(48, 768), sds(96, 768), sds(24, 768, dtype=F32)],
        [grad_up_rows, first_rows, second_rows],
        [pltpu.VMEM((4, 48, 768), F32)],
    )
    came_far = send(far, "x", 1)
    came_near, came_near_far = send(near, "core", 1), send(came_far, "core", 1)
    out_patches, out_special, grad_patches, grad_special = call(
        finish_rows,
        [
            sds(176, 768), sds(20, 768), sds(176, 768, dtype=F32), sds(20, 768, dtype=F32),
        ],
        [stay, far_rows, middle, grad_rows, patches, tail, gain_rows],
    )
    grad_qkv, grad_up, grad_gains = call(
        join_grads,
        [sds(24, 2304, dtype=F32), sds(24, 3072, dtype=F32), sds(4, 24, dtype=F32)],
        [own, came_near, came_far, came_near_far, w_qkv, w_up, gains],
        [pltpu.VMEM((4, 48, 768), F32)],
    )
    return (
        out_patches, out_special, grad_patches, grad_special,
        grad_qkv, grad_out, grad_up, grad_down, grad_gains,
    )


def solution(mesh):
    placed = (
        P(("dp", "blk"), None),
        P("dp", None),
        P("dp"),
        P(("dp", "blk"), None),
        P(("dp", "blk"), None),
        P(("dp", "blk"), None),
        P(("dp", "blk"), None),
        P(None, ("dp", "blk")),
        P(("dp", "blk"), None),
        P("dp", None),
    )
    whole = dict(mesh.shape) != {"dp": 8, "blk": 4}
    return jax.shard_map(
        on_device if whole else on_device_split,
        mesh=mesh,
        in_specs=placed,
        out_specs=(
            P(("dp", "blk"), None),
            P("dp", None),
            P(("dp", "blk"), None),
            P("dp", None),
            P(("dp", "blk"), None),
            P(("dp", "blk"), None),
            P(("dp", "blk"), None),
            P(("dp", "blk"), None),
            P(None, ("dp", "blk")),
        ),
        check_vma=False,
    )
```

```python
import jax
import jax.numpy as jnp
from jax import lax
from jax.experimental import pallas as pl
from jax.experimental.pallas import tpu as pltpu
from jax.sharding import PartitionSpec as P

HEAD_DIM = 64
SPECIAL = 5
MICRO = 2
TOK_MB = 88

SCORE_SCALE = 0.125
MASKED = -1e30
EPSILON = 1e-06

BF16 = jnp.bfloat16
F32 = jnp.float32


def merged(shard, axis, combine):
    everything = jax.tree.map(
        lambda part, kind: lax.all_gather(part.astype(kind), axis),
        shard,
        (jnp.bfloat16, jnp.bfloat16, jnp.bfloat16),
    )

    def take(k):
        return jax.tree.map(lambda part, own: part[k].astype(own.dtype), everything, shard)

    return lax.fori_loop(
        1, lax.axis_size(axis), lambda k, so_far: combine(so_far, take(k)), take(0)
    )


def from_behind(shard, axis, by):
    peers = lax.axis_size(axis)
    return lax.ppermute(shard, axis, [(i, (i + by) % peers) for i in range(peers)])


def norm_rows(values, gain_row):
    centre = values - jnp.mean(values, -1, keepdims=True)
    spread = jnp.mean(centre * centre, -1, keepdims=True)
    return centre * lax.rsqrt(spread + EPSILON) * gain_row


def split_heads(matrix):
    return matrix.reshape(matrix.shape[0], -1, HEAD_DIM)


def widen(per_head):
    return jnp.repeat(per_head.T, HEAD_DIM, axis=1)


def empty_state(length, head_count, feature_width):
    return (
        jnp.full((head_count, length), MASKED, jnp.float32),
        jnp.zeros((head_count, length), jnp.float32),
        jnp.zeros((length, feature_width), jnp.float32),
    )


def online(carried, queries, query_ids, key_rows, value_rows, key_ids):
    top_score, totals, accumulated = carried
    same_image = (query_ids[:, None] == key_ids[None, :])[None]
    scores = (
        jnp.einsum(
            "qhd,khd->hqk",
            split_heads(queries),
            split_heads(key_rows),
            preferred_element_type=jnp.float32,
        )
        * SCORE_SCALE
    )
    scores = jnp.where(same_image, scores, MASKED)
    new_top = jnp.maximum(top_score, jnp.max(scores, -1))
    weights = jnp.where(same_image, jnp.exp(scores - new_top[..., None]), 0.0)
    factor = jnp.exp(top_score - new_top)
    totals = totals * factor + jnp.sum(weights, -1)
    mixture = jnp.einsum(
        "hqk,khd->qhd",
        weights.astype(jnp.bfloat16),
        split_heads(value_rows),
        preferred_element_type=jnp.float32,
    )
    accumulated = accumulated * widen(factor) + mixture.reshape(accumulated.shape)
    return (new_top, totals, accumulated)


def combine(former, latter):
    highest = jnp.maximum(former[0], latter[0])
    scale_former = jnp.exp(former[0] - highest)
    scale_latter = jnp.exp(latter[0] - highest)
    return (
        highest,
        former[1] * scale_former + latter[1] * scale_latter,
        former[2] * widen(scale_former) + latter[2] * widen(scale_latter),
    )


def finish(carried):
    top_score, totals, accumulated = carried
    return (accumulated / widen(totals), top_score + jnp.log(totals))


def block_grads(queries, grad_attn, log_total, row_delta, query_ids, key_rows, value_rows, key_ids):
    same_image = (query_ids[:, None] == key_ids[None, :])[None]
    q_heads = split_heads(queries)
    g_heads = split_heads(grad_attn)
    scores = (
        jnp.einsum(
            "qhd,khd->hqk", q_heads, split_heads(key_rows), preferred_element_type=jnp.float32
        )
        * SCORE_SCALE
    )
    probabilities = jnp.where(same_image, jnp.exp(scores - log_total[..., None]), 0.0)
    grad_prob = jnp.einsum(
        "qhd,khd->hqk", g_heads, split_heads(value_rows), preferred_element_type=jnp.float32
    )
    dscore = (probabilities * (grad_prob - row_delta[..., None])).astype(jnp.bfloat16)
    grad_query = (
        jnp.einsum(
            "hqk,khd->qhd", dscore, split_heads(key_rows), preferred_element_type=jnp.float32
        ).reshape(queries.shape[0], -1)
        * SCORE_SCALE
    )
    grad_key = (
        jnp.einsum("hqk,qhd->khd", dscore, q_heads, preferred_element_type=jnp.float32).reshape(
            key_rows.shape[0], -1
        )
        * SCORE_SCALE
    )
    grad_value = jnp.einsum(
        "hqk,qhd->khd",
        probabilities.astype(jnp.bfloat16),
        g_heads,
        preferred_element_type=jnp.float32,
    ).reshape(key_rows.shape[0], -1)
    return (grad_query, grad_key, grad_value)


def fetch_weights(w_qkv, w_out, w_up, w_down, gains):
    return (
        lax.all_gather(w_qkv, ("dp", "blk"), axis=0, tiled=True),
        lax.all_gather(w_out, ("dp", "blk"), axis=0, tiled=True),
        lax.all_gather(w_up, ("dp", "blk"), axis=0, tiled=True),
        lax.all_gather(w_down, ("dp", "blk"), axis=0, tiled=True),
        lax.all_gather(gains, ("dp", "blk"), axis=1, tiled=True),
    )


def reduce_grads(grad_terms):
    g_qkv, g_out, g_up, g_down, g_gains = grad_terms
    return (
        lax.psum_scatter(g_qkv, ("dp", "blk"), scatter_dimension=0, tiled=True),
        lax.psum_scatter(g_out, ("dp", "blk"), scatter_dimension=0, tiled=True),
        lax.psum_scatter(g_up, ("dp", "blk"), scatter_dimension=0, tiled=True),
        lax.psum_scatter(g_down, ("dp", "blk"), scatter_dimension=0, tiled=True),
        lax.psum_scatter(g_gains, ("dp", "blk"), scatter_dimension=1, tiled=True),
    )


def contract_rows(left_rows, right_rows):
    return jnp.einsum("ra,rb->ab", left_rows, right_rows, preferred_element_type=jnp.float32)


def row_delta_of(grad_attn, attended):
    product = grad_attn.astype(jnp.float32) * attended
    return product.reshape(product.shape[0], -1, HEAD_DIM).sum(-1).T


def on_device(
    patches, special, image_ids, w_qkv, w_out, w_up, w_down, gains, cot_patches, cot_special
):
    cycle_size = lax.axis_size("blk")
    cycle_index = lax.axis_index("blk")
    width = w_out.shape[1]
    head_count = width // HEAD_DIM
    tok_rows = TOK_MB
    spec_rows = special.shape[0] // MICRO
    ids_group = image_ids.reshape(cycle_size, MICRO, tok_rows)
    spec_ids = jnp.arange(spec_rows, dtype=jnp.int32) // SPECIAL
    row_weight = jnp.concatenate(
        [jnp.ones((tok_rows,), jnp.float32), jnp.full((spec_rows,), 1.0 / cycle_size, jnp.float32)]
    )
    row_weight_low = row_weight.astype(jnp.bfloat16)[:, None]
    summed_terms = None
    shard_terms = None
    out_parts = []
    spec_parts = []
    grad_parts = []
    grad_spec_parts = []
    for micro_index in range(MICRO):
        full_weights = fetch_weights(w_qkv, w_out, w_up, w_down, gains)
        qkv_full, out_full, up_full, down_full, gains_full = full_weights
        gain_rows = gains_full.astype(jnp.float32)
        tokens = jnp.concatenate(
            [
                patches[micro_index * tok_rows : (micro_index + 1) * tok_rows],
                special[micro_index * spec_rows : (micro_index + 1) * spec_rows],
            ],
            0,
        ).astype(jnp.float32)
        ids_flat = ids_group[:, micro_index].reshape(-1)
        patch_ids = lax.dynamic_slice_in_dim(ids_flat, cycle_index * tok_rows, tok_rows)
        normed = norm_rows(tokens, gain_rows[0]).astype(jnp.bfloat16)
        projected = jnp.dot(normed, qkv_full, preferred_element_type=jnp.float32).astype(
            jnp.bfloat16
        )
        patch_q = projected[:tok_rows, :width]
        patch_k = projected[:tok_rows, width : 2 * width]
        patch_v = projected[:tok_rows, 2 * width :]
        spec_q = projected[tok_rows:, :width]
        spec_k = projected[tok_rows:, width : 2 * width]
        spec_v = projected[tok_rows:, 2 * width :]
        start_state = online(
            empty_state(tok_rows, head_count, width), patch_q, patch_ids, spec_k, spec_v, spec_ids
        )
        partial_value = start_state
        key_rows = lax.all_gather(patch_k, "blk", axis=0, tiled=True)
        value_rows = lax.all_gather(patch_v, "blk", axis=0, tiled=True)
        length = key_rows.shape[0]
        key_ids = ids_flat
        blocks = length // tok_rows

        def visit_block(running, block_item):
            return (
                online(running, patch_q, patch_ids, block_item[0], block_item[1], block_item[2]),
                None,
            )

        partial_value, unused = lax.scan(
            visit_block,
            partial_value,
            (
                key_rows.reshape(blocks, tok_rows, -1),
                value_rows.reshape(blocks, tok_rows, -1),
                key_ids.reshape(blocks, tok_rows),
            ),
        )
        spec_top, spec_total, spec_accum = online(
            empty_state(spec_rows, head_count, width), spec_q, spec_ids, patch_k, patch_v, patch_ids
        )
        spec_state = merged((spec_top, spec_total, spec_accum), "blk", combine)
        spec_state = online(spec_state, spec_q, spec_ids, spec_k, spec_v, spec_ids)
        patch_attn, patch_lse = finish(partial_value)
        spec_attn, spec_lse = finish(spec_state)
        attended = jnp.concatenate([patch_attn, spec_attn], 0)
        attended_low = attended.astype(jnp.bfloat16)
        branch = jnp.dot(attended_low, out_full, preferred_element_type=jnp.float32)
        middle = tokens + gain_rows[1] * branch
        normed_mlp = norm_rows(middle, gain_rows[2]).astype(jnp.bfloat16)
        hidden = jnp.dot(normed_mlp, up_full, preferred_element_type=jnp.float32)
        active = jax.nn.gelu(hidden, approximate=False).astype(jnp.bfloat16)
        mlp_out = jnp.dot(active, down_full, preferred_element_type=jnp.float32)
        final = middle + gain_rows[3] * mlp_out
        out_parts.append(final[:tok_rows].astype(jnp.bfloat16))
        spec_parts.append(final[tok_rows:].astype(jnp.bfloat16))
        upstream = jnp.concatenate(
            [
                cot_patches[micro_index * tok_rows : (micro_index + 1) * tok_rows],
                cot_special[micro_index * spec_rows : (micro_index + 1) * spec_rows],
            ],
            0,
        ).astype(jnp.float32)
        grad_mlp = (gain_rows[3] * upstream).astype(jnp.bfloat16)
        g_down = contract_rows(active, grad_mlp * row_weight_low)
        grad_active = jnp.einsum(
            "rd,fd->rf", grad_mlp, down_full, preferred_element_type=jnp.float32
        )
        unused_value, gelu_pull = jax.vjp(
            lambda pre_act: jax.nn.gelu(pre_act, approximate=False), hidden
        )
        grad_hidden = gelu_pull(grad_active)[0].astype(jnp.bfloat16)
        g_up = contract_rows(normed_mlp, grad_hidden * row_weight_low)
        grad_normed_mlp = jnp.einsum(
            "rf,df->rd", grad_hidden, up_full, preferred_element_type=jnp.float32
        )
        unused_value, norm_pull_mlp = jax.vjp(
            lambda rows_in: norm_rows(rows_in, gain_rows[2]), middle
        )
        grad_middle = upstream + norm_pull_mlp(grad_normed_mlp)[0]
        g_ln2 = jnp.sum(row_weight[:, None] * grad_normed_mlp * norm_rows(middle, 1.0), 0)
        g_ls2 = jnp.sum(row_weight[:, None] * upstream * mlp_out, 0)
        g_ls1 = jnp.sum(row_weight[:, None] * grad_middle * branch, 0)
        grad_branch = (gain_rows[1] * grad_middle).astype(jnp.bfloat16)
        g_out = contract_rows(attended_low, grad_branch * row_weight_low)
        grad_attended = jnp.einsum(
            "re,de->rd", grad_branch, out_full, preferred_element_type=jnp.float32
        ).astype(jnp.bfloat16)
        all_delta = row_delta_of(grad_attended, attended)
        patch_delta = all_delta[:, :tok_rows]
        spec_delta = all_delta[:, tok_rows:]
        patch_grad_attn = grad_attended[:tok_rows]
        spec_grad_attn = grad_attended[tok_rows:]
        grad_pq_first, grad_sk_part, grad_sv_part = block_grads(
            patch_q, patch_grad_attn, patch_lse, patch_delta, patch_ids, spec_k, spec_v, spec_ids
        )
        grad_sq_part, grad_pk_local, grad_pv_local = block_grads(
            spec_q, spec_grad_attn, spec_lse, spec_delta, spec_ids, patch_k, patch_v, patch_ids
        )
        sum_sq, sum_sk, sum_sv = (
            lax.psum(grad_sq_part.astype(jnp.bfloat16), "blk").astype(jnp.float32),
            lax.psum(grad_sk_part.astype(jnp.bfloat16), "blk").astype(jnp.float32),
            lax.psum(grad_sv_part.astype(jnp.bfloat16), "blk").astype(jnp.float32),
        )
        grad_sq_own, grad_sk_own, grad_sv_own = block_grads(
            spec_q, spec_grad_attn, spec_lse, spec_delta, spec_ids, spec_k, spec_v, spec_ids
        )

        def cycle_step(hop_index, carried):
            keys_now, values_now, grad_keys, grad_values, grad_queries = carried
            source = (cycle_index - hop_index) % cycle_size
            key_ids = lax.dynamic_slice_in_dim(ids_flat, source * tok_rows, tok_rows)
            term_q, term_k, term_v = block_grads(
                patch_q,
                patch_grad_attn,
                patch_lse,
                patch_delta,
                patch_ids,
                keys_now,
                values_now,
                key_ids,
            )
            keys_now, values_now = from_behind((keys_now, values_now), "blk", 1)
            grad_keys, grad_values = (
                from_behind((grad_keys + term_k).astype(jnp.bfloat16), "blk", 1).astype(
                    jnp.float32
                ),
                from_behind((grad_values + term_v).astype(jnp.bfloat16), "blk", 1).astype(
                    jnp.float32
                ),
            )
            return (keys_now, values_now, grad_keys, grad_values, grad_queries + term_q)

        zero_rows = jnp.zeros((tok_rows, width), jnp.float32)
        unused_keys, unused_values, grad_pk, grad_pv, grad_pq = lax.fori_loop(
            0, cycle_size, cycle_step, (patch_k, patch_v, zero_rows, zero_rows, grad_pq_first)
        )
        grad_pk = grad_pk + grad_pk_local
        grad_pv = grad_pv + grad_pv_local
        grad_patch_qkv = jnp.concatenate([grad_pq, grad_pk, grad_pv], 1)
        grad_spec_qkv = jnp.concatenate(
            [sum_sq + grad_sq_own, sum_sk + grad_sk_own, sum_sv + grad_sv_own], 1
        )
        grad_projected = jnp.concatenate([grad_patch_qkv, grad_spec_qkv], 0).astype(jnp.bfloat16)
        g_qkv = contract_rows(normed, grad_projected * row_weight_low)
        grad_normed = jnp.einsum(
            "re,de->rd", grad_projected, qkv_full, preferred_element_type=jnp.float32
        )
        unused_value, norm_pull_attn = jax.vjp(
            lambda rows_in: norm_rows(rows_in, gain_rows[0]), tokens
        )
        grad_tokens = grad_middle + norm_pull_attn(grad_normed)[0]
        g_ln1 = jnp.sum(row_weight[:, None] * grad_normed * norm_rows(tokens, 1.0), 0)
        grad_parts.append(grad_tokens[:tok_rows])
        grad_spec_parts.append(grad_tokens[tok_rows:])
        grad_terms = (g_qkv, g_out, g_up, g_down, jnp.stack([g_ln1, g_ls1, g_ln2, g_ls2], 0))
        summed_terms = (
            grad_terms
            if summed_terms is None
            else tuple((held + extra for held, extra in zip(summed_terms, grad_terms)))
        )
    shard_terms = reduce_grads(summed_terms)
    return (
        jnp.concatenate(out_parts, 0),
        jnp.concatenate(spec_parts, 0),
        jnp.concatenate(grad_parts, 0),
        jnp.concatenate(grad_spec_parts, 0),
        shard_terms[0],
        shard_terms[1],
        shard_terms[2],
        shard_terms[3],
        shard_terms[4],
    )


PAD_ID = 99
TUNE = {'after_add_pieces': 'y_gdown', 'after_add_rows': 'branch_rows raise_rows pack_z1', 'after_attend': 'both0_y1', 'after_both2_y1': 'both1_y1', 'after_branch_rows': 'far_out_core1 order_out out_core1', 'after_far_cut_core1': 'pick_pieces', 'after_far_heads_core1': '', 'after_far_out_core1': '', 'after_far_rows_core1': 'pick_pieces', 'after_finish_rows': '', 'after_gb_y1': 'score_back', 'after_gb_z2': 'gdown_z2', 'after_gb_z3': 'h_core1', 'after_gdown_y1': 'raise_rows', 'after_gdown_z1': 'm_core1', 'after_gdown_z2': 'total_core1', 'after_grads_x1': 'project_back pick_grads', 'after_half_gdown': 'branch_back gdown_z1', 'after_heads_core1': 'far_out_core1', 'after_heads_x1': 'out_x1', 'after_join_pieces': 'pick_pieces', 'after_lower_rows': '', 'after_norm_rows_in': 'far_both_z1', 'after_open_pack': '', 'after_order_out': 'both3_y1', 'after_out_x1': 'both_z2', 'after_raise_rows': 'far_rows_core1', 'after_total_core1': 'out_core1', 'after_y_gdown': '', 'after_y_gup': '', 'half_down': 2, 'us_add_pair': 0.002, 'us_branch_back': 0.2, 'us_branch_rows': 6, 'us_down_grads': 45.0, 'us_finish_rows': 0.001, 'us_half_gdown': 0.035, 'us_half_gup': 0.001, 'us_join_grads': 0.11, 'us_join_pieces': 21.0, 'us_lower_rows': 111.0, 'us_mlp_grads': 12, 'us_open_pack': 3.6, 'us_order_out': 48.0, 'us_pick_grads': 0.001, 'us_pick_pieces': 7.5, 'us_score_back': 0.42, 'us_y_gup': 7.0, 'us_z_gdown': 0.001, 'us_z_gup': 0.07}


def knob(name, default, among=None):
    KNOBS.setdefault(name, (default, list(among) if among is not None else None))
    return TUNE.get(name, default)


def wait_for(name, default=""):
    chosen = knob("after_" + name, default, MARK)
    return [MARK[c] for c in chosen.split() if c in MARK]


MARK = {}
KNOBS = {}
COST = {'pick_pieces': 1.5, 'join_pieces': 0.7, 'norm_rows_in': 2, 'open_pack': 1.2, 'attend': 4, 'order_out': 1.6, 'branch_rows': 2, 'raise_rows': 2.8, 'down_grads': 1.5, 'lower_rows': 3.7, 'add_rows': 0.9, 'mlp_grads': 4, 'add_pair': 0.9, 'branch_back': 4, 'score_back': 4.2, 'project_back': 1.3, 'add_pieces': 1.2, 'pick_grads': 0.7, 'finish_rows': 1.4, 'join_grads': 1.1}


def mm(a, b):
    return jnp.dot(a, b, preferred_element_type=F32)


def mm_nt(a, b):
    return lax.dot_general(a, b, (((1,), (1,)), ((), ())), preferred_element_type=F32)


def mm_tn(a, b):
    return lax.dot_general(a, b, (((0,), (0,)), ((), ())), preferred_element_type=F32)


def here():
    place = lax.axis_index("blk")
    group = lax.axis_index("dp")
    return place, place // 2, place % 2, group // 2, group % 2


def chunk_index(slot, z, y):
    return (z ^ (slot % 4)) * 2 + (y ^ (slot // 4))


def row_blocks(block, among=slice(0, 736)):
    return [slice(first, first + block) for first in range(among.start, among.stop, block)]


def fold(rows):
    return rows.reshape(rows.shape[0] // 8, 8, rows.shape[1]).sum(0)


class Keep:
    def __init__(self, value):
        self.value = value


class Far:
    def __init__(self, value, held=True):
        self.value, self.held = value, held


class Load:
    def __init__(self, buffer, copy):
        self.buffer, self.copy, self.waited = buffer, copy, False

    def ready(self):
        if not self.waited:
            self.copy.wait()
            self.waited = True
        return self.buffer


class Store:
    def __init__(self, buffer, target, semaphore):
        self.buffer, self.target, self.semaphore, self.copies = buffer, target, semaphore, []

    def __setitem__(self, at, rows):
        self.buffer[at] = rows

    def __getitem__(self, at):
        return self.buffer[at]

    def go(self, at=None, source=None):
        source, target = self.buffer if source is None else source, self.target
        if at is not None:
            source, target = source.at[at], target.at[at]
        copy = pltpu.make_async_copy(source, target, self.semaphore.at[len(self.copies)])
        copy.start()
        self.copies.append(copy)


def call(kernel, outs, ins, scratch=(), limit=20, after="", label=None):
    label = label or kernel.__name__
    after = wait_for(label, after)
    far = [i for i, v in enumerate(ins) if isinstance(v, Far)]
    far_out = [i for i, v in enumerate(outs) if isinstance(v, Far)]
    plain = [v.value if isinstance(v, (Far, Keep)) else v for v in ins]
    shapes = [v.value if isinstance(v, (Far, Keep)) else v for v in outs]
    near, away = pl.BlockSpec(memory_space=pltpu.VMEM), pl.BlockSpec(memory_space=pltpu.HBM)
    held = [i for i in far_out if outs[i].held]
    room = [pltpu.VMEM(plain[i].shape, plain[i].dtype) for i in far]
    room += [pltpu.VMEM(shapes[i].shape, shapes[i].dtype) for i in held]
    if far or far_out:
        room.append(pltpu.SemaphoreType.DMA((len(far) + len(far_out), MICRO)))

    def body(*refs):
        given = [*refs[: len(ins)], *refs[len(ins) + len(after) :]]
        own = given[len(ins) + len(outs) + len(scratch) :]
        given = given[: len(ins) + len(outs) + len(scratch)]
        copies = []
        for k, i in enumerate(far):
            copies.append(pltpu.make_async_copy(given[i], own[k], own[-1].at[k, 0]))
            given[i] = Load(own[k], copies[-1])
        buffers = dict(zip(held, own[len(far) :]))
        stores = []
        for k, i in enumerate(far_out):
            stores.append(Store(buffers.get(i), given[len(ins) + i], own[-1].at[len(far) + k]))
            given[len(ins) + i] = stores[-1]
        for copy in copies:
            copy.start()
        kernel(*given)
        for store in stores:
            for copy in store.copies:
                copy.wait()

    def placed(v):
        if isinstance(v, Keep):
            return pltpu.with_memory_space_constraint(v.value, pltpu.VMEM)
        return pltpu.with_memory_space_constraint(v.value, pltpu.HBM) if isinstance(v, Far) else v

    def made(v):
        if isinstance(v, Keep):
            return pltpu.VMEM(v.value.shape, v.value.dtype)
        return pltpu.HBM(v.value.shape, v.value.dtype) if isinstance(v, Far) else v

    made_arrays = pl.pallas_call(
        body,
        out_shape=tuple(made(v) for v in outs),
        in_specs=[away if i in far else near for i in range(len(ins))]
        + [pl.BlockSpec(memory_space=pl.ANY)] * len(after),
        out_specs=tuple(away if i in far_out else near for i in range(len(outs))),
        scratch_shapes=[*scratch, *room],
        compiler_params=pltpu.CompilerParams(vmem_limit_bytes=limit * 2**20),
        cost_estimate=pl.CostEstimate(flops=int(knob("us_" + label, COST.get(kernel.__name__, 0.7)) * 10**9), bytes_accessed=0, transcendentals=0),
        name=kernel.__name__,
    )(*[placed(v) for v in ins], *after)
    MARK[label] = made_arrays[0]
    return made_arrays


def keep(*arrays):
    return [Keep(v) for v in arrays]


def sds(*shape, dtype=BF16):
    return jax.ShapeDtypeStruct(shape, dtype)


def pick_pieces(w_qkv, w_up, gains, patches, cots, own, near, far, rows, held):
    place = here()[0]
    held[...] = jnp.zeros_like(held)
    up = w_up.ready()[...].astype(F32)
    qkv = w_qkv.ready()[...].astype(F32)
    gain = gains.ready()[...].astype(F32)
    for b in range(4):
        for d in range(8):
            held[b, 0:24, d * 96 : d * 96 + 96] = up[:, d * 384 + b * 96 : d * 384 + b * 96 + 96]
        for part in range(3):
            held[b, 24:48, part * 192 : part * 192 + 192] = qkv[
                :, part * 768 + b * 192 : part * 768 + b * 192 + 192
            ]
        held[b, 24:28, 576:600] = gain
    own[...] = held[place].astype(BF16)
    near[...] = held[place ^ 1].astype(BF16)
    far[0:48, :] = held[place ^ 2].astype(BF16)
    far[48:96, :] = held[place ^ 3].astype(BF16)
    rows[0:176, :] = patches.ready()[...]
    rows[176:352, :] = cots.ready()[...]


def join_pieces(own, near, far, near_far, w_out, w_down, pack, both, pack_f, up_f):
    place = here()[0]
    pack_f[96:112, :] = jnp.zeros((16, 768), F32)
    pieces = (
        own[...].astype(F32),
        near[...].astype(F32),
        far[0:48, :].astype(F32),
        near_far[48:96, :].astype(F32),
    )
    for k, piece in enumerate(pieces):
        source = place ^ k
        at = pl.ds(pl.multiple_of(source * 24, 8), 24)
        up_f[at, :] = piece[0:24]
        pack_f[at, 0:576] = piece[24:48, 0:576]
        lanes = pl.ds(pl.multiple_of(source * 128, 128), 128)
        pack_f[96:104, lanes] = piece[24:32, 576:704]
    out = w_out[...].astype(F32)
    for i in range(4):
        pack_f[i * 24 : i * 24 + 24, 576:768] = out[:, i * 192 : i * 192 + 192]
    pack[...] = pack_f[...].astype(BF16)
    both[0:96, :] = up_f[...].astype(BF16)
    both[96:192, :] = w_down[...]


def open_pack(*refs):
    chunks, (w_qkv, w_out, gain_rows, out_f, gain_f) = refs[:8], refs[8:]
    _, _, _, z, y = here()
    for slot, chunk in enumerate(chunks):
        d = chunk_index(slot, z, y)
        w_qkv[pl.ds(pl.multiple_of(d * 96, 96), 96), :] = chunk[0:96, 0:576]
        tail = chunk[0:96, 576:768].astype(F32)
        for i in range(4):
            out_f[pl.ds(pl.multiple_of(d * 24, 8), 24), i * 192 : i * 192 + 192] = tail[
                i * 24 : i * 24 + 24
            ]
        gain_f[d] = chunk[96:112, :].astype(F32)
    w_out[...] = out_f[...].astype(BF16)
    gain_rows[...] = jnp.zeros_like(gain_rows)
    for d in range(8):
        for b in range(4):
            at = (d * 4 + b) * 24
            gain_rows[0:4, at : at + 24] = gain_f[d, 0:4, b * 128 : b * 128 + 24]


def normalise(rows):
    centre = rows - jnp.mean(rows, -1, keepdims=True)
    spread = jnp.mean(centre * centre, -1, keepdims=True)
    scale = lax.rsqrt(spread + EPSILON)
    return centre * scale, scale


def place_rows(scratch, blocks, tail, first):
    place = here()[0]
    for k, block in enumerate(blocks):
        rows = block[first : first + 176, :].astype(F32)
        source = place ^ k
        for m in range(MICRO):
            scratch[pl.ds(pl.multiple_of(m * 368 + source * 88, 8), 88), :] = rows[m * 88 : m * 88 + 88]
    rows = tail[...].astype(F32)
    for m in range(MICRO):
        scratch[m * 368 + 352 : m * 368 + 368, :] = jnp.zeros((16, 768), F32)
        scratch[m * 368 + 352 : m * 368 + 362, :] = rows[m * 10 : m * 10 + 10]


def norm_rows_in(rows_0, rows_1, rows_2, rows_3, tail, cot_tail, unit, tokens, cots, rows_f):
    blocks = (rows_0, rows_1, rows_2, rows_3)
    place_rows(rows_f, blocks, cot_tail, 176)
    for at in row_blocks(32):
        cots[at, :] = rows_f[at, :].astype(BF16)
    cots.go()
    place_rows(rows_f, blocks, tail, 0)
    for at in row_blocks(32):
        rows = rows_f[at, :]
        tokens[at, :] = rows.astype(BF16)
        unit[at, :] = normalise(rows)[0]
    tokens.go()


def attend(ids_col, ids_row, unit, w_qkv, gain_rows, attended, w_kept, normed, projected, probs):
    w_kept.go(source=w_qkv)
    gain = gain_rows[0:1, :]
    for m in range(MICRO):
        at = slice(m * 368, m * 368 + 368)
        normed[at, :] = (unit[at, :] * gain).astype(BF16)
        normed.go(at)
        qkv = mm(normed[at, :], w_qkv[...])
        qkv = jnp.concatenate([qkv[:, 0:192] * SCORE_SCALE, qkv[:, 192:576]], -1).astype(BF16)
        projected[at, :] = qkv
        projected.go(at)
        same = ids_col[at, :] == ids_row[m : m + 1, :]
        bias = jnp.where(same, 0.0, MASKED)
        heads = []
        for h in range(3):
            q = qkv[:, h * 64 : h * 64 + 64]
            k = qkv[:, 192 + h * 64 : 192 + h * 64 + 64]
            v = qkv[:, 384 + h * 64 : 384 + h * 64 + 64]
            scores = mm_nt(q, k) + bias
            weights = jnp.exp(scores - jnp.max(scores, -1, keepdims=True))
            weights = weights * (1.0 / jnp.sum(weights, -1, keepdims=True))
            weights = weights.astype(BF16)
            probs[m * 3 + h] = weights
            heads.append(mm(weights, v))
        probs.go(slice(m * 3, m * 3 + 3))
        attended[at, :] = jnp.concatenate(heads, -1).astype(BF16)


def order_out(out_0, out_1, out_2, out_3, cots, gain_rows, ordered, mine, grad_mlp, out_f):
    place = here()[0]
    for k, part in enumerate((out_0, out_1, out_2, out_3)):
        source = place ^ k
        rows = part[...].astype(F32)
        for d in range(8):
            at = pl.multiple_of((d * 4 + source) * 24, 8)
            out_f[pl.ds(at, 24), :] = rows[d * 24 : d * 24 + 24]
    ordered[...] = out_f[...].astype(BF16)
    mine[...] = out_f[pl.ds(pl.multiple_of(place * 192, 8), 192), :].astype(BF16)
    mine.go()
    gain = gain_rows[3:4, :]
    for at in row_blocks(32):
        grad_mlp[at, :] = (gain * cots[at, :].astype(F32)).astype(BF16)
    grad_mlp.go()


def branch_rows(
    head_0, head_1, head_2, head_3, w_out, tokens, gain_rows, normed, branch, middle, rows_f
):
    place = here()[0]
    gain_s, gain_n = gain_rows[1:2, :], gain_rows[2:3, :]
    for m in range(MICRO):
        group = slice(m * 368, m * 368 + 368)
        total = None
        for k, part in enumerate((head_0, head_1, head_2, head_3)):
            rows = w_out[pl.ds(pl.multiple_of((place ^ k) * 192, 16), 192), :]
            term = mm(part[group, :], rows)
            total = term if total is None else total + term
        rows_f[group, :] = total
        for at in row_blocks(16, group):
            a = rows_f[at, :]
            branch[at, :] = a.astype(BF16)
            rows = tokens[at, :].astype(F32) + gain_s * a
            middle[at, :] = rows
            normed[at, :] = (normalise(rows)[0] * gain_n).astype(BF16)
        branch.go(group)
        middle.go(group)


def raise_rows(*refs):
    normed, chunks = refs[0], refs[1:9]
    active, slope, w_up, w_down, normed_kept, down_kept, rows_f = refs[9:]
    normed_kept.go(source=normed)
    _, _, _, z, y = here()
    for slot, chunk in enumerate(chunks):
        d = chunk_index(slot, z, y)
        w_up[pl.ds(pl.multiple_of(d * 96, 96), 96), :] = chunk[0:96, :]
        w_down[pl.ds(pl.multiple_of(d * 96, 96), 96), :] = chunk[96:192, :]
    down_kept.go(source=w_down)
    for m in range(MICRO):
        at = slice(m * 368, m * 368 + 368)
        rows_f[at, :] = mm(normed[at, :], w_up[...])
    for at in row_blocks(32):
        u = rows_f[at, :]
        half = 0.5 + 0.5 * lax.erf(u * 0.7071067811865476)
        active[at, :] = (u * half).astype(BF16)
        slope[at, :] = half + u * (0.3989422804014327 * jnp.exp(-0.5 * u * u))


def down_grads(active, grad_mlp, away, kept, active_kept, work):
    active_kept.go(source=active)
    y = here()[4]
    work[...] = mm_tn(active[...], grad_mlp[...])
    halve(work, y, away, kept, 96)


def lower_rows(slope, grad_mlp, w_up, w_down, away, kept, grad_hidden, work):
    core = here()[2]
    for m in range(MICRO):
        at = slice(m * 368, m * 368 + 368)
        grad = mm_nt(grad_mlp[at, :], w_down[...])
        grad_hidden[at, :] = (slope[at, :] * grad).astype(BF16)
        grad_hidden.go(at)
        work[m] = mm_nt(grad_hidden[at, :], w_up[...])
    away[...] = work[1 - core].astype(BF16)
    kept[...] = work[core]


def split_rows(pieces, place, away, kept):
    away[0:208, :] = pieces[place ^ 1].astype(BF16)
    away[208:416, :] = pieces[place ^ 3].astype(BF16)
    kept[0:208, :] = pieces[place]
    kept[208:416, :] = pieces[place ^ 2]


def cut_rows(rows_f, pieces):
    for b in range(4):
        for m in range(MICRO):
            pieces[b, m * 104 : m * 104 + 88, :] = rows_f[m * 368 + b * 88 : m * 368 + b * 88 + 88, :]
            pieces[b, m * 104 + 88 : m * 104 + 104, :] = rows_f[m * 368 + 352 : m * 368 + 368, :]


def halve(grad_f, y, away, kept, rows):
    for zz in range(4):
        other = pl.ds(pl.multiple_of((zz * 2 + 1 - y) * rows, 8), rows)
        ours = pl.ds(pl.multiple_of((zz * 2 + y) * rows, 8), rows)
        away[zz] = grad_f[other, 0 : away.shape[2]].astype(BF16)
        kept[zz] = grad_f[ours, 0 : away.shape[2]]


def mlp_grads(
    active, normed, grad_hidden, w_down, cots, targets, head_0, head_1, head_2, head_3,
    up_away, up_kept, rows_away, rows_kept, scale_grad, chosen, work, pieces,
):
    place, _, _, _, y = here()
    work[0:768, :] = mm_tn(normed.ready()[...], grad_hidden.ready()[...])
    halve(work, y, up_away, up_kept, 96)
    active, w_down, cots = active.ready(), w_down.ready(), cots.ready()
    for m in range(MICRO):
        at = slice(m * 368, m * 368 + 368)
        work[at, :] = mm(active[at, :], w_down[...])
    total = jnp.zeros((8, 768), F32)
    for at in row_blocks(32):
        total = total + fold(cots[at, :].astype(F32) * work[at, :])
    scale_grad[...] = total
    cut_rows(work, pieces)
    split_rows(pieces, place, rows_away, rows_kept)
    picked = None
    for k, part in enumerate((head_0, head_1, head_2, head_3)):
        index = lax.broadcasted_iota(jnp.int32, (192, 192), 0) + (place ^ k) * 192
        pick = jnp.where(index == targets[...], 1.0, 0.0).astype(BF16)
        term = mm(part[...], pick)
        picked = term if picked is None else picked + term
    chosen[...] = picked.astype(BF16)


def add_rows(kept, came, total):
    total[...] = (kept[...] + came[...].astype(F32)).astype(BF16)


def add_pair(here_rows, came, total):
    total[...] = (here_rows[...].astype(F32) + came[...].astype(F32)).astype(BF16)


def branch_back(
    sum_own, sum_near, middle, cots, branch, gain_rows, w_mine, probs, normed, scale_grad_mlp, chosen,
    grad_rows, grad_heads, grad_v, away, kept,
    work, grad_branch, grad_mid, extra, early,
):
    place, _, core, _, y = here()
    for m in range(MICRO):
        at = slice(m * 368, m * 368 + 368)

        @pl.when(core == m)
        def _():
            work[at, :] = sum_own[...].astype(F32)

        @pl.when(core != m)
        def _():
            work[at, :] = sum_near[...].astype(F32)

    gain_s, gain_n = gain_rows[1:2, :], gain_rows[2:3, :]
    scale_sum = jnp.zeros((8, 768), F32)
    for at in row_blocks(32):
        unit, scale = normalise(middle[at, :])
        pulled = work[at, :] * gain_n
        pulled = pulled - jnp.mean(pulled, -1, keepdims=True) - unit * jnp.mean(
            pulled * unit, -1, keepdims=True
        )
        through = cots[at, :].astype(F32) + scale * pulled
        grad_mid[at, :] = through
        grad_branch[at, :] = (gain_s * through).astype(BF16)
        scale_sum = scale_sum + fold(through * branch[at, :].astype(F32))
    for m in range(MICRO):
        for part, first in ((0, place * 88), (88, 352)):
            rows = 88 if part == 0 else 16
            grad_rows[m * 104 + part : m * 104 + part + rows, :] = grad_mid[
                pl.ds(pl.multiple_of(m * 368 + first, 8), rows), :
            ]
    for m in range(MICRO):
        at = slice(m * 368, m * 368 + 368)
        heads = mm_nt(grad_branch[at, :], w_mine[...]).astype(BF16)
        grad_heads[at, :] = heads
        terms = [mm_tn(probs[m * 3 + h], heads[:, h * 64 : h * 64 + 64]) for h in range(3)]
        grad_v[at, :] = jnp.concatenate(terms, -1).astype(BF16)
    grad_mid[0:768, 0:192] = mm_tn(normed[...], grad_v[...])
    extra[...] = mm_tn(chosen[...], grad_branch[...])
    scale_rows = (
        0.25 * jnp.sum(scale_sum, 0, keepdims=True),
        jnp.sum(scale_grad_mlp[...], 0, keepdims=True),
    )
    for d in range(8):
        base = d * 112
        early[base : base + 96, 0:192] = grad_mid[d * 96 : d * 96 + 96, 0:192]
        for i in range(4):
            early[base + i * 24 : base + i * 24 + 24, 192:384] = extra[
                d * 24 : d * 24 + 24, i * 192 : i * 192 + 192
            ]
        early[base + 96 : base + 112, :] = jnp.zeros((16, 384), F32)
        for i in range(2):
            early[base + 96 + i : base + 97 + i, 0:96] = scale_rows[i][:, d * 96 : d * 96 + 96]
    halve(early, y, away, kept, 112)


def score_back(probs, projected, grad_heads, normed, grad_qk, away, kept, work):
    _, _, _, _, y = here()
    for m in range(MICRO):
        at = slice(m * 368, m * 368 + 368)
        qkv = projected[at, :]
        g_heads = grad_heads[at, :]
        grads = [[], []]
        for h in range(3):
            q = qkv[:, h * 64 : h * 64 + 64]
            k = qkv[:, 192 + h * 64 : 192 + h * 64 + 64]
            v = qkv[:, 384 + h * 64 : 384 + h * 64 + 64]
            grad_prob = mm_nt(g_heads[:, h * 64 : h * 64 + 64], v)
            wide = probs[m * 3 + h].astype(F32)
            moved = wide * grad_prob
            delta = jnp.sum(moved, -1, keepdims=True)
            grad_score = (moved - wide * delta).astype(BF16)
            grads[0].append(mm(grad_score, k) * SCORE_SCALE)
            grads[1].append(mm_tn(grad_score, q))
        grad_qk[at, :] = jnp.concatenate(grads[0] + grads[1], -1).astype(BF16)
    work[...] = mm_tn(normed[...], grad_qk[...])
    halve(work, y, away, kept, 96)


def project_back(grad_qk, grad_v, w_qkv, rows_away, rows_kept, work, pieces):
    place = here()[0]
    for m in range(MICRO):
        at = slice(m * 368, m * 368 + 368)
        work[at, :] = mm_nt(grad_qk[at, :], w_qkv[:, 0:384]) + mm_nt(grad_v[at, :], w_qkv[:, 384:576])
    cut_rows(work, pieces)
    split_rows(pieces, place, rows_away, rows_kept)


def sum_y(kept, came, own, send_1, send_2, send_3):
    _, _, _, z, _ = here()
    own[...] = kept[z] + came[z].astype(F32)
    for k, send in ((1, send_1), (2, send_2), (3, send_3)):
        send[...] = (kept[z ^ k] + came[z ^ k].astype(F32)).astype(BF16)


def sum_y_pairs(kept, came, own, away):
    _, _, _, z, _ = here()
    for k in range(2):
        own[k] = kept[z ^ (2 * k)] + came[z ^ (2 * k)].astype(F32)
        there = z ^ (2 * k + 1)
        away[k] = (kept[there] + came[there].astype(F32)).astype(BF16)


def sum_pairs(kept, came, own, away):
    own[...] = kept[0] + came[0].astype(F32)
    away[...] = (kept[1] + came[1].astype(F32)).astype(BF16)


def sum_last(own, came, total):
    total[...] = own[...] + came[...].astype(F32)


def sum_z(own, came_1, came_2, came_3, total):
    total[...] = (
        own[...]
        + came_1[...].astype(F32)
        + came_2[...].astype(F32)
        + came_3[...].astype(F32)
    )


def add_pieces(kept_m, came_m, kept_h, came_h, stay, go):
    for i, (kept, came) in enumerate(((kept_m, came_m), (kept_h, came_h))):
        stay[i * 208 : i * 208 + 208, :] = kept[0:208, :] + came[0:208, :].astype(F32)
        go[i * 208 : i * 208 + 208, :] = (kept[208:416, :] + came[208:416, :].astype(F32)).astype(BF16)


def finish_rows(
    stay, came, middle, grad_rows, patches, tail, gain_rows,
    out_patches, out_special, grad_patches, grad_special,
):
    place = here()[0]
    own = patches[...].astype(F32)
    rest = tail[...].astype(F32)
    outs, out_tails = [], []
    for m in range(MICRO):
        for part, first in ((0, place * 88), (88, 352)):
            count = 88 if part == 0 else 10
            at = slice(m * 104 + part, m * 104 + part + count)
            far_at = slice(208 + m * 104 + part, 208 + m * 104 + part + count)
            mid = middle[pl.ds(pl.multiple_of(m * 368 + first, 8), count), :]
            final = mid + gain_rows[3:4, :] * (stay[at, :] + came[at, :].astype(F32))
            (outs if part == 0 else out_tails).append(final)
            rows = own[m * 88 : m * 88 + 88] if part == 0 else rest[m * 10 : m * 10 + 10]
            unit, scale = normalise(rows)
            pulled = gain_rows[0:1, :] * (stay[far_at, :] + came[far_at, :].astype(F32))
            pulled = pulled - jnp.mean(pulled, -1, keepdims=True) - unit * jnp.mean(
                pulled * unit, -1, keepdims=True
            )
            grad = grad_rows[at, :] + scale * pulled
            if part == 0:
                grad_patches[m * 88 : m * 88 + 88, :] = grad
            else:
                grad_special[m * 10 : m * 10 + 10, :] = grad
    out_patches[...] = jnp.concatenate(outs, 0).astype(BF16)
    out_special[...] = jnp.concatenate(out_tails, 0).astype(BF16)


def pick_grads(up, first, second, own, near, far, grad_out, held):
    place = here()[0]
    for b in range(4):
        at = slice(b * 24, b * 24 + 24)
        held[b, 0:24, :] = up[at, :]
        held[b, 24:48, 0:384] = second[at, :]
        held[b, 24:48, 384:576] = first[at, 0:192]
        held[b, 24:48, 576:768] = jnp.zeros((24, 192), F32)
        held[b, 24:26, 576:600] = first[96:98, at]
        grad_out[:, b * 192 : b * 192 + 192] = first[at, 192:384]
    own[...] = held[place]
    near[...] = held[place ^ 1].astype(BF16)
    far[0:48, :] = held[place ^ 2].astype(BF16)
    far[48:96, :] = held[place ^ 3].astype(BF16)


def as_row(column):
    count = column.shape[0]
    square = lax.broadcasted_iota(jnp.int32, (count, count), 0)
    across = lax.broadcasted_iota(jnp.int32, (count, count), 1)
    return jnp.sum(jnp.where(square == across, column, 0.0), 0, keepdims=True)


def join_grads(
    own, near, far, near_far, w_qkv, w_up, gains, grad_qkv, grad_up, grad_gains, held
):
    place = here()[0]
    held[place] = own[...]
    held[place ^ 1] = near[...].astype(F32)
    held[place ^ 2] = far[0:48, :].astype(F32)
    held[place ^ 3] = near_far[48:96, :].astype(F32)
    scales = None
    for b in range(4):
        for d in range(8):
            at = d * 384 + b * 96
            grad_up[:, at : at + 96] = held[b, 0:24, d * 96 : d * 96 + 96]
        for part in range(3):
            at = part * 768 + b * 192
            grad_qkv[:, at : at + 192] = held[b, 24:48, part * 192 : part * 192 + 192]
        term = held[b, 24:26, 576:600]
        scales = term if scales is None else scales + term
    norm_1 = as_row(jnp.sum(w_qkv[...].astype(F32) * grad_qkv[...], -1, keepdims=True))
    norm_2 = as_row(jnp.sum(w_up[...].astype(F32) * grad_up[...], -1, keepdims=True))
    gain = gains[...].astype(F32)
    grad_gains[0:1, :] = norm_1 / gain[0:1, :]
    grad_gains[1:2, :] = scales[0:1, :]
    grad_gains[2:3, :] = norm_2 / gain[2:3, :]
    grad_gains[3:4, :] = scales[1:2, :]


def send(rows, axis, step, label, after=""):
    pairs = []
    for group in range(8):
        z, y = group // 2, group % 2
        for place in range(4):
            target = {
                "core": (group, place ^ 1),
                "x": (group, place ^ 2),
                "y": (z * 2 + 1 - y, place),
                "z": ((z ^ step) * 2 + y, place),
            }[axis]
            pairs.append((group * 4 + place, target[0] * 4 + target[1]))
    label = f"{label}_{axis}{step}"
    ready = wait_for(label, after)
    if ready:
        rows = lax.optimization_barrier((rows, *ready))[0]
    with jax.named_scope(label):
        MARK[label] = lax.ppermute(rows, ("dp", "blk"), pairs)
    return MARK[label]


def gather_z(chunk, label, after=""):
    second = send(chunk, "z", 2, label, after)
    return [chunk, send(chunk, "z", 1, label, after), second, send(second, "z", 1, f"far_{label}")]


def gather_y(along_z, label):
    return along_z + [send(part, "y", 1, f"{label}{k}") for k, part in enumerate(along_z)]


def add_y(kept, came, label, after):
    rows, width = kept.shape[1:]
    own, *parts = call(
        sum_y,
        [Keep(sds(rows, width, dtype=F32))] + [sds(rows, width)] * 3,
        [Keep(kept), came],
        after=after,
        label="y_" + label,
    )
    return [own, *[send(part, "z", k, label) for k, part in zip((1, 2, 3), parts)]]


def halve_y(kept, came, label, after):
    rows, width = kept.shape[1:]
    own, away = call(
        sum_y_pairs,
        [Keep(sds(2, rows, width, dtype=F32)), sds(2, rows, width)],
        [Keep(kept), came],
        after=after,
        label="y_" + label,
    )
    return own, send(away, "z", 1, label)


def halve_z(pair, label, after):
    kept, came = pair
    rows, width = kept.shape[1:]
    own, away = call(
        sum_pairs,
        [Keep(sds(rows, width, dtype=F32)), sds(rows, width)],
        [Keep(kept), came],
        after=after,
        label="half_" + label,
    )
    return own, send(away, "z", 2, label)


def add_last(last, label, after):
    own, came = last
    return call(
        sum_last, [sds(*own.shape, dtype=F32)], [Keep(own), came], after=after, label="z_" + label
    )[0]


def add_z(steps, label, after):
    own, *came = steps
    return call(
        sum_z, [sds(*own.shape, dtype=F32)], [Keep(own), *came], after=after, label="z_" + label
    )[0]


def on_device_split(
    patches, special, image_ids, w_qkv, w_out, w_up, w_down, gains, cot_patches, cot_special
):
    MARK.clear()
    place = lax.axis_index("blk")
    spec_ids = jnp.concatenate(
        [jnp.arange(10, dtype=jnp.int32) // SPECIAL, jnp.full((6,), PAD_ID, jnp.int32)]
    )
    ids = image_ids.reshape(4, 2, 88).transpose(1, 0, 2).reshape(2, 352)
    ids_row = jnp.concatenate([ids, jnp.broadcast_to(spec_ids, (2, 16))], 1)
    ids_col = ids_row.reshape(736, 1)
    column = jnp.arange(192, dtype=jnp.int32)
    targets = (column + column // 24 * 72 + place * 24).reshape(1, 192)

    own, near, far, rows = call(
        pick_pieces,
        [sds(48, 768), sds(48, 768), sds(96, 768), sds(352, 768)],
        [Far(w_qkv), Far(w_up), Far(gains), Far(patches), Far(cot_patches)],
        [pltpu.VMEM((4, 48, 768), F32)],
    )
    came_far = send(far, "x", 1, "cut")
    came_near, came_near_far = send(near, "core", 1, "cut"), send(came_far, "core", 1, "far_cut")
    pack, both = call(
        join_pieces,
        [sds(112, 768), sds(192, 768)],
        [own, came_near, came_far, came_near_far, w_out, w_down],
        [pltpu.VMEM((112, 768), F32), pltpu.VMEM((96, 768), F32)],
    )
    pack_z = gather_z(pack, "pack")
    far_rows = send(rows, "x", 1, "rows", "cut_x1")
    near_rows = send(rows, "core", 1, "rows")
    row_parts = [rows, near_rows, far_rows, send(far_rows, "core", 1, "far_rows", "pack_z1")]
    pack_chunks = gather_y(pack_z, "pack")
    both_z = gather_z(both, "both", "pack_z2")
    unit, tokens, cots = call(
        norm_rows_in,
        [Keep(sds(736, 768, dtype=F32)), *[Far(sds(736, 768))] * 2],
        [*row_parts, special, cot_special],
        [pltpu.VMEM((736, 768), F32)],
        after="pack_z2",
    )
    qkv_full, out_part, gain_rows = call(
        open_pack,
        [Keep(sds(768, 576)), sds(192, 768), Keep(sds(8, 768, dtype=F32))],
        pack_chunks,
        [pltpu.VMEM((192, 768), F32), pltpu.VMEM((8, 16, 768), F32)],
        after="norm_rows_in",
    )
    far_out = send(out_part, "x", 1, "out")
    both_chunks = gather_y(both_z, "both")
    attended, qkv_far, normed_far, projected, probs = call(
        attend,
        [
            sds(736, 192), Far(sds(768, 576), held=False), Far(sds(736, 768)),
            Far(sds(736, 576)), Far(sds(6, 368, 368)),
        ],
        [ids_col, ids_row, *keep(unit, qkv_full, gain_rows)],
    )
    far_heads = send(attended, "x", 1, "heads")
    out_parts = [
        out_part, send(out_part, "core", 1, "out", "attend"),
        far_out, send(far_out, "core", 1, "far_out", "attend"),
    ]
    out_full, out_mine, grad_mlp = call(
        order_out,
        [Keep(sds(768, 768)), Far(sds(192, 768)), Far(sds(736, 768))],
        [*out_parts, cots, Keep(gain_rows)],
        [pltpu.VMEM((768, 768), F32)],
    )
    heads = [
        attended, send(attended, "core", 1, "heads"),
        far_heads, send(far_heads, "core", 1, "far_heads", "order_out"),
    ]
    normed_mlp, branch, middle = call(
        branch_rows,
        [Keep(sds(736, 768)), Far(sds(736, 768)), Far(sds(736, 768, dtype=F32))],
        [*heads, Keep(out_full), tokens, Keep(gain_rows)],
        [pltpu.VMEM((736, 768), F32)],
    )
    active, slope, up_full, down_full, normed_mlp, down_far = call(
        raise_rows,
        [
            *keep(sds(736, 768), sds(736, 768, dtype=F32), sds(768, 768), sds(768, 768)),
            Far(sds(736, 768), held=False), Far(sds(768, 768), held=False),
        ],
        [Keep(normed_mlp), *both_chunks],
        [pltpu.VMEM((736, 768), F32)],
    )
    half = [sds(4, 96, 768), Keep(sds(4, 96, 768, dtype=F32))]
    rows_split = [sds(416, 768), Keep(sds(416, 768, dtype=F32))]
    down_away, down_kept, active = call(
        down_grads,
        [*half, Far(sds(736, 768), held=False)],
        [Keep(active), grad_mlp],
        [pltpu.VMEM((768, 768), F32)],
    )
    down_came = send(down_away, "y", 1, "gdown")
    sum_away, sum_kept, grad_hidden = call(
        lower_rows,
        [sds(368, 768), Keep(sds(368, 768, dtype=F32)), Far(sds(736, 768))],
        [Keep(slope), grad_mlp, *keep(up_full, down_full)],
        [pltpu.VMEM((2, 368, 768), F32)],
        after="down_grads",
    )
    sum_came = send(sum_away, "core", 1, "sum")
    chip_sum = call(add_rows, [sds(368, 768)], [Keep(sum_kept), sum_came])[0]
    chip_came = send(chip_sum, "x", 1, "sum")
    up_away, up_kept, m_away, m_kept, scale_mlp, chosen = call(
        mlp_grads,
        [*half, *rows_split, *keep(sds(8, 768, dtype=F32), sds(736, 192))],
        [*[Far(v) for v in (active, normed_mlp, grad_hidden, down_far, cots)], targets, *heads],
        [pltpu.VMEM((768, 768), F32), pltpu.VMEM((4, 208, 768), F32)],
        after="add_rows",
    )
    up_came = send(up_away, "y", 1, "gup")
    m_came = send(m_away, "core", 1, "m")
    down_steps = halve_y(down_kept, down_came, "gdown", "mlp_grads")
    sum_own = call(add_pair, [sds(368, 768)], [chip_sum, chip_came], after="y_gdown")[0]
    sum_near = send(sum_own, "core", 1, "total")
    grad_rows, grad_heads, grad_v, a_away, a_kept = call(
        branch_back,
        [
            *keep(sds(208, 768, dtype=F32), sds(736, 192), sds(736, 192)),
            sds(4, 112, 384), Keep(sds(4, 112, 384, dtype=F32)),
        ],
        [
            sum_own, sum_near, middle, cots, branch, Keep(gain_rows), out_mine,
            probs, normed_far, *keep(scale_mlp, chosen),
        ],
        [
            pltpu.VMEM((736, 768), F32), pltpu.VMEM((736, 768), BF16),
            pltpu.VMEM((768, 768), F32), pltpu.VMEM((192, 768), F32), pltpu.VMEM((896, 384), F32),
        ],
    )
    a_came = send(a_away, "y", 1, "ga")
    order = knob("up_steps", 1, [0, 1, 2])
    if order == 0:
        up_steps = halve_y(up_kept, up_came, "gup", "branch_back")
    when = knob("half_down", 0, [0, 1, 2])
    if when == 0:
        down_last = halve_z(down_steps, "gdown", "branch_back")
    grad_qk, b_away, b_kept = call(
        score_back,
        [Keep(sds(736, 384)), sds(4, 96, 384), Keep(sds(4, 96, 384, dtype=F32))],
        [probs, projected, Keep(grad_heads), normed_far],
        [pltpu.VMEM((768, 384), F32)],
    )
    b_came = send(b_away, "y", 1, "gb")
    early_a = knob("early_a", False)
    if early_a:
        a_pair = halve_y(a_kept, a_came, "ga", "score_back")
    if order == 1:
        up_steps = halve_y(up_kept, up_came, "gup", "score_back")
    h_away, h_kept = call(
        project_back,
        rows_split,
        [*keep(grad_qk, grad_v), qkv_far],
        [pltpu.VMEM((736, 768), F32), pltpu.VMEM((4, 208, 768), F32)],
    )
    h_came = send(h_away, "core", 1, "h")
    if when == 1:
        down_last = halve_z(down_steps, "gdown", "project_back")
    if order == 2:
        up_steps = halve_y(up_kept, up_came, "gup", "project_back")
    stay, go = call(
        add_pieces,
        [Keep(sds(416, 768, dtype=F32)), sds(416, 768)],
        [Keep(m_kept), m_came, Keep(h_kept), h_came],
    )
    far_rows = send(go, "x", 1, "mh")
    if when == 2:
        down_last = halve_z(down_steps, "gdown", "add_pieces")
    up_last = None
    if knob("half_up", True):
        up_last = halve_z(up_steps, "gup", "add_pieces")
    if not early_a:
        a_pair = halve_y(a_kept, a_came, "ga", "project_back")
    b_steps = add_y(b_kept, b_came, "gb", "add_pieces")
    a_last = halve_z(a_pair, "ga", "y_gb")
    if up_last is None:
        up_last = halve_z(up_steps, "gup", "y_gb")
    grad_down = add_last(down_last, "gdown", "y_gb")
    grad_up_rows = add_last(up_last, "gup", "z_gdown")
    first_rows = add_last(a_last, "ga", "z_gup")
    second_rows = add_z(b_steps, "gb", "z_ga")
    own, near, far, grad_out = call(
        pick_grads,
        [Keep(sds(48, 768, dtype=F32)), sds(48, 768), sds(96, 768), sds(24, 768, dtype=F32)],
        [grad_up_rows, first_rows, second_rows],
        [pltpu.VMEM((4, 48, 768), F32)],
    )
    came_far = send(far, "x", 1, "grads")
    came_near, came_near_far = send(near, "core", 1, "grads"), send(came_far, "core", 1, "far_grads")
    out_patches, out_special, grad_patches, grad_special = call(
        finish_rows,
        [
            sds(176, 768), sds(20, 768), sds(176, 768, dtype=F32), sds(20, 768, dtype=F32),
        ],
        [Keep(stay), far_rows, middle, Keep(grad_rows), patches, special, Keep(gain_rows)],
        after="pick_grads",
    )
    grad_qkv, grad_up, grad_gains = call(
        join_grads,
        [sds(24, 2304, dtype=F32), sds(24, 3072, dtype=F32), sds(4, 24, dtype=F32)],
        [Keep(own), came_near, came_far, came_near_far, w_qkv, w_up, gains],
        [pltpu.VMEM((4, 48, 768), F32)],
        after="finish_rows",
    )
    return (
        out_patches, out_special, grad_patches, grad_special,
        grad_qkv, grad_out, grad_up, grad_down, grad_gains,
    )


def solution(mesh):
    placed = (
        P(("dp", "blk"), None),
        P("dp", None),
        P("dp"),
        P(("dp", "blk"), None),
        P(("dp", "blk"), None),
        P(("dp", "blk"), None),
        P(("dp", "blk"), None),
        P(None, ("dp", "blk")),
        P(("dp", "blk"), None),
        P("dp", None),
    )
    whole = dict(mesh.shape) != {"dp": 8, "blk": 4}
    return jax.shard_map(
        on_device if whole else on_device_split,
        mesh=mesh,
        in_specs=placed,
        out_specs=(
            P(("dp", "blk"), None),
            P("dp", None),
            P(("dp", "blk"), None),
            P("dp", None),
            P(("dp", "blk"), None),
            P(("dp", "blk"), None),
            P(("dp", "blk"), None),
            P(("dp", "blk"), None),
            P(None, ("dp", "blk")),
        ),
        check_vma=False,
    )
```

```python
import jax
import jax.numpy as jnp
from jax import lax
from jax.experimental import pallas as pl
from jax.experimental.pallas import tpu as pltpu
from jax.sharding import PartitionSpec as P

HEAD_DIM = 64
SPECIAL = 5
MICRO = 2
TOK_MB = 88

SCORE_SCALE = 0.125
MASKED = -1e30
EPSILON = 1e-06

BF16 = jnp.bfloat16
F32 = jnp.float32


def merged(shard, axis, combine):
    everything = jax.tree.map(
        lambda part, kind: lax.all_gather(part.astype(kind), axis),
        shard,
        (jnp.bfloat16, jnp.bfloat16, jnp.bfloat16),
    )

    def take(k):
        return jax.tree.map(lambda part, own: part[k].astype(own.dtype), everything, shard)

    return lax.fori_loop(
        1, lax.axis_size(axis), lambda k, so_far: combine(so_far, take(k)), take(0)
    )


def from_behind(shard, axis, by):
    peers = lax.axis_size(axis)
    return lax.ppermute(shard, axis, [(i, (i + by) % peers) for i in range(peers)])


def norm_rows(values, gain_row):
    centre = values - jnp.mean(values, -1, keepdims=True)
    spread = jnp.mean(centre * centre, -1, keepdims=True)
    return centre * lax.rsqrt(spread + EPSILON) * gain_row


def split_heads(matrix):
    return matrix.reshape(matrix.shape[0], -1, HEAD_DIM)


def widen(per_head):
    return jnp.repeat(per_head.T, HEAD_DIM, axis=1)


def empty_state(length, head_count, feature_width):
    return (
        jnp.full((head_count, length), MASKED, jnp.float32),
        jnp.zeros((head_count, length), jnp.float32),
        jnp.zeros((length, feature_width), jnp.float32),
    )


def online(carried, queries, query_ids, key_rows, value_rows, key_ids):
    top_score, totals, accumulated = carried
    same_image = (query_ids[:, None] == key_ids[None, :])[None]
    scores = (
        jnp.einsum(
            "qhd,khd->hqk",
            split_heads(queries),
            split_heads(key_rows),
            preferred_element_type=jnp.float32,
        )
        * SCORE_SCALE
    )
    scores = jnp.where(same_image, scores, MASKED)
    new_top = jnp.maximum(top_score, jnp.max(scores, -1))
    weights = jnp.where(same_image, jnp.exp(scores - new_top[..., None]), 0.0)
    factor = jnp.exp(top_score - new_top)
    totals = totals * factor + jnp.sum(weights, -1)
    mixture = jnp.einsum(
        "hqk,khd->qhd",
        weights.astype(jnp.bfloat16),
        split_heads(value_rows),
        preferred_element_type=jnp.float32,
    )
    accumulated = accumulated * widen(factor) + mixture.reshape(accumulated.shape)
    return (new_top, totals, accumulated)


def combine(former, latter):
    highest = jnp.maximum(former[0], latter[0])
    scale_former = jnp.exp(former[0] - highest)
    scale_latter = jnp.exp(latter[0] - highest)
    return (
        highest,
        former[1] * scale_former + latter[1] * scale_latter,
        former[2] * widen(scale_former) + latter[2] * widen(scale_latter),
    )


def finish(carried):
    top_score, totals, accumulated = carried
    return (accumulated / widen(totals), top_score + jnp.log(totals))


def block_grads(queries, grad_attn, log_total, row_delta, query_ids, key_rows, value_rows, key_ids):
    same_image = (query_ids[:, None] == key_ids[None, :])[None]
    q_heads = split_heads(queries)
    g_heads = split_heads(grad_attn)
    scores = (
        jnp.einsum(
            "qhd,khd->hqk", q_heads, split_heads(key_rows), preferred_element_type=jnp.float32
        )
        * SCORE_SCALE
    )
    probabilities = jnp.where(same_image, jnp.exp(scores - log_total[..., None]), 0.0)
    grad_prob = jnp.einsum(
        "qhd,khd->hqk", g_heads, split_heads(value_rows), preferred_element_type=jnp.float32
    )
    dscore = (probabilities * (grad_prob - row_delta[..., None])).astype(jnp.bfloat16)
    grad_query = (
        jnp.einsum(
            "hqk,khd->qhd", dscore, split_heads(key_rows), preferred_element_type=jnp.float32
        ).reshape(queries.shape[0], -1)
        * SCORE_SCALE
    )
    grad_key = (
        jnp.einsum("hqk,qhd->khd", dscore, q_heads, preferred_element_type=jnp.float32).reshape(
            key_rows.shape[0], -1
        )
        * SCORE_SCALE
    )
    grad_value = jnp.einsum(
        "hqk,qhd->khd",
        probabilities.astype(jnp.bfloat16),
        g_heads,
        preferred_element_type=jnp.float32,
    ).reshape(key_rows.shape[0], -1)
    return (grad_query, grad_key, grad_value)


def fetch_weights(w_qkv, w_out, w_up, w_down, gains):
    return (
        lax.all_gather(w_qkv, ("dp", "blk"), axis=0, tiled=True),
        lax.all_gather(w_out, ("dp", "blk"), axis=0, tiled=True),
        lax.all_gather(w_up, ("dp", "blk"), axis=0, tiled=True),
        lax.all_gather(w_down, ("dp", "blk"), axis=0, tiled=True),
        lax.all_gather(gains, ("dp", "blk"), axis=1, tiled=True),
    )


def reduce_grads(grad_terms):
    g_qkv, g_out, g_up, g_down, g_gains = grad_terms
    return (
        lax.psum_scatter(g_qkv, ("dp", "blk"), scatter_dimension=0, tiled=True),
        lax.psum_scatter(g_out, ("dp", "blk"), scatter_dimension=0, tiled=True),
        lax.psum_scatter(g_up, ("dp", "blk"), scatter_dimension=0, tiled=True),
        lax.psum_scatter(g_down, ("dp", "blk"), scatter_dimension=0, tiled=True),
        lax.psum_scatter(g_gains, ("dp", "blk"), scatter_dimension=1, tiled=True),
    )


def contract_rows(left_rows, right_rows):
    return jnp.einsum("ra,rb->ab", left_rows, right_rows, preferred_element_type=jnp.float32)


def row_delta_of(grad_attn, attended):
    product = grad_attn.astype(jnp.float32) * attended
    return product.reshape(product.shape[0], -1, HEAD_DIM).sum(-1).T


def on_device(
    patches, special, image_ids, w_qkv, w_out, w_up, w_down, gains, cot_patches, cot_special
):
    cycle_size = lax.axis_size("blk")
    cycle_index = lax.axis_index("blk")
    width = w_out.shape[1]
    head_count = width // HEAD_DIM
    tok_rows = TOK_MB
    spec_rows = special.shape[0] // MICRO
    ids_group = image_ids.reshape(cycle_size, MICRO, tok_rows)
    spec_ids = jnp.arange(spec_rows, dtype=jnp.int32) // SPECIAL
    row_weight = jnp.concatenate(
        [jnp.ones((tok_rows,), jnp.float32), jnp.full((spec_rows,), 1.0 / cycle_size, jnp.float32)]
    )
    row_weight_low = row_weight.astype(jnp.bfloat16)[:, None]
    summed_terms = None
    shard_terms = None
    out_parts = []
    spec_parts = []
    grad_parts = []
    grad_spec_parts = []
    for micro_index in range(MICRO):
        full_weights = fetch_weights(w_qkv, w_out, w_up, w_down, gains)
        qkv_full, out_full, up_full, down_full, gains_full = full_weights
        gain_rows = gains_full.astype(jnp.float32)
        tokens = jnp.concatenate(
            [
                patches[micro_index * tok_rows : (micro_index + 1) * tok_rows],
                special[micro_index * spec_rows : (micro_index + 1) * spec_rows],
            ],
            0,
        ).astype(jnp.float32)
        ids_flat = ids_group[:, micro_index].reshape(-1)
        patch_ids = lax.dynamic_slice_in_dim(ids_flat, cycle_index * tok_rows, tok_rows)
        normed = norm_rows(tokens, gain_rows[0]).astype(jnp.bfloat16)
        projected = jnp.dot(normed, qkv_full, preferred_element_type=jnp.float32).astype(
            jnp.bfloat16
        )
        patch_q = projected[:tok_rows, :width]
        patch_k = projected[:tok_rows, width : 2 * width]
        patch_v = projected[:tok_rows, 2 * width :]
        spec_q = projected[tok_rows:, :width]
        spec_k = projected[tok_rows:, width : 2 * width]
        spec_v = projected[tok_rows:, 2 * width :]
        start_state = online(
            empty_state(tok_rows, head_count, width), patch_q, patch_ids, spec_k, spec_v, spec_ids
        )
        partial_value = start_state
        key_rows = lax.all_gather(patch_k, "blk", axis=0, tiled=True)
        value_rows = lax.all_gather(patch_v, "blk", axis=0, tiled=True)
        length = key_rows.shape[0]
        key_ids = ids_flat
        blocks = length // tok_rows

        def visit_block(running, block_item):
            return (
                online(running, patch_q, patch_ids, block_item[0], block_item[1], block_item[2]),
                None,
            )

        partial_value, unused = lax.scan(
            visit_block,
            partial_value,
            (
                key_rows.reshape(blocks, tok_rows, -1),
                value_rows.reshape(blocks, tok_rows, -1),
                key_ids.reshape(blocks, tok_rows),
            ),
        )
        spec_top, spec_total, spec_accum = online(
            empty_state(spec_rows, head_count, width), spec_q, spec_ids, patch_k, patch_v, patch_ids
        )
        spec_state = merged((spec_top, spec_total, spec_accum), "blk", combine)
        spec_state = online(spec_state, spec_q, spec_ids, spec_k, spec_v, spec_ids)
        patch_attn, patch_lse = finish(partial_value)
        spec_attn, spec_lse = finish(spec_state)
        attended = jnp.concatenate([patch_attn, spec_attn], 0)
        attended_low = attended.astype(jnp.bfloat16)
        branch = jnp.dot(attended_low, out_full, preferred_element_type=jnp.float32)
        middle = tokens + gain_rows[1] * branch
        normed_mlp = norm_rows(middle, gain_rows[2]).astype(jnp.bfloat16)
        hidden = jnp.dot(normed_mlp, up_full, preferred_element_type=jnp.float32)
        active = jax.nn.gelu(hidden, approximate=False).astype(jnp.bfloat16)
        mlp_out = jnp.dot(active, down_full, preferred_element_type=jnp.float32)
        final = middle + gain_rows[3] * mlp_out
        out_parts.append(final[:tok_rows].astype(jnp.bfloat16))
        spec_parts.append(final[tok_rows:].astype(jnp.bfloat16))
        upstream = jnp.concatenate(
            [
                cot_patches[micro_index * tok_rows : (micro_index + 1) * tok_rows],
                cot_special[micro_index * spec_rows : (micro_index + 1) * spec_rows],
            ],
            0,
        ).astype(jnp.float32)
        grad_mlp = (gain_rows[3] * upstream).astype(jnp.bfloat16)
        g_down = contract_rows(active, grad_mlp * row_weight_low)
        grad_active = jnp.einsum(
            "rd,fd->rf", grad_mlp, down_full, preferred_element_type=jnp.float32
        )
        unused_value, gelu_pull = jax.vjp(
            lambda pre_act: jax.nn.gelu(pre_act, approximate=False), hidden
        )
        grad_hidden = gelu_pull(grad_active)[0].astype(jnp.bfloat16)
        g_up = contract_rows(normed_mlp, grad_hidden * row_weight_low)
        grad_normed_mlp = jnp.einsum(
            "rf,df->rd", grad_hidden, up_full, preferred_element_type=jnp.float32
        )
        unused_value, norm_pull_mlp = jax.vjp(
            lambda rows_in: norm_rows(rows_in, gain_rows[2]), middle
        )
        grad_middle = upstream + norm_pull_mlp(grad_normed_mlp)[0]
        g_ln2 = jnp.sum(row_weight[:, None] * grad_normed_mlp * norm_rows(middle, 1.0), 0)
        g_ls2 = jnp.sum(row_weight[:, None] * upstream * mlp_out, 0)
        g_ls1 = jnp.sum(row_weight[:, None] * grad_middle * branch, 0)
        grad_branch = (gain_rows[1] * grad_middle).astype(jnp.bfloat16)
        g_out = contract_rows(attended_low, grad_branch * row_weight_low)
        grad_attended = jnp.einsum(
            "re,de->rd", grad_branch, out_full, preferred_element_type=jnp.float32
        ).astype(jnp.bfloat16)
        all_delta = row_delta_of(grad_attended, attended)
        patch_delta = all_delta[:, :tok_rows]
        spec_delta = all_delta[:, tok_rows:]
        patch_grad_attn = grad_attended[:tok_rows]
        spec_grad_attn = grad_attended[tok_rows:]
        grad_pq_first, grad_sk_part, grad_sv_part = block_grads(
            patch_q, patch_grad_attn, patch_lse, patch_delta, patch_ids, spec_k, spec_v, spec_ids
        )
        grad_sq_part, grad_pk_local, grad_pv_local = block_grads(
            spec_q, spec_grad_attn, spec_lse, spec_delta, spec_ids, patch_k, patch_v, patch_ids
        )
        sum_sq, sum_sk, sum_sv = (
            lax.psum(grad_sq_part.astype(jnp.bfloat16), "blk").astype(jnp.float32),
            lax.psum(grad_sk_part.astype(jnp.bfloat16), "blk").astype(jnp.float32),
            lax.psum(grad_sv_part.astype(jnp.bfloat16), "blk").astype(jnp.float32),
        )
        grad_sq_own, grad_sk_own, grad_sv_own = block_grads(
            spec_q, spec_grad_attn, spec_lse, spec_delta, spec_ids, spec_k, spec_v, spec_ids
        )

        def cycle_step(hop_index, carried):
            keys_now, values_now, grad_keys, grad_values, grad_queries = carried
            source = (cycle_index - hop_index) % cycle_size
            key_ids = lax.dynamic_slice_in_dim(ids_flat, source * tok_rows, tok_rows)
            term_q, term_k, term_v = block_grads(
                patch_q,
                patch_grad_attn,
                patch_lse,
                patch_delta,
                patch_ids,
                keys_now,
                values_now,
                key_ids,
            )
            keys_now, values_now = from_behind((keys_now, values_now), "blk", 1)
            grad_keys, grad_values = (
                from_behind((grad_keys + term_k).astype(jnp.bfloat16), "blk", 1).astype(
                    jnp.float32
                ),
                from_behind((grad_values + term_v).astype(jnp.bfloat16), "blk", 1).astype(
                    jnp.float32
                ),
            )
            return (keys_now, values_now, grad_keys, grad_values, grad_queries + term_q)

        zero_rows = jnp.zeros((tok_rows, width), jnp.float32)
        unused_keys, unused_values, grad_pk, grad_pv, grad_pq = lax.fori_loop(
            0, cycle_size, cycle_step, (patch_k, patch_v, zero_rows, zero_rows, grad_pq_first)
        )
        grad_pk = grad_pk + grad_pk_local
        grad_pv = grad_pv + grad_pv_local
        grad_patch_qkv = jnp.concatenate([grad_pq, grad_pk, grad_pv], 1)
        grad_spec_qkv = jnp.concatenate(
            [sum_sq + grad_sq_own, sum_sk + grad_sk_own, sum_sv + grad_sv_own], 1
        )
        grad_projected = jnp.concatenate([grad_patch_qkv, grad_spec_qkv], 0).astype(jnp.bfloat16)
        g_qkv = contract_rows(normed, grad_projected * row_weight_low)
        grad_normed = jnp.einsum(
            "re,de->rd", grad_projected, qkv_full, preferred_element_type=jnp.float32
        )
        unused_value, norm_pull_attn = jax.vjp(
            lambda rows_in: norm_rows(rows_in, gain_rows[0]), tokens
        )
        grad_tokens = grad_middle + norm_pull_attn(grad_normed)[0]
        g_ln1 = jnp.sum(row_weight[:, None] * grad_normed * norm_rows(tokens, 1.0), 0)
        grad_parts.append(grad_tokens[:tok_rows])
        grad_spec_parts.append(grad_tokens[tok_rows:])
        grad_terms = (g_qkv, g_out, g_up, g_down, jnp.stack([g_ln1, g_ls1, g_ln2, g_ls2], 0))
        summed_terms = (
            grad_terms
            if summed_terms is None
            else tuple((held + extra for held, extra in zip(summed_terms, grad_terms)))
        )
    shard_terms = reduce_grads(summed_terms)
    return (
        jnp.concatenate(out_parts, 0),
        jnp.concatenate(spec_parts, 0),
        jnp.concatenate(grad_parts, 0),
        jnp.concatenate(grad_spec_parts, 0),
        shard_terms[0],
        shard_terms[1],
        shard_terms[2],
        shard_terms[3],
        shard_terms[4],
    )


PAD_ID = 99
PLAN = (
    (45.0, ()), (0, (0,)), (0, (0,)), (0, (2,)), (7.0, ()), (0, ()), (0, ()), (0, (0,)), (0, ()), (0, (6,)),
    (0, ()), (0, (0,)), (0, ()), (0, (5,)), (0, (5, 12, 1)), (0, ()), (0, ()), (0.2, (9,)), (0, ()),
    (0, (11,)), (0.36, (8,)), (0, ()), (40, (3,)), (0, ()), (0, ()), (0, (19,)), (0, ()), (0, ()),
    (0, (22, 6)), (1.6, ()), (0, (29,)), (0, ()), (0.001, (21, 23)), (0.84, (31, 24)), (0.185, (33,)),
    (0, (34,)), (27.0, (19, 34)), (0, (33, 25)), (1.5, (31,)), (0, (33,)), (0.6, (36,)), (0, (40, 9)),
    (2.0, (40,)), (0, (30, 31)), (0.7, ()), (0, ()), (0.54, (44,)), (0, (36,)), (0.001, ()), (0, (48,)),
    (0.001, ()), (0, ()), (0.35, ()), (0, ()), (21.0, ()), (0, ()), (0.001, (46,)), (0, (56, 43)),
    (3.6, (37, 22)), (0, ()), (0.001, (39, 44)), (0, (47,)), (0.14, ()), (0, ()), (0.21, (58,)), (0, ()),
    (0, (64,)), (0, ()), (0.7, ()), (0, (60,)), (0.001, ()), (0.002, (70,)), (0.35, (71,)), (0.001, (72,)),
    (0.07, ()), (0, ()), (0, ()), (0, (76, 75)), (0.42, (75,)), (11.0, (78,)),
)
STEPS = []


def plan():
    us, steps = PLAN[len(STEPS)]
    return us, [STEPS[i] for i in steps]


def mm(a, b):
    return jnp.dot(a, b, preferred_element_type=F32)


def mm_nt(a, b):
    return lax.dot_general(a, b, (((1,), (1,)), ((), ())), preferred_element_type=F32)


def mm_tn(a, b):
    return lax.dot_general(a, b, (((0,), (0,)), ((), ())), preferred_element_type=F32)


def here():
    place = lax.axis_index("blk")
    group = lax.axis_index("dp")
    return place, place // 2, place % 2, group // 2, group % 2


def chunk_index(slot, z, y):
    return (z ^ (slot % 4)) * 2 + (y ^ (slot // 4))


def row_blocks(block, among=slice(0, 736)):
    return [slice(first, first + block) for first in range(among.start, among.stop, block)]


def fold(rows):
    return rows.reshape(rows.shape[0] // 8, 8, rows.shape[1]).sum(0)


class Keep:
    def __init__(self, value):
        self.value = value


class Far:
    def __init__(self, value, held=True):
        self.value, self.held = value, held


class Load:
    def __init__(self, buffer, copy):
        self.buffer, self.copy, self.waited = buffer, copy, False

    def ready(self):
        if not self.waited:
            self.copy.wait()
            self.waited = True
        return self.buffer


class Store:
    def __init__(self, buffer, target, semaphore):
        self.buffer, self.target, self.semaphore, self.copies = buffer, target, semaphore, []

    def __setitem__(self, at, rows):
        self.buffer[at] = rows

    def __getitem__(self, at):
        return self.buffer[at]

    def go(self, at=None, source=None):
        source, target = self.buffer if source is None else source, self.target
        if at is not None:
            source, target = source.at[at], target.at[at]
        copy = pltpu.make_async_copy(source, target, self.semaphore.at[len(self.copies)])
        copy.start()
        self.copies.append(copy)


def call(kernel, outs, ins, scratch=(), limit=20):
    us, after = plan()
    far = [i for i, v in enumerate(ins) if isinstance(v, Far)]
    far_out = [i for i, v in enumerate(outs) if isinstance(v, Far)]
    plain = [v.value if isinstance(v, (Far, Keep)) else v for v in ins]
    shapes = [v.value if isinstance(v, (Far, Keep)) else v for v in outs]
    near, away = pl.BlockSpec(memory_space=pltpu.VMEM), pl.BlockSpec(memory_space=pltpu.HBM)
    held = [i for i in far_out if outs[i].held]
    room = [pltpu.VMEM(plain[i].shape, plain[i].dtype) for i in far]
    room += [pltpu.VMEM(shapes[i].shape, shapes[i].dtype) for i in held]
    if far or far_out:
        room.append(pltpu.SemaphoreType.DMA((len(far) + len(far_out), MICRO)))

    def body(*refs):
        given = [*refs[: len(ins)], *refs[len(ins) + len(after) :]]
        own = given[len(ins) + len(outs) + len(scratch) :]
        given = given[: len(ins) + len(outs) + len(scratch)]
        copies = []
        for k, i in enumerate(far):
            copies.append(pltpu.make_async_copy(given[i], own[k], own[-1].at[k, 0]))
            given[i] = Load(own[k], copies[-1])
        buffers = dict(zip(held, own[len(far) :]))
        stores = []
        for k, i in enumerate(far_out):
            stores.append(Store(buffers.get(i), given[len(ins) + i], own[-1].at[len(far) + k]))
            given[len(ins) + i] = stores[-1]
        for copy in copies:
            copy.start()
        kernel(*given)
        for store in stores:
            for copy in store.copies:
                copy.wait()

    def placed(v):
        if isinstance(v, Keep):
            return pltpu.with_memory_space_constraint(v.value, pltpu.VMEM)
        return pltpu.with_memory_space_constraint(v.value, pltpu.HBM) if isinstance(v, Far) else v

    def made(v):
        if isinstance(v, Keep):
            return pltpu.VMEM(v.value.shape, v.value.dtype)
        return pltpu.HBM(v.value.shape, v.value.dtype) if isinstance(v, Far) else v

    made_arrays = pl.pallas_call(
        body,
        out_shape=tuple(made(v) for v in outs),
        in_specs=[away if i in far else near for i in range(len(ins))]
        + [pl.BlockSpec(memory_space=pl.ANY)] * len(after),
        out_specs=tuple(away if i in far_out else near for i in range(len(outs))),
        scratch_shapes=[*scratch, *room],
        compiler_params=pltpu.CompilerParams(vmem_limit_bytes=limit * 2**20),
        cost_estimate=pl.CostEstimate(flops=int(us * 10**9), bytes_accessed=0, transcendentals=0),
        name=kernel.__name__,
    )(*[placed(v) for v in ins], *after)
    STEPS.append(made_arrays[0])
    return made_arrays


def keep(*arrays):
    return [Keep(v) for v in arrays]


def sds(*shape, dtype=BF16):
    return jax.ShapeDtypeStruct(shape, dtype)


def pick_pieces(w_qkv, w_up, gains, patches, cots, own, near, far, rows, held):
    place = here()[0]
    held[...] = jnp.zeros_like(held)
    up = w_up.ready()[...].astype(F32)
    qkv = w_qkv.ready()[...].astype(F32)
    gain = gains.ready()[...].astype(F32)
    for b in range(4):
        for d in range(8):
            held[b, 0:24, d * 96 : d * 96 + 96] = up[:, d * 384 + b * 96 : d * 384 + b * 96 + 96]
        for part in range(3):
            held[b, 24:48, part * 192 : part * 192 + 192] = qkv[
                :, part * 768 + b * 192 : part * 768 + b * 192 + 192
            ]
        held[b, 24:28, 576:600] = gain
    own[...] = held[place].astype(BF16)
    near[...] = held[place ^ 1].astype(BF16)
    far[0:48, :] = held[place ^ 2].astype(BF16)
    far[48:96, :] = held[place ^ 3].astype(BF16)
    rows[0:176, :] = patches.ready()[...]
    rows[176:352, :] = cots.ready()[...]


def join_pieces(own, near, far, near_far, w_out, w_down, pack, both, pack_f, up_f):
    place = here()[0]
    pack_f[96:112, :] = jnp.zeros((16, 768), F32)
    pieces = (
        own[...].astype(F32),
        near[...].astype(F32),
        far[0:48, :].astype(F32),
        near_far[48:96, :].astype(F32),
    )
    for k, piece in enumerate(pieces):
        source = place ^ k
        at = pl.ds(pl.multiple_of(source * 24, 8), 24)
        up_f[at, :] = piece[0:24]
        pack_f[at, 0:576] = piece[24:48, 0:576]
        lanes = pl.ds(pl.multiple_of(source * 128, 128), 128)
        pack_f[96:104, lanes] = piece[24:32, 576:704]
    out = w_out[...].astype(F32)
    for i in range(4):
        pack_f[i * 24 : i * 24 + 24, 576:768] = out[:, i * 192 : i * 192 + 192]
    pack[...] = pack_f[...].astype(BF16)
    both[0:96, :] = up_f[...].astype(BF16)
    both[96:192, :] = w_down[...]


def open_pack(*refs):
    chunks, (w_qkv, w_out, gain_rows, out_f, gain_f) = refs[:8], refs[8:]
    _, _, _, z, y = here()
    for slot, chunk in enumerate(chunks):
        d = chunk_index(slot, z, y)
        w_qkv[pl.ds(pl.multiple_of(d * 96, 96), 96), :] = chunk[0:96, 0:576]
        tail = chunk[0:96, 576:768].astype(F32)
        for i in range(4):
            out_f[pl.ds(pl.multiple_of(d * 24, 8), 24), i * 192 : i * 192 + 192] = tail[
                i * 24 : i * 24 + 24
            ]
        gain_f[d] = chunk[96:112, :].astype(F32)
    w_out[...] = out_f[...].astype(BF16)
    gain_rows[...] = jnp.zeros_like(gain_rows)
    for d in range(8):
        for b in range(4):
            at = (d * 4 + b) * 24
            gain_rows[0:4, at : at + 24] = gain_f[d, 0:4, b * 128 : b * 128 + 24]


def normalise(rows):
    centre = rows - jnp.mean(rows, -1, keepdims=True)
    spread = jnp.mean(centre * centre, -1, keepdims=True)
    scale = lax.rsqrt(spread + EPSILON)
    return centre * scale, scale


def place_rows(scratch, blocks, tail, first):
    place = here()[0]
    for k, block in enumerate(blocks):
        rows = block[first : first + 176, :].astype(F32)
        source = place ^ k
        for m in range(MICRO):
            scratch[pl.ds(pl.multiple_of(m * 368 + source * 88, 8), 88), :] = rows[m * 88 : m * 88 + 88]
    rows = tail[...].astype(F32)
    for m in range(MICRO):
        scratch[m * 368 + 352 : m * 368 + 368, :] = jnp.zeros((16, 768), F32)
        scratch[m * 368 + 352 : m * 368 + 362, :] = rows[m * 10 : m * 10 + 10]


def norm_rows_in(rows_0, rows_1, rows_2, rows_3, tail, cot_tail, unit, tokens, cots, rows_f):
    blocks = (rows_0, rows_1, rows_2, rows_3)
    place_rows(rows_f, blocks, cot_tail, 176)
    for at in row_blocks(32):
        cots[at, :] = rows_f[at, :].astype(BF16)
    cots.go()
    place_rows(rows_f, blocks, tail, 0)
    for at in row_blocks(32):
        rows = rows_f[at, :]
        tokens[at, :] = rows.astype(BF16)
        unit[at, :] = normalise(rows)[0]
    tokens.go()


def attend(ids_col, ids_row, unit, w_qkv, gain_rows, attended, w_kept, normed, projected, probs):
    w_kept.go(source=w_qkv)
    gain = gain_rows[0:1, :]
    for m in range(MICRO):
        at = slice(m * 368, m * 368 + 368)
        normed[at, :] = (unit[at, :] * gain).astype(BF16)
        normed.go(at)
        qkv = mm(normed[at, :], w_qkv[...])
        qkv = jnp.concatenate([qkv[:, 0:192] * SCORE_SCALE, qkv[:, 192:576]], -1).astype(BF16)
        projected[at, :] = qkv
        projected.go(at)
        same = ids_col[at, :] == ids_row[m : m + 1, :]
        bias = jnp.where(same, 0.0, MASKED)
        heads = []
        for h in range(3):
            q = qkv[:, h * 64 : h * 64 + 64]
            k = qkv[:, 192 + h * 64 : 192 + h * 64 + 64]
            v = qkv[:, 384 + h * 64 : 384 + h * 64 + 64]
            scores = mm_nt(q, k) + bias
            weights = jnp.exp(scores - jnp.max(scores, -1, keepdims=True))
            weights = weights * (1.0 / jnp.sum(weights, -1, keepdims=True))
            weights = weights.astype(BF16)
            probs[m * 3 + h] = weights
            heads.append(mm(weights, v))
        probs.go(slice(m * 3, m * 3 + 3))
        attended[at, :] = jnp.concatenate(heads, -1).astype(BF16)


def order_out(out_0, out_1, out_2, out_3, cots, gain_rows, ordered, mine, grad_mlp, out_f):
    place = here()[0]
    for k, part in enumerate((out_0, out_1, out_2, out_3)):
        source = place ^ k
        rows = part[...].astype(F32)
        for d in range(8):
            at = pl.multiple_of((d * 4 + source) * 24, 8)
            out_f[pl.ds(at, 24), :] = rows[d * 24 : d * 24 + 24]
    ordered[...] = out_f[...].astype(BF16)
    mine[...] = out_f[pl.ds(pl.multiple_of(place * 192, 8), 192), :].astype(BF16)
    mine.go()
    gain = gain_rows[3:4, :]
    for at in row_blocks(32):
        grad_mlp[at, :] = (gain * cots[at, :].astype(F32)).astype(BF16)
    grad_mlp.go()


def branch_rows(
    head_0, head_1, head_2, head_3, w_out, tokens, gain_rows, normed, branch, middle, rows_f
):
    place = here()[0]
    gain_s, gain_n = gain_rows[1:2, :], gain_rows[2:3, :]
    for m in range(MICRO):
        group = slice(m * 368, m * 368 + 368)
        total = None
        for k, part in enumerate((head_0, head_1, head_2, head_3)):
            rows = w_out[pl.ds(pl.multiple_of((place ^ k) * 192, 16), 192), :]
            term = mm(part[group, :], rows)
            total = term if total is None else total + term
        rows_f[group, :] = total
        for at in row_blocks(16, group):
            a = rows_f[at, :]
            branch[at, :] = a.astype(BF16)
            rows = tokens[at, :].astype(F32) + gain_s * a
            middle[at, :] = rows
            normed[at, :] = (normalise(rows)[0] * gain_n).astype(BF16)
        branch.go(group)
        middle.go(group)


def raise_rows(*refs):
    normed, chunks = refs[0], refs[1:9]
    active, slope, w_up, w_down, normed_kept, down_kept, rows_f = refs[9:]
    normed_kept.go(source=normed)
    _, _, _, z, y = here()
    for slot, chunk in enumerate(chunks):
        d = chunk_index(slot, z, y)
        w_up[pl.ds(pl.multiple_of(d * 96, 96), 96), :] = chunk[0:96, :]
        w_down[pl.ds(pl.multiple_of(d * 96, 96), 96), :] = chunk[96:192, :]
    down_kept.go(source=w_down)
    for m in range(MICRO):
        at = slice(m * 368, m * 368 + 368)
        rows_f[at, :] = mm(normed[at, :], w_up[...])
    for at in row_blocks(32):
        u = rows_f[at, :]
        half = 0.5 + 0.5 * lax.erf(u * 0.7071067811865476)
        active[at, :] = (u * half).astype(BF16)
        slope[at, :] = half + u * (0.3989422804014327 * jnp.exp(-0.5 * u * u))


def down_grads(active, grad_mlp, away, kept, active_kept, work):
    active_kept.go(source=active)
    _, _, _, z, _ = here()
    work[...] = mm_tn(active[...], grad_mlp[...])
    for pair in range(2):
        for side in range(2):
            ours = pl.multiple_of(((z ^ (2 * pair)) * 2 + side) * 96, 8)
            theirs = pl.multiple_of(((z ^ (2 * pair + 1)) * 2 + side) * 96, 8)
            kept[pair * 2 + side] = work[pl.ds(ours, 96), :]
            away[pair * 2 + side] = work[pl.ds(theirs, 96), :].astype(BF16)


def sum_fours(kept, came, own, away):
    own[...] = kept[0:2] + came[0:2].astype(F32)
    away[...] = (kept[2:4] + came[2:4].astype(F32)).astype(BF16)


def sum_sides(kept, came, own, away):
    y = here()[4]
    own[...] = kept[y] + came[y].astype(F32)
    away[...] = (kept[1 - y] + came[1 - y].astype(F32)).astype(BF16)


def lower_rows(slope, grad_mlp, w_up, w_down, away, kept, grad_hidden, work):
    core = here()[2]
    for m in range(MICRO):
        at = slice(m * 368, m * 368 + 368)
        grad = mm_nt(grad_mlp[at, :], w_down[...])
        grad_hidden[at, :] = (slope[at, :] * grad).astype(BF16)
        grad_hidden.go(at)
        work[m] = mm_nt(grad_hidden[at, :], w_up[...])
    away[...] = work[1 - core].astype(BF16)
    kept[...] = work[core]


def split_rows(pieces, place, away, kept):
    away[0:208, :] = pieces[place ^ 1].astype(BF16)
    away[208:416, :] = pieces[place ^ 3].astype(BF16)
    kept[0:208, :] = pieces[place]
    kept[208:416, :] = pieces[place ^ 2]


def cut_rows(rows_f, pieces):
    for b in range(4):
        for m in range(MICRO):
            pieces[b, m * 104 : m * 104 + 88, :] = rows_f[m * 368 + b * 88 : m * 368 + b * 88 + 88, :]
            pieces[b, m * 104 + 88 : m * 104 + 104, :] = rows_f[m * 368 + 352 : m * 368 + 368, :]


def halve(grad_f, y, away, kept, rows):
    for zz in range(4):
        other = pl.ds(pl.multiple_of((zz * 2 + 1 - y) * rows, 8), rows)
        ours = pl.ds(pl.multiple_of((zz * 2 + y) * rows, 8), rows)
        away[zz] = grad_f[other, 0 : away.shape[2]].astype(BF16)
        kept[zz] = grad_f[ours, 0 : away.shape[2]]


def up_grads(normed, grad_hidden, away, kept, work):
    y = here()[4]
    work[...] = mm_tn(normed.ready()[...], grad_hidden.ready()[...])
    halve(work, y, away, kept, 96)


def mlp_rows(
    active, w_down, cots, targets, head_0, head_1, head_2, head_3,
    rows_away, rows_kept, scale_grad, chosen, work, pieces,
):
    place = here()[0]
    active, w_down = active.ready(), w_down.ready()
    for m in range(MICRO):
        at = slice(m * 368, m * 368 + 368)
        work[at, :] = mm(active[at, :], w_down[...])
    cots = cots.ready()
    total = jnp.zeros((8, 768), F32)
    for at in row_blocks(32):
        total = total + fold(cots[at, :].astype(F32) * work[at, :])
    scale_grad[...] = total
    cut_rows(work, pieces)
    split_rows(pieces, place, rows_away, rows_kept)
    picked = None
    for k, part in enumerate((head_0, head_1, head_2, head_3)):
        index = lax.broadcasted_iota(jnp.int32, (192, 192), 0) + (place ^ k) * 192
        pick = jnp.where(index == targets[...], 1.0, 0.0).astype(BF16)
        term = mm(part[...], pick)
        picked = term if picked is None else picked + term
    chosen[...] = picked.astype(BF16)


def add_rows(kept, came, total):
    total[...] = (kept[...] + came[...].astype(F32)).astype(BF16)


def add_pair(here_rows, came, total):
    total[...] = (here_rows[...].astype(F32) + came[...].astype(F32)).astype(BF16)


def branch_back(
    sum_own, sum_near, middle, cots, branch, gain_rows, w_mine, probs, normed, scale_grad_mlp, chosen,
    grad_rows, grad_heads, grad_v, away, kept,
    work, grad_branch, grad_mid, extra, early,
):
    place, _, core, _, y = here()
    for m in range(MICRO):
        at = slice(m * 368, m * 368 + 368)

        @pl.when(core == m)
        def _():
            work[at, :] = sum_own[...].astype(F32)

        @pl.when(core != m)
        def _():
            work[at, :] = sum_near[...].astype(F32)

    gain_s, gain_n = gain_rows[1:2, :], gain_rows[2:3, :]
    scale_sum = jnp.zeros((8, 768), F32)
    for at in row_blocks(32):
        unit, scale = normalise(middle[at, :])
        pulled = work[at, :] * gain_n
        pulled = pulled - jnp.mean(pulled, -1, keepdims=True) - unit * jnp.mean(
            pulled * unit, -1, keepdims=True
        )
        through = cots[at, :].astype(F32) + scale * pulled
        grad_mid[at, :] = through
        grad_branch[at, :] = (gain_s * through).astype(BF16)
        scale_sum = scale_sum + fold(through * branch[at, :].astype(F32))
    for m in range(MICRO):
        for part, first in ((0, place * 88), (88, 352)):
            rows = 88 if part == 0 else 16
            grad_rows[m * 104 + part : m * 104 + part + rows, :] = grad_mid[
                pl.ds(pl.multiple_of(m * 368 + first, 8), rows), :
            ]
    for m in range(MICRO):
        at = slice(m * 368, m * 368 + 368)
        heads = mm_nt(grad_branch[at, :], w_mine[...]).astype(BF16)
        grad_heads[at, :] = heads
        terms = [mm_tn(probs[m * 3 + h], heads[:, h * 64 : h * 64 + 64]) for h in range(3)]
        grad_v[at, :] = jnp.concatenate(terms, -1).astype(BF16)
    grad_mid[0:768, 0:192] = mm_tn(normed[...], grad_v[...])
    extra[...] = mm_tn(chosen[...], grad_branch[...])
    scale_rows = (
        0.25 * jnp.sum(scale_sum, 0, keepdims=True),
        jnp.sum(scale_grad_mlp[...], 0, keepdims=True),
    )
    for d in range(8):
        base = d * 112
        early[base : base + 96, 0:192] = grad_mid[d * 96 : d * 96 + 96, 0:192]
        for i in range(4):
            early[base + i * 24 : base + i * 24 + 24, 192:384] = extra[
                d * 24 : d * 24 + 24, i * 192 : i * 192 + 192
            ]
        early[base + 96 : base + 112, :] = jnp.zeros((16, 384), F32)
        for i in range(2):
            early[base + 96 + i : base + 97 + i, 0:96] = scale_rows[i][:, d * 96 : d * 96 + 96]
    halve(early, y, away, kept, 112)


def score_back(probs, projected, grad_heads, normed, grad_qk, away, kept, work):
    _, _, _, _, y = here()
    for m in range(MICRO):
        at = slice(m * 368, m * 368 + 368)
        qkv = projected[at, :]
        g_heads = grad_heads[at, :]
        grads = [[], []]
        for h in range(3):
            q = qkv[:, h * 64 : h * 64 + 64]
            k = qkv[:, 192 + h * 64 : 192 + h * 64 + 64]
            v = qkv[:, 384 + h * 64 : 384 + h * 64 + 64]
            grad_prob = mm_nt(g_heads[:, h * 64 : h * 64 + 64], v)
            wide = probs[m * 3 + h].astype(F32)
            moved = wide * grad_prob
            delta = jnp.sum(moved, -1, keepdims=True)
            grad_score = (moved - wide * delta).astype(BF16)
            grads[0].append(mm(grad_score, k) * SCORE_SCALE)
            grads[1].append(mm_tn(q, grad_score))
        grad_qk[at, 0:192] = jnp.concatenate(grads[0], -1).astype(BF16)
        grad_qk[at, 192:384] = jnp.concatenate(grads[1], 0).T.astype(BF16)
    work[...] = mm_tn(normed[...], grad_qk[...])
    halve(work, y, away, kept, 96)


def project_back(grad_qk, grad_v, w_qkv, rows_away, rows_kept, work, pieces):
    place = here()[0]
    for m in range(MICRO):
        at = slice(m * 368, m * 368 + 368)
        work[at, :] = mm_nt(grad_qk[at, :], w_qkv[:, 0:384]) + mm_nt(grad_v[at, :], w_qkv[:, 384:576])
    cut_rows(work, pieces)
    split_rows(pieces, place, rows_away, rows_kept)


def sum_y(kept, came, own, send_1, send_2, send_3):
    _, _, _, z, _ = here()
    own[...] = kept[z] + came[z].astype(F32)
    for k, send in ((1, send_1), (2, send_2), (3, send_3)):
        send[...] = (kept[z ^ k] + came[z ^ k].astype(F32)).astype(BF16)


def sum_y_pairs(kept, came, own, away):
    _, _, _, z, _ = here()
    for k in range(2):
        own[k] = kept[z ^ (2 * k)] + came[z ^ (2 * k)].astype(F32)
        there = z ^ (2 * k + 1)
        away[k] = (kept[there] + came[there].astype(F32)).astype(BF16)


def sum_pairs(kept, came, own, away):
    own[...] = kept[0] + came[0].astype(F32)
    away[...] = (kept[1] + came[1].astype(F32)).astype(BF16)


def sum_last(own, came, total):
    total[...] = own[...] + came[...].astype(F32)


def sum_z(own, came_1, came_2, came_3, total):
    total[...] = (
        own[...]
        + came_1[...].astype(F32)
        + came_2[...].astype(F32)
        + came_3[...].astype(F32)
    )


def add_pieces(kept_m, came_m, kept_h, came_h, stay, go):
    for i, (kept, came) in enumerate(((kept_m, came_m), (kept_h, came_h))):
        stay[i * 208 : i * 208 + 208, :] = kept[0:208, :] + came[0:208, :].astype(F32)
        go[i * 208 : i * 208 + 208, :] = (kept[208:416, :] + came[208:416, :].astype(F32)).astype(BF16)


def finish_rows(
    stay, came, middle, grad_rows, patches, tail, gain_rows,
    out_patches, out_special, grad_patches, grad_special,
):
    place = here()[0]
    own = patches[...].astype(F32)
    rest = tail[...].astype(F32)
    outs, out_tails = [], []
    for m in range(MICRO):
        for part, first in ((0, place * 88), (88, 352)):
            count = 88 if part == 0 else 10
            at = slice(m * 104 + part, m * 104 + part + count)
            far_at = slice(208 + m * 104 + part, 208 + m * 104 + part + count)
            mid = middle[pl.ds(pl.multiple_of(m * 368 + first, 8), count), :]
            final = mid + gain_rows[3:4, :] * (stay[at, :] + came[at, :].astype(F32))
            (outs if part == 0 else out_tails).append(final)
            rows = own[m * 88 : m * 88 + 88] if part == 0 else rest[m * 10 : m * 10 + 10]
            unit, scale = normalise(rows)
            pulled = gain_rows[0:1, :] * (stay[far_at, :] + came[far_at, :].astype(F32))
            pulled = pulled - jnp.mean(pulled, -1, keepdims=True) - unit * jnp.mean(
                pulled * unit, -1, keepdims=True
            )
            grad = grad_rows[at, :] + scale * pulled
            if part == 0:
                grad_patches[m * 88 : m * 88 + 88, :] = grad
            else:
                grad_special[m * 10 : m * 10 + 10, :] = grad
    out_patches[...] = jnp.concatenate(outs, 0).astype(BF16)
    out_special[...] = jnp.concatenate(out_tails, 0).astype(BF16)


def pick_grads(up, first, second, own, near, far, grad_out, held):
    place = here()[0]
    for b in range(4):
        at = slice(b * 24, b * 24 + 24)
        held[b, 0:24, :] = up[at, :]
        held[b, 24:48, 0:384] = second[at, :]
        held[b, 24:48, 384:576] = first[at, 0:192]
        held[b, 24:48, 576:768] = jnp.zeros((24, 192), F32)
        held[b, 24:26, 576:600] = first[96:98, at]
        grad_out[:, b * 192 : b * 192 + 192] = first[at, 192:384]
    own[...] = held[place]
    near[...] = held[place ^ 1].astype(BF16)
    far[0:48, :] = held[place ^ 2].astype(BF16)
    far[48:96, :] = held[place ^ 3].astype(BF16)


def as_row(column):
    count = column.shape[0]
    square = lax.broadcasted_iota(jnp.int32, (count, count), 0)
    across = lax.broadcasted_iota(jnp.int32, (count, count), 1)
    return jnp.sum(jnp.where(square == across, column, 0.0), 0, keepdims=True)


def join_grads(
    own, near, far, near_far, w_qkv, w_up, gains, grad_qkv, grad_up, grad_gains, held
):
    place = here()[0]
    held[place] = own[...]
    held[place ^ 1] = near[...].astype(F32)
    held[place ^ 2] = far[0:48, :].astype(F32)
    held[place ^ 3] = near_far[48:96, :].astype(F32)
    scales = None
    for b in range(4):
        for d in range(8):
            at = d * 384 + b * 96
            grad_up[:, at : at + 96] = held[b, 0:24, d * 96 : d * 96 + 96]
        for part in range(3):
            at = part * 768 + b * 192
            grad_qkv[:, at : at + 192] = held[b, 24:48, part * 192 : part * 192 + 192]
        term = held[b, 24:26, 576:600]
        scales = term if scales is None else scales + term
    norm_1 = as_row(jnp.sum(w_qkv[...].astype(F32) * grad_qkv[...], -1, keepdims=True))
    norm_2 = as_row(jnp.sum(w_up[...].astype(F32) * grad_up[...], -1, keepdims=True))
    gain = gains[...].astype(F32)
    grad_gains[0:1, :] = norm_1 / gain[0:1, :]
    grad_gains[1:2, :] = scales[0:1, :]
    grad_gains[2:3, :] = norm_2 / gain[2:3, :]
    grad_gains[3:4, :] = scales[1:2, :]


def send(rows, axis, step):
    pairs = []
    for group in range(8):
        z, y = group // 2, group % 2
        for place in range(4):
            target = {
                "core": (group, place ^ 1),
                "x": (group, place ^ 2),
                "y": (z * 2 + 1 - y, place),
                "z": ((z ^ step) * 2 + y, place),
            }[axis]
            pairs.append((group * 4 + place, target[0] * 4 + target[1]))
    _, ready = plan()
    if ready:
        rows = lax.optimization_barrier((rows, *ready))[0]
    STEPS.append(lax.ppermute(rows, ("dp", "blk"), pairs))
    return STEPS[-1]


def add_y(kept, came):
    rows, width = kept.shape[1:]
    own, *parts = call(
        sum_y,
        [Keep(sds(rows, width, dtype=F32))] + [sds(rows, width)] * 3,
        [Keep(kept), came],
    )
    return [own, *[send(part, "z", k) for k, part in zip((1, 2, 3), parts)]]


def halve_y(kept, came):
    rows, width = kept.shape[1:]
    own, away = call(
        sum_y_pairs,
        [Keep(sds(2, rows, width, dtype=F32)), sds(2, rows, width)],
        [Keep(kept), came],
    )
    return own, send(away, "z", 1)


def halve_z(pair):
    kept, came = pair
    rows, width = kept.shape[1:]
    own, away = call(
        sum_pairs,
        [Keep(sds(rows, width, dtype=F32)), sds(rows, width)],
        [Keep(kept), came],
    )
    return own, send(away, "z", 2)


def side_y(kept, came):
    own, away = call(
        sum_sides,
        [Keep(sds(96, 768, dtype=F32)), sds(96, 768)],
        [Keep(kept), came],
    )
    return own, send(away, "y", 1)


def add_last(last):
    own, came = last
    return call(
        sum_last, [sds(*own.shape, dtype=F32)], [Keep(own), came]
    )[0]


def add_z(steps):
    own, *came = steps
    return call(
        sum_z, [sds(*own.shape, dtype=F32)], [Keep(own), *came]
    )[0]


def on_device_split(
    patches, special, image_ids, w_qkv, w_out, w_up, w_down, gains, cot_patches, cot_special
):
    STEPS.clear()
    place = lax.axis_index("blk")
    spec_ids = jnp.concatenate(
        [jnp.arange(10, dtype=jnp.int32) // SPECIAL, jnp.full((6,), PAD_ID, jnp.int32)]
    )
    ids = image_ids.reshape(4, 2, 88).transpose(1, 0, 2).reshape(2, 352)
    ids_row = jnp.concatenate([ids, jnp.broadcast_to(spec_ids, (2, 16))], 1)
    ids_col = ids_row.reshape(736, 1)
    column = jnp.arange(192, dtype=jnp.int32)
    targets = (column + column // 24 * 72 + place * 24).reshape(1, 192)

    own, near, far, rows = call(
        pick_pieces,
        [sds(48, 768), sds(48, 768), sds(96, 768), sds(352, 768)],
        [Far(w_qkv), Far(w_up), Far(gains), Far(patches), Far(cot_patches)],
        [pltpu.VMEM((4, 48, 768), F32)],
    )
    came_far = send(far, "x", 1)
    came_near, came_near_far = send(near, "core", 1), send(came_far, "core", 1)
    pack, both = call(
        join_pieces,
        [sds(112, 768), sds(192, 768)],
        [own, came_near, came_far, came_near_far, w_out, w_down],
        [pltpu.VMEM((112, 768), F32), pltpu.VMEM((96, 768), F32)],
    )
    pack_2 = send(pack, "z", 2)
    pack_1 = send(pack, "z", 1)
    pack_y0 = send(pack, "y", 1)
    far_rows = send(rows, "x", 1)
    both_y0 = send(both, "y", 1)
    pack_y1 = send(pack_1, "y", 1)
    pack_3 = send(pack_2, "z", 1)
    pack_y2 = send(pack_2, "y", 1)
    both_2 = send(both, "z", 2)
    both_1 = send(both, "z", 1)
    near_rows = send(rows, "core", 1)
    row_parts = [rows, near_rows, far_rows, send(far_rows, "core", 1)]
    unit, tokens, cots = call(
        norm_rows_in,
        [Keep(sds(736, 768, dtype=F32)), *[Far(sds(736, 768))] * 2],
        [*row_parts, special, cot_special],
        [pltpu.VMEM((736, 768), F32)],
    )
    pack_y3 = send(pack_3, "y", 1)
    both_y1 = send(both_1, "y", 1)
    qkv_full, out_part, gain_rows = call(
        open_pack,
        [Keep(sds(768, 576)), sds(192, 768), Keep(sds(8, 768, dtype=F32))],
        [pack, pack_1, pack_2, pack_3, pack_y0, pack_y1, pack_y2, pack_y3],
        [pltpu.VMEM((192, 768), F32), pltpu.VMEM((8, 16, 768), F32)],
    )
    far_out = send(out_part, "x", 1)
    attended, qkv_far, normed_far, projected, probs = call(
        attend,
        [
            sds(736, 192), Far(sds(768, 576), held=False), Far(sds(736, 768)),
            Far(sds(736, 576)), Far(sds(6, 368, 368)),
        ],
        [ids_col, ids_row, *keep(unit, qkv_full, gain_rows)],
    )
    far_heads = send(attended, "x", 1)
    both_3 = send(both_2, "z", 1)
    both_y2 = send(both_2, "y", 1)
    out_parts = [
        out_part, send(out_part, "core", 1),
        far_out, send(far_out, "core", 1),
    ]
    both_y3 = send(both_3, "y", 1)
    out_full, out_mine, grad_mlp = call(
        order_out,
        [Keep(sds(768, 768)), Far(sds(192, 768)), Far(sds(736, 768))],
        [*out_parts, cots, Keep(gain_rows)],
        [pltpu.VMEM((768, 768), F32)],
    )
    heads = [
        attended, send(attended, "core", 1),
        far_heads, send(far_heads, "core", 1),
    ]
    both_chunks = [both, both_1, both_2, both_3, both_y0, both_y1, both_y2, both_y3]
    normed_mlp, branch, middle = call(
        branch_rows,
        [Keep(sds(736, 768)), Far(sds(736, 768)), Far(sds(736, 768, dtype=F32))],
        [*heads, Keep(out_full), tokens, Keep(gain_rows)],
        [pltpu.VMEM((736, 768), F32)],
    )
    active, slope, up_full, down_full, normed_mlp, down_far = call(
        raise_rows,
        [
            *keep(sds(736, 768), sds(736, 768, dtype=F32), sds(768, 768), sds(768, 768)),
            Far(sds(736, 768), held=False), Far(sds(768, 768), held=False),
        ],
        [Keep(normed_mlp), *both_chunks],
        [pltpu.VMEM((736, 768), F32)],
    )
    half = [sds(4, 96, 768), Keep(sds(4, 96, 768, dtype=F32))]
    rows_split = [sds(416, 768), Keep(sds(416, 768, dtype=F32))]

    def make_down(active):
        return call(
            down_grads,
            [*half, Far(sds(736, 768), held=False)],
            [Keep(active), grad_mlp],
            [pltpu.VMEM((768, 768), F32)],
        )

    sum_away, sum_kept, grad_hidden = call(
        lower_rows,
        [sds(368, 768), Keep(sds(368, 768, dtype=F32)), Far(sds(736, 768))],
        [Keep(slope), grad_mlp, *keep(up_full, down_full)],
        [pltpu.VMEM((2, 368, 768), F32)],
    )
    sum_came = send(sum_away, "core", 1)
    chip_sum = call(add_rows, [sds(368, 768)], [Keep(sum_kept), sum_came])[0]
    chip_came = send(chip_sum, "x", 1)
    down_away, down_kept, active = make_down(active)
    down_came = send(down_away, "z", 1)
    up_away, up_kept = call(
        up_grads,
        half,
        [Far(normed_mlp), Far(grad_hidden)],
        [pltpu.VMEM((768, 768), F32)],
    )
    up_came = send(up_away, "y", 1)
    m_away, m_kept, scale_mlp, chosen = call(
        mlp_rows,
        [*rows_split, *keep(sds(8, 768, dtype=F32), sds(736, 192))],
        [*[Far(v) for v in (active, down_far, cots)], targets, *heads],
        [pltpu.VMEM((736, 768), F32), pltpu.VMEM((4, 208, 768), F32)],
    )
    m_came = send(m_away, "core", 1)
    down_two, down_away = call(
        sum_fours,
        [Keep(sds(2, 96, 768, dtype=F32)), sds(2, 96, 768)],
        [Keep(down_kept), down_came],
    )
    down_came = send(down_away, "z", 2)
    sum_own = call(add_pair, [sds(368, 768)], [chip_sum, chip_came])[0]
    sum_near = send(sum_own, "core", 1)
    grad_rows, grad_heads, grad_v, a_away, a_kept = call(
        branch_back,
        [
            *keep(sds(208, 768, dtype=F32), sds(736, 192), sds(736, 192)),
            sds(4, 112, 384), Keep(sds(4, 112, 384, dtype=F32)),
        ],
        [
            sum_own, sum_near, middle, cots, branch, Keep(gain_rows), out_mine,
            probs, normed_far, *keep(scale_mlp, chosen),
        ],
        [
            pltpu.VMEM((736, 768), F32), pltpu.VMEM((736, 768), BF16),
            pltpu.VMEM((768, 768), F32), pltpu.VMEM((192, 768), F32), pltpu.VMEM((896, 384), F32),
        ],
    )
    a_came = send(a_away, "y", 1)
    grad_qk, b_away, b_kept = call(
        score_back,
        [Keep(sds(736, 384)), sds(4, 96, 384), Keep(sds(4, 96, 384, dtype=F32))],
        [probs, projected, Keep(grad_heads), normed_far],
        [pltpu.VMEM((768, 384), F32)],
    )
    b_came = send(b_away, "y", 1)
    a_pair = halve_y(a_kept, a_came)
    up_steps = halve_y(up_kept, up_came)
    h_away, h_kept = call(
        project_back,
        rows_split,
        [*keep(grad_qk, grad_v), qkv_far],
        [pltpu.VMEM((736, 768), F32), pltpu.VMEM((4, 208, 768), F32)],
    )
    h_came = send(h_away, "core", 1)
    stay, go = call(
        add_pieces,
        [Keep(sds(416, 768, dtype=F32)), sds(416, 768)],
        [Keep(m_kept), m_came, Keep(h_kept), h_came],
    )
    far_rows = send(go, "x", 1)
    down_last = side_y(down_two, down_came)
    up_last = halve_z(up_steps)
    b_steps = add_y(b_kept, b_came)
    a_last = halve_z(a_pair)
    grad_down = add_last(down_last)
    grad_up_rows = add_last(up_last)
    first_rows = add_last(a_last)
    second_rows = add_z(b_steps)
    own, near, far, grad_out = call(
        pick_grads,
        [Keep(sds(48, 768, dtype=F32)), sds(48, 768), sds(96, 768), sds(24, 768, dtype=F32)],
        [grad_up_rows, first_rows, second_rows],
        [pltpu.VMEM((4, 48, 768), F32)],
    )
    came_far = send(far, "x", 1)
    came_near, came_near_far = send(near, "core", 1), send(came_far, "core", 1)
    out_patches, out_special, grad_patches, grad_special = call(
        finish_rows,
        [
            sds(176, 768), sds(20, 768), sds(176, 768, dtype=F32), sds(20, 768, dtype=F32),
        ],
        [Keep(stay), far_rows, middle, Keep(grad_rows), patches, special, Keep(gain_rows)],
    )
    grad_qkv, grad_up, grad_gains = call(
        join_grads,
        [sds(24, 2304, dtype=F32), sds(24, 3072, dtype=F32), sds(4, 24, dtype=F32)],
        [Keep(own), came_near, came_far, came_near_far, w_qkv, w_up, gains],
        [pltpu.VMEM((4, 48, 768), F32)],
    )
    return (
        out_patches, out_special, grad_patches, grad_special,
        grad_qkv, grad_out, grad_up, grad_down, grad_gains,
    )


def solution(mesh):
    placed = (
        P(("dp", "blk"), None),
        P("dp", None),
        P("dp"),
        P(("dp", "blk"), None),
        P(("dp", "blk"), None),
        P(("dp", "blk"), None),
        P(("dp", "blk"), None),
        P(None, ("dp", "blk")),
        P(("dp", "blk"), None),
        P("dp", None),
    )
    whole = dict(mesh.shape) != {"dp": 8, "blk": 4}
    return jax.shard_map(
        on_device if whole else on_device_split,
        mesh=mesh,
        in_specs=placed,
        out_specs=(
            P(("dp", "blk"), None),
            P("dp", None),
            P(("dp", "blk"), None),
            P("dp", None),
            P(("dp", "blk"), None),
            P(("dp", "blk"), None),
            P(("dp", "blk"), None),
            P(("dp", "blk"), None),
            P(None, ("dp", "blk")),
        ),
        check_vma=False,
    )
```

```python
import jax
import jax.numpy as jnp
from jax import lax
from jax.experimental import pallas as pl
from jax.experimental.pallas import tpu as pltpu
from jax.sharding import PartitionSpec as P

HEAD_DIM = 64
SPECIAL = 5
MICRO = 2
TOK_MB = 88

SCORE_SCALE = 0.125
MASKED = -1e30
EPSILON = 1e-06

BF16 = jnp.bfloat16
F32 = jnp.float32


def merged(shard, axis, combine):
    everything = jax.tree.map(
        lambda part, kind: lax.all_gather(part.astype(kind), axis),
        shard,
        (jnp.bfloat16, jnp.bfloat16, jnp.bfloat16),
    )

    def take(k):
        return jax.tree.map(lambda part, own: part[k].astype(own.dtype), everything, shard)

    return lax.fori_loop(
        1, lax.axis_size(axis), lambda k, so_far: combine(so_far, take(k)), take(0)
    )


def from_behind(shard, axis, by):
    peers = lax.axis_size(axis)
    return lax.ppermute(shard, axis, [(i, (i + by) % peers) for i in range(peers)])


def norm_rows(values, gain_row):
    centre = values - jnp.mean(values, -1, keepdims=True)
    spread = jnp.mean(centre * centre, -1, keepdims=True)
    return centre * lax.rsqrt(spread + EPSILON) * gain_row


def split_heads(matrix):
    return matrix.reshape(matrix.shape[0], -1, HEAD_DIM)


def widen(per_head):
    return jnp.repeat(per_head.T, HEAD_DIM, axis=1)


def empty_state(length, head_count, feature_width):
    return (
        jnp.full((head_count, length), MASKED, jnp.float32),
        jnp.zeros((head_count, length), jnp.float32),
        jnp.zeros((length, feature_width), jnp.float32),
    )


def online(carried, queries, query_ids, key_rows, value_rows, key_ids):
    top_score, totals, accumulated = carried
    same_image = (query_ids[:, None] == key_ids[None, :])[None]
    scores = (
        jnp.einsum(
            "qhd,khd->hqk",
            split_heads(queries),
            split_heads(key_rows),
            preferred_element_type=jnp.float32,
        )
        * SCORE_SCALE
    )
    scores = jnp.where(same_image, scores, MASKED)
    new_top = jnp.maximum(top_score, jnp.max(scores, -1))
    weights = jnp.where(same_image, jnp.exp(scores - new_top[..., None]), 0.0)
    factor = jnp.exp(top_score - new_top)
    totals = totals * factor + jnp.sum(weights, -1)
    mixture = jnp.einsum(
        "hqk,khd->qhd",
        weights.astype(jnp.bfloat16),
        split_heads(value_rows),
        preferred_element_type=jnp.float32,
    )
    accumulated = accumulated * widen(factor) + mixture.reshape(accumulated.shape)
    return (new_top, totals, accumulated)


def combine(former, latter):
    highest = jnp.maximum(former[0], latter[0])
    scale_former = jnp.exp(former[0] - highest)
    scale_latter = jnp.exp(latter[0] - highest)
    return (
        highest,
        former[1] * scale_former + latter[1] * scale_latter,
        former[2] * widen(scale_former) + latter[2] * widen(scale_latter),
    )


def finish(carried):
    top_score, totals, accumulated = carried
    return (accumulated / widen(totals), top_score + jnp.log(totals))


def block_grads(queries, grad_attn, log_total, row_delta, query_ids, key_rows, value_rows, key_ids):
    same_image = (query_ids[:, None] == key_ids[None, :])[None]
    q_heads = split_heads(queries)
    g_heads = split_heads(grad_attn)
    scores = (
        jnp.einsum(
            "qhd,khd->hqk", q_heads, split_heads(key_rows), preferred_element_type=jnp.float32
        )
        * SCORE_SCALE
    )
    probabilities = jnp.where(same_image, jnp.exp(scores - log_total[..., None]), 0.0)
    grad_prob = jnp.einsum(
        "qhd,khd->hqk", g_heads, split_heads(value_rows), preferred_element_type=jnp.float32
    )
    dscore = (probabilities * (grad_prob - row_delta[..., None])).astype(jnp.bfloat16)
    grad_query = (
        jnp.einsum(
            "hqk,khd->qhd", dscore, split_heads(key_rows), preferred_element_type=jnp.float32
        ).reshape(queries.shape[0], -1)
        * SCORE_SCALE
    )
    grad_key = (
        jnp.einsum("hqk,qhd->khd", dscore, q_heads, preferred_element_type=jnp.float32).reshape(
            key_rows.shape[0], -1
        )
        * SCORE_SCALE
    )
    grad_value = jnp.einsum(
        "hqk,qhd->khd",
        probabilities.astype(jnp.bfloat16),
        g_heads,
        preferred_element_type=jnp.float32,
    ).reshape(key_rows.shape[0], -1)
    return (grad_query, grad_key, grad_value)


def fetch_weights(w_qkv, w_out, w_up, w_down, gains):
    return (
        lax.all_gather(w_qkv, ("dp", "blk"), axis=0, tiled=True),
        lax.all_gather(w_out, ("dp", "blk"), axis=0, tiled=True),
        lax.all_gather(w_up, ("dp", "blk"), axis=0, tiled=True),
        lax.all_gather(w_down, ("dp", "blk"), axis=0, tiled=True),
        lax.all_gather(gains, ("dp", "blk"), axis=1, tiled=True),
    )


def reduce_grads(grad_terms):
    g_qkv, g_out, g_up, g_down, g_gains = grad_terms
    return (
        lax.psum_scatter(g_qkv, ("dp", "blk"), scatter_dimension=0, tiled=True),
        lax.psum_scatter(g_out, ("dp", "blk"), scatter_dimension=0, tiled=True),
        lax.psum_scatter(g_up, ("dp", "blk"), scatter_dimension=0, tiled=True),
        lax.psum_scatter(g_down, ("dp", "blk"), scatter_dimension=0, tiled=True),
        lax.psum_scatter(g_gains, ("dp", "blk"), scatter_dimension=1, tiled=True),
    )


def contract_rows(left_rows, right_rows):
    return jnp.einsum("ra,rb->ab", left_rows, right_rows, preferred_element_type=jnp.float32)


def row_delta_of(grad_attn, attended):
    product = grad_attn.astype(jnp.float32) * attended
    return product.reshape(product.shape[0], -1, HEAD_DIM).sum(-1).T


def on_device(
    patches, special, image_ids, w_qkv, w_out, w_up, w_down, gains, cot_patches, cot_special
):
    cycle_size = lax.axis_size("blk")
    cycle_index = lax.axis_index("blk")
    width = w_out.shape[1]
    head_count = width // HEAD_DIM
    tok_rows = TOK_MB
    spec_rows = special.shape[0] // MICRO
    ids_group = image_ids.reshape(cycle_size, MICRO, tok_rows)
    spec_ids = jnp.arange(spec_rows, dtype=jnp.int32) // SPECIAL
    row_weight = jnp.concatenate(
        [jnp.ones((tok_rows,), jnp.float32), jnp.full((spec_rows,), 1.0 / cycle_size, jnp.float32)]
    )
    row_weight_low = row_weight.astype(jnp.bfloat16)[:, None]
    summed_terms = None
    shard_terms = None
    out_parts = []
    spec_parts = []
    grad_parts = []
    grad_spec_parts = []
    for micro_index in range(MICRO):
        full_weights = fetch_weights(w_qkv, w_out, w_up, w_down, gains)
        qkv_full, out_full, up_full, down_full, gains_full = full_weights
        gain_rows = gains_full.astype(jnp.float32)
        tokens = jnp.concatenate(
            [
                patches[micro_index * tok_rows : (micro_index + 1) * tok_rows],
                special[micro_index * spec_rows : (micro_index + 1) * spec_rows],
            ],
            0,
        ).astype(jnp.float32)
        ids_flat = ids_group[:, micro_index].reshape(-1)
        patch_ids = lax.dynamic_slice_in_dim(ids_flat, cycle_index * tok_rows, tok_rows)
        normed = norm_rows(tokens, gain_rows[0]).astype(jnp.bfloat16)
        projected = jnp.dot(normed, qkv_full, preferred_element_type=jnp.float32).astype(
            jnp.bfloat16
        )
        patch_q = projected[:tok_rows, :width]
        patch_k = projected[:tok_rows, width : 2 * width]
        patch_v = projected[:tok_rows, 2 * width :]
        spec_q = projected[tok_rows:, :width]
        spec_k = projected[tok_rows:, width : 2 * width]
        spec_v = projected[tok_rows:, 2 * width :]
        start_state = online(
            empty_state(tok_rows, head_count, width), patch_q, patch_ids, spec_k, spec_v, spec_ids
        )
        partial_value = start_state
        key_rows = lax.all_gather(patch_k, "blk", axis=0, tiled=True)
        value_rows = lax.all_gather(patch_v, "blk", axis=0, tiled=True)
        length = key_rows.shape[0]
        key_ids = ids_flat
        blocks = length // tok_rows

        def visit_block(running, block_item):
            return (
                online(running, patch_q, patch_ids, block_item[0], block_item[1], block_item[2]),
                None,
            )

        partial_value, unused = lax.scan(
            visit_block,
            partial_value,
            (
                key_rows.reshape(blocks, tok_rows, -1),
                value_rows.reshape(blocks, tok_rows, -1),
                key_ids.reshape(blocks, tok_rows),
            ),
        )
        spec_top, spec_total, spec_accum = online(
            empty_state(spec_rows, head_count, width), spec_q, spec_ids, patch_k, patch_v, patch_ids
        )
        spec_state = merged((spec_top, spec_total, spec_accum), "blk", combine)
        spec_state = online(spec_state, spec_q, spec_ids, spec_k, spec_v, spec_ids)
        patch_attn, patch_lse = finish(partial_value)
        spec_attn, spec_lse = finish(spec_state)
        attended = jnp.concatenate([patch_attn, spec_attn], 0)
        attended_low = attended.astype(jnp.bfloat16)
        branch = jnp.dot(attended_low, out_full, preferred_element_type=jnp.float32)
        middle = tokens + gain_rows[1] * branch
        normed_mlp = norm_rows(middle, gain_rows[2]).astype(jnp.bfloat16)
        hidden = jnp.dot(normed_mlp, up_full, preferred_element_type=jnp.float32)
        active = jax.nn.gelu(hidden, approximate=False).astype(jnp.bfloat16)
        mlp_out = jnp.dot(active, down_full, preferred_element_type=jnp.float32)
        final = middle + gain_rows[3] * mlp_out
        out_parts.append(final[:tok_rows].astype(jnp.bfloat16))
        spec_parts.append(final[tok_rows:].astype(jnp.bfloat16))
        upstream = jnp.concatenate(
            [
                cot_patches[micro_index * tok_rows : (micro_index + 1) * tok_rows],
                cot_special[micro_index * spec_rows : (micro_index + 1) * spec_rows],
            ],
            0,
        ).astype(jnp.float32)
        grad_mlp = (gain_rows[3] * upstream).astype(jnp.bfloat16)
        g_down = contract_rows(active, grad_mlp * row_weight_low)
        grad_active = jnp.einsum(
            "rd,fd->rf", grad_mlp, down_full, preferred_element_type=jnp.float32
        )
        unused_value, gelu_pull = jax.vjp(
            lambda pre_act: jax.nn.gelu(pre_act, approximate=False), hidden
        )
        grad_hidden = gelu_pull(grad_active)[0].astype(jnp.bfloat16)
        g_up = contract_rows(normed_mlp, grad_hidden * row_weight_low)
        grad_normed_mlp = jnp.einsum(
            "rf,df->rd", grad_hidden, up_full, preferred_element_type=jnp.float32
        )
        unused_value, norm_pull_mlp = jax.vjp(
            lambda rows_in: norm_rows(rows_in, gain_rows[2]), middle
        )
        grad_middle = upstream + norm_pull_mlp(grad_normed_mlp)[0]
        g_ln2 = jnp.sum(row_weight[:, None] * grad_normed_mlp * norm_rows(middle, 1.0), 0)
        g_ls2 = jnp.sum(row_weight[:, None] * upstream * mlp_out, 0)
        g_ls1 = jnp.sum(row_weight[:, None] * grad_middle * branch, 0)
        grad_branch = (gain_rows[1] * grad_middle).astype(jnp.bfloat16)
        g_out = contract_rows(attended_low, grad_branch * row_weight_low)
        grad_attended = jnp.einsum(
            "re,de->rd", grad_branch, out_full, preferred_element_type=jnp.float32
        ).astype(jnp.bfloat16)
        all_delta = row_delta_of(grad_attended, attended)
        patch_delta = all_delta[:, :tok_rows]
        spec_delta = all_delta[:, tok_rows:]
        patch_grad_attn = grad_attended[:tok_rows]
        spec_grad_attn = grad_attended[tok_rows:]
        grad_pq_first, grad_sk_part, grad_sv_part = block_grads(
            patch_q, patch_grad_attn, patch_lse, patch_delta, patch_ids, spec_k, spec_v, spec_ids
        )
        grad_sq_part, grad_pk_local, grad_pv_local = block_grads(
            spec_q, spec_grad_attn, spec_lse, spec_delta, spec_ids, patch_k, patch_v, patch_ids
        )
        sum_sq, sum_sk, sum_sv = (
            lax.psum(grad_sq_part.astype(jnp.bfloat16), "blk").astype(jnp.float32),
            lax.psum(grad_sk_part.astype(jnp.bfloat16), "blk").astype(jnp.float32),
            lax.psum(grad_sv_part.astype(jnp.bfloat16), "blk").astype(jnp.float32),
        )
        grad_sq_own, grad_sk_own, grad_sv_own = block_grads(
            spec_q, spec_grad_attn, spec_lse, spec_delta, spec_ids, spec_k, spec_v, spec_ids
        )

        def cycle_step(hop_index, carried):
            keys_now, values_now, grad_keys, grad_values, grad_queries = carried
            source = (cycle_index - hop_index) % cycle_size
            key_ids = lax.dynamic_slice_in_dim(ids_flat, source * tok_rows, tok_rows)
            term_q, term_k, term_v = block_grads(
                patch_q,
                patch_grad_attn,
                patch_lse,
                patch_delta,
                patch_ids,
                keys_now,
                values_now,
                key_ids,
            )
            keys_now, values_now = from_behind((keys_now, values_now), "blk", 1)
            grad_keys, grad_values = (
                from_behind((grad_keys + term_k).astype(jnp.bfloat16), "blk", 1).astype(
                    jnp.float32
                ),
                from_behind((grad_values + term_v).astype(jnp.bfloat16), "blk", 1).astype(
                    jnp.float32
                ),
            )
            return (keys_now, values_now, grad_keys, grad_values, grad_queries + term_q)

        zero_rows = jnp.zeros((tok_rows, width), jnp.float32)
        unused_keys, unused_values, grad_pk, grad_pv, grad_pq = lax.fori_loop(
            0, cycle_size, cycle_step, (patch_k, patch_v, zero_rows, zero_rows, grad_pq_first)
        )
        grad_pk = grad_pk + grad_pk_local
        grad_pv = grad_pv + grad_pv_local
        grad_patch_qkv = jnp.concatenate([grad_pq, grad_pk, grad_pv], 1)
        grad_spec_qkv = jnp.concatenate(
            [sum_sq + grad_sq_own, sum_sk + grad_sk_own, sum_sv + grad_sv_own], 1
        )
        grad_projected = jnp.concatenate([grad_patch_qkv, grad_spec_qkv], 0).astype(jnp.bfloat16)
        g_qkv = contract_rows(normed, grad_projected * row_weight_low)
        grad_normed = jnp.einsum(
            "re,de->rd", grad_projected, qkv_full, preferred_element_type=jnp.float32
        )
        unused_value, norm_pull_attn = jax.vjp(
            lambda rows_in: norm_rows(rows_in, gain_rows[0]), tokens
        )
        grad_tokens = grad_middle + norm_pull_attn(grad_normed)[0]
        g_ln1 = jnp.sum(row_weight[:, None] * grad_normed * norm_rows(tokens, 1.0), 0)
        grad_parts.append(grad_tokens[:tok_rows])
        grad_spec_parts.append(grad_tokens[tok_rows:])
        grad_terms = (g_qkv, g_out, g_up, g_down, jnp.stack([g_ln1, g_ls1, g_ln2, g_ls2], 0))
        summed_terms = (
            grad_terms
            if summed_terms is None
            else tuple((held + extra for held, extra in zip(summed_terms, grad_terms)))
        )
    shard_terms = reduce_grads(summed_terms)
    return (
        jnp.concatenate(out_parts, 0),
        jnp.concatenate(spec_parts, 0),
        jnp.concatenate(grad_parts, 0),
        jnp.concatenate(grad_spec_parts, 0),
        shard_terms[0],
        shard_terms[1],
        shard_terms[2],
        shard_terms[3],
        shard_terms[4],
    )


PAD_ID = 99
PLAN = (
    (9.0, ()), (0, (0,)), (0, (0,)), (0, (2,)), (7.0, (2,)), (0, ()), (0, ()), (0, ()), (0, ()), (0, (4,)),
    (0, (1,)), (0, (3,)), (0, (8,)), (0, ()), (0, (12, 1)), (0, (5, 10)), (0, (7, 3)), (20, ()), (0, ()),
    (0, (11, 16)), (0, ()), (3.6, (17,)), (0, ()), (4, (3, 16, 0)), (0, (23,)), (0, (19, 0, 15)),
    (0, (10,)), (0, ()), (0, (23, 6, 9)), (1.6, ()), (0, (18,)), (0, (29, 15)), (0.001, (28, 30)),
    (2.8, ()), (45.0, (19,)), (0, (33, 31)), (0.185, (33, 20)), (0, (36,)), (0.09, (19, 36, 13)),
    (0, (33, 25)), (0.6, (38,)), (0, (40, 9, 38)), (1.2, ()), (0, ()), (0.7, (31,)), (0, ()),
    (0.001, (44,)), (0, (38, 44)), (0.001, ()), (0, (48,)), (21.0, ()), (0, ()), (0.002, ()), (0, (45,)),
    (1.4, ()), (0, ()), (0.065, (46,)), (0, (56, 43, 48)), (1.8, (23,)), (0, (58, 37)), (0.07, (35, 44)),
    (0, (47,)), (0.001, ()), (0, ()), (0.105, (58,)), (0, (55,)), (0, (65,)), (0, ()), (2.1, (33,)),
    (0, (60,)), (0.7, (55, 54)), (0.7, (70,)), (0, ()), (0, ()), (0, (55,)), (3, ()), (0.9, (50,)), (0, ()),
    (0, (59,)), (0, (78, 77)), (0.001, ()), (3, (80,)),
)
STEPS = []


def plan():
    us, steps = PLAN[len(STEPS)]
    return us, [STEPS[i] for i in steps]


def mm(a, b):
    return jnp.dot(a, b, preferred_element_type=F32)


def mm_nt(a, b):
    return lax.dot_general(a, b, (((1,), (1,)), ((), ())), preferred_element_type=F32)


def mm_tn(a, b):
    return lax.dot_general(a, b, (((0,), (0,)), ((), ())), preferred_element_type=F32)


def here():
    place = lax.axis_index("blk")
    group = lax.axis_index("dp")
    return place, place // 2, place % 2, group // 2, group % 2


def chunk_index(slot, z, y):
    return (z ^ (slot % 4)) * 2 + (y ^ (slot // 4))


def row_blocks(block, among=slice(0, 736)):
    return [slice(first, first + block) for first in range(among.start, among.stop, block)]


def fold(rows):
    return rows.reshape(rows.shape[0] // 8, 8, rows.shape[1]).sum(0)


class Keep:
    def __init__(self, value):
        self.value = value


class Far:
    def __init__(self, value):
        self.value = value


class Load:
    def __init__(self, buffer, copy):
        self.buffer, self.copy, self.waited = buffer, copy, False

    def ready(self):
        if not self.waited:
            self.copy.wait()
            self.waited = True
        return self.buffer


def call(kernel, outs, ins, scratch=(), limit=20):
    us, after = plan()
    far = [i for i, v in enumerate(ins) if isinstance(v, Far)]
    plain = [v.value if isinstance(v, (Far, Keep)) else v for v in ins]
    near, away = pl.BlockSpec(memory_space=pltpu.VMEM), pl.BlockSpec(memory_space=pltpu.HBM)
    room = [pltpu.VMEM(plain[i].shape, plain[i].dtype) for i in far]
    if far:
        room.append(pltpu.SemaphoreType.DMA((len(far),)))

    def body(*refs):
        given = [*refs[: len(ins)], *refs[len(ins) + len(after) :]]
        own = given[len(ins) + len(outs) + len(scratch) :]
        given = given[: len(ins) + len(outs) + len(scratch)]
        for k, i in enumerate(far):
            copy = pltpu.make_async_copy(given[i], own[k], own[-1].at[k])
            copy.start()
            given[i] = Load(own[k], copy)
        kernel(*given)

    def placed(v):
        if isinstance(v, Keep):
            return pltpu.with_memory_space_constraint(v.value, pltpu.VMEM)
        return pltpu.with_memory_space_constraint(v.value, pltpu.HBM) if isinstance(v, Far) else v

    made_arrays = pl.pallas_call(
        body,
        out_shape=tuple(
            pltpu.VMEM(v.value.shape, v.value.dtype) if isinstance(v, Keep) else v for v in outs
        ),
        in_specs=[away if i in far else near for i in range(len(ins))]
        + [pl.BlockSpec(memory_space=pl.ANY)] * len(after),
        out_specs=tuple(near for _ in outs),
        scratch_shapes=[*scratch, *room],
        compiler_params=pltpu.CompilerParams(vmem_limit_bytes=limit * 2**20),
        cost_estimate=pl.CostEstimate(flops=int(us * 10**9), bytes_accessed=0, transcendentals=0),
        name=kernel.__name__,
    )(*[placed(v) for v in ins], *after)
    STEPS.append(made_arrays[0])
    return made_arrays


def keep(*arrays):
    return [Keep(v) for v in arrays]


def sds(*shape, dtype=BF16):
    return jax.ShapeDtypeStruct(shape, dtype)


def pick_pieces(w_qkv, w_up, gains, patches, cots, own, near, far, rows, held):
    place = here()[0]
    held[...] = jnp.zeros_like(held)
    up = w_up.ready()[...].astype(F32)
    qkv = w_qkv.ready()[...].astype(F32)
    gain = gains.ready()[...].astype(F32)
    for b in range(4):
        for d in range(8):
            held[b, 0:24, d * 96 : d * 96 + 96] = up[:, d * 384 + b * 96 : d * 384 + b * 96 + 96]
        for part in range(3):
            held[b, 24:48, part * 192 : part * 192 + 192] = qkv[
                :, part * 768 + b * 192 : part * 768 + b * 192 + 192
            ]
        held[b, 24:28, 576:600] = gain
    own[...] = held[place].astype(BF16)
    near[...] = held[place ^ 1].astype(BF16)
    far[0:48, :] = held[place ^ 2].astype(BF16)
    far[48:96, :] = held[place ^ 3].astype(BF16)
    rows[0:176, :] = patches.ready()[...]
    rows[176:352, :] = cots.ready()[...]


def join_pieces(own, near, far, near_far, w_out, w_down, pack, both, pack_f, up_f):
    place = here()[0]
    pack_f[96:112, :] = jnp.zeros((16, 768), F32)
    pieces = (
        own[...].astype(F32),
        near[...].astype(F32),
        far[0:48, :].astype(F32),
        near_far[48:96, :].astype(F32),
    )
    for k, piece in enumerate(pieces):
        source = place ^ k
        at = pl.ds(pl.multiple_of(source * 24, 8), 24)
        up_f[at, :] = piece[0:24]
        pack_f[at, 0:576] = piece[24:48, 0:576]
        lanes = pl.ds(pl.multiple_of(source * 128, 128), 128)
        pack_f[96:104, lanes] = piece[24:32, 576:704]
    out = w_out[...].astype(F32)
    for i in range(4):
        pack_f[i * 24 : i * 24 + 24, 576:768] = out[:, i * 192 : i * 192 + 192]
    pack[...] = pack_f[...].astype(BF16)
    both[0:96, :] = up_f[...].astype(BF16)
    both[96:192, :] = w_down[...]


def open_pack(*refs):
    chunks, (w_qkv, w_out, gain_rows, out_f, gain_f) = refs[:8], refs[8:]
    _, _, _, z, y = here()
    for slot, chunk in enumerate(chunks):
        d = chunk_index(slot, z, y)
        w_qkv[pl.ds(pl.multiple_of(d * 96, 96), 96), :] = chunk[0:96, 0:576]
        tail = chunk[0:96, 576:768].astype(F32)
        for i in range(4):
            out_f[pl.ds(pl.multiple_of(d * 24, 8), 24), i * 192 : i * 192 + 192] = tail[
                i * 24 : i * 24 + 24
            ]
        gain_f[d] = chunk[96:112, :].astype(F32)
    w_out[...] = out_f[...].astype(BF16)
    gain_rows[...] = jnp.zeros_like(gain_rows)
    for d in range(8):
        for b in range(4):
            at = (d * 4 + b) * 24
            gain_rows[0:4, at : at + 24] = gain_f[d, 0:4, b * 128 : b * 128 + 24]


def normalise(rows):
    centre = rows - jnp.mean(rows, -1, keepdims=True)
    spread = jnp.mean(centre * centre, -1, keepdims=True)
    scale = lax.rsqrt(spread + EPSILON)
    return centre * scale, scale


def place_rows(scratch, blocks, tail, first):
    place = here()[0]
    for k, block in enumerate(blocks):
        rows = block[first : first + 176, :].astype(F32)
        source = place ^ k
        for m in range(MICRO):
            scratch[pl.ds(pl.multiple_of(m * 368 + source * 88, 8), 88), :] = rows[m * 88 : m * 88 + 88]
    rows = tail[...].astype(F32)
    for m in range(MICRO):
        scratch[m * 368 + 352 : m * 368 + 368, :] = jnp.zeros((16, 768), F32)
        scratch[m * 368 + 352 : m * 368 + 362, :] = rows[m * 10 : m * 10 + 10]


def turned(line):
    count = max(line.shape)
    down = lax.broadcasted_iota(jnp.int32, (count, count), 0)
    across = lax.broadcasted_iota(jnp.int32, (count, count), 1)
    return jnp.sum(jnp.where(down == across, line, 0.0), line.shape.index(count), keepdims=True)


def norm_rows_in(
    rows_0, rows_1, rows_2, rows_3, tail, cot_tail, ids,
    unit, bias, tokens, cots, unit_low, rows_f,
):
    slot = lax.broadcasted_iota(jnp.int32, (1, 16), 1)
    tail_ids = jnp.where(slot < 2 * SPECIAL, (slot >= SPECIAL).astype(jnp.int32), PAD_ID)
    for m in range(MICRO):
        row = jnp.concatenate([ids[b * 2 + m : b * 2 + m + 1, :] for b in range(4)] + [tail_ids], 1)
        row = row.astype(F32)
        bias[m] = jnp.where(turned(row) == row, 0.0, MASKED)
    blocks = (rows_0, rows_1, rows_2, rows_3)
    place_rows(rows_f, blocks, cot_tail, 176)
    for at in row_blocks(32):
        cots[at, :] = rows_f[at, :].astype(BF16)
    place_rows(rows_f, blocks, tail, 0)
    for at in row_blocks(32):
        rows = rows_f[at, :]
        tokens[at, :] = rows.astype(BF16)
        even = normalise(rows)[0]
        unit[at, :] = even
        unit_low[at, :] = even.astype(BF16)


def attend(unit, bias, w_qkv, gain_rows, attended, projected, probs):
    gain = gain_rows[0:1, :]
    for m in range(MICRO):
        at = slice(m * 368, m * 368 + 368)
        qkv = mm((unit[at, :] * gain).astype(BF16), w_qkv[...])
        qkv = jnp.concatenate([qkv[:, 0:192] * SCORE_SCALE, qkv[:, 192:576]], -1).astype(BF16)
        projected[at, :] = qkv
        heads = []
        for h in range(3):
            q = qkv[:, h * 64 : h * 64 + 64]
            k = qkv[:, 192 + h * 64 : 192 + h * 64 + 64]
            v = qkv[:, 384 + h * 64 : 384 + h * 64 + 64]
            scores = mm_nt(q, k) + bias[m]
            weights = jnp.exp(scores - jnp.max(scores, -1, keepdims=True))
            weights = weights * (1.0 / jnp.sum(weights, -1, keepdims=True))
            weights = weights.astype(BF16)
            probs[m * 3 + h] = weights
            heads.append(mm(weights, v))
        attended[at, :] = jnp.concatenate(heads, -1).astype(BF16)


def order_out(
    out_0, out_1, out_2, out_3, cots, gain_rows, ordered, mine, grad_mlp, out_f
):
    place = here()[0]
    for k, part in enumerate((out_0, out_1, out_2, out_3)):
        source = place ^ k
        rows = part[...].astype(F32)
        for d in range(8):
            at = pl.multiple_of((d * 4 + source) * 24, 8)
            out_f[pl.ds(at, 24), :] = rows[d * 24 : d * 24 + 24]
    ordered[...] = out_f[...].astype(BF16)
    mine[...] = out_f[pl.ds(pl.multiple_of(place * 192, 8), 192), :].astype(BF16)
    gain = gain_rows[3:4, :]
    for at in row_blocks(32):
        grad_mlp[at, :] = (gain * cots[at, :].astype(F32)).astype(BF16)


def branch_rows(
    head_0, head_1, head_2, head_3, w_out, tokens, gain_rows, normed, branch, own_rows, rows_f
):
    place = here()[0]
    gain_s, gain_n = gain_rows[1:2, :], gain_rows[2:3, :]
    for m in range(MICRO):
        group = slice(m * 368, m * 368 + 368)
        total = None
        for k, part in enumerate((head_0, head_1, head_2, head_3)):
            rows = w_out[pl.ds(pl.multiple_of((place ^ k) * 192, 16), 192), :]
            term = mm(part[group, :], rows)
            total = term if total is None else total + term
        rows_f[group, :] = total
        for at in row_blocks(16, group):
            a = rows_f[at, :]
            branch[at, :] = a.astype(BF16)
            rows = tokens[at, :].astype(F32) + gain_s * a
            rows_f[at, :] = rows
            normed[at, :] = (normalise(rows)[0] * gain_n).astype(BF16)
        for part, first in ((0, place * 88), (88, 352)):
            rows = 88 if part == 0 else 16
            own_rows[m * 104 + part : m * 104 + part + rows, :] = rows_f[
                pl.ds(pl.multiple_of(m * 368 + first, 8), rows), :
            ]


def raise_rows(*refs):
    normed, chunks = refs[0], refs[1:9]
    active, slope, w_up, w_down, rows_f = refs[9:]
    _, _, _, z, y = here()
    for slot, chunk in enumerate(chunks):
        d = chunk_index(slot, z, y)
        w_up[pl.ds(pl.multiple_of(d * 96, 96), 96), :] = chunk[0:96, :]
        w_down[pl.ds(pl.multiple_of(d * 96, 96), 96), :] = chunk[96:192, :]
    for m in range(MICRO):
        at = slice(m * 368, m * 368 + 368)
        rows_f[at, :] = mm(normed[at, :], w_up[...])
    for at in row_blocks(32):
        u = rows_f[at, :]
        half = 0.5 + 0.5 * lax.erf(u * 0.7071067811865476)
        active[at, :] = (u * half).astype(BF16)
        slope[at, :] = half + u * (0.3989422804014327 * jnp.exp(-0.5 * u * u))


def down_grads(active, grad_mlp, away, kept, work):
    _, _, _, z, _ = here()
    work[...] = mm_tn(active[...], grad_mlp[...])
    for pair in range(2):
        for side in range(2):
            ours = pl.multiple_of(((z ^ (2 * pair)) * 2 + side) * 96, 8)
            theirs = pl.multiple_of(((z ^ (2 * pair + 1)) * 2 + side) * 96, 8)
            kept[pair * 2 + side] = work[pl.ds(ours, 96), :]
            away[pair * 2 + side] = work[pl.ds(theirs, 96), :].astype(BF16)


def sum_fours(kept, came, own, away):
    own[...] = kept[0:2] + came[0:2].astype(F32)
    away[...] = (kept[2:4] + came[2:4].astype(F32)).astype(BF16)


def sum_sides(kept, came, own, away):
    y = here()[4]
    own[...] = kept[y] + came[y].astype(F32)
    away[...] = (kept[1 - y] + came[1 - y].astype(F32)).astype(BF16)


def lower_rows(slope, grad_mlp, w_up, w_down, away, kept, grad_hidden, work):
    core = here()[2]
    for m in range(MICRO):
        at = slice(m * 368, m * 368 + 368)
        grad = mm_nt(grad_mlp[at, :], w_down[...])
        grad_hidden[at, :] = (slope[at, :] * grad).astype(BF16)
        work[m] = mm_nt(grad_hidden[at, :], w_up[...])
    away[...] = work[1 - core].astype(BF16)
    kept[...] = work[core]


def split_rows(pieces, place, away, kept):
    away[0:208, :] = pieces[place ^ 1].astype(BF16)
    away[208:416, :] = pieces[place ^ 3].astype(BF16)
    kept[0:208, :] = pieces[place]
    kept[208:416, :] = pieces[place ^ 2]


def cut_rows(rows_f, pieces):
    for b in range(4):
        for m in range(MICRO):
            pieces[b, m * 104 : m * 104 + 88, :] = rows_f[m * 368 + b * 88 : m * 368 + b * 88 + 88, :]
            pieces[b, m * 104 + 88 : m * 104 + 104, :] = rows_f[m * 368 + 352 : m * 368 + 368, :]


def halve(grad_f, y, away, kept, rows):
    for zz in range(4):
        other = pl.ds(pl.multiple_of((zz * 2 + 1 - y) * rows, 8), rows)
        ours = pl.ds(pl.multiple_of((zz * 2 + y) * rows, 8), rows)
        away[zz] = grad_f[other, 0 : away.shape[2]].astype(BF16)
        kept[zz] = grad_f[ours, 0 : away.shape[2]]


def up_grads(normed, grad_hidden, away, kept, work):
    y = here()[4]
    work[...] = mm_tn(normed[...], grad_hidden[...])
    halve(work, y, away, kept, 96)


def mlp_rows(
    active, w_down, cots, head_0, head_1, head_2, head_3,
    rows_away, rows_kept, scale_grad, chosen, work, pieces,
):
    place = here()[0]
    for m in range(MICRO):
        at = slice(m * 368, m * 368 + 368)
        work[at, :] = mm(active[at, :], w_down[...])
    total = jnp.zeros((8, 768), F32)
    for at in row_blocks(32):
        total = total + fold(cots[at, :].astype(F32) * work[at, :])
    scale_grad[...] = total
    cut_rows(work, pieces)
    split_rows(pieces, place, rows_away, rows_kept)
    picked = None
    column = lax.broadcasted_iota(jnp.int32, (192, 192), 1)
    chunk = sum((column >= 24 * d).astype(jnp.int32) for d in range(1, 8))
    targets = column + chunk * 72 + place * 24
    for k, part in enumerate((head_0, head_1, head_2, head_3)):
        index = lax.broadcasted_iota(jnp.int32, (192, 192), 0) + (place ^ k) * 192
        pick = jnp.where(index == targets, 1.0, 0.0).astype(BF16)
        term = mm(part[...], pick)
        picked = term if picked is None else picked + term
    chosen[...] = picked.astype(BF16)


def add_rows(kept, came, total):
    total[...] = (kept[...] + came[...].astype(F32)).astype(BF16)


def add_pair(here_rows, came, total):
    total[...] = (here_rows[...].astype(F32) + came[...].astype(F32)).astype(BF16)


def branch_back(
    sum_own, sum_near, tokens, cots, branch, gain_rows, w_mine, probs, normed, scale_grad_mlp, chosen,
    grad_rows, grad_heads, grad_v, away, kept,
    work, grad_branch, grad_mid, extra, early,
):
    place, _, core, _, y = here()
    for m in range(MICRO):
        at = slice(m * 368, m * 368 + 368)

        @pl.when(core == m)
        def _():
            work[at, :] = sum_own[...].astype(F32)

        @pl.when(core != m)
        def _():
            work[at, :] = sum_near[...].astype(F32)

    gain_s, gain_n = gain_rows[1:2, :], gain_rows[2:3, :]
    scale_sum = jnp.zeros((8, 768), F32)
    for at in row_blocks(32):
        grown = branch[at, :].astype(F32)
        unit, scale = normalise(tokens[at, :].astype(F32) + gain_s * grown)
        pulled = work[at, :] * gain_n
        pulled = pulled - jnp.mean(pulled, -1, keepdims=True) - unit * jnp.mean(
            pulled * unit, -1, keepdims=True
        )
        through = cots[at, :].astype(F32) + scale * pulled
        grad_mid[at, :] = through
        grad_branch[at, :] = (gain_s * through).astype(BF16)
        scale_sum = scale_sum + fold(through * grown)
    for m in range(MICRO):
        for part, first in ((0, place * 88), (88, 352)):
            rows = 88 if part == 0 else 16
            grad_rows[m * 104 + part : m * 104 + part + rows, :] = grad_mid[
                pl.ds(pl.multiple_of(m * 368 + first, 8), rows), :
            ]
    for m in range(MICRO):
        at = slice(m * 368, m * 368 + 368)
        heads = mm_nt(grad_branch[at, :], w_mine[...]).astype(BF16)
        grad_heads[at, :] = heads
        terms = [mm_tn(probs[m * 3 + h], heads[:, h * 64 : h * 64 + 64]) for h in range(3)]
        grad_v[at, :] = jnp.concatenate(terms, -1).astype(BF16)
    grad_mid[0:768, 0:192] = mm_tn(normed[...], grad_v[...])
    extra[...] = mm_tn(chosen[...], grad_branch[...])
    scale_rows = (
        0.25 * jnp.sum(scale_sum, 0, keepdims=True),
        jnp.sum(scale_grad_mlp[...], 0, keepdims=True),
    )
    for d in range(8):
        base = d * 112
        early[base : base + 96, 0:192] = grad_mid[d * 96 : d * 96 + 96, 0:192]
        for i in range(4):
            early[base + i * 24 : base + i * 24 + 24, 192:384] = extra[
                d * 24 : d * 24 + 24, i * 192 : i * 192 + 192
            ]
        early[base + 96 : base + 112, :] = jnp.zeros((16, 384), F32)
        for i in range(2):
            early[base + 96 + i : base + 97 + i, 0:96] = scale_rows[i][:, d * 96 : d * 96 + 96]
    halve(early, y, away, kept, 112)


def score_back(probs, projected, grad_heads, normed, grad_qk, away, kept, work):
    _, _, _, _, y = here()
    for m in range(MICRO):
        at = slice(m * 368, m * 368 + 368)
        qkv = projected[at, :]
        g_heads = grad_heads[at, :]
        grads = [[], []]
        for h in range(3):
            q = qkv[:, h * 64 : h * 64 + 64]
            k = qkv[:, 192 + h * 64 : 192 + h * 64 + 64]
            v = qkv[:, 384 + h * 64 : 384 + h * 64 + 64]
            grad_prob = mm_nt(g_heads[:, h * 64 : h * 64 + 64], v)
            wide = probs[m * 3 + h].astype(F32)
            moved = wide * grad_prob
            delta = jnp.sum(moved, -1, keepdims=True)
            grad_score = (moved - wide * delta).astype(BF16)
            grads[0].append(mm(grad_score, k) * SCORE_SCALE)
            grads[1].append(mm_tn(q, grad_score))
        grad_qk[at, 0:192] = jnp.concatenate(grads[0], -1).astype(BF16)
        grad_qk[at, 192:384] = jnp.concatenate(grads[1], 0).T.astype(BF16)
    work[...] = mm_tn(normed[...], grad_qk[...])
    halve(work, y, away, kept, 96)


def project_back(grad_qk, grad_v, w_qkv, rows_away, rows_kept, work, pieces):
    place = here()[0]
    for m in range(MICRO):
        at = slice(m * 368, m * 368 + 368)
        work[at, :] = mm_nt(grad_qk[at, :], w_qkv[:, 0:384]) + mm_nt(grad_v[at, :], w_qkv[:, 384:576])
    cut_rows(work, pieces)
    split_rows(pieces, place, rows_away, rows_kept)


def sum_y(kept, came, own, send_1, send_2, send_3):
    _, _, _, z, _ = here()
    own[...] = kept[z] + came[z].astype(F32)
    for k, send in ((1, send_1), (2, send_2), (3, send_3)):
        send[...] = (kept[z ^ k] + came[z ^ k].astype(F32)).astype(BF16)


def sum_y_pairs(kept, came, own, away):
    _, _, _, z, _ = here()
    for k in range(2):
        own[k] = kept[z ^ (2 * k)] + came[z ^ (2 * k)].astype(F32)
        there = z ^ (2 * k + 1)
        away[k] = (kept[there] + came[there].astype(F32)).astype(BF16)


def sum_pairs(kept, came, own, away):
    own[...] = kept[0] + came[0].astype(F32)
    away[...] = (kept[1] + came[1].astype(F32)).astype(BF16)


def sum_last(own, came, total):
    total[...] = own[...] + came[...].astype(F32)


def add_pieces(kept_m, came_m, kept_h, came_h, stay, go):
    for i, (kept, came) in enumerate(((kept_m, came_m), (kept_h, came_h))):
        stay[i * 208 : i * 208 + 208, :] = kept[0:208, :] + came[0:208, :].astype(F32)
        go[i * 208 : i * 208 + 208, :] = (kept[208:416, :] + came[208:416, :].astype(F32)).astype(BF16)


def finish_rows(
    stay, came, own_rows, grad_rows, patches, tail, gain_rows,
    out_patches, out_special, grad_patches, grad_special,
):
    own = patches[...].astype(F32)
    rest = tail[...].astype(F32)
    outs, out_tails = [], []
    for m in range(MICRO):
        for part, count in ((0, 88), (88, 10)):
            at = slice(m * 104 + part, m * 104 + part + count)
            far_at = slice(208 + m * 104 + part, 208 + m * 104 + part + count)
            final = own_rows[at, :] + gain_rows[3:4, :] * (stay[at, :] + came[at, :].astype(F32))
            (outs if part == 0 else out_tails).append(final)
            rows = own[m * 88 : m * 88 + 88] if part == 0 else rest[m * 10 : m * 10 + 10]
            unit, scale = normalise(rows)
            pulled = gain_rows[0:1, :] * (stay[far_at, :] + came[far_at, :].astype(F32))
            pulled = pulled - jnp.mean(pulled, -1, keepdims=True) - unit * jnp.mean(
                pulled * unit, -1, keepdims=True
            )
            grad = grad_rows[at, :] + scale * pulled
            if part == 0:
                grad_patches[m * 88 : m * 88 + 88, :] = grad
            else:
                grad_special[m * 10 : m * 10 + 10, :] = grad
    out_patches[...] = jnp.concatenate(outs, 0).astype(BF16)
    out_special[...] = jnp.concatenate(out_tails, 0).astype(BF16)


def hand_out(held, own, near, far):
    place = here()[0]
    own[...] = held[place]
    near[...] = held[place ^ 1].astype(BF16)
    far[0:32, :] = held[place ^ 2].astype(BF16)
    far[32:64, :] = held[place ^ 3].astype(BF16)


def take_in(held, own, near, far, near_far):
    place = here()[0]
    held[place] = own[...]
    held[place ^ 1] = near[...].astype(F32)
    held[place ^ 2] = far[0:32, :].astype(F32)
    held[place ^ 3] = near_far[32:64, :].astype(F32)


def pick_up(kept, came, own, near, far, held):
    held[...] = jnp.zeros_like(held)
    for b in range(4):
        at = slice(b * 24, b * 24 + 24)
        held[b, 0:24, :] = kept[at, :] + came[at, :].astype(F32)
    hand_out(held, own, near, far)


def pick_attention(kept_a, came_a, kept_b, came_1, came_2, came_3, own, near, far, grad_out, held, sums):
    held[...] = jnp.zeros_like(held)
    sums[:, 0:384] = kept_a[...] + came_a[...].astype(F32)
    sums[0:96, 384:768] = (
        kept_b[...] + came_1[...].astype(F32) + came_2[...].astype(F32) + came_3[...].astype(F32)
    )
    for b in range(4):
        at = slice(b * 24, b * 24 + 24)
        held[b, 0:24, 0:384] = sums[at, 384:768]
        held[b, 0:24, 384:576] = sums[at, 0:192]
        held[b, 0:2, 576:600] = sums[96:98, at]
        grad_out[:, b * 192 : b * 192 + 192] = sums[at, 192:384]
    hand_out(held, own, near, far)


def join_up(own, near, far, near_far, w_up, gains, grad_up, norm_grad, held):
    take_in(held, own, near, far, near_far)
    for b in range(4):
        for d in range(8):
            at = d * 384 + b * 96
            grad_up[:, at : at + 96] = held[b, 0:24, d * 96 : d * 96 + 96]
    total = turned(jnp.sum(w_up[...].astype(F32) * grad_up[...], -1, keepdims=True))
    norm_grad[...] = total / gains[2:3, :].astype(F32)


def join_attention(
    own, near, far, near_far, w_qkv, gains, norm_grad, grad_qkv, grad_gains, held
):
    take_in(held, own, near, far, near_far)
    scales = None
    for b in range(4):
        for part in range(3):
            at = slice(part * 768 + b * 192, part * 768 + b * 192 + 192)
            grad_qkv[:, at] = held[b, 0:24, part * 192 : part * 192 + 192]
        term = held[b, 0:2, 576:600]
        scales = term if scales is None else scales + term
    plain = grad_qkv[...]
    grad_gains[0:1, :] = turned(jnp.sum(w_qkv[...].astype(F32) * plain, -1, keepdims=True))
    grad_gains[1:2, :] = scales[0:1, :]
    grad_gains[2:3, :] = norm_grad[...]
    grad_gains[3:4, :] = scales[1:2, :]
    grad_qkv[...] = plain * turned(gains[0:1, :].astype(F32))


def send(rows, axis, step):
    pairs = []
    for group in range(8):
        z, y = group // 2, group % 2
        for place in range(4):
            target = {
                "core": (group, place ^ 1),
                "x": (group, place ^ 2),
                "y": (z * 2 + 1 - y, place),
                "z": ((z ^ step) * 2 + y, place),
            }[axis]
            pairs.append((group * 4 + place, target[0] * 4 + target[1]))
    _, ready = plan()
    if ready:
        rows = lax.optimization_barrier((rows, *ready))[0]
    STEPS.append(lax.ppermute(rows, ("dp", "blk"), pairs))
    return STEPS[-1]


def add_y(kept, came):
    rows, width = kept.shape[1:]
    own, *parts = call(
        sum_y,
        [Keep(sds(rows, width, dtype=F32))] + [sds(rows, width)] * 3,
        [Keep(kept), came],
    )
    return [own, *[send(part, "z", k) for k, part in zip((1, 2, 3), parts)]]


def halve_y(kept, came):
    rows, width = kept.shape[1:]
    own, away = call(
        sum_y_pairs,
        [Keep(sds(2, rows, width, dtype=F32)), sds(2, rows, width)],
        [Keep(kept), came],
    )
    return own, send(away, "z", 1)


def halve_z(pair):
    kept, came = pair
    rows, width = kept.shape[1:]
    own, away = call(
        sum_pairs,
        [Keep(sds(rows, width, dtype=F32)), sds(rows, width)],
        [Keep(kept), came],
    )
    return own, send(away, "z", 2)


def side_y(kept, came):
    own, away = call(
        sum_sides,
        [Keep(sds(96, 768, dtype=F32)), sds(96, 768)],
        [Keep(kept), came],
    )
    return own, send(away, "y", 1)


def add_last(last):
    own, came = last
    return call(
        sum_last, [sds(*own.shape, dtype=F32)], [Keep(own), came]
    )[0]


def on_device_split(
    patches, special, image_ids, w_qkv, w_out, w_up, w_down, gains, cot_patches, cot_special
):
    STEPS.clear()
    own, near, far, rows = call(
        pick_pieces,
        [sds(48, 768), sds(48, 768), sds(96, 768), sds(352, 768)],
        [Far(w_qkv), Far(w_up), Far(gains), Far(patches), Far(cot_patches)],
        [pltpu.VMEM((4, 48, 768), F32)],
    )
    came_far = send(far, "x", 1)
    came_near, came_near_far = send(near, "core", 1), send(came_far, "core", 1)
    pack, both = call(
        join_pieces,
        [sds(112, 768), sds(192, 768)],
        [own, came_near, came_far, came_near_far, w_out, w_down],
        [pltpu.VMEM((112, 768), F32), pltpu.VMEM((96, 768), F32)],
    )
    pack_2 = send(pack, "z", 2)
    pack_1 = send(pack, "z", 1)
    pack_y0 = send(pack, "y", 1)
    far_rows = send(rows, "x", 1)
    both_y0 = send(both, "y", 1)
    pack_y1 = send(pack_1, "y", 1)
    pack_3 = send(pack_2, "z", 1)
    pack_y2 = send(pack_2, "y", 1)
    both_2 = send(both, "z", 2)
    both_1 = send(both, "z", 1)
    near_rows = send(rows, "core", 1)
    row_parts = [rows, near_rows, far_rows, send(far_rows, "core", 1)]
    unit, bias, tokens, cots, unit_low = call(
        norm_rows_in,
        keep(sds(736, 768, dtype=F32), sds(2, 368, 368, dtype=F32), *[sds(736, 768)] * 3),
        [*row_parts, special, cot_special, image_ids.reshape(8, 88)],
        [pltpu.VMEM((736, 768), F32)],
    )
    pack_y3 = send(pack_3, "y", 1)
    both_y1 = send(both_1, "y", 1)
    both_3 = send(both_2, "z", 1)
    qkv_full, out_part, gain_rows = call(
        open_pack,
        [Keep(sds(768, 576)), sds(192, 768), Keep(sds(8, 768, dtype=F32))],
        [pack, pack_1, pack_2, pack_3, pack_y0, pack_y1, pack_y2, pack_y3],
        [pltpu.VMEM((192, 768), F32), pltpu.VMEM((8, 16, 768), F32)],
    )
    far_out = send(out_part, "x", 1)
    attended, projected, probs = call(
        attend,
        [sds(736, 192), *keep(sds(736, 576), sds(6, 368, 368))],
        keep(unit, bias, qkv_full, gain_rows),
    )
    far_heads = send(attended, "x", 1)
    both_y2 = send(both_2, "y", 1)
    out_parts = [
        out_part, send(out_part, "core", 1),
        far_out, send(far_out, "core", 1),
    ]
    both_y3 = send(both_3, "y", 1)
    out_full, out_mine, grad_mlp = call(
        order_out,
        keep(sds(768, 768), sds(192, 768), sds(736, 768)),
        [*out_parts, *keep(cots, gain_rows)],
        [pltpu.VMEM((768, 768), F32)],
    )
    heads = [
        attended, send(attended, "core", 1),
        far_heads, send(far_heads, "core", 1),
    ]
    both_chunks = [both, both_1, both_2, both_3, both_y0, both_y1, both_y2, both_y3]
    normed_mlp, branch, own_rows = call(
        branch_rows,
        keep(sds(736, 768), sds(736, 768), sds(208, 768, dtype=F32)),
        [*heads, *keep(out_full, tokens, gain_rows)],
        [pltpu.VMEM((736, 768), F32)],
    )
    active, slope, up_full, down_full = call(
        raise_rows,
        keep(sds(736, 768), sds(736, 768, dtype=F32), sds(768, 768), sds(768, 768)),
        [Keep(normed_mlp), *both_chunks],
        [pltpu.VMEM((736, 768), F32)],
    )
    half = [sds(4, 96, 768), Keep(sds(4, 96, 768, dtype=F32))]
    rows_split = [sds(416, 768), Keep(sds(416, 768, dtype=F32))]

    def make_down(active):
        return call(
            down_grads,
            half,
            keep(active, grad_mlp),
            [pltpu.VMEM((768, 768), F32)],
        )

    down_away, down_kept = make_down(active)
    down_came = send(down_away, "z", 1)
    sum_away, sum_kept, grad_hidden = call(
        lower_rows,
        [sds(368, 768), *keep(sds(368, 768, dtype=F32), sds(736, 768))],
        keep(slope, grad_mlp, up_full, down_full),
        [pltpu.VMEM((2, 368, 768), F32)],
    )
    sum_came = send(sum_away, "core", 1)
    chip_sum = call(add_rows, [sds(368, 768)], [Keep(sum_kept), sum_came])[0]
    chip_came = send(chip_sum, "x", 1)
    up_away, up_kept = call(
        up_grads,
        half,
        keep(normed_mlp, grad_hidden),
        [pltpu.VMEM((768, 768), F32)],
    )
    up_came = send(up_away, "y", 1)
    m_away, m_kept, scale_mlp, chosen = call(
        mlp_rows,
        [*rows_split, *keep(sds(8, 768, dtype=F32), sds(736, 192))],
        [*keep(active, down_full, cots), *heads],
        [pltpu.VMEM((736, 768), F32), pltpu.VMEM((4, 208, 768), F32)],
    )
    m_came = send(m_away, "core", 1)
    down_two, down_away = call(
        sum_fours,
        [Keep(sds(2, 96, 768, dtype=F32)), sds(2, 96, 768)],
        [Keep(down_kept), down_came],
    )
    down_came = send(down_away, "z", 2)
    sum_own = call(add_pair, [sds(368, 768)], [chip_sum, chip_came])[0]
    sum_near = send(sum_own, "core", 1)
    grad_rows, grad_heads, grad_v, a_away, a_kept = call(
        branch_back,
        [
            *keep(sds(208, 768, dtype=F32), sds(736, 192), sds(736, 192)),
            sds(4, 112, 384), Keep(sds(4, 112, 384, dtype=F32)),
        ],
        [
            sum_own, sum_near, *keep(tokens, cots, branch, gain_rows, out_mine, probs, unit_low), *keep(scale_mlp, chosen),
        ],
        [
            pltpu.VMEM((736, 768), F32), pltpu.VMEM((736, 768), BF16),
            pltpu.VMEM((768, 768), F32), pltpu.VMEM((192, 768), F32), pltpu.VMEM((896, 384), F32),
        ],
    )
    a_came = send(a_away, "y", 1)
    up_steps = halve_y(up_kept, up_came)
    grad_qk, b_away, b_kept = call(
        score_back,
        [Keep(sds(736, 384)), sds(4, 96, 384), Keep(sds(4, 96, 384, dtype=F32))],
        keep(probs, projected, grad_heads, unit_low),
        [pltpu.VMEM((768, 384), F32)],
    )
    b_came = send(b_away, "y", 1)
    a_pair = halve_y(a_kept, a_came)
    h_away, h_kept = call(
        project_back,
        rows_split,
        keep(grad_qk, grad_v, qkv_full),
        [pltpu.VMEM((736, 768), F32), pltpu.VMEM((4, 208, 768), F32)],
    )
    h_came = send(h_away, "core", 1)
    stay, go = call(
        add_pieces,
        [Keep(sds(416, 768, dtype=F32)), sds(416, 768)],
        [Keep(m_kept), m_came, Keep(h_kept), h_came],
    )
    far_rows = send(go, "x", 1)
    down_last = side_y(down_two, down_came)
    up_last = halve_z(up_steps)
    b_steps = add_y(b_kept, b_came)
    a_last = halve_z(a_pair)
    grad_down = add_last(down_last)
    pieces = [Keep(sds(32, 768, dtype=F32)), sds(32, 768), sds(64, 768)]
    held = pltpu.VMEM((4, 32, 768), F32)
    own, near, far = call(pick_up, pieces, [Keep(up_last[0]), up_last[1]], [held])
    came_far = send(far, "x", 1)
    came_near, came_near_far = send(near, "core", 1), send(came_far, "core", 1)
    grad_up, norm_grad = call(
        join_up,
        [sds(24, 3072, dtype=F32), Keep(sds(1, 24, dtype=F32))],
        [Keep(own), came_near, came_far, came_near_far, w_up, gains],
        [held],
    )
    own, near, far, grad_out = call(
        pick_attention,
        [*pieces, sds(24, 768, dtype=F32)],
        [Keep(a_last[0]), a_last[1], Keep(b_steps[0]), *b_steps[1:]],
        [held, pltpu.VMEM((112, 768), F32)],
    )
    came_far = send(far, "x", 1)
    came_near, came_near_far = send(near, "core", 1), send(came_far, "core", 1)
    out_patches, out_special, grad_patches, grad_special = call(
        finish_rows,
        [
            sds(176, 768), sds(20, 768), sds(176, 768, dtype=F32), sds(20, 768, dtype=F32),
        ],
        [Keep(stay), far_rows, *keep(own_rows, grad_rows), patches, special, Keep(gain_rows)],
    )
    grad_qkv, grad_gains = call(
        join_attention,
        [sds(24, 2304, dtype=F32), sds(4, 24, dtype=F32)],
        [Keep(own), came_near, came_far, came_near_far, w_qkv, gains, Keep(norm_grad)],
        [held],
    )
    return (
        out_patches, out_special, grad_patches, grad_special,
        grad_qkv, grad_out, grad_up, grad_down, grad_gains,
    )


def solution(mesh):
    placed = (
        P(("dp", "blk"), None),
        P("dp", None),
        P("dp"),
        P(("dp", "blk"), None),
        P(("dp", "blk"), None),
        P(("dp", "blk"), None),
        P(("dp", "blk"), None),
        P(None, ("dp", "blk")),
        P(("dp", "blk"), None),
        P("dp", None),
    )
    whole = dict(mesh.shape) != {"dp": 8, "blk": 4}
    return jax.shard_map(
        on_device if whole else on_device_split,
        mesh=mesh,
        in_specs=placed,
        out_specs=(
            P(("dp", "blk"), None),
            P("dp", None),
            P(("dp", "blk"), None),
            P("dp", None),
            P(("dp", "blk"), None),
            P(("dp", "blk"), None),
            P(("dp", "blk"), None),
            P(("dp", "blk"), None),
            P(None, ("dp", "blk")),
        ),
        check_vma=False,
    )
```

```python
import jax
import jax.numpy as jnp
from jax import lax
from jax.experimental import pallas as pl
from jax.experimental.pallas import tpu as pltpu
from jax.sharding import PartitionSpec as P

HEAD_DIM = 64
SPECIAL = 5
MICRO = 2
TOK_MB = 88

SCORE_SCALE = 0.125
MASKED = -1e30
EPSILON = 1e-06

BF16 = jnp.bfloat16
F32 = jnp.float32


def merged(shard, axis, combine):
    everything = jax.tree.map(
        lambda part, kind: lax.all_gather(part.astype(kind), axis),
        shard,
        (jnp.bfloat16, jnp.bfloat16, jnp.bfloat16),
    )

    def take(k):
        return jax.tree.map(lambda part, own: part[k].astype(own.dtype), everything, shard)

    return lax.fori_loop(
        1, lax.axis_size(axis), lambda k, so_far: combine(so_far, take(k)), take(0)
    )


def from_behind(shard, axis, by):
    peers = lax.axis_size(axis)
    return lax.ppermute(shard, axis, [(i, (i + by) % peers) for i in range(peers)])


def norm_rows(values, gain_row):
    centre = values - jnp.mean(values, -1, keepdims=True)
    spread = jnp.mean(centre * centre, -1, keepdims=True)
    return centre * lax.rsqrt(spread + EPSILON) * gain_row


def split_heads(matrix):
    return matrix.reshape(matrix.shape[0], -1, HEAD_DIM)


def widen(per_head):
    return jnp.repeat(per_head.T, HEAD_DIM, axis=1)


def empty_state(length, head_count, feature_width):
    return (
        jnp.full((head_count, length), MASKED, jnp.float32),
        jnp.zeros((head_count, length), jnp.float32),
        jnp.zeros((length, feature_width), jnp.float32),
    )


def online(carried, queries, query_ids, key_rows, value_rows, key_ids):
    top_score, totals, accumulated = carried
    same_image = (query_ids[:, None] == key_ids[None, :])[None]
    scores = (
        jnp.einsum(
            "qhd,khd->hqk",
            split_heads(queries),
            split_heads(key_rows),
            preferred_element_type=jnp.float32,
        )
        * SCORE_SCALE
    )
    scores = jnp.where(same_image, scores, MASKED)
    new_top = jnp.maximum(top_score, jnp.max(scores, -1))
    weights = jnp.where(same_image, jnp.exp(scores - new_top[..., None]), 0.0)
    factor = jnp.exp(top_score - new_top)
    totals = totals * factor + jnp.sum(weights, -1)
    mixture = jnp.einsum(
        "hqk,khd->qhd",
        weights.astype(jnp.bfloat16),
        split_heads(value_rows),
        preferred_element_type=jnp.float32,
    )
    accumulated = accumulated * widen(factor) + mixture.reshape(accumulated.shape)
    return (new_top, totals, accumulated)


def combine(former, latter):
    highest = jnp.maximum(former[0], latter[0])
    scale_former = jnp.exp(former[0] - highest)
    scale_latter = jnp.exp(latter[0] - highest)
    return (
        highest,
        former[1] * scale_former + latter[1] * scale_latter,
        former[2] * widen(scale_former) + latter[2] * widen(scale_latter),
    )


def finish(carried):
    top_score, totals, accumulated = carried
    return (accumulated / widen(totals), top_score + jnp.log(totals))


def block_grads(queries, grad_attn, log_total, row_delta, query_ids, key_rows, value_rows, key_ids):
    same_image = (query_ids[:, None] == key_ids[None, :])[None]
    q_heads = split_heads(queries)
    g_heads = split_heads(grad_attn)
    scores = (
        jnp.einsum(
            "qhd,khd->hqk", q_heads, split_heads(key_rows), preferred_element_type=jnp.float32
        )
        * SCORE_SCALE
    )
    probabilities = jnp.where(same_image, jnp.exp(scores - log_total[..., None]), 0.0)
    grad_prob = jnp.einsum(
        "qhd,khd->hqk", g_heads, split_heads(value_rows), preferred_element_type=jnp.float32
    )
    dscore = (probabilities * (grad_prob - row_delta[..., None])).astype(jnp.bfloat16)
    grad_query = (
        jnp.einsum(
            "hqk,khd->qhd", dscore, split_heads(key_rows), preferred_element_type=jnp.float32
        ).reshape(queries.shape[0], -1)
        * SCORE_SCALE
    )
    grad_key = (
        jnp.einsum("hqk,qhd->khd", dscore, q_heads, preferred_element_type=jnp.float32).reshape(
            key_rows.shape[0], -1
        )
        * SCORE_SCALE
    )
    grad_value = jnp.einsum(
        "hqk,qhd->khd",
        probabilities.astype(jnp.bfloat16),
        g_heads,
        preferred_element_type=jnp.float32,
    ).reshape(key_rows.shape[0], -1)
    return (grad_query, grad_key, grad_value)


def fetch_weights(w_qkv, w_out, w_up, w_down, gains):
    return (
        lax.all_gather(w_qkv, ("dp", "blk"), axis=0, tiled=True),
        lax.all_gather(w_out, ("dp", "blk"), axis=0, tiled=True),
        lax.all_gather(w_up, ("dp", "blk"), axis=0, tiled=True),
        lax.all_gather(w_down, ("dp", "blk"), axis=0, tiled=True),
        lax.all_gather(gains, ("dp", "blk"), axis=1, tiled=True),
    )


def reduce_grads(grad_terms):
    g_qkv, g_out, g_up, g_down, g_gains = grad_terms
    return (
        lax.psum_scatter(g_qkv, ("dp", "blk"), scatter_dimension=0, tiled=True),
        lax.psum_scatter(g_out, ("dp", "blk"), scatter_dimension=0, tiled=True),
        lax.psum_scatter(g_up, ("dp", "blk"), scatter_dimension=0, tiled=True),
        lax.psum_scatter(g_down, ("dp", "blk"), scatter_dimension=0, tiled=True),
        lax.psum_scatter(g_gains, ("dp", "blk"), scatter_dimension=1, tiled=True),
    )


def contract_rows(left_rows, right_rows):
    return jnp.einsum("ra,rb->ab", left_rows, right_rows, preferred_element_type=jnp.float32)


def row_delta_of(grad_attn, attended):
    product = grad_attn.astype(jnp.float32) * attended
    return product.reshape(product.shape[0], -1, HEAD_DIM).sum(-1).T


def on_device(
    patches, special, image_ids, w_qkv, w_out, w_up, w_down, gains, cot_patches, cot_special
):
    cycle_size = lax.axis_size("blk")
    cycle_index = lax.axis_index("blk")
    width = w_out.shape[1]
    head_count = width // HEAD_DIM
    tok_rows = TOK_MB
    spec_rows = special.shape[0] // MICRO
    ids_group = image_ids.reshape(cycle_size, MICRO, tok_rows)
    spec_ids = jnp.arange(spec_rows, dtype=jnp.int32) // SPECIAL
    row_weight = jnp.concatenate(
        [jnp.ones((tok_rows,), jnp.float32), jnp.full((spec_rows,), 1.0 / cycle_size, jnp.float32)]
    )
    row_weight_low = row_weight.astype(jnp.bfloat16)[:, None]
    summed_terms = None
    shard_terms = None
    out_parts = []
    spec_parts = []
    grad_parts = []
    grad_spec_parts = []
    for micro_index in range(MICRO):
        full_weights = fetch_weights(w_qkv, w_out, w_up, w_down, gains)
        qkv_full, out_full, up_full, down_full, gains_full = full_weights
        gain_rows = gains_full.astype(jnp.float32)
        tokens = jnp.concatenate(
            [
                patches[micro_index * tok_rows : (micro_index + 1) * tok_rows],
                special[micro_index * spec_rows : (micro_index + 1) * spec_rows],
            ],
            0,
        ).astype(jnp.float32)
        ids_flat = ids_group[:, micro_index].reshape(-1)
        patch_ids = lax.dynamic_slice_in_dim(ids_flat, cycle_index * tok_rows, tok_rows)
        normed = norm_rows(tokens, gain_rows[0]).astype(jnp.bfloat16)
        projected = jnp.dot(normed, qkv_full, preferred_element_type=jnp.float32).astype(
            jnp.bfloat16
        )
        patch_q = projected[:tok_rows, :width]
        patch_k = projected[:tok_rows, width : 2 * width]
        patch_v = projected[:tok_rows, 2 * width :]
        spec_q = projected[tok_rows:, :width]
        spec_k = projected[tok_rows:, width : 2 * width]
        spec_v = projected[tok_rows:, 2 * width :]
        start_state = online(
            empty_state(tok_rows, head_count, width), patch_q, patch_ids, spec_k, spec_v, spec_ids
        )
        partial_value = start_state
        key_rows = lax.all_gather(patch_k, "blk", axis=0, tiled=True)
        value_rows = lax.all_gather(patch_v, "blk", axis=0, tiled=True)
        length = key_rows.shape[0]
        key_ids = ids_flat
        blocks = length // tok_rows

        def visit_block(running, block_item):
            return (
                online(running, patch_q, patch_ids, block_item[0], block_item[1], block_item[2]),
                None,
            )

        partial_value, unused = lax.scan(
            visit_block,
            partial_value,
            (
                key_rows.reshape(blocks, tok_rows, -1),
                value_rows.reshape(blocks, tok_rows, -1),
                key_ids.reshape(blocks, tok_rows),
            ),
        )
        spec_top, spec_total, spec_accum = online(
            empty_state(spec_rows, head_count, width), spec_q, spec_ids, patch_k, patch_v, patch_ids
        )
        spec_state = merged((spec_top, spec_total, spec_accum), "blk", combine)
        spec_state = online(spec_state, spec_q, spec_ids, spec_k, spec_v, spec_ids)
        patch_attn, patch_lse = finish(partial_value)
        spec_attn, spec_lse = finish(spec_state)
        attended = jnp.concatenate([patch_attn, spec_attn], 0)
        attended_low = attended.astype(jnp.bfloat16)
        branch = jnp.dot(attended_low, out_full, preferred_element_type=jnp.float32)
        middle = tokens + gain_rows[1] * branch
        normed_mlp = norm_rows(middle, gain_rows[2]).astype(jnp.bfloat16)
        hidden = jnp.dot(normed_mlp, up_full, preferred_element_type=jnp.float32)
        active = jax.nn.gelu(hidden, approximate=False).astype(jnp.bfloat16)
        mlp_out = jnp.dot(active, down_full, preferred_element_type=jnp.float32)
        final = middle + gain_rows[3] * mlp_out
        out_parts.append(final[:tok_rows].astype(jnp.bfloat16))
        spec_parts.append(final[tok_rows:].astype(jnp.bfloat16))
        upstream = jnp.concatenate(
            [
                cot_patches[micro_index * tok_rows : (micro_index + 1) * tok_rows],
                cot_special[micro_index * spec_rows : (micro_index + 1) * spec_rows],
            ],
            0,
        ).astype(jnp.float32)
        grad_mlp = (gain_rows[3] * upstream).astype(jnp.bfloat16)
        g_down = contract_rows(active, grad_mlp * row_weight_low)
        grad_active = jnp.einsum(
            "rd,fd->rf", grad_mlp, down_full, preferred_element_type=jnp.float32
        )
        unused_value, gelu_pull = jax.vjp(
            lambda pre_act: jax.nn.gelu(pre_act, approximate=False), hidden
        )
        grad_hidden = gelu_pull(grad_active)[0].astype(jnp.bfloat16)
        g_up = contract_rows(normed_mlp, grad_hidden * row_weight_low)
        grad_normed_mlp = jnp.einsum(
            "rf,df->rd", grad_hidden, up_full, preferred_element_type=jnp.float32
        )
        unused_value, norm_pull_mlp = jax.vjp(
            lambda rows_in: norm_rows(rows_in, gain_rows[2]), middle
        )
        grad_middle = upstream + norm_pull_mlp(grad_normed_mlp)[0]
        g_ln2 = jnp.sum(row_weight[:, None] * grad_normed_mlp * norm_rows(middle, 1.0), 0)
        g_ls2 = jnp.sum(row_weight[:, None] * upstream * mlp_out, 0)
        g_ls1 = jnp.sum(row_weight[:, None] * grad_middle * branch, 0)
        grad_branch = (gain_rows[1] * grad_middle).astype(jnp.bfloat16)
        g_out = contract_rows(attended_low, grad_branch * row_weight_low)
        grad_attended = jnp.einsum(
            "re,de->rd", grad_branch, out_full, preferred_element_type=jnp.float32
        ).astype(jnp.bfloat16)
        all_delta = row_delta_of(grad_attended, attended)
        patch_delta = all_delta[:, :tok_rows]
        spec_delta = all_delta[:, tok_rows:]
        patch_grad_attn = grad_attended[:tok_rows]
        spec_grad_attn = grad_attended[tok_rows:]
        grad_pq_first, grad_sk_part, grad_sv_part = block_grads(
            patch_q, patch_grad_attn, patch_lse, patch_delta, patch_ids, spec_k, spec_v, spec_ids
        )
        grad_sq_part, grad_pk_local, grad_pv_local = block_grads(
            spec_q, spec_grad_attn, spec_lse, spec_delta, spec_ids, patch_k, patch_v, patch_ids
        )
        sum_sq, sum_sk, sum_sv = (
            lax.psum(grad_sq_part.astype(jnp.bfloat16), "blk").astype(jnp.float32),
            lax.psum(grad_sk_part.astype(jnp.bfloat16), "blk").astype(jnp.float32),
            lax.psum(grad_sv_part.astype(jnp.bfloat16), "blk").astype(jnp.float32),
        )
        grad_sq_own, grad_sk_own, grad_sv_own = block_grads(
            spec_q, spec_grad_attn, spec_lse, spec_delta, spec_ids, spec_k, spec_v, spec_ids
        )

        def cycle_step(hop_index, carried):
            keys_now, values_now, grad_keys, grad_values, grad_queries = carried
            source = (cycle_index - hop_index) % cycle_size
            key_ids = lax.dynamic_slice_in_dim(ids_flat, source * tok_rows, tok_rows)
            term_q, term_k, term_v = block_grads(
                patch_q,
                patch_grad_attn,
                patch_lse,
                patch_delta,
                patch_ids,
                keys_now,
                values_now,
                key_ids,
            )
            keys_now, values_now = from_behind((keys_now, values_now), "blk", 1)
            grad_keys, grad_values = (
                from_behind((grad_keys + term_k).astype(jnp.bfloat16), "blk", 1).astype(
                    jnp.float32
                ),
                from_behind((grad_values + term_v).astype(jnp.bfloat16), "blk", 1).astype(
                    jnp.float32
                ),
            )
            return (keys_now, values_now, grad_keys, grad_values, grad_queries + term_q)

        zero_rows = jnp.zeros((tok_rows, width), jnp.float32)
        unused_keys, unused_values, grad_pk, grad_pv, grad_pq = lax.fori_loop(
            0, cycle_size, cycle_step, (patch_k, patch_v, zero_rows, zero_rows, grad_pq_first)
        )
        grad_pk = grad_pk + grad_pk_local
        grad_pv = grad_pv + grad_pv_local
        grad_patch_qkv = jnp.concatenate([grad_pq, grad_pk, grad_pv], 1)
        grad_spec_qkv = jnp.concatenate(
            [sum_sq + grad_sq_own, sum_sk + grad_sk_own, sum_sv + grad_sv_own], 1
        )
        grad_projected = jnp.concatenate([grad_patch_qkv, grad_spec_qkv], 0).astype(jnp.bfloat16)
        g_qkv = contract_rows(normed, grad_projected * row_weight_low)
        grad_normed = jnp.einsum(
            "re,de->rd", grad_projected, qkv_full, preferred_element_type=jnp.float32
        )
        unused_value, norm_pull_attn = jax.vjp(
            lambda rows_in: norm_rows(rows_in, gain_rows[0]), tokens
        )
        grad_tokens = grad_middle + norm_pull_attn(grad_normed)[0]
        g_ln1 = jnp.sum(row_weight[:, None] * grad_normed * norm_rows(tokens, 1.0), 0)
        grad_parts.append(grad_tokens[:tok_rows])
        grad_spec_parts.append(grad_tokens[tok_rows:])
        grad_terms = (g_qkv, g_out, g_up, g_down, jnp.stack([g_ln1, g_ls1, g_ln2, g_ls2], 0))
        summed_terms = (
            grad_terms
            if summed_terms is None
            else tuple((held + extra for held, extra in zip(summed_terms, grad_terms)))
        )
    shard_terms = reduce_grads(summed_terms)
    return (
        jnp.concatenate(out_parts, 0),
        jnp.concatenate(spec_parts, 0),
        jnp.concatenate(grad_parts, 0),
        jnp.concatenate(grad_spec_parts, 0),
        shard_terms[0],
        shard_terms[1],
        shard_terms[2],
        shard_terms[3],
        shard_terms[4],
    )


PAD_ID = 99
PLAN = (
    (9.0, ()), (0, (0,)), (0, (0,)), (0, (2,)), (7.0, (2,)), (0, ()), (0, ()), (0, (0,)), (0, (0,)),
    (0, (4, 0)), (0, (2,)), (0, (3,)), (0, (8,)), (0, ()), (0, (12, 1)), (0, (5, 10)), (0, (7, 3)),
    (60, ()), (0, ()), (0, (11, 16)), (0, ()), (36.0, (17,)), (0, ()), (1.2, (3, 16, 0)), (0, (23,)),
    (0, (19, 0, 15)), (0, (5,)), (0, ()), (0, (23, 6, 9)), (48.0, ()), (0, (18,)), (0, (29, 15, 27)),
    (0.002, (28, 30, 23)), (5.6, ()), (0.37, (22,)), (0, (34,)), (0.001, (19, 34, 13)), (0, (33, 25)),
    (0.002, (19, 30)), (0, ()), (0.6, (36,)), (0, (9, 36)), (1.2, ()), (0, ()), (0.07, ()), (0, ()),
    (0.27, ()), (0, (36, 44, 46)), (0.001, ()), (0, ()), (21.0, ()), (0, ()), (7.0, (34,)), (0, (47,)),
    (0.002, ()), (0, (45, 47)), (2.1, ()), (0, ()), (0.0325, ()), (0, (43, 48)), (0.36, (23, 59)),
    (0, (58,)), (0.105, (60,)), (0, (57,)), (0, (63,)), (0, (49,)), (2.1, (33,)), (0, (52,)), (2.1, ()),
    (0, ()), (2.1, ()), (0.7, (61,)), (0, ()), (0, ()), (0, (57, 67)), (3, (66,)), (9.0, (70,)), (0, (70,)),
    (0, (61,)), (0, (78, 77, 13)), (0.002, ()), (0.1, ()),
)
STEPS = []


def plan():
    us, steps = PLAN[len(STEPS)]
    return us, [STEPS[i] for i in steps]


def mm(a, b):
    return jnp.dot(a, b, preferred_element_type=F32)


def mm_nt(a, b):
    return lax.dot_general(a, b, (((1,), (1,)), ((), ())), preferred_element_type=F32)


def mm_tn(a, b):
    return lax.dot_general(a, b, (((0,), (0,)), ((), ())), preferred_element_type=F32)


def here():
    place = lax.axis_index("blk")
    group = lax.axis_index("dp")
    return place, place // 2, place % 2, group // 2, group % 2


def chunk_index(slot, z, y):
    return (z ^ (slot % 4)) * 2 + (y ^ (slot // 4))


def row_blocks(block, among=slice(0, 736)):
    return [slice(first, first + block) for first in range(among.start, among.stop, block)]


def fold(rows):
    return rows.reshape(rows.shape[0] // 8, 8, rows.shape[1]).sum(0)


class Keep:
    def __init__(self, value):
        self.value = value


class Far:
    def __init__(self, value):
        self.value = value


class Load:
    def __init__(self, buffer, copy):
        self.buffer, self.copy, self.waited = buffer, copy, False

    def ready(self):
        if not self.waited:
            self.copy.wait()
            self.waited = True
        return self.buffer


def call(kernel, outs, ins, scratch=(), limit=20):
    us, after = plan()
    far = [i for i, v in enumerate(ins) if isinstance(v, Far)]
    plain = [v.value if isinstance(v, (Far, Keep)) else v for v in ins]
    near, away = pl.BlockSpec(memory_space=pltpu.VMEM), pl.BlockSpec(memory_space=pltpu.HBM)
    room = [pltpu.VMEM(plain[i].shape, plain[i].dtype) for i in far]
    if far:
        room.append(pltpu.SemaphoreType.DMA((len(far),)))

    def body(*refs):
        given = [*refs[: len(ins)], *refs[len(ins) + len(after) :]]
        own = given[len(ins) + len(outs) + len(scratch) :]
        given = given[: len(ins) + len(outs) + len(scratch)]
        for k, i in enumerate(far):
            copy = pltpu.make_async_copy(given[i], own[k], own[-1].at[k])
            copy.start()
            given[i] = Load(own[k], copy)
        kernel(*given)

    def placed(v):
        if isinstance(v, Keep):
            return pltpu.with_memory_space_constraint(v.value, pltpu.VMEM)
        return pltpu.with_memory_space_constraint(v.value, pltpu.HBM) if isinstance(v, Far) else v

    made_arrays = pl.pallas_call(
        body,
        out_shape=tuple(
            pltpu.VMEM(v.value.shape, v.value.dtype) if isinstance(v, Keep) else v for v in outs
        ),
        in_specs=[away if i in far else near for i in range(len(ins))]
        + [pl.BlockSpec(memory_space=pl.ANY)] * len(after),
        out_specs=tuple(near for _ in outs),
        scratch_shapes=[*scratch, *room],
        compiler_params=pltpu.CompilerParams(vmem_limit_bytes=limit * 2**20),
        cost_estimate=pl.CostEstimate(flops=int(us * 10**9), bytes_accessed=0, transcendentals=0),
        name=kernel.__name__,
    )(*[placed(v) for v in ins], *after)
    STEPS.append(made_arrays[0])
    return made_arrays


def keep(*arrays):
    return [Keep(v) for v in arrays]


def sds(*shape, dtype=BF16):
    return jax.ShapeDtypeStruct(shape, dtype)


def pick_pieces(w_qkv, w_up, gains, patches, cots, own, near, far, rows, held):
    place = here()[0]
    held[...] = jnp.zeros_like(held)
    up = w_up.ready()[...].astype(F32)
    qkv = w_qkv.ready()[...].astype(F32)
    gain = gains.ready()[...].astype(F32)
    for b in range(4):
        for d in range(8):
            held[b, 0:24, d * 96 : d * 96 + 96] = up[:, d * 384 + b * 96 : d * 384 + b * 96 + 96]
        for part in range(3):
            held[b, 24:48, part * 192 : part * 192 + 192] = qkv[
                :, part * 768 + b * 192 : part * 768 + b * 192 + 192
            ]
        held[b, 24:28, 576:600] = gain
    own[...] = held[place].astype(BF16)
    near[...] = held[place ^ 1].astype(BF16)
    far[0:48, :] = held[place ^ 2].astype(BF16)
    far[48:96, :] = held[place ^ 3].astype(BF16)
    rows[0:176, :] = patches.ready()[...]
    rows[176:352, :] = cots.ready()[...]


def join_pieces(own, near, far, near_far, w_out, w_down, pack, both, pack_f, up_f):
    place = here()[0]
    pack_f[96:112, :] = jnp.zeros((16, 768), F32)
    pieces = (
        own[...].astype(F32),
        near[...].astype(F32),
        far[0:48, :].astype(F32),
        near_far[48:96, :].astype(F32),
    )
    for k, piece in enumerate(pieces):
        source = place ^ k
        at = pl.ds(pl.multiple_of(source * 24, 8), 24)
        up_f[at, :] = piece[0:24]
        pack_f[at, 0:576] = piece[24:48, 0:576]
        lanes = pl.ds(pl.multiple_of(source * 128, 128), 128)
        pack_f[96:104, lanes] = piece[24:32, 576:704]
    out = w_out[...].astype(F32)
    for i in range(4):
        pack_f[i * 24 : i * 24 + 24, 576:768] = out[:, i * 192 : i * 192 + 192]
    pack[...] = pack_f[...].astype(BF16)
    both[0:96, :] = up_f[...].astype(BF16)
    both[96:192, :] = w_down[...]


def open_pack(*refs):
    chunks, (w_qkv, w_out, gain_rows, out_f, gain_f) = refs[:8], refs[8:]
    _, _, _, z, y = here()
    for slot, chunk in enumerate(chunks):
        d = chunk_index(slot, z, y)
        w_qkv[pl.ds(pl.multiple_of(d * 96, 96), 96), :] = chunk[0:96, 0:576]
        tail = chunk[0:96, 576:768].astype(F32)
        for i in range(4):
            out_f[pl.ds(pl.multiple_of(d * 24, 8), 24), i * 192 : i * 192 + 192] = tail[
                i * 24 : i * 24 + 24
            ]
        gain_f[d] = chunk[96:112, :].astype(F32)
    w_out[...] = out_f[...].astype(BF16)
    gain_rows[...] = jnp.zeros_like(gain_rows)
    for d in range(8):
        for b in range(4):
            at = (d * 4 + b) * 24
            gain_rows[0:4, at : at + 24] = gain_f[d, 0:4, b * 128 : b * 128 + 24]


def normalise(rows):
    centre = rows - jnp.mean(rows, -1, keepdims=True)
    spread = jnp.mean(centre * centre, -1, keepdims=True)
    scale = lax.rsqrt(spread + EPSILON)
    return centre * scale, scale


def place_rows(scratch, blocks, tail, first):
    place = here()[0]
    for k, block in enumerate(blocks):
        rows = block[first : first + 176, :].astype(F32)
        source = place ^ k
        for m in range(MICRO):
            scratch[pl.ds(pl.multiple_of(m * 368 + source * 88, 8), 88), :] = rows[m * 88 : m * 88 + 88]
    rows = tail[...].astype(F32)
    for m in range(MICRO):
        scratch[m * 368 + 352 : m * 368 + 368, :] = jnp.zeros((16, 768), F32)
        scratch[m * 368 + 352 : m * 368 + 362, :] = rows[m * 10 : m * 10 + 10]


def turned(line):
    count = max(line.shape)
    down = lax.broadcasted_iota(jnp.int32, (count, count), 0)
    across = lax.broadcasted_iota(jnp.int32, (count, count), 1)
    return jnp.sum(jnp.where(down == across, line, 0.0), line.shape.index(count), keepdims=True)


def norm_rows_in(
    rows_0, rows_1, rows_2, rows_3, tail, cot_tail, ids,
    unit, bias, tokens, cots, unit_low, rows_f,
):
    slot = lax.broadcasted_iota(jnp.int32, (1, 16), 1)
    tail_ids = jnp.where(slot < 2 * SPECIAL, (slot >= SPECIAL).astype(jnp.int32), PAD_ID)
    for m in range(MICRO):
        row = jnp.concatenate([ids[b * 2 + m : b * 2 + m + 1, :] for b in range(4)] + [tail_ids], 1)
        row = row.astype(F32)
        bias[m] = jnp.where(turned(row) == row, 0.0, MASKED)
    blocks = (rows_0, rows_1, rows_2, rows_3)
    place_rows(rows_f, blocks, cot_tail, 176)
    for at in row_blocks(32):
        cots[at, :] = rows_f[at, :].astype(BF16)
    place_rows(rows_f, blocks, tail, 0)
    for at in row_blocks(32):
        rows = rows_f[at, :]
        tokens[at, :] = rows.astype(BF16)
        even = normalise(rows)[0]
        unit[at, :] = even
        unit_low[at, :] = even.astype(BF16)


def attend(unit, bias, w_qkv, gain_rows, attended, projected, probs):
    gain = gain_rows[0:1, :]
    for m in range(MICRO):
        at = slice(m * 368, m * 368 + 368)
        qkv = mm((unit[at, :] * gain).astype(BF16), w_qkv[...])
        qkv = jnp.concatenate([qkv[:, 0:192] * SCORE_SCALE, qkv[:, 192:576]], -1).astype(BF16)
        projected[at, :] = qkv
        heads = []
        for h in range(3):
            q = qkv[:, h * 64 : h * 64 + 64]
            k = qkv[:, 192 + h * 64 : 192 + h * 64 + 64]
            v = qkv[:, 384 + h * 64 : 384 + h * 64 + 64]
            scores = mm_nt(q, k) + bias[m]
            weights = jnp.exp(scores - jnp.max(scores, -1, keepdims=True))
            weights = weights * (1.0 / jnp.sum(weights, -1, keepdims=True))
            weights = weights.astype(BF16)
            probs[m * 3 + h] = weights
            heads.append(mm(weights, v))
        attended[at, :] = jnp.concatenate(heads, -1).astype(BF16)


def order_out(
    out_0, out_1, out_2, out_3, cots, gain_rows, ordered, mine, grad_mlp, out_f
):
    place = here()[0]
    for k, part in enumerate((out_0, out_1, out_2, out_3)):
        source = place ^ k
        rows = part[...].astype(F32)
        for d in range(8):
            at = pl.multiple_of((d * 4 + source) * 24, 8)
            out_f[pl.ds(at, 24), :] = rows[d * 24 : d * 24 + 24]
    ordered[...] = out_f[...].astype(BF16)
    mine[...] = out_f[pl.ds(pl.multiple_of(place * 192, 8), 192), :].astype(BF16)
    gain = gain_rows[3:4, :]
    for at in row_blocks(32):
        grad_mlp[at, :] = (gain * cots[at, :].astype(F32)).astype(BF16)


def branch_rows(
    head_0, head_1, head_2, head_3, w_out, tokens, gain_rows, normed, branch, own_rows, rows_f
):
    place = here()[0]
    gain_s, gain_n = gain_rows[1:2, :], gain_rows[2:3, :]
    for m in range(MICRO):
        group = slice(m * 368, m * 368 + 368)
        total = None
        for k, part in enumerate((head_0, head_1, head_2, head_3)):
            rows = w_out[pl.ds(pl.multiple_of((place ^ k) * 192, 16), 192), :]
            term = mm(part[group, :], rows)
            total = term if total is None else total + term
        rows_f[group, :] = total
        for at in row_blocks(16, group):
            a = rows_f[at, :]
            branch[at, :] = a.astype(BF16)
            rows = tokens[at, :].astype(F32) + gain_s * a
            rows_f[at, :] = rows
            normed[at, :] = (normalise(rows)[0] * gain_n).astype(BF16)
        for part, first in ((0, place * 88), (88, 352)):
            rows = 88 if part == 0 else 16
            own_rows[m * 104 + part : m * 104 + part + rows, :] = rows_f[
                pl.ds(pl.multiple_of(m * 368 + first, 8), rows), :
            ]


def raise_rows(*refs):
    normed, chunks = refs[0], refs[1:9]
    active, slope, w_up, w_down, rows_f = refs[9:]
    _, _, _, z, y = here()
    for slot, chunk in enumerate(chunks):
        d = chunk_index(slot, z, y)
        w_up[pl.ds(pl.multiple_of(d * 96, 96), 96), :] = chunk[0:96, :]
        w_down[pl.ds(pl.multiple_of(d * 96, 96), 96), :] = chunk[96:192, :]
    for m in range(MICRO):
        at = slice(m * 368, m * 368 + 368)
        rows_f[at, :] = mm(normed[at, :], w_up[...])
    for at in row_blocks(32):
        u = rows_f[at, :]
        half = 0.5 + 0.5 * lax.erf(u * 0.7071067811865476)
        active[at, :] = (u * half).astype(BF16)
        slope[at, :] = half + u * (0.3989422804014327 * jnp.exp(-0.5 * u * u))


def down_grads(active, grad_mlp, away, kept, work):
    _, _, _, z, _ = here()
    work[...] = mm_tn(active[...], grad_mlp[...])
    for pair in range(2):
        for side in range(2):
            ours = pl.multiple_of(((z ^ (2 * pair)) * 2 + side) * 96, 8)
            theirs = pl.multiple_of(((z ^ (2 * pair + 1)) * 2 + side) * 96, 8)
            kept[pair * 2 + side] = work[pl.ds(ours, 96), :]
            away[pair * 2 + side] = work[pl.ds(theirs, 96), :].astype(BF16)


def sum_fours(kept, came, own, away):
    own[...] = kept[0:2] + came[0:2].astype(F32)
    away[...] = (kept[2:4] + came[2:4].astype(F32)).astype(BF16)


def sum_sides(kept, came, own, away):
    y = here()[4]
    own[...] = kept[y] + came[y].astype(F32)
    away[...] = (kept[1 - y] + came[1 - y].astype(F32)).astype(BF16)


def lower_rows(slope, grad_mlp, w_up, w_down, away, kept, grad_hidden, work):
    core = here()[2]
    for m in range(MICRO):
        at = slice(m * 368, m * 368 + 368)
        grad = mm_nt(grad_mlp[at, :], w_down[...])
        grad_hidden[at, :] = (slope[at, :] * grad).astype(BF16)
        work[m] = mm_nt(grad_hidden[at, :], w_up[...])
    away[...] = work[1 - core].astype(BF16)
    kept[...] = work[core]


def split_rows(pieces, place, away, kept):
    away[0:208, :] = pieces[place ^ 1].astype(BF16)
    away[208:416, :] = pieces[place ^ 3].astype(BF16)
    kept[0:208, :] = pieces[place]
    kept[208:416, :] = pieces[place ^ 2]


def cut_rows(rows_f, pieces):
    for b in range(4):
        for m in range(MICRO):
            pieces[b, m * 104 : m * 104 + 88, :] = rows_f[m * 368 + b * 88 : m * 368 + b * 88 + 88, :]
            pieces[b, m * 104 + 88 : m * 104 + 104, :] = rows_f[m * 368 + 352 : m * 368 + 368, :]


def halve(grad_f, y, away, kept, rows):
    for zz in range(4):
        other = pl.ds(pl.multiple_of((zz * 2 + 1 - y) * rows, 8), rows)
        ours = pl.ds(pl.multiple_of((zz * 2 + y) * rows, 8), rows)
        away[zz] = grad_f[other, 0 : away.shape[2]].astype(BF16)
        kept[zz] = grad_f[ours, 0 : away.shape[2]]


def up_grads(normed, grad_hidden, away, kept, work):
    y = here()[4]
    work[...] = mm_tn(normed[...], grad_hidden[...])
    halve(work, y, away, kept, 96)


def mlp_rows(
    active, w_down, cots, head_0, head_1, head_2, head_3,
    rows_away, rows_kept, scale_grad, chosen, work, pieces,
):
    place = here()[0]
    for m in range(MICRO):
        at = slice(m * 368, m * 368 + 368)
        work[at, :] = mm(active[at, :], w_down[...])
    total = jnp.zeros((8, 768), F32)
    for at in row_blocks(32):
        total = total + fold(cots[at, :].astype(F32) * work[at, :])
    scale_grad[...] = total
    cut_rows(work, pieces)
    split_rows(pieces, place, rows_away, rows_kept)
    picked = None
    column = lax.broadcasted_iota(jnp.int32, (192, 192), 1)
    chunk = sum((column >= 24 * d).astype(jnp.int32) for d in range(1, 8))
    targets = column + chunk * 72 + place * 24
    for k, part in enumerate((head_0, head_1, head_2, head_3)):
        index = lax.broadcasted_iota(jnp.int32, (192, 192), 0) + (place ^ k) * 192
        pick = jnp.where(index == targets, 1.0, 0.0).astype(BF16)
        term = mm(part[...], pick)
        picked = term if picked is None else picked + term
    chosen[...] = picked.astype(BF16)


def add_rows(kept, came, total):
    total[...] = (kept[...] + came[...].astype(F32)).astype(BF16)


def add_pair(here_rows, came, total):
    total[...] = (here_rows[...].astype(F32) + came[...].astype(F32)).astype(BF16)


def branch_back(
    sum_own, sum_near, tokens, cots, branch, gain_rows, w_mine, probs, normed, scale_grad_mlp, chosen,
    grad_rows, grad_heads, grad_v, away, kept,
    work, grad_branch, grad_mid, extra, early,
):
    place, _, core, _, y = here()
    for m in range(MICRO):
        at = slice(m * 368, m * 368 + 368)

        @pl.when(core == m)
        def _():
            work[at, :] = sum_own[...].astype(F32)

        @pl.when(core != m)
        def _():
            work[at, :] = sum_near[...].astype(F32)

    gain_s, gain_n = gain_rows[1:2, :], gain_rows[2:3, :]
    scale_sum = jnp.zeros((8, 768), F32)
    for at in row_blocks(32):
        grown = branch[at, :].astype(F32)
        unit, scale = normalise(tokens[at, :].astype(F32) + gain_s * grown)
        pulled = work[at, :] * gain_n
        pulled = pulled - jnp.mean(pulled, -1, keepdims=True) - unit * jnp.mean(
            pulled * unit, -1, keepdims=True
        )
        through = cots[at, :].astype(F32) + scale * pulled
        grad_mid[at, :] = through
        grad_branch[at, :] = (gain_s * through).astype(BF16)
        scale_sum = scale_sum + fold(through * grown)
    for m in range(MICRO):
        for part, first in ((0, place * 88), (88, 352)):
            rows = 88 if part == 0 else 16
            grad_rows[m * 104 + part : m * 104 + part + rows, :] = grad_mid[
                pl.ds(pl.multiple_of(m * 368 + first, 8), rows), :
            ]
    for m in range(MICRO):
        at = slice(m * 368, m * 368 + 368)
        heads = mm_nt(grad_branch[at, :], w_mine[...]).astype(BF16)
        grad_heads[at, :] = heads
        terms = [mm_tn(probs[m * 3 + h], heads[:, h * 64 : h * 64 + 64]) for h in range(3)]
        grad_v[at, :] = jnp.concatenate(terms, -1).astype(BF16)
    grad_mid[0:768, 0:192] = mm_tn(normed[...], grad_v[...])
    extra[...] = mm_tn(chosen[...], grad_branch[...])
    scale_rows = (
        0.25 * jnp.sum(scale_sum, 0, keepdims=True),
        jnp.sum(scale_grad_mlp[...], 0, keepdims=True),
    )
    for d in range(8):
        base = d * 112
        early[base : base + 96, 0:192] = grad_mid[d * 96 : d * 96 + 96, 0:192]
        for i in range(4):
            early[base + i * 24 : base + i * 24 + 24, 192:384] = extra[
                d * 24 : d * 24 + 24, i * 192 : i * 192 + 192
            ]
        early[base + 96 : base + 112, :] = jnp.zeros((16, 384), F32)
        for i in range(2):
            early[base + 96 + i : base + 97 + i, 0:96] = scale_rows[i][:, d * 96 : d * 96 + 96]
    halve(early, y, away, kept, 112)


def score_back(probs, projected, grad_heads, normed, grad_qk, away, kept, work):
    _, _, _, _, y = here()
    for m in range(MICRO):
        at = slice(m * 368, m * 368 + 368)
        qkv = projected[at, :]
        g_heads = grad_heads[at, :]
        grads = [[], []]
        for h in range(3):
            q = qkv[:, h * 64 : h * 64 + 64]
            k = qkv[:, 192 + h * 64 : 192 + h * 64 + 64]
            v = qkv[:, 384 + h * 64 : 384 + h * 64 + 64]
            grad_prob = mm_nt(g_heads[:, h * 64 : h * 64 + 64], v)
            wide = probs[m * 3 + h].astype(F32)
            moved = wide * grad_prob
            delta = jnp.sum(moved, -1, keepdims=True)
            grad_score = (moved - wide * delta).astype(BF16)
            grads[0].append(mm(grad_score, k) * SCORE_SCALE)
            grads[1].append(mm_tn(q, grad_score))
        grad_qk[at, 0:192] = jnp.concatenate(grads[0], -1).astype(BF16)
        grad_qk[at, 192:384] = jnp.concatenate(grads[1], 0).T.astype(BF16)
    work[...] = mm_tn(normed[...], grad_qk[...])
    halve(work, y, away, kept, 96)


def project_back(grad_qk, grad_v, w_qkv, rows_away, rows_kept, work, pieces):
    place = here()[0]
    for m in range(MICRO):
        at = slice(m * 368, m * 368 + 368)
        work[at, :] = mm_nt(grad_qk[at, :], w_qkv[:, 0:384]) + mm_nt(grad_v[at, :], w_qkv[:, 384:576])
    cut_rows(work, pieces)
    split_rows(pieces, place, rows_away, rows_kept)


def sum_y(kept, came, own, send_1, send_2, send_3):
    _, _, _, z, _ = here()
    own[...] = kept[z] + came[z].astype(F32)
    for k, send in ((1, send_1), (2, send_2), (3, send_3)):
        send[...] = (kept[z ^ k] + came[z ^ k].astype(F32)).astype(BF16)


def sum_y_pairs(kept, came, own, away):
    _, _, _, z, _ = here()
    for k in range(2):
        own[k] = kept[z ^ (2 * k)] + came[z ^ (2 * k)].astype(F32)
        there = z ^ (2 * k + 1)
        away[k] = (kept[there] + came[there].astype(F32)).astype(BF16)


def sum_pairs(kept, came, own, away):
    own[...] = kept[0] + came[0].astype(F32)
    away[...] = (kept[1] + came[1].astype(F32)).astype(BF16)


def sum_last(own, came, total):
    total[...] = own[...] + came[...].astype(F32)


def add_pieces(kept_m, came_m, kept_h, came_h, stay, go):
    for i, (kept, came) in enumerate(((kept_m, came_m), (kept_h, came_h))):
        stay[i * 208 : i * 208 + 208, :] = kept[0:208, :] + came[0:208, :].astype(F32)
        go[i * 208 : i * 208 + 208, :] = (kept[208:416, :] + came[208:416, :].astype(F32)).astype(BF16)


def finish_rows(
    stay, came, own_rows, grad_rows, patches, tail, gain_rows,
    out_patches, out_special, grad_patches, grad_special,
):
    own = patches[...].astype(F32)
    rest = tail[...].astype(F32)
    outs, out_tails = [], []
    for m in range(MICRO):
        for part, count in ((0, 88), (88, 10)):
            at = slice(m * 104 + part, m * 104 + part + count)
            far_at = slice(208 + m * 104 + part, 208 + m * 104 + part + count)
            final = own_rows[at, :] + gain_rows[3:4, :] * (stay[at, :] + came[at, :].astype(F32))
            (outs if part == 0 else out_tails).append(final)
            rows = own[m * 88 : m * 88 + 88] if part == 0 else rest[m * 10 : m * 10 + 10]
            unit, scale = normalise(rows)
            pulled = gain_rows[0:1, :] * (stay[far_at, :] + came[far_at, :].astype(F32))
            pulled = pulled - jnp.mean(pulled, -1, keepdims=True) - unit * jnp.mean(
                pulled * unit, -1, keepdims=True
            )
            grad = grad_rows[at, :] + scale * pulled
            if part == 0:
                grad_patches[m * 88 : m * 88 + 88, :] = grad
            else:
                grad_special[m * 10 : m * 10 + 10, :] = grad
    out_patches[...] = jnp.concatenate(outs, 0).astype(BF16)
    out_special[...] = jnp.concatenate(out_tails, 0).astype(BF16)


def hand_out(held, own, near, far):
    place = here()[0]
    own[...] = held[place]
    near[...] = held[place ^ 1].astype(BF16)
    far[0:32, :] = held[place ^ 2].astype(BF16)
    far[32:64, :] = held[place ^ 3].astype(BF16)


def take_in(held, own, near, far, near_far):
    place = here()[0]
    held[place] = own[...]
    held[place ^ 1] = near[...].astype(F32)
    held[place ^ 2] = far[0:32, :].astype(F32)
    held[place ^ 3] = near_far[32:64, :].astype(F32)


def pick_up(kept, came, own, near, far, held):
    held[...] = jnp.zeros_like(held)
    for b in range(4):
        at = slice(b * 24, b * 24 + 24)
        held[b, 0:24, :] = kept[at, :] + came[at, :].astype(F32)
    hand_out(held, own, near, far)


def pick_attention(kept_a, came_a, kept_b, came_1, came_2, came_3, own, near, far, grad_out, held, sums):
    held[...] = jnp.zeros_like(held)
    sums[:, 0:384] = kept_a[...] + came_a[...].astype(F32)
    sums[0:96, 384:768] = (
        kept_b[...] + came_1[...].astype(F32) + came_2[...].astype(F32) + came_3[...].astype(F32)
    )
    for b in range(4):
        at = slice(b * 24, b * 24 + 24)
        held[b, 0:24, 0:384] = sums[at, 384:768]
        held[b, 0:24, 384:576] = sums[at, 0:192]
        held[b, 0:2, 576:600] = sums[96:98, at]
        grad_out[:, b * 192 : b * 192 + 192] = sums[at, 192:384]
    hand_out(held, own, near, far)


def join_up(own, near, far, near_far, w_up, gains, grad_up, norm_grad, held):
    take_in(held, own, near, far, near_far)
    for b in range(4):
        for d in range(8):
            at = d * 384 + b * 96
            grad_up[:, at : at + 96] = held[b, 0:24, d * 96 : d * 96 + 96]
    total = turned(jnp.sum(w_up[...].astype(F32) * grad_up[...], -1, keepdims=True))
    norm_grad[...] = total / gains[2:3, :].astype(F32)


def join_attention(
    own, near, far, near_far, w_qkv, gains, norm_grad, grad_qkv, grad_gains, held
):
    take_in(held, own, near, far, near_far)
    scales = None
    for b in range(4):
        for part in range(3):
            at = slice(part * 768 + b * 192, part * 768 + b * 192 + 192)
            grad_qkv[:, at] = held[b, 0:24, part * 192 : part * 192 + 192]
        term = held[b, 0:2, 576:600]
        scales = term if scales is None else scales + term
    plain = grad_qkv[...]
    grad_gains[0:1, :] = turned(jnp.sum(w_qkv[...].astype(F32) * plain, -1, keepdims=True))
    grad_gains[1:2, :] = scales[0:1, :]
    grad_gains[2:3, :] = norm_grad[...]
    grad_gains[3:4, :] = scales[1:2, :]
    grad_qkv[...] = plain * turned(gains[0:1, :].astype(F32))


def send(rows, axis, step):
    pairs = []
    for group in range(8):
        z, y = group // 2, group % 2
        for place in range(4):
            target = {
                "core": (group, place ^ 1),
                "x": (group, place ^ 2),
                "y": (z * 2 + 1 - y, place),
                "z": ((z ^ step) * 2 + y, place),
            }[axis]
            pairs.append((group * 4 + place, target[0] * 4 + target[1]))
    _, ready = plan()
    if ready:
        rows = lax.optimization_barrier((rows, *ready))[0]
    STEPS.append(lax.ppermute(rows, ("dp", "blk"), pairs))
    return STEPS[-1]


def add_y(kept, came):
    rows, width = kept.shape[1:]
    own, *parts = call(
        sum_y,
        [Keep(sds(rows, width, dtype=F32))] + [sds(rows, width)] * 3,
        [Keep(kept), came],
    )
    return [own, *[send(part, "z", k) for k, part in zip((1, 2, 3), parts)]]


def halve_y(kept, came):
    rows, width = kept.shape[1:]
    own, away = call(
        sum_y_pairs,
        [Keep(sds(2, rows, width, dtype=F32)), sds(2, rows, width)],
        [Keep(kept), came],
    )
    return own, send(away, "z", 1)


def halve_z(pair):
    kept, came = pair
    rows, width = kept.shape[1:]
    own, away = call(
        sum_pairs,
        [Keep(sds(rows, width, dtype=F32)), sds(rows, width)],
        [Keep(kept), came],
    )
    return own, send(away, "z", 2)


def side_y(kept, came):
    own, away = call(
        sum_sides,
        [Keep(sds(96, 768, dtype=F32)), sds(96, 768)],
        [Keep(kept), came],
    )
    return own, send(away, "y", 1)


def add_last(last):
    own, came = last
    return call(
        sum_last, [sds(*own.shape, dtype=F32)], [Keep(own), came]
    )[0]


def on_device_split(
    patches, special, image_ids, w_qkv, w_out, w_up, w_down, gains, cot_patches, cot_special
):
    STEPS.clear()
    own, near, far, rows = call(
        pick_pieces,
        [sds(48, 768), sds(48, 768), sds(96, 768), sds(352, 768)],
        [Far(w_qkv), Far(w_up), Far(gains), Far(patches), Far(cot_patches)],
        [pltpu.VMEM((4, 48, 768), F32)],
    )
    came_far = send(far, "x", 1)
    came_near, came_near_far = send(near, "core", 1), send(came_far, "core", 1)
    pack, both = call(
        join_pieces,
        [sds(112, 768), sds(192, 768)],
        [own, came_near, came_far, came_near_far, w_out, w_down],
        [pltpu.VMEM((112, 768), F32), pltpu.VMEM((96, 768), F32)],
    )
    pack_2 = send(pack, "z", 2)
    pack_1 = send(pack, "z", 1)
    pack_y0 = send(pack, "y", 1)
    far_rows = send(rows, "x", 1)
    both_y0 = send(both, "y", 1)
    pack_y1 = send(pack_1, "y", 1)
    pack_3 = send(pack_2, "z", 1)
    pack_y2 = send(pack_2, "y", 1)
    both_2 = send(both, "z", 2)
    both_1 = send(both, "z", 1)
    near_rows = send(rows, "core", 1)
    row_parts = [rows, near_rows, far_rows, send(far_rows, "core", 1)]
    unit, bias, tokens, cots, unit_low = call(
        norm_rows_in,
        keep(sds(736, 768, dtype=F32), sds(2, 368, 368, dtype=F32), *[sds(736, 768)] * 3),
        [*row_parts, special, cot_special, image_ids.reshape(8, 88)],
        [pltpu.VMEM((736, 768), F32)],
    )
    pack_y3 = send(pack_3, "y", 1)
    both_y1 = send(both_1, "y", 1)
    both_3 = send(both_2, "z", 1)
    qkv_full, out_part, gain_rows = call(
        open_pack,
        [Keep(sds(768, 576)), sds(192, 768), Keep(sds(8, 768, dtype=F32))],
        [pack, pack_1, pack_2, pack_3, pack_y0, pack_y1, pack_y2, pack_y3],
        [pltpu.VMEM((192, 768), F32), pltpu.VMEM((8, 16, 768), F32)],
    )
    far_out = send(out_part, "x", 1)
    attended, projected, probs = call(
        attend,
        [sds(736, 192), *keep(sds(736, 576), sds(6, 368, 368))],
        keep(unit, bias, qkv_full, gain_rows),
    )
    far_heads = send(attended, "x", 1)
    both_y2 = send(both_2, "y", 1)
    out_parts = [
        out_part, send(out_part, "core", 1),
        far_out, send(far_out, "core", 1),
    ]
    both_y3 = send(both_3, "y", 1)
    out_full, out_mine, grad_mlp = call(
        order_out,
        keep(sds(768, 768), sds(192, 768), sds(736, 768)),
        [*out_parts, *keep(cots, gain_rows)],
        [pltpu.VMEM((768, 768), F32)],
    )
    heads = [
        attended, send(attended, "core", 1),
        far_heads, send(far_heads, "core", 1),
    ]
    both_chunks = [both, both_1, both_2, both_3, both_y0, both_y1, both_y2, both_y3]
    normed_mlp, branch, own_rows = call(
        branch_rows,
        keep(sds(736, 768), sds(736, 768), sds(208, 768, dtype=F32)),
        [*heads, *keep(out_full, tokens, gain_rows)],
        [pltpu.VMEM((736, 768), F32)],
    )
    active, slope, up_full, down_full = call(
        raise_rows,
        keep(sds(736, 768), sds(736, 768, dtype=F32), sds(768, 768), sds(768, 768)),
        [Keep(normed_mlp), *both_chunks],
        [pltpu.VMEM((736, 768), F32)],
    )
    half = [sds(4, 96, 768), Keep(sds(4, 96, 768, dtype=F32))]
    rows_split = [sds(416, 768), Keep(sds(416, 768, dtype=F32))]

    def make_down(active):
        return call(
            down_grads,
            half,
            keep(active, grad_mlp),
            [pltpu.VMEM((768, 768), F32)],
        )

    sum_away, sum_kept, grad_hidden = call(
        lower_rows,
        [sds(368, 768), *keep(sds(368, 768, dtype=F32), sds(736, 768))],
        keep(slope, grad_mlp, up_full, down_full),
        [pltpu.VMEM((2, 368, 768), F32)],
    )
    sum_came = send(sum_away, "core", 1)
    chip_sum = call(add_rows, [sds(368, 768)], [Keep(sum_kept), sum_came])[0]
    chip_came = send(chip_sum, "x", 1)
    down_away, down_kept = make_down(active)
    down_came = send(down_away, "z", 1)
    up_away, up_kept = call(
        up_grads,
        half,
        keep(normed_mlp, grad_hidden),
        [pltpu.VMEM((768, 768), F32)],
    )
    up_came = send(up_away, "y", 1)
    m_away, m_kept, scale_mlp, chosen = call(
        mlp_rows,
        [*rows_split, *keep(sds(8, 768, dtype=F32), sds(736, 192))],
        [*keep(active, down_full, cots), *heads],
        [pltpu.VMEM((736, 768), F32), pltpu.VMEM((4, 208, 768), F32)],
    )
    m_came = send(m_away, "core", 1)
    down_two, down_away = call(
        sum_fours,
        [Keep(sds(2, 96, 768, dtype=F32)), sds(2, 96, 768)],
        [Keep(down_kept), down_came],
    )
    down_came = send(down_away, "z", 2)
    sum_own = call(add_pair, [sds(368, 768)], [chip_sum, chip_came])[0]
    sum_near = send(sum_own, "core", 1)
    grad_rows, grad_heads, grad_v, a_away, a_kept = call(
        branch_back,
        [
            *keep(sds(208, 768, dtype=F32), sds(736, 192), sds(736, 192)),
            sds(4, 112, 384), Keep(sds(4, 112, 384, dtype=F32)),
        ],
        [
            sum_own, sum_near, *keep(tokens, cots, branch, gain_rows, out_mine, probs, unit_low), *keep(scale_mlp, chosen),
        ],
        [
            pltpu.VMEM((736, 768), F32), pltpu.VMEM((736, 768), BF16),
            pltpu.VMEM((768, 768), F32), pltpu.VMEM((192, 768), F32), pltpu.VMEM((896, 384), F32),
        ],
    )
    a_came = send(a_away, "y", 1)
    up_steps = halve_y(up_kept, up_came)
    down_last = side_y(down_two, down_came)
    grad_qk, b_away, b_kept = call(
        score_back,
        [Keep(sds(736, 384)), sds(4, 96, 384), Keep(sds(4, 96, 384, dtype=F32))],
        keep(probs, projected, grad_heads, unit_low),
        [pltpu.VMEM((768, 384), F32)],
    )
    b_came = send(b_away, "y", 1)
    a_pair = halve_y(a_kept, a_came)
    h_away, h_kept = call(
        project_back,
        rows_split,
        keep(grad_qk, grad_v, qkv_full),
        [pltpu.VMEM((736, 768), F32), pltpu.VMEM((4, 208, 768), F32)],
    )
    h_came = send(h_away, "core", 1)
    stay, go = call(
        add_pieces,
        [Keep(sds(416, 768, dtype=F32)), sds(416, 768)],
        [Keep(m_kept), m_came, Keep(h_kept), h_came],
    )
    far_rows = send(go, "x", 1)
    b_steps = add_y(b_kept, b_came)
    a_last = halve_z(a_pair)
    up_last = halve_z(up_steps)
    grad_down = add_last(down_last)
    pieces = [Keep(sds(32, 768, dtype=F32)), sds(32, 768), sds(64, 768)]
    held = pltpu.VMEM((4, 32, 768), F32)
    own, near, far = call(pick_up, pieces, [Keep(up_last[0]), up_last[1]], [held])
    came_far = send(far, "x", 1)
    came_near, came_near_far = send(near, "core", 1), send(came_far, "core", 1)
    grad_up, norm_grad = call(
        join_up,
        [sds(24, 3072, dtype=F32), Keep(sds(1, 24, dtype=F32))],
        [Keep(own), came_near, came_far, came_near_far, w_up, gains],
        [held],
    )
    own, near, far, grad_out = call(
        pick_attention,
        [*pieces, sds(24, 768, dtype=F32)],
        [Keep(a_last[0]), a_last[1], Keep(b_steps[0]), *b_steps[1:]],
        [held, pltpu.VMEM((112, 768), F32)],
    )
    came_far = send(far, "x", 1)
    came_near, came_near_far = send(near, "core", 1), send(came_far, "core", 1)
    out_patches, out_special, grad_patches, grad_special = call(
        finish_rows,
        [
            sds(176, 768), sds(20, 768), sds(176, 768, dtype=F32), sds(20, 768, dtype=F32),
        ],
        [Keep(stay), far_rows, *keep(own_rows, grad_rows), patches, special, Keep(gain_rows)],
    )
    grad_qkv, grad_gains = call(
        join_attention,
        [sds(24, 2304, dtype=F32), sds(4, 24, dtype=F32)],
        [Keep(own), came_near, came_far, came_near_far, w_qkv, gains, Keep(norm_grad)],
        [held],
    )
    return (
        out_patches, out_special, grad_patches, grad_special,
        grad_qkv, grad_out, grad_up, grad_down, grad_gains,
    )


def solution(mesh):
    placed = (
        P(("dp", "blk"), None),
        P("dp", None),
        P("dp"),
        P(("dp", "blk"), None),
        P(("dp", "blk"), None),
        P(("dp", "blk"), None),
        P(("dp", "blk"), None),
        P(None, ("dp", "blk")),
        P(("dp", "blk"), None),
        P("dp", None),
    )
    whole = dict(mesh.shape) != {"dp": 8, "blk": 4}
    return jax.shard_map(
        on_device if whole else on_device_split,
        mesh=mesh,
        in_specs=placed,
        out_specs=(
            P(("dp", "blk"), None),
            P("dp", None),
            P(("dp", "blk"), None),
            P("dp", None),
            P(("dp", "blk"), None),
            P(("dp", "blk"), None),
            P(("dp", "blk"), None),
            P(("dp", "blk"), None),
            P(None, ("dp", "blk")),
        ),
        check_vma=False,
    )
```

```python
import jax
import jax.numpy as jnp
from jax import lax
from jax.experimental import pallas as pl
from jax.experimental.pallas import tpu as pltpu
from jax.sharding import PartitionSpec as P

HEAD_DIM = 64
SPECIAL = 5
MICRO = 2
TOK_MB = 88

SCORE_SCALE = 0.125
MASKED = -1e30
EPSILON = 1e-06

BF16 = jnp.bfloat16
F32 = jnp.float32


def merged(shard, axis, combine):
    everything = jax.tree.map(
        lambda part, kind: lax.all_gather(part.astype(kind), axis),
        shard,
        (jnp.bfloat16, jnp.bfloat16, jnp.bfloat16),
    )

    def take(k):
        return jax.tree.map(lambda part, own: part[k].astype(own.dtype), everything, shard)

    return lax.fori_loop(
        1, lax.axis_size(axis), lambda k, so_far: combine(so_far, take(k)), take(0)
    )


def from_behind(shard, axis, by):
    peers = lax.axis_size(axis)
    return lax.ppermute(shard, axis, [(i, (i + by) % peers) for i in range(peers)])


def norm_rows(values, gain_row):
    centre = values - jnp.mean(values, -1, keepdims=True)
    spread = jnp.mean(centre * centre, -1, keepdims=True)
    return centre * lax.rsqrt(spread + EPSILON) * gain_row


def split_heads(matrix):
    return matrix.reshape(matrix.shape[0], -1, HEAD_DIM)


def widen(per_head):
    return jnp.repeat(per_head.T, HEAD_DIM, axis=1)


def empty_state(length, head_count, feature_width):
    return (
        jnp.full((head_count, length), MASKED, jnp.float32),
        jnp.zeros((head_count, length), jnp.float32),
        jnp.zeros((length, feature_width), jnp.float32),
    )


def online(carried, queries, query_ids, key_rows, value_rows, key_ids):
    top_score, totals, accumulated = carried
    same_image = (query_ids[:, None] == key_ids[None, :])[None]
    scores = (
        jnp.einsum(
            "qhd,khd->hqk",
            split_heads(queries),
            split_heads(key_rows),
            preferred_element_type=jnp.float32,
        )
        * SCORE_SCALE
    )
    scores = jnp.where(same_image, scores, MASKED)
    new_top = jnp.maximum(top_score, jnp.max(scores, -1))
    weights = jnp.where(same_image, jnp.exp(scores - new_top[..., None]), 0.0)
    factor = jnp.exp(top_score - new_top)
    totals = totals * factor + jnp.sum(weights, -1)
    mixture = jnp.einsum(
        "hqk,khd->qhd",
        weights.astype(jnp.bfloat16),
        split_heads(value_rows),
        preferred_element_type=jnp.float32,
    )
    accumulated = accumulated * widen(factor) + mixture.reshape(accumulated.shape)
    return (new_top, totals, accumulated)


def combine(former, latter):
    highest = jnp.maximum(former[0], latter[0])
    scale_former = jnp.exp(former[0] - highest)
    scale_latter = jnp.exp(latter[0] - highest)
    return (
        highest,
        former[1] * scale_former + latter[1] * scale_latter,
        former[2] * widen(scale_former) + latter[2] * widen(scale_latter),
    )


def finish(carried):
    top_score, totals, accumulated = carried
    return (accumulated / widen(totals), top_score + jnp.log(totals))


def block_grads(queries, grad_attn, log_total, row_delta, query_ids, key_rows, value_rows, key_ids):
    same_image = (query_ids[:, None] == key_ids[None, :])[None]
    q_heads = split_heads(queries)
    g_heads = split_heads(grad_attn)
    scores = (
        jnp.einsum(
            "qhd,khd->hqk", q_heads, split_heads(key_rows), preferred_element_type=jnp.float32
        )
        * SCORE_SCALE
    )
    probabilities = jnp.where(same_image, jnp.exp(scores - log_total[..., None]), 0.0)
    grad_prob = jnp.einsum(
        "qhd,khd->hqk", g_heads, split_heads(value_rows), preferred_element_type=jnp.float32
    )
    dscore = (probabilities * (grad_prob - row_delta[..., None])).astype(jnp.bfloat16)
    grad_query = (
        jnp.einsum(
            "hqk,khd->qhd", dscore, split_heads(key_rows), preferred_element_type=jnp.float32
        ).reshape(queries.shape[0], -1)
        * SCORE_SCALE
    )
    grad_key = (
        jnp.einsum("hqk,qhd->khd", dscore, q_heads, preferred_element_type=jnp.float32).reshape(
            key_rows.shape[0], -1
        )
        * SCORE_SCALE
    )
    grad_value = jnp.einsum(
        "hqk,qhd->khd",
        probabilities.astype(jnp.bfloat16),
        g_heads,
        preferred_element_type=jnp.float32,
    ).reshape(key_rows.shape[0], -1)
    return (grad_query, grad_key, grad_value)


def fetch_weights(w_qkv, w_out, w_up, w_down, gains):
    return (
        lax.all_gather(w_qkv, ("dp", "blk"), axis=0, tiled=True),
        lax.all_gather(w_out, ("dp", "blk"), axis=0, tiled=True),
        lax.all_gather(w_up, ("dp", "blk"), axis=0, tiled=True),
        lax.all_gather(w_down, ("dp", "blk"), axis=0, tiled=True),
        lax.all_gather(gains, ("dp", "blk"), axis=1, tiled=True),
    )


def reduce_grads(grad_terms):
    g_qkv, g_out, g_up, g_down, g_gains = grad_terms
    return (
        lax.psum_scatter(g_qkv, ("dp", "blk"), scatter_dimension=0, tiled=True),
        lax.psum_scatter(g_out, ("dp", "blk"), scatter_dimension=0, tiled=True),
        lax.psum_scatter(g_up, ("dp", "blk"), scatter_dimension=0, tiled=True),
        lax.psum_scatter(g_down, ("dp", "blk"), scatter_dimension=0, tiled=True),
        lax.psum_scatter(g_gains, ("dp", "blk"), scatter_dimension=1, tiled=True),
    )


def contract_rows(left_rows, right_rows):
    return jnp.einsum("ra,rb->ab", left_rows, right_rows, preferred_element_type=jnp.float32)


def row_delta_of(grad_attn, attended):
    product = grad_attn.astype(jnp.float32) * attended
    return product.reshape(product.shape[0], -1, HEAD_DIM).sum(-1).T


def on_device(
    patches, special, image_ids, w_qkv, w_out, w_up, w_down, gains, cot_patches, cot_special
):
    cycle_size = lax.axis_size("blk")
    cycle_index = lax.axis_index("blk")
    width = w_out.shape[1]
    head_count = width // HEAD_DIM
    tok_rows = TOK_MB
    spec_rows = special.shape[0] // MICRO
    ids_group = image_ids.reshape(cycle_size, MICRO, tok_rows)
    spec_ids = jnp.arange(spec_rows, dtype=jnp.int32) // SPECIAL
    row_weight = jnp.concatenate(
        [jnp.ones((tok_rows,), jnp.float32), jnp.full((spec_rows,), 1.0 / cycle_size, jnp.float32)]
    )
    row_weight_low = row_weight.astype(jnp.bfloat16)[:, None]
    summed_terms = None
    shard_terms = None
    out_parts = []
    spec_parts = []
    grad_parts = []
    grad_spec_parts = []
    for micro_index in range(MICRO):
        full_weights = fetch_weights(w_qkv, w_out, w_up, w_down, gains)
        qkv_full, out_full, up_full, down_full, gains_full = full_weights
        gain_rows = gains_full.astype(jnp.float32)
        tokens = jnp.concatenate(
            [
                patches[micro_index * tok_rows : (micro_index + 1) * tok_rows],
                special[micro_index * spec_rows : (micro_index + 1) * spec_rows],
            ],
            0,
        ).astype(jnp.float32)
        ids_flat = ids_group[:, micro_index].reshape(-1)
        patch_ids = lax.dynamic_slice_in_dim(ids_flat, cycle_index * tok_rows, tok_rows)
        normed = norm_rows(tokens, gain_rows[0]).astype(jnp.bfloat16)
        projected = jnp.dot(normed, qkv_full, preferred_element_type=jnp.float32).astype(
            jnp.bfloat16
        )
        patch_q = projected[:tok_rows, :width]
        patch_k = projected[:tok_rows, width : 2 * width]
        patch_v = projected[:tok_rows, 2 * width :]
        spec_q = projected[tok_rows:, :width]
        spec_k = projected[tok_rows:, width : 2 * width]
        spec_v = projected[tok_rows:, 2 * width :]
        start_state = online(
            empty_state(tok_rows, head_count, width), patch_q, patch_ids, spec_k, spec_v, spec_ids
        )
        partial_value = start_state
        key_rows = lax.all_gather(patch_k, "blk", axis=0, tiled=True)
        value_rows = lax.all_gather(patch_v, "blk", axis=0, tiled=True)
        length = key_rows.shape[0]
        key_ids = ids_flat
        blocks = length // tok_rows

        def visit_block(running, block_item):
            return (
                online(running, patch_q, patch_ids, block_item[0], block_item[1], block_item[2]),
                None,
            )

        partial_value, unused = lax.scan(
            visit_block,
            partial_value,
            (
                key_rows.reshape(blocks, tok_rows, -1),
                value_rows.reshape(blocks, tok_rows, -1),
                key_ids.reshape(blocks, tok_rows),
            ),
        )
        spec_top, spec_total, spec_accum = online(
            empty_state(spec_rows, head_count, width), spec_q, spec_ids, patch_k, patch_v, patch_ids
        )
        spec_state = merged((spec_top, spec_total, spec_accum), "blk", combine)
        spec_state = online(spec_state, spec_q, spec_ids, spec_k, spec_v, spec_ids)
        patch_attn, patch_lse = finish(partial_value)
        spec_attn, spec_lse = finish(spec_state)
        attended = jnp.concatenate([patch_attn, spec_attn], 0)
        attended_low = attended.astype(jnp.bfloat16)
        branch = jnp.dot(attended_low, out_full, preferred_element_type=jnp.float32)
        middle = tokens + gain_rows[1] * branch
        normed_mlp = norm_rows(middle, gain_rows[2]).astype(jnp.bfloat16)
        hidden = jnp.dot(normed_mlp, up_full, preferred_element_type=jnp.float32)
        active = jax.nn.gelu(hidden, approximate=False).astype(jnp.bfloat16)
        mlp_out = jnp.dot(active, down_full, preferred_element_type=jnp.float32)
        final = middle + gain_rows[3] * mlp_out
        out_parts.append(final[:tok_rows].astype(jnp.bfloat16))
        spec_parts.append(final[tok_rows:].astype(jnp.bfloat16))
        upstream = jnp.concatenate(
            [
                cot_patches[micro_index * tok_rows : (micro_index + 1) * tok_rows],
                cot_special[micro_index * spec_rows : (micro_index + 1) * spec_rows],
            ],
            0,
        ).astype(jnp.float32)
        grad_mlp = (gain_rows[3] * upstream).astype(jnp.bfloat16)
        g_down = contract_rows(active, grad_mlp * row_weight_low)
        grad_active = jnp.einsum(
            "rd,fd->rf", grad_mlp, down_full, preferred_element_type=jnp.float32
        )
        unused_value, gelu_pull = jax.vjp(
            lambda pre_act: jax.nn.gelu(pre_act, approximate=False), hidden
        )
        grad_hidden = gelu_pull(grad_active)[0].astype(jnp.bfloat16)
        g_up = contract_rows(normed_mlp, grad_hidden * row_weight_low)
        grad_normed_mlp = jnp.einsum(
            "rf,df->rd", grad_hidden, up_full, preferred_element_type=jnp.float32
        )
        unused_value, norm_pull_mlp = jax.vjp(
            lambda rows_in: norm_rows(rows_in, gain_rows[2]), middle
        )
        grad_middle = upstream + norm_pull_mlp(grad_normed_mlp)[0]
        g_ln2 = jnp.sum(row_weight[:, None] * grad_normed_mlp * norm_rows(middle, 1.0), 0)
        g_ls2 = jnp.sum(row_weight[:, None] * upstream * mlp_out, 0)
        g_ls1 = jnp.sum(row_weight[:, None] * grad_middle * branch, 0)
        grad_branch = (gain_rows[1] * grad_middle).astype(jnp.bfloat16)
        g_out = contract_rows(attended_low, grad_branch * row_weight_low)
        grad_attended = jnp.einsum(
            "re,de->rd", grad_branch, out_full, preferred_element_type=jnp.float32
        ).astype(jnp.bfloat16)
        all_delta = row_delta_of(grad_attended, attended)
        patch_delta = all_delta[:, :tok_rows]
        spec_delta = all_delta[:, tok_rows:]
        patch_grad_attn = grad_attended[:tok_rows]
        spec_grad_attn = grad_attended[tok_rows:]
        grad_pq_first, grad_sk_part, grad_sv_part = block_grads(
            patch_q, patch_grad_attn, patch_lse, patch_delta, patch_ids, spec_k, spec_v, spec_ids
        )
        grad_sq_part, grad_pk_local, grad_pv_local = block_grads(
            spec_q, spec_grad_attn, spec_lse, spec_delta, spec_ids, patch_k, patch_v, patch_ids
        )
        sum_sq, sum_sk, sum_sv = (
            lax.psum(grad_sq_part.astype(jnp.bfloat16), "blk").astype(jnp.float32),
            lax.psum(grad_sk_part.astype(jnp.bfloat16), "blk").astype(jnp.float32),
            lax.psum(grad_sv_part.astype(jnp.bfloat16), "blk").astype(jnp.float32),
        )
        grad_sq_own, grad_sk_own, grad_sv_own = block_grads(
            spec_q, spec_grad_attn, spec_lse, spec_delta, spec_ids, spec_k, spec_v, spec_ids
        )

        def cycle_step(hop_index, carried):
            keys_now, values_now, grad_keys, grad_values, grad_queries = carried
            source = (cycle_index - hop_index) % cycle_size
            key_ids = lax.dynamic_slice_in_dim(ids_flat, source * tok_rows, tok_rows)
            term_q, term_k, term_v = block_grads(
                patch_q,
                patch_grad_attn,
                patch_lse,
                patch_delta,
                patch_ids,
                keys_now,
                values_now,
                key_ids,
            )
            keys_now, values_now = from_behind((keys_now, values_now), "blk", 1)
            grad_keys, grad_values = (
                from_behind((grad_keys + term_k).astype(jnp.bfloat16), "blk", 1).astype(
                    jnp.float32
                ),
                from_behind((grad_values + term_v).astype(jnp.bfloat16), "blk", 1).astype(
                    jnp.float32
                ),
            )
            return (keys_now, values_now, grad_keys, grad_values, grad_queries + term_q)

        zero_rows = jnp.zeros((tok_rows, width), jnp.float32)
        unused_keys, unused_values, grad_pk, grad_pv, grad_pq = lax.fori_loop(
            0, cycle_size, cycle_step, (patch_k, patch_v, zero_rows, zero_rows, grad_pq_first)
        )
        grad_pk = grad_pk + grad_pk_local
        grad_pv = grad_pv + grad_pv_local
        grad_patch_qkv = jnp.concatenate([grad_pq, grad_pk, grad_pv], 1)
        grad_spec_qkv = jnp.concatenate(
            [sum_sq + grad_sq_own, sum_sk + grad_sk_own, sum_sv + grad_sv_own], 1
        )
        grad_projected = jnp.concatenate([grad_patch_qkv, grad_spec_qkv], 0).astype(jnp.bfloat16)
        g_qkv = contract_rows(normed, grad_projected * row_weight_low)
        grad_normed = jnp.einsum(
            "re,de->rd", grad_projected, qkv_full, preferred_element_type=jnp.float32
        )
        unused_value, norm_pull_attn = jax.vjp(
            lambda rows_in: norm_rows(rows_in, gain_rows[0]), tokens
        )
        grad_tokens = grad_middle + norm_pull_attn(grad_normed)[0]
        g_ln1 = jnp.sum(row_weight[:, None] * grad_normed * norm_rows(tokens, 1.0), 0)
        grad_parts.append(grad_tokens[:tok_rows])
        grad_spec_parts.append(grad_tokens[tok_rows:])
        grad_terms = (g_qkv, g_out, g_up, g_down, jnp.stack([g_ln1, g_ls1, g_ln2, g_ls2], 0))
        summed_terms = (
            grad_terms
            if summed_terms is None
            else tuple((held + extra for held, extra in zip(summed_terms, grad_terms)))
        )
    shard_terms = reduce_grads(summed_terms)
    return (
        jnp.concatenate(out_parts, 0),
        jnp.concatenate(spec_parts, 0),
        jnp.concatenate(grad_parts, 0),
        jnp.concatenate(grad_spec_parts, 0),
        shard_terms[0],
        shard_terms[1],
        shard_terms[2],
        shard_terms[3],
        shard_terms[4],
    )


PAD_ID = 99
PLAN = (
    (9.0, ()), (0, (0,)), (0, ()), (0, (2, 0)), (21.0, ()), (0, ()), (0, ()), (0, ()), (0, (0,)), (0, ()),
    (0, ()), (0, (8,)), (0, ()), (0, (1,)), (0, (5, 9, 11)), (0, (7, 3)), (0, ()), (0, (10, 15, 16)),
    (0, ()), (36.0, (12,)), (0, ()), (2.4, (13,)), (0, (9,)), (0, (17,)), (0, (21,)), (0, (21,)), (0, ()),
    (4.8, (11,)), (0, (27,)), (0, (27,)), (0.001, ()), (0.001, ()), (1.11, (20,)), (0, ()), (2.7, ()),
    (0, ()), (0.002, (17, 28)), (0, ()), (0.6, ()), (0, (34,)), (0.6, ()), (0, ()), (0.07, ()), (0, ()),
    (0.27, ()), (0, ()), (0.4, (44,)), (0, ()), (21.0, ()), (0, ()), (7.0, (32,)), (0, (45,)), (0.42, ()),
    (0, (43, 45)), (1.05, ()), (0, ()), (0.0325, ()), (0, ()), (0.18, ()), (0, (56,)), (0.105, (58,)),
    (0, ()), (0, ()), (0, (47,)), (2.1, ()), (0, ()), (2.1, ()), (0, ()), (2.1, ()), (0.35, (59,)), (0, ()),
    (0, ()), (0, (55, 65)), (1.5, (64, 72)), (9.0, (68,)), (0, ()), (0, ()), (0, (70,)), (0.001, ()),
    (30, ()),
)
STEPS = []


def plan():
    us, steps = PLAN[len(STEPS)]
    return us, [STEPS[i] for i in steps]


def mm(a, b):
    return jnp.dot(a, b, preferred_element_type=F32)


def mm_nt(a, b):
    return lax.dot_general(a, b, (((1,), (1,)), ((), ())), preferred_element_type=F32)


def mm_tn(a, b):
    return lax.dot_general(a, b, (((0,), (0,)), ((), ())), preferred_element_type=F32)


def here():
    place = lax.axis_index("blk")
    group = lax.axis_index("dp")
    return place, place // 2, place % 2, group // 2, group % 2


def chunk_index(slot, z, y):
    return (z ^ (slot % 4)) * 2 + (y ^ (slot // 4))


def row_blocks(block, among=slice(0, 736)):
    return [slice(first, first + block) for first in range(among.start, among.stop, block)]


def fold(rows):
    return rows.reshape(rows.shape[0] // 8, 8, rows.shape[1]).sum(0)


class Keep:
    def __init__(self, value):
        self.value = value


class Far:
    def __init__(self, value):
        self.value = value


class Load:
    def __init__(self, buffer, copy):
        self.buffer, self.copy, self.waited = buffer, copy, False

    def ready(self):
        if not self.waited:
            self.copy.wait()
            self.waited = True
        return self.buffer


def call(kernel, outs, ins, scratch=(), limit=20):
    us, after = plan()
    far = [i for i, v in enumerate(ins) if isinstance(v, Far)]
    plain = [v.value if isinstance(v, (Far, Keep)) else v for v in ins]
    near, away = pl.BlockSpec(memory_space=pltpu.VMEM), pl.BlockSpec(memory_space=pltpu.HBM)
    room = [pltpu.VMEM(plain[i].shape, plain[i].dtype) for i in far]
    if far:
        room.append(pltpu.SemaphoreType.DMA((len(far),)))

    def body(*refs):
        given = [*refs[: len(ins)], *refs[len(ins) + len(after) :]]
        own = given[len(ins) + len(outs) + len(scratch) :]
        given = given[: len(ins) + len(outs) + len(scratch)]
        for k, i in enumerate(far):
            copy = pltpu.make_async_copy(given[i], own[k], own[-1].at[k])
            copy.start()
            given[i] = Load(own[k], copy)
        kernel(*given)

    def placed(v):
        if isinstance(v, Keep):
            return pltpu.with_memory_space_constraint(v.value, pltpu.VMEM)
        return pltpu.with_memory_space_constraint(v.value, pltpu.HBM) if isinstance(v, Far) else v

    made_arrays = pl.pallas_call(
        body,
        out_shape=tuple(
            pltpu.VMEM(v.value.shape, v.value.dtype) if isinstance(v, Keep) else v for v in outs
        ),
        in_specs=[away if i in far else near for i in range(len(ins))]
        + [pl.BlockSpec(memory_space=pl.ANY)] * len(after),
        out_specs=tuple(near for _ in outs),
        scratch_shapes=[*scratch, *room],
        compiler_params=pltpu.CompilerParams(vmem_limit_bytes=limit * 2**20),
        cost_estimate=pl.CostEstimate(flops=int(us * 10**9), bytes_accessed=0, transcendentals=0),
        name=kernel.__name__,
    )(*[placed(v) for v in ins], *after)
    STEPS.append(made_arrays[0])
    return made_arrays


def keep(*arrays):
    return [Keep(v) for v in arrays]


def sds(*shape, dtype=BF16):
    return jax.ShapeDtypeStruct(shape, dtype)


def pick_pieces(w_qkv, w_up, gains, patches, cots, own, near, far, rows, held):
    place = here()[0]
    held[...] = jnp.zeros_like(held)
    up = w_up.ready()[...].astype(F32)
    qkv = w_qkv.ready()[...].astype(F32)
    gain = gains.ready()[...].astype(F32)
    for b in range(4):
        for d in range(8):
            held[b, 0:24, d * 96 : d * 96 + 96] = up[:, d * 384 + b * 96 : d * 384 + b * 96 + 96]
        for part in range(3):
            held[b, 24:48, part * 192 : part * 192 + 192] = qkv[
                :, part * 768 + b * 192 : part * 768 + b * 192 + 192
            ]
        held[b, 24:28, 576:600] = gain
    own[...] = held[place].astype(BF16)
    near[...] = held[place ^ 1].astype(BF16)
    far[0:48, :] = held[place ^ 2].astype(BF16)
    far[48:96, :] = held[place ^ 3].astype(BF16)
    rows[0:176, :] = patches.ready()[...]
    rows[176:352, :] = cots.ready()[...]


def join_pieces(own, near, far, near_far, w_out, w_down, pack, both, wide, pack_f, up_f):
    place = here()[0]
    pack_f[96:112, :] = jnp.zeros((16, 768), F32)
    pieces = (
        own[...].astype(F32),
        near[...].astype(F32),
        far[0:48, :].astype(F32),
        near_far[48:96, :].astype(F32),
    )
    for k, piece in enumerate(pieces):
        source = place ^ k
        at = pl.ds(pl.multiple_of(source * 24, 8), 24)
        up_f[at, :] = piece[0:24]
        pack_f[at, 0:576] = piece[24:48, 0:576]
        lanes = pl.ds(pl.multiple_of(source * 128, 128), 128)
        pack_f[96:104, lanes] = piece[24:32, 576:704]
    out = w_out[...].astype(F32)
    for i in range(4):
        pack_f[i * 24 : i * 24 + 24, 576:768] = out[:, i * 192 : i * 192 + 192]
    pack[...] = pack_f[...].astype(BF16)
    both[0:96, :] = up_f[...].astype(BF16)
    both[96:192, :] = w_down[...]
    wide[0:112, :] = pack[...]
    wide[112:304, :] = both[...]


def open_pack(*refs):
    chunks, (w_qkv, w_out, gain_rows, out_f, gain_f) = refs[:8], refs[8:]
    _, _, _, z, y = here()
    for slot, chunk in enumerate(chunks):
        d = chunk_index(slot, z, y)
        w_qkv[pl.ds(pl.multiple_of(d * 96, 96), 96), :] = chunk[0:96, 0:576]
        tail = chunk[0:96, 576:768].astype(F32)
        for i in range(4):
            out_f[pl.ds(pl.multiple_of(d * 24, 8), 24), i * 192 : i * 192 + 192] = tail[
                i * 24 : i * 24 + 24
            ]
        gain_f[d] = chunk[96:112, :].astype(F32)
    w_out[...] = out_f[...].astype(BF16)
    gain_rows[...] = jnp.zeros_like(gain_rows)
    for d in range(8):
        for b in range(4):
            at = (d * 4 + b) * 24
            gain_rows[0:4, at : at + 24] = gain_f[d, 0:4, b * 128 : b * 128 + 24]


def normalise(rows):
    centre = rows - jnp.mean(rows, -1, keepdims=True)
    spread = jnp.mean(centre * centre, -1, keepdims=True)
    scale = lax.rsqrt(spread + EPSILON)
    return centre * scale, scale


def place_rows(scratch, blocks, tail, first):
    place = here()[0]
    for k, block in enumerate(blocks):
        rows = block[first : first + 176, :].astype(F32)
        source = place ^ k
        for m in range(MICRO):
            scratch[pl.ds(pl.multiple_of(m * 368 + source * 88, 8), 88), :] = rows[m * 88 : m * 88 + 88]
    rows = tail[...].astype(F32)
    for m in range(MICRO):
        scratch[m * 368 + 352 : m * 368 + 368, :] = jnp.zeros((16, 768), F32)
        scratch[m * 368 + 352 : m * 368 + 362, :] = rows[m * 10 : m * 10 + 10]


def turned(line):
    count = max(line.shape)
    down = lax.broadcasted_iota(jnp.int32, (count, count), 0)
    across = lax.broadcasted_iota(jnp.int32, (count, count), 1)
    return jnp.sum(jnp.where(down == across, line, 0.0), line.shape.index(count), keepdims=True)


def attend(
    rows_0, rows_1, rows_2, rows_3, tail, ids, w_qkv, gain_rows,
    attended, projected, probs, tokens, unit_low, rows_f,
):
    place_rows(rows_f, (rows_0, rows_1, rows_2, rows_3), tail, 0)
    gain = gain_rows[0:1, :]
    slot = lax.broadcasted_iota(jnp.int32, (1, 16), 1)
    tail_ids = jnp.where(slot < 2 * SPECIAL, (slot >= SPECIAL).astype(jnp.int32), PAD_ID)
    for m in range(MICRO):
        at = slice(m * 368, m * 368 + 368)
        row = jnp.concatenate([ids[b * 2 + m : b * 2 + m + 1, :] for b in range(4)] + [tail_ids], 1)
        row = row.astype(F32)
        bias = jnp.where(turned(row) == row, 0.0, MASKED)
        normed = []
        for block in row_blocks(16, at):
            rows = rows_f[block, :]
            tokens[block, :] = rows.astype(BF16)
            unit = normalise(rows)[0]
            unit_low[block, :] = unit.astype(BF16)
            normed.append((unit * gain).astype(BF16))
        qkv = mm(jnp.concatenate(normed, 0), w_qkv[...])
        qkv = jnp.concatenate([qkv[:, 0:192] * SCORE_SCALE, qkv[:, 192:576]], -1).astype(BF16)
        projected[at, :] = qkv
        heads = []
        for h in range(3):
            q = qkv[:, h * 64 : h * 64 + 64]
            k = qkv[:, 192 + h * 64 : 192 + h * 64 + 64]
            v = qkv[:, 384 + h * 64 : 384 + h * 64 + 64]
            scores = mm_nt(q, k) + bias
            weights = jnp.exp(scores - jnp.max(scores, -1, keepdims=True))
            weights = weights * (1.0 / jnp.sum(weights, -1, keepdims=True))
            weights = weights.astype(BF16)
            probs[m * 3 + h] = weights
            heads.append(mm(weights, v))
        attended[at, :] = jnp.concatenate(heads, -1).astype(BF16)


def order_out(
    out_0, out_1, out_2, out_3, rows_0, rows_1, rows_2, rows_3, cot_tail, gain_rows,
    ordered, mine, grad_mlp, cots, out_f,
):
    place = here()[0]
    for k, part in enumerate((out_0, out_1, out_2, out_3)):
        source = place ^ k
        rows = part[...].astype(F32)
        for d in range(8):
            at = pl.multiple_of((d * 4 + source) * 24, 8)
            out_f[pl.ds(at, 24), :] = rows[d * 24 : d * 24 + 24]
    ordered[...] = out_f[...].astype(BF16)
    mine[...] = out_f[pl.ds(pl.multiple_of(place * 192, 8), 192), :].astype(BF16)
    place_rows(out_f, (rows_0, rows_1, rows_2, rows_3), cot_tail, 176)
    gain = gain_rows[3:4, :]
    for at in row_blocks(32):
        rows = out_f[at, :]
        cots[at, :] = rows.astype(BF16)
        grad_mlp[at, :] = (gain * rows).astype(BF16)


def branch_rows(
    head_0, head_1, head_2, head_3, w_out, tokens, gain_rows, normed, branch, own_rows, rows_f
):
    place = here()[0]
    gain_s, gain_n = gain_rows[1:2, :], gain_rows[2:3, :]
    for m in range(MICRO):
        group = slice(m * 368, m * 368 + 368)
        total = None
        for k, part in enumerate((head_0, head_1, head_2, head_3)):
            rows = w_out[pl.ds(pl.multiple_of((place ^ k) * 192, 16), 192), :]
            term = mm(part[group, :], rows)
            total = term if total is None else total + term
        rows_f[group, :] = total
        for at in row_blocks(16, group):
            a = rows_f[at, :]
            branch[at, :] = a.astype(BF16)
            rows = tokens[at, :].astype(F32) + gain_s * a
            rows_f[at, :] = rows
            normed[at, :] = (normalise(rows)[0] * gain_n).astype(BF16)
        for part, first in ((0, place * 88), (88, 352)):
            rows = 88 if part == 0 else 16
            own_rows[m * 104 + part : m * 104 + part + rows, :] = rows_f[
                pl.ds(pl.multiple_of(m * 368 + first, 8), rows), :
            ]


def raise_rows(*refs):
    normed, chunks = refs[0], refs[1:9]
    active, slope, w_up, w_down, rows_f = refs[9:]
    _, _, _, z, y = here()
    for slot, chunk in enumerate(chunks):
        d = chunk_index(slot, z, y)
        skip = chunk.shape[0] - 192
        w_up[pl.ds(pl.multiple_of(d * 96, 96), 96), :] = chunk[skip : skip + 96, :]
        w_down[pl.ds(pl.multiple_of(d * 96, 96), 96), :] = chunk[skip + 96 : skip + 192, :]
    for m in range(MICRO):
        at = slice(m * 368, m * 368 + 368)
        rows_f[at, :] = mm(normed[at, :], w_up[...])
    for at in row_blocks(32):
        u = rows_f[at, :]
        half = 0.5 + 0.5 * lax.erf(u * 0.7071067811865476)
        active[at, :] = (u * half).astype(BF16)
        slope[at, :] = half + u * (0.3989422804014327 * jnp.exp(-0.5 * u * u))


def down_grads(active, grad_mlp, away, kept, work):
    _, _, _, z, _ = here()
    work[...] = mm_tn(active[...], grad_mlp[...])
    for pair in range(2):
        for side in range(2):
            ours = pl.multiple_of(((z ^ (2 * pair)) * 2 + side) * 96, 8)
            theirs = pl.multiple_of(((z ^ (2 * pair + 1)) * 2 + side) * 96, 8)
            kept[pair * 2 + side] = work[pl.ds(ours, 96), :]
            away[pair * 2 + side] = work[pl.ds(theirs, 96), :].astype(BF16)


def sum_fours(kept, came, own, away):
    own[...] = kept[0:2] + came[0:2].astype(F32)
    away[...] = (kept[2:4] + came[2:4].astype(F32)).astype(BF16)


def sum_sides(kept, came, own, away):
    y = here()[4]
    own[...] = kept[y] + came[y].astype(F32)
    away[...] = (kept[1 - y] + came[1 - y].astype(F32)).astype(BF16)


def lower_rows(slope, grad_mlp, w_up, w_down, away, kept, grad_hidden, work):
    core = here()[2]
    for m in range(MICRO):
        at = slice(m * 368, m * 368 + 368)
        grad = mm_nt(grad_mlp[at, :], w_down[...])
        grad_hidden[at, :] = (slope[at, :] * grad).astype(BF16)
        work[m] = mm_nt(grad_hidden[at, :], w_up[...])
    away[...] = work[1 - core].astype(BF16)
    kept[...] = work[core]


def split_rows(pieces, place, away, kept):
    away[0:208, :] = pieces[place ^ 1].astype(BF16)
    away[208:416, :] = pieces[place ^ 3].astype(BF16)
    kept[0:208, :] = pieces[place]
    kept[208:416, :] = pieces[place ^ 2]


def cut_rows(rows_f, pieces):
    for b in range(4):
        for m in range(MICRO):
            pieces[b, m * 104 : m * 104 + 88, :] = rows_f[m * 368 + b * 88 : m * 368 + b * 88 + 88, :]
            pieces[b, m * 104 + 88 : m * 104 + 104, :] = rows_f[m * 368 + 352 : m * 368 + 368, :]


def halve(grad_f, y, away, kept, rows):
    for zz in range(4):
        other = pl.ds(pl.multiple_of((zz * 2 + 1 - y) * rows, 8), rows)
        ours = pl.ds(pl.multiple_of((zz * 2 + y) * rows, 8), rows)
        away[zz] = grad_f[other, 0 : away.shape[2]].astype(BF16)
        kept[zz] = grad_f[ours, 0 : away.shape[2]]


def up_grads(normed, grad_hidden, away, kept, work):
    y = here()[4]
    work[...] = mm_tn(normed[...], grad_hidden[...])
    halve(work, y, away, kept, 96)


def mlp_rows(
    active, w_down, cots, head_0, head_1, head_2, head_3,
    rows_away, rows_kept, scale_grad, chosen, work, pieces,
):
    place = here()[0]
    for m in range(MICRO):
        at = slice(m * 368, m * 368 + 368)
        work[at, :] = mm(active[at, :], w_down[...])
    total = jnp.zeros((8, 768), F32)
    for at in row_blocks(32):
        total = total + fold(cots[at, :].astype(F32) * work[at, :])
    scale_grad[...] = total
    cut_rows(work, pieces)
    split_rows(pieces, place, rows_away, rows_kept)
    picked = None
    column = lax.broadcasted_iota(jnp.int32, (192, 192), 1)
    chunk = sum((column >= 24 * d).astype(jnp.int32) for d in range(1, 8))
    targets = column + chunk * 72 + place * 24
    for k, part in enumerate((head_0, head_1, head_2, head_3)):
        index = lax.broadcasted_iota(jnp.int32, (192, 192), 0) + (place ^ k) * 192
        pick = jnp.where(index == targets, 1.0, 0.0).astype(BF16)
        term = mm(part[...], pick)
        picked = term if picked is None else picked + term
    chosen[...] = picked.astype(BF16)


def add_rows(kept, came, total):
    total[...] = (kept[...] + came[...].astype(F32)).astype(BF16)


def add_pair(here_rows, came, total):
    total[...] = (here_rows[...].astype(F32) + came[...].astype(F32)).astype(BF16)


def branch_back(
    sum_own, sum_near, tokens, cots, branch, gain_rows, w_mine, probs, normed, scale_grad_mlp, chosen,
    grad_rows, grad_heads, grad_v, away, kept,
    work, grad_branch, grad_mid, extra, early,
):
    place, _, core, _, y = here()
    for m in range(MICRO):
        at = slice(m * 368, m * 368 + 368)

        @pl.when(core == m)
        def _():
            work[at, :] = sum_own[...].astype(F32)

        @pl.when(core != m)
        def _():
            work[at, :] = sum_near[...].astype(F32)

    gain_s, gain_n = gain_rows[1:2, :], gain_rows[2:3, :]
    scale_sum = jnp.zeros((8, 768), F32)
    for at in row_blocks(32):
        grown = branch[at, :].astype(F32)
        unit, scale = normalise(tokens[at, :].astype(F32) + gain_s * grown)
        pulled = work[at, :] * gain_n
        pulled = pulled - jnp.mean(pulled, -1, keepdims=True) - unit * jnp.mean(
            pulled * unit, -1, keepdims=True
        )
        through = cots[at, :].astype(F32) + scale * pulled
        grad_mid[at, :] = through
        grad_branch[at, :] = (gain_s * through).astype(BF16)
        scale_sum = scale_sum + fold(through * grown)
    for m in range(MICRO):
        for part, first in ((0, place * 88), (88, 352)):
            rows = 88 if part == 0 else 16
            grad_rows[m * 104 + part : m * 104 + part + rows, :] = grad_mid[
                pl.ds(pl.multiple_of(m * 368 + first, 8), rows), :
            ]
    for m in range(MICRO):
        at = slice(m * 368, m * 368 + 368)
        heads = mm_nt(grad_branch[at, :], w_mine[...]).astype(BF16)
        grad_heads[at, :] = heads
        terms = [mm_tn(probs[m * 3 + h], heads[:, h * 64 : h * 64 + 64]) for h in range(3)]
        grad_v[at, :] = jnp.concatenate(terms, -1).astype(BF16)
    grad_mid[0:768, 0:192] = mm_tn(normed[...], grad_v[...])
    extra[...] = mm_tn(chosen[...], grad_branch[...])
    scale_rows = (
        0.25 * jnp.sum(scale_sum, 0, keepdims=True),
        jnp.sum(scale_grad_mlp[...], 0, keepdims=True),
    )
    for d in range(8):
        base = d * 112
        early[base : base + 96, 0:192] = grad_mid[d * 96 : d * 96 + 96, 0:192]
        for i in range(4):
            early[base + i * 24 : base + i * 24 + 24, 192:384] = extra[
                d * 24 : d * 24 + 24, i * 192 : i * 192 + 192
            ]
        early[base + 96 : base + 112, :] = jnp.zeros((16, 384), F32)
        for i in range(2):
            early[base + 96 + i : base + 97 + i, 0:96] = scale_rows[i][:, d * 96 : d * 96 + 96]
    halve(early, y, away, kept, 112)


def score_back(probs, projected, grad_heads, normed, grad_qk, away, kept, work):
    _, _, _, _, y = here()
    for m in range(MICRO):
        at = slice(m * 368, m * 368 + 368)
        qkv = projected[at, :]
        g_heads = grad_heads[at, :]
        grads = [[], []]
        for h in range(3):
            q = qkv[:, h * 64 : h * 64 + 64]
            k = qkv[:, 192 + h * 64 : 192 + h * 64 + 64]
            v = qkv[:, 384 + h * 64 : 384 + h * 64 + 64]
            grad_prob = mm_nt(g_heads[:, h * 64 : h * 64 + 64], v)
            wide = probs[m * 3 + h].astype(F32)
            moved = wide * grad_prob
            delta = jnp.sum(moved, -1, keepdims=True)
            grad_score = (moved - wide * delta).astype(BF16)
            grads[0].append(mm(grad_score, k) * SCORE_SCALE)
            grads[1].append(mm_tn(q, grad_score))
        grad_qk[at, 0:192] = jnp.concatenate(grads[0], -1).astype(BF16)
        grad_qk[at, 192:384] = jnp.concatenate(grads[1], 0).T.astype(BF16)
    work[...] = mm_tn(normed[...], grad_qk[...])
    halve(work, y, away, kept, 96)


def project_back(grad_qk, grad_v, w_qkv, rows_away, rows_kept, work, pieces):
    place = here()[0]
    for m in range(MICRO):
        at = slice(m * 368, m * 368 + 368)
        work[at, :] = mm_nt(grad_qk[at, :], w_qkv[:, 0:384]) + mm_nt(grad_v[at, :], w_qkv[:, 384:576])
    cut_rows(work, pieces)
    split_rows(pieces, place, rows_away, rows_kept)


def sum_y(kept, came, own, send_1, send_2, send_3):
    _, _, _, z, _ = here()
    own[...] = kept[z] + came[z].astype(F32)
    for k, send in ((1, send_1), (2, send_2), (3, send_3)):
        send[...] = (kept[z ^ k] + came[z ^ k].astype(F32)).astype(BF16)


def sum_y_pairs(kept, came, own, away):
    _, _, _, z, _ = here()
    for k in range(2):
        own[k] = kept[z ^ (2 * k)] + came[z ^ (2 * k)].astype(F32)
        there = z ^ (2 * k + 1)
        away[k] = (kept[there] + came[there].astype(F32)).astype(BF16)


def sum_pairs(kept, came, own, away):
    own[...] = kept[0] + came[0].astype(F32)
    away[...] = (kept[1] + came[1].astype(F32)).astype(BF16)


def sum_last(own, came, total):
    total[...] = own[...] + came[...].astype(F32)


def add_pieces(kept_m, came_m, kept_h, came_h, stay, go):
    for i, (kept, came) in enumerate(((kept_m, came_m), (kept_h, came_h))):
        stay[i * 208 : i * 208 + 208, :] = kept[0:208, :] + came[0:208, :].astype(F32)
        go[i * 208 : i * 208 + 208, :] = (kept[208:416, :] + came[208:416, :].astype(F32)).astype(BF16)


def finish_rows(
    stay, came, own_rows, grad_rows, patches, tail, gain_rows,
    out_patches, out_special, grad_patches, grad_special,
):
    own = patches[...].astype(F32)
    rest = tail[...].astype(F32)
    outs, out_tails = [], []
    for m in range(MICRO):
        for part, count in ((0, 88), (88, 10)):
            at = slice(m * 104 + part, m * 104 + part + count)
            far_at = slice(208 + m * 104 + part, 208 + m * 104 + part + count)
            final = own_rows[at, :] + gain_rows[3:4, :] * (stay[at, :] + came[at, :].astype(F32))
            (outs if part == 0 else out_tails).append(final)
            rows = own[m * 88 : m * 88 + 88] if part == 0 else rest[m * 10 : m * 10 + 10]
            unit, scale = normalise(rows)
            pulled = gain_rows[0:1, :] * (stay[far_at, :] + came[far_at, :].astype(F32))
            pulled = pulled - jnp.mean(pulled, -1, keepdims=True) - unit * jnp.mean(
                pulled * unit, -1, keepdims=True
            )
            grad = grad_rows[at, :] + scale * pulled
            if part == 0:
                grad_patches[m * 88 : m * 88 + 88, :] = grad
            else:
                grad_special[m * 10 : m * 10 + 10, :] = grad
    out_patches[...] = jnp.concatenate(outs, 0).astype(BF16)
    out_special[...] = jnp.concatenate(out_tails, 0).astype(BF16)


def hand_out(held, own, near, far):
    place = here()[0]
    own[...] = held[place]
    near[...] = held[place ^ 1].astype(BF16)
    far[0:32, :] = held[place ^ 2].astype(BF16)
    far[32:64, :] = held[place ^ 3].astype(BF16)


def take_in(held, own, near, far, near_far):
    place = here()[0]
    held[place] = own[...]
    held[place ^ 1] = near[...].astype(F32)
    held[place ^ 2] = far[0:32, :].astype(F32)
    held[place ^ 3] = near_far[32:64, :].astype(F32)


def pick_up(kept, came, own, near, far, held):
    held[...] = jnp.zeros_like(held)
    for b in range(4):
        at = slice(b * 24, b * 24 + 24)
        held[b, 0:24, :] = kept[at, :] + came[at, :].astype(F32)
    hand_out(held, own, near, far)


def pick_attention(kept_a, came_a, kept_b, came_1, came_2, came_3, own, near, far, grad_out, held, sums):
    held[...] = jnp.zeros_like(held)
    sums[:, 0:384] = kept_a[...] + came_a[...].astype(F32)
    sums[0:96, 384:768] = (
        kept_b[...] + came_1[...].astype(F32) + came_2[...].astype(F32) + came_3[...].astype(F32)
    )
    for b in range(4):
        at = slice(b * 24, b * 24 + 24)
        held[b, 0:24, 0:384] = sums[at, 384:768]
        held[b, 0:24, 384:576] = sums[at, 0:192]
        held[b, 0:2, 576:600] = sums[96:98, at]
        grad_out[:, b * 192 : b * 192 + 192] = sums[at, 192:384]
    hand_out(held, own, near, far)


def join_up(own, near, far, near_far, w_up, gains, grad_up, norm_grad, held):
    take_in(held, own, near, far, near_far)
    for b in range(4):
        for d in range(8):
            at = d * 384 + b * 96
            grad_up[:, at : at + 96] = held[b, 0:24, d * 96 : d * 96 + 96]
    total = turned(jnp.sum(w_up[...].astype(F32) * grad_up[...], -1, keepdims=True))
    norm_grad[...] = total / gains[2:3, :].astype(F32)


def join_attention(
    own, near, far, near_far, w_qkv, gains, norm_grad, grad_qkv, grad_gains, held
):
    take_in(held, own, near, far, near_far)
    scales = None
    for b in range(4):
        for part in range(3):
            at = slice(part * 768 + b * 192, part * 768 + b * 192 + 192)
            grad_qkv[:, at] = held[b, 0:24, part * 192 : part * 192 + 192]
        term = held[b, 0:2, 576:600]
        scales = term if scales is None else scales + term
    plain = grad_qkv[...]
    grad_gains[0:1, :] = turned(jnp.sum(w_qkv[...].astype(F32) * plain, -1, keepdims=True))
    grad_gains[1:2, :] = scales[0:1, :]
    grad_gains[2:3, :] = norm_grad[...]
    grad_gains[3:4, :] = scales[1:2, :]
    grad_qkv[...] = plain * turned(gains[0:1, :].astype(F32))


def send(rows, axis, step):
    pairs = []
    for group in range(8):
        z, y = group // 2, group % 2
        for place in range(4):
            target = {
                "core": (group, place ^ 1),
                "x": (group, place ^ 2),
                "y": (z * 2 + 1 - y, place),
                "z": ((z ^ step) * 2 + y, place),
            }[axis]
            pairs.append((group * 4 + place, target[0] * 4 + target[1]))
    _, ready = plan()
    if ready:
        rows = lax.optimization_barrier((rows, *ready))[0]
    STEPS.append(lax.ppermute(rows, ("dp", "blk"), pairs))
    return STEPS[-1]


def add_y(kept, came):
    rows, width = kept.shape[1:]
    own, *parts = call(
        sum_y,
        [Keep(sds(rows, width, dtype=F32))] + [sds(rows, width)] * 3,
        [Keep(kept), came],
    )
    return [own, *[send(part, "z", k) for k, part in zip((1, 2, 3), parts)]]


def halve_y(kept, came):
    rows, width = kept.shape[1:]
    own, away = call(
        sum_y_pairs,
        [Keep(sds(2, rows, width, dtype=F32)), sds(2, rows, width)],
        [Keep(kept), came],
    )
    return own, send(away, "z", 1)


def halve_z(pair):
    kept, came = pair
    rows, width = kept.shape[1:]
    own, away = call(
        sum_pairs,
        [Keep(sds(rows, width, dtype=F32)), sds(rows, width)],
        [Keep(kept), came],
    )
    return own, send(away, "z", 2)


def side_y(kept, came):
    own, away = call(
        sum_sides,
        [Keep(sds(96, 768, dtype=F32)), sds(96, 768)],
        [Keep(kept), came],
    )
    return own, send(away, "y", 1)


def add_last(last):
    own, came = last
    return call(
        sum_last, [sds(*own.shape, dtype=F32)], [Keep(own), came]
    )[0]


def on_device_split(
    patches, special, image_ids, w_qkv, w_out, w_up, w_down, gains, cot_patches, cot_special
):
    STEPS.clear()
    own, near, far, rows = call(
        pick_pieces,
        [sds(48, 768), sds(48, 768), sds(96, 768), sds(352, 768)],
        [Far(w_qkv), Far(w_up), Far(gains), Far(patches), Far(cot_patches)],
        [pltpu.VMEM((4, 48, 768), F32)],
    )
    came_far = send(far, "x", 1)
    came_near, came_near_far = send(near, "core", 1), send(came_far, "core", 1)
    pack, both, wide = call(
        join_pieces,
        [sds(112, 768), sds(192, 768), sds(304, 768)],
        [own, came_near, came_far, came_near_far, w_out, w_down],
        [pltpu.VMEM((112, 768), F32), pltpu.VMEM((96, 768), F32)],
    )
    pack_2 = send(pack, "z", 2)
    pack_1 = send(pack, "z", 1)
    wide_y0 = send(wide, "y", 1)
    far_rows = send(rows, "x", 1)
    pack_y1 = send(pack_1, "y", 1)
    pack_3 = send(pack_2, "z", 1)
    pack_y2 = send(pack_2, "y", 1)
    both_2 = send(both, "z", 2)
    both_1 = send(both, "z", 1)
    near_rows = send(rows, "core", 1)
    row_parts = [rows, near_rows, far_rows, send(far_rows, "core", 1)]
    pack_y3 = send(pack_3, "y", 1)
    both_y1 = send(both_1, "y", 1)
    both_3 = send(both_2, "z", 1)
    qkv_full, out_part, gain_rows = call(
        open_pack,
        [Keep(sds(768, 576)), sds(192, 768), Keep(sds(8, 768, dtype=F32))],
        [pack, pack_1, pack_2, pack_3, wide_y0, pack_y1, pack_y2, pack_y3],
        [pltpu.VMEM((192, 768), F32), pltpu.VMEM((8, 16, 768), F32)],
    )
    far_out = send(out_part, "x", 1)
    attended, projected, probs, tokens, unit_low = call(
        attend,
        [sds(736, 192), *keep(sds(736, 576), sds(6, 368, 368), sds(736, 768), sds(736, 768))],
        [*row_parts, special, image_ids.reshape(8, 88), *keep(qkv_full, gain_rows)],
        [pltpu.VMEM((736, 768), F32)],
    )
    far_heads = send(attended, "x", 1)
    both_y2 = send(both_2, "y", 1)
    out_parts = [
        out_part, send(out_part, "core", 1),
        far_out, send(far_out, "core", 1),
    ]
    both_y3 = send(both_3, "y", 1)
    out_full, out_mine, grad_mlp, cots = call(
        order_out,
        keep(sds(768, 768), sds(192, 768), sds(736, 768), sds(736, 768)),
        [*out_parts, *row_parts, cot_special, Keep(gain_rows)],
        [pltpu.VMEM((768, 768), F32)],
    )
    heads = [
        attended, send(attended, "core", 1),
        far_heads, send(far_heads, "core", 1),
    ]
    both_chunks = [both, both_1, both_2, both_3, wide_y0, both_y1, both_y2, both_y3]
    normed_mlp, branch, own_rows = call(
        branch_rows,
        keep(sds(736, 768), sds(736, 768), sds(208, 768, dtype=F32)),
        [*heads, *keep(out_full, tokens, gain_rows)],
        [pltpu.VMEM((736, 768), F32)],
    )
    active, slope, up_full, down_full = call(
        raise_rows,
        keep(sds(736, 768), sds(736, 768, dtype=F32), sds(768, 768), sds(768, 768)),
        [Keep(normed_mlp), *both_chunks],
        [pltpu.VMEM((736, 768), F32)],
    )
    half = [sds(4, 96, 768), Keep(sds(4, 96, 768, dtype=F32))]
    rows_split = [sds(416, 768), Keep(sds(416, 768, dtype=F32))]

    def make_down(active):
        return call(
            down_grads,
            half,
            keep(active, grad_mlp),
            [pltpu.VMEM((768, 768), F32)],
        )

    sum_away, sum_kept, grad_hidden = call(
        lower_rows,
        [sds(368, 768), *keep(sds(368, 768, dtype=F32), sds(736, 768))],
        keep(slope, grad_mlp, up_full, down_full),
        [pltpu.VMEM((2, 368, 768), F32)],
    )
    sum_came = send(sum_away, "core", 1)
    chip_sum = call(add_rows, [sds(368, 768)], [Keep(sum_kept), sum_came])[0]
    chip_came = send(chip_sum, "x", 1)
    down_away, down_kept = make_down(active)
    down_came = send(down_away, "z", 1)
    up_away, up_kept = call(
        up_grads,
        half,
        keep(normed_mlp, grad_hidden),
        [pltpu.VMEM((768, 768), F32)],
    )
    up_came = send(up_away, "y", 1)
    m_away, m_kept, scale_mlp, chosen = call(
        mlp_rows,
        [*rows_split, *keep(sds(8, 768, dtype=F32), sds(736, 192))],
        [*keep(active, down_full, cots), *heads],
        [pltpu.VMEM((736, 768), F32), pltpu.VMEM((4, 208, 768), F32)],
    )
    m_came = send(m_away, "core", 1)
    down_two, down_away = call(
        sum_fours,
        [Keep(sds(2, 96, 768, dtype=F32)), sds(2, 96, 768)],
        [Keep(down_kept), down_came],
    )
    down_came = send(down_away, "z", 2)
    sum_own = call(add_pair, [sds(368, 768)], [chip_sum, chip_came])[0]
    sum_near = send(sum_own, "core", 1)
    grad_rows, grad_heads, grad_v, a_away, a_kept = call(
        branch_back,
        [
            *keep(sds(208, 768, dtype=F32), sds(736, 192), sds(736, 192)),
            sds(4, 112, 384), Keep(sds(4, 112, 384, dtype=F32)),
        ],
        [
            sum_own, sum_near, *keep(tokens, cots, branch, gain_rows, out_mine, probs, unit_low), *keep(scale_mlp, chosen),
        ],
        [
            pltpu.VMEM((736, 768), F32), pltpu.VMEM((736, 768), BF16),
            pltpu.VMEM((768, 768), F32), pltpu.VMEM((192, 768), F32), pltpu.VMEM((896, 384), F32),
        ],
    )
    a_came = send(a_away, "y", 1)
    up_steps = halve_y(up_kept, up_came)
    down_last = side_y(down_two, down_came)
    grad_qk, b_away, b_kept = call(
        score_back,
        [Keep(sds(736, 384)), sds(4, 96, 384), Keep(sds(4, 96, 384, dtype=F32))],
        keep(probs, projected, grad_heads, unit_low),
        [pltpu.VMEM((768, 384), F32)],
    )
    b_came = send(b_away, "y", 1)
    a_pair = halve_y(a_kept, a_came)
    h_away, h_kept = call(
        project_back,
        rows_split,
        keep(grad_qk, grad_v, qkv_full),
        [pltpu.VMEM((736, 768), F32), pltpu.VMEM((4, 208, 768), F32)],
    )
    h_came = send(h_away, "core", 1)
    stay, go = call(
        add_pieces,
        [Keep(sds(416, 768, dtype=F32)), sds(416, 768)],
        [Keep(m_kept), m_came, Keep(h_kept), h_came],
    )
    far_rows = send(go, "x", 1)
    b_steps = add_y(b_kept, b_came)
    a_last = halve_z(a_pair)
    up_last = halve_z(up_steps)
    grad_down = add_last(down_last)
    pieces = [Keep(sds(32, 768, dtype=F32)), sds(32, 768), sds(64, 768)]
    held = pltpu.VMEM((4, 32, 768), F32)
    own, near, far = call(pick_up, pieces, [Keep(up_last[0]), up_last[1]], [held])
    came_far = send(far, "x", 1)
    came_near, came_near_far = send(near, "core", 1), send(came_far, "core", 1)
    grad_up, norm_grad = call(
        join_up,
        [sds(24, 3072, dtype=F32), Keep(sds(1, 24, dtype=F32))],
        [Keep(own), came_near, came_far, came_near_far, w_up, gains],
        [held],
    )
    own, near, far, grad_out = call(
        pick_attention,
        [*pieces, sds(24, 768, dtype=F32)],
        [Keep(a_last[0]), a_last[1], Keep(b_steps[0]), *b_steps[1:]],
        [held, pltpu.VMEM((112, 768), F32)],
    )
    came_far = send(far, "x", 1)
    came_near, came_near_far = send(near, "core", 1), send(came_far, "core", 1)
    out_patches, out_special, grad_patches, grad_special = call(
        finish_rows,
        [
            sds(176, 768), sds(20, 768), sds(176, 768, dtype=F32), sds(20, 768, dtype=F32),
        ],
        [Keep(stay), far_rows, *keep(own_rows, grad_rows), patches, special, Keep(gain_rows)],
    )
    grad_qkv, grad_gains = call(
        join_attention,
        [sds(24, 2304, dtype=F32), sds(4, 24, dtype=F32)],
        [Keep(own), came_near, came_far, came_near_far, w_qkv, gains, Keep(norm_grad)],
        [held],
    )
    return (
        out_patches, out_special, grad_patches, grad_special,
        grad_qkv, grad_out, grad_up, grad_down, grad_gains,
    )


def solution(mesh):
    placed = (
        P(("dp", "blk"), None),
        P("dp", None),
        P("dp"),
        P(("dp", "blk"), None),
        P(("dp", "blk"), None),
        P(("dp", "blk"), None),
        P(("dp", "blk"), None),
        P(None, ("dp", "blk")),
        P(("dp", "blk"), None),
        P("dp", None),
    )
    whole = dict(mesh.shape) != {"dp": 8, "blk": 4}
    return jax.shard_map(
        on_device if whole else on_device_split,
        mesh=mesh,
        in_specs=placed,
        out_specs=(
            P(("dp", "blk"), None),
            P("dp", None),
            P(("dp", "blk"), None),
            P("dp", None),
            P(("dp", "blk"), None),
            P(("dp", "blk"), None),
            P(("dp", "blk"), None),
            P(("dp", "blk"), None),
            P(None, ("dp", "blk")),
        ),
        check_vma=False,
    )
```

```python
import jax
import jax.numpy as jnp
from jax import lax
from jax.experimental import pallas as pl
from jax.experimental.pallas import tpu as pltpu
from jax.sharding import PartitionSpec as P

HEAD_DIM = 64
SPECIAL = 5
MICRO = 2
TOK_MB = 88

SCORE_SCALE = 0.125
MASKED = -1e30
EPSILON = 1e-06

BF16 = jnp.bfloat16
F32 = jnp.float32


def merged(shard, axis, combine):
    everything = jax.tree.map(
        lambda part, kind: lax.all_gather(part.astype(kind), axis),
        shard,
        (jnp.bfloat16, jnp.bfloat16, jnp.bfloat16),
    )

    def take(k):
        return jax.tree.map(lambda part, own: part[k].astype(own.dtype), everything, shard)

    return lax.fori_loop(
        1, lax.axis_size(axis), lambda k, so_far: combine(so_far, take(k)), take(0)
    )


def from_behind(shard, axis, by):
    peers = lax.axis_size(axis)
    return lax.ppermute(shard, axis, [(i, (i + by) % peers) for i in range(peers)])


def norm_rows(values, gain_row):
    centre = values - jnp.mean(values, -1, keepdims=True)
    spread = jnp.mean(centre * centre, -1, keepdims=True)
    return centre * lax.rsqrt(spread + EPSILON) * gain_row


def split_heads(matrix):
    return matrix.reshape(matrix.shape[0], -1, HEAD_DIM)


def widen(per_head):
    return jnp.repeat(per_head.T, HEAD_DIM, axis=1)


def empty_state(length, head_count, feature_width):
    return (
        jnp.full((head_count, length), MASKED, jnp.float32),
        jnp.zeros((head_count, length), jnp.float32),
        jnp.zeros((length, feature_width), jnp.float32),
    )


def online(carried, queries, query_ids, key_rows, value_rows, key_ids):
    top_score, totals, accumulated = carried
    same_image = (query_ids[:, None] == key_ids[None, :])[None]
    scores = (
        jnp.einsum(
            "qhd,khd->hqk",
            split_heads(queries),
            split_heads(key_rows),
            preferred_element_type=jnp.float32,
        )
        * SCORE_SCALE
    )
    scores = jnp.where(same_image, scores, MASKED)
    new_top = jnp.maximum(top_score, jnp.max(scores, -1))
    weights = jnp.where(same_image, jnp.exp(scores - new_top[..., None]), 0.0)
    factor = jnp.exp(top_score - new_top)
    totals = totals * factor + jnp.sum(weights, -1)
    mixture = jnp.einsum(
        "hqk,khd->qhd",
        weights.astype(jnp.bfloat16),
        split_heads(value_rows),
        preferred_element_type=jnp.float32,
    )
    accumulated = accumulated * widen(factor) + mixture.reshape(accumulated.shape)
    return (new_top, totals, accumulated)


def combine(former, latter):
    highest = jnp.maximum(former[0], latter[0])
    scale_former = jnp.exp(former[0] - highest)
    scale_latter = jnp.exp(latter[0] - highest)
    return (
        highest,
        former[1] * scale_former + latter[1] * scale_latter,
        former[2] * widen(scale_former) + latter[2] * widen(scale_latter),
    )


def finish(carried):
    top_score, totals, accumulated = carried
    return (accumulated / widen(totals), top_score + jnp.log(totals))


def block_grads(queries, grad_attn, log_total, row_delta, query_ids, key_rows, value_rows, key_ids):
    same_image = (query_ids[:, None] == key_ids[None, :])[None]
    q_heads = split_heads(queries)
    g_heads = split_heads(grad_attn)
    scores = (
        jnp.einsum(
            "qhd,khd->hqk", q_heads, split_heads(key_rows), preferred_element_type=jnp.float32
        )
        * SCORE_SCALE
    )
    probabilities = jnp.where(same_image, jnp.exp(scores - log_total[..., None]), 0.0)
    grad_prob = jnp.einsum(
        "qhd,khd->hqk", g_heads, split_heads(value_rows), preferred_element_type=jnp.float32
    )
    dscore = (probabilities * (grad_prob - row_delta[..., None])).astype(jnp.bfloat16)
    grad_query = (
        jnp.einsum(
            "hqk,khd->qhd", dscore, split_heads(key_rows), preferred_element_type=jnp.float32
        ).reshape(queries.shape[0], -1)
        * SCORE_SCALE
    )
    grad_key = (
        jnp.einsum("hqk,qhd->khd", dscore, q_heads, preferred_element_type=jnp.float32).reshape(
            key_rows.shape[0], -1
        )
        * SCORE_SCALE
    )
    grad_value = jnp.einsum(
        "hqk,qhd->khd",
        probabilities.astype(jnp.bfloat16),
        g_heads,
        preferred_element_type=jnp.float32,
    ).reshape(key_rows.shape[0], -1)
    return (grad_query, grad_key, grad_value)


def fetch_weights(w_qkv, w_out, w_up, w_down, gains):
    return (
        lax.all_gather(w_qkv, ("dp", "blk"), axis=0, tiled=True),
        lax.all_gather(w_out, ("dp", "blk"), axis=0, tiled=True),
        lax.all_gather(w_up, ("dp", "blk"), axis=0, tiled=True),
        lax.all_gather(w_down, ("dp", "blk"), axis=0, tiled=True),
        lax.all_gather(gains, ("dp", "blk"), axis=1, tiled=True),
    )


def reduce_grads(grad_terms):
    g_qkv, g_out, g_up, g_down, g_gains = grad_terms
    return (
        lax.psum_scatter(g_qkv, ("dp", "blk"), scatter_dimension=0, tiled=True),
        lax.psum_scatter(g_out, ("dp", "blk"), scatter_dimension=0, tiled=True),
        lax.psum_scatter(g_up, ("dp", "blk"), scatter_dimension=0, tiled=True),
        lax.psum_scatter(g_down, ("dp", "blk"), scatter_dimension=0, tiled=True),
        lax.psum_scatter(g_gains, ("dp", "blk"), scatter_dimension=1, tiled=True),
    )


def contract_rows(left_rows, right_rows):
    return jnp.einsum("ra,rb->ab", left_rows, right_rows, preferred_element_type=jnp.float32)


def row_delta_of(grad_attn, attended):
    product = grad_attn.astype(jnp.float32) * attended
    return product.reshape(product.shape[0], -1, HEAD_DIM).sum(-1).T


def on_device(
    patches, special, image_ids, w_qkv, w_out, w_up, w_down, gains, cot_patches, cot_special
):
    cycle_size = lax.axis_size("blk")
    cycle_index = lax.axis_index("blk")
    width = w_out.shape[1]
    head_count = width // HEAD_DIM
    tok_rows = TOK_MB
    spec_rows = special.shape[0] // MICRO
    ids_group = image_ids.reshape(cycle_size, MICRO, tok_rows)
    spec_ids = jnp.arange(spec_rows, dtype=jnp.int32) // SPECIAL
    row_weight = jnp.concatenate(
        [jnp.ones((tok_rows,), jnp.float32), jnp.full((spec_rows,), 1.0 / cycle_size, jnp.float32)]
    )
    row_weight_low = row_weight.astype(jnp.bfloat16)[:, None]
    summed_terms = None
    shard_terms = None
    out_parts = []
    spec_parts = []
    grad_parts = []
    grad_spec_parts = []
    for micro_index in range(MICRO):
        full_weights = fetch_weights(w_qkv, w_out, w_up, w_down, gains)
        qkv_full, out_full, up_full, down_full, gains_full = full_weights
        gain_rows = gains_full.astype(jnp.float32)
        tokens = jnp.concatenate(
            [
                patches[micro_index * tok_rows : (micro_index + 1) * tok_rows],
                special[micro_index * spec_rows : (micro_index + 1) * spec_rows],
            ],
            0,
        ).astype(jnp.float32)
        ids_flat = ids_group[:, micro_index].reshape(-1)
        patch_ids = lax.dynamic_slice_in_dim(ids_flat, cycle_index * tok_rows, tok_rows)
        normed = norm_rows(tokens, gain_rows[0]).astype(jnp.bfloat16)
        projected = jnp.dot(normed, qkv_full, preferred_element_type=jnp.float32).astype(
            jnp.bfloat16
        )
        patch_q = projected[:tok_rows, :width]
        patch_k = projected[:tok_rows, width : 2 * width]
        patch_v = projected[:tok_rows, 2 * width :]
        spec_q = projected[tok_rows:, :width]
        spec_k = projected[tok_rows:, width : 2 * width]
        spec_v = projected[tok_rows:, 2 * width :]
        start_state = online(
            empty_state(tok_rows, head_count, width), patch_q, patch_ids, spec_k, spec_v, spec_ids
        )
        partial_value = start_state
        key_rows = lax.all_gather(patch_k, "blk", axis=0, tiled=True)
        value_rows = lax.all_gather(patch_v, "blk", axis=0, tiled=True)
        length = key_rows.shape[0]
        key_ids = ids_flat
        blocks = length // tok_rows

        def visit_block(running, block_item):
            return (
                online(running, patch_q, patch_ids, block_item[0], block_item[1], block_item[2]),
                None,
            )

        partial_value, unused = lax.scan(
            visit_block,
            partial_value,
            (
                key_rows.reshape(blocks, tok_rows, -1),
                value_rows.reshape(blocks, tok_rows, -1),
                key_ids.reshape(blocks, tok_rows),
            ),
        )
        spec_top, spec_total, spec_accum = online(
            empty_state(spec_rows, head_count, width), spec_q, spec_ids, patch_k, patch_v, patch_ids
        )
        spec_state = merged((spec_top, spec_total, spec_accum), "blk", combine)
        spec_state = online(spec_state, spec_q, spec_ids, spec_k, spec_v, spec_ids)
        patch_attn, patch_lse = finish(partial_value)
        spec_attn, spec_lse = finish(spec_state)
        attended = jnp.concatenate([patch_attn, spec_attn], 0)
        attended_low = attended.astype(jnp.bfloat16)
        branch = jnp.dot(attended_low, out_full, preferred_element_type=jnp.float32)
        middle = tokens + gain_rows[1] * branch
        normed_mlp = norm_rows(middle, gain_rows[2]).astype(jnp.bfloat16)
        hidden = jnp.dot(normed_mlp, up_full, preferred_element_type=jnp.float32)
        active = jax.nn.gelu(hidden, approximate=False).astype(jnp.bfloat16)
        mlp_out = jnp.dot(active, down_full, preferred_element_type=jnp.float32)
        final = middle + gain_rows[3] * mlp_out
        out_parts.append(final[:tok_rows].astype(jnp.bfloat16))
        spec_parts.append(final[tok_rows:].astype(jnp.bfloat16))
        upstream = jnp.concatenate(
            [
                cot_patches[micro_index * tok_rows : (micro_index + 1) * tok_rows],
                cot_special[micro_index * spec_rows : (micro_index + 1) * spec_rows],
            ],
            0,
        ).astype(jnp.float32)
        grad_mlp = (gain_rows[3] * upstream).astype(jnp.bfloat16)
        g_down = contract_rows(active, grad_mlp * row_weight_low)
        grad_active = jnp.einsum(
            "rd,fd->rf", grad_mlp, down_full, preferred_element_type=jnp.float32
        )
        unused_value, gelu_pull = jax.vjp(
            lambda pre_act: jax.nn.gelu(pre_act, approximate=False), hidden
        )
        grad_hidden = gelu_pull(grad_active)[0].astype(jnp.bfloat16)
        g_up = contract_rows(normed_mlp, grad_hidden * row_weight_low)
        grad_normed_mlp = jnp.einsum(
            "rf,df->rd", grad_hidden, up_full, preferred_element_type=jnp.float32
        )
        unused_value, norm_pull_mlp = jax.vjp(
            lambda rows_in: norm_rows(rows_in, gain_rows[2]), middle
        )
        grad_middle = upstream + norm_pull_mlp(grad_normed_mlp)[0]
        g_ln2 = jnp.sum(row_weight[:, None] * grad_normed_mlp * norm_rows(middle, 1.0), 0)
        g_ls2 = jnp.sum(row_weight[:, None] * upstream * mlp_out, 0)
        g_ls1 = jnp.sum(row_weight[:, None] * grad_middle * branch, 0)
        grad_branch = (gain_rows[1] * grad_middle).astype(jnp.bfloat16)
        g_out = contract_rows(attended_low, grad_branch * row_weight_low)
        grad_attended = jnp.einsum(
            "re,de->rd", grad_branch, out_full, preferred_element_type=jnp.float32
        ).astype(jnp.bfloat16)
        all_delta = row_delta_of(grad_attended, attended)
        patch_delta = all_delta[:, :tok_rows]
        spec_delta = all_delta[:, tok_rows:]
        patch_grad_attn = grad_attended[:tok_rows]
        spec_grad_attn = grad_attended[tok_rows:]
        grad_pq_first, grad_sk_part, grad_sv_part = block_grads(
            patch_q, patch_grad_attn, patch_lse, patch_delta, patch_ids, spec_k, spec_v, spec_ids
        )
        grad_sq_part, grad_pk_local, grad_pv_local = block_grads(
            spec_q, spec_grad_attn, spec_lse, spec_delta, spec_ids, patch_k, patch_v, patch_ids
        )
        sum_sq, sum_sk, sum_sv = (
            lax.psum(grad_sq_part.astype(jnp.bfloat16), "blk").astype(jnp.float32),
            lax.psum(grad_sk_part.astype(jnp.bfloat16), "blk").astype(jnp.float32),
            lax.psum(grad_sv_part.astype(jnp.bfloat16), "blk").astype(jnp.float32),
        )
        grad_sq_own, grad_sk_own, grad_sv_own = block_grads(
            spec_q, spec_grad_attn, spec_lse, spec_delta, spec_ids, spec_k, spec_v, spec_ids
        )

        def cycle_step(hop_index, carried):
            keys_now, values_now, grad_keys, grad_values, grad_queries = carried
            source = (cycle_index - hop_index) % cycle_size
            key_ids = lax.dynamic_slice_in_dim(ids_flat, source * tok_rows, tok_rows)
            term_q, term_k, term_v = block_grads(
                patch_q,
                patch_grad_attn,
                patch_lse,
                patch_delta,
                patch_ids,
                keys_now,
                values_now,
                key_ids,
            )
            keys_now, values_now = from_behind((keys_now, values_now), "blk", 1)
            grad_keys, grad_values = (
                from_behind((grad_keys + term_k).astype(jnp.bfloat16), "blk", 1).astype(
                    jnp.float32
                ),
                from_behind((grad_values + term_v).astype(jnp.bfloat16), "blk", 1).astype(
                    jnp.float32
                ),
            )
            return (keys_now, values_now, grad_keys, grad_values, grad_queries + term_q)

        zero_rows = jnp.zeros((tok_rows, width), jnp.float32)
        unused_keys, unused_values, grad_pk, grad_pv, grad_pq = lax.fori_loop(
            0, cycle_size, cycle_step, (patch_k, patch_v, zero_rows, zero_rows, grad_pq_first)
        )
        grad_pk = grad_pk + grad_pk_local
        grad_pv = grad_pv + grad_pv_local
        grad_patch_qkv = jnp.concatenate([grad_pq, grad_pk, grad_pv], 1)
        grad_spec_qkv = jnp.concatenate(
            [sum_sq + grad_sq_own, sum_sk + grad_sk_own, sum_sv + grad_sv_own], 1
        )
        grad_projected = jnp.concatenate([grad_patch_qkv, grad_spec_qkv], 0).astype(jnp.bfloat16)
        g_qkv = contract_rows(normed, grad_projected * row_weight_low)
        grad_normed = jnp.einsum(
            "re,de->rd", grad_projected, qkv_full, preferred_element_type=jnp.float32
        )
        unused_value, norm_pull_attn = jax.vjp(
            lambda rows_in: norm_rows(rows_in, gain_rows[0]), tokens
        )
        grad_tokens = grad_middle + norm_pull_attn(grad_normed)[0]
        g_ln1 = jnp.sum(row_weight[:, None] * grad_normed * norm_rows(tokens, 1.0), 0)
        grad_parts.append(grad_tokens[:tok_rows])
        grad_spec_parts.append(grad_tokens[tok_rows:])
        grad_terms = (g_qkv, g_out, g_up, g_down, jnp.stack([g_ln1, g_ls1, g_ln2, g_ls2], 0))
        summed_terms = (
            grad_terms
            if summed_terms is None
            else tuple((held + extra for held, extra in zip(summed_terms, grad_terms)))
        )
    shard_terms = reduce_grads(summed_terms)
    return (
        jnp.concatenate(out_parts, 0),
        jnp.concatenate(spec_parts, 0),
        jnp.concatenate(grad_parts, 0),
        jnp.concatenate(grad_spec_parts, 0),
        shard_terms[0],
        shard_terms[1],
        shard_terms[2],
        shard_terms[3],
        shard_terms[4],
    )


PAD_ID = 99
PLAN = (
    (9.0, ()), (0, (0,)), (0, (0,)), (0, (2,)), (21.0, (2,)), (0, ()), (0, ()), (0, ()), (0, (0,)),
    (0, (2, 4, 5)), (0, ()), (0, (8,)), (0, ()), (0, ()), (0, (9, 11)), (0, (7,)), (0, ()),
    (0, (10, 15, 16)), (0, ()), (36.0, (12,)), (0, ()), (2.4, ()), (0, (9,)), (0, (17,)), (0, (21,)),
    (0, (21,)), (0, (21, 6, 18)), (4.8, ()), (0, (27,)), (0, (27,)), (0.001, (26, 28, 21)), (0.001, ()),
    (1.11, ()), (0, ()), (2.7, ()), (0, ()), (0.002, ()), (0, (30,)), (0.6, (29,)), (0, (34,)), (0.6, ()),
    (0, ()), (0.07, ()), (0, ()), (0.27, ()), (0, ()), (0.4, ()), (0, ()), (21.0, ()), (0, ()),
    (7.0, (32,)), (0, (45,)), (0.42, ()), (0, ()), (1.05, ()), (0, ()), (0.0325, ()), (0, ()), (0.18, ()),
    (0, (56,)), (0.105, (58,)), (0, ()), (0, ()), (0, ()), (2.1, ()), (0, (47,)), (2.1, ()), (0, ()),
    (2.1, ()), (0.35, (59,)), (0, ()), (0, (69,)), (0, (55, 65)), (1.5, ()), (9.0, (68,)), (0, (68,)),
    (0, ()), (0, (70,)), (0.001, ()), (30, ()),
)
STEPS = []


def plan():
    us, steps = PLAN[len(STEPS)]
    return us, [STEPS[i] for i in steps]


def mm(a, b):
    return jnp.dot(a, b, preferred_element_type=F32)


def mm_nt(a, b):
    return lax.dot_general(a, b, (((1,), (1,)), ((), ())), preferred_element_type=F32)


def mm_tn(a, b):
    return lax.dot_general(a, b, (((0,), (0,)), ((), ())), preferred_element_type=F32)


def here():
    place = lax.axis_index("blk")
    group = lax.axis_index("dp")
    return place, place // 2, place % 2, group // 2, group % 2


def chunk_index(slot, z, y):
    return (z ^ (slot % 4)) * 2 + (y ^ (slot // 4))


def row_blocks(block, among=slice(0, 736)):
    return [slice(first, first + block) for first in range(among.start, among.stop, block)]


def fold(rows):
    return rows.reshape(rows.shape[0] // 8, 8, rows.shape[1]).sum(0)


class Keep:
    def __init__(self, value):
        self.value = value


class Far:
    def __init__(self, value):
        self.value = value


class Load:
    def __init__(self, buffer, copy):
        self.buffer, self.copy, self.waited = buffer, copy, False

    def ready(self):
        if not self.waited:
            self.copy.wait()
            self.waited = True
        return self.buffer


def call(kernel, outs, ins, scratch=(), limit=20):
    us, after = plan()
    far = [i for i, v in enumerate(ins) if isinstance(v, Far)]
    plain = [v.value if isinstance(v, (Far, Keep)) else v for v in ins]
    near, away = pl.BlockSpec(memory_space=pltpu.VMEM), pl.BlockSpec(memory_space=pltpu.HBM)
    room = [pltpu.VMEM(plain[i].shape, plain[i].dtype) for i in far]
    if far:
        room.append(pltpu.SemaphoreType.DMA((len(far),)))

    def body(*refs):
        given = [*refs[: len(ins)], *refs[len(ins) + len(after) :]]
        own = given[len(ins) + len(outs) + len(scratch) :]
        given = given[: len(ins) + len(outs) + len(scratch)]
        for k, i in enumerate(far):
            copy = pltpu.make_async_copy(given[i], own[k], own[-1].at[k])
            copy.start()
            given[i] = Load(own[k], copy)
        kernel(*given)

    def placed(v):
        if isinstance(v, Keep):
            return pltpu.with_memory_space_constraint(v.value, pltpu.VMEM)
        return pltpu.with_memory_space_constraint(v.value, pltpu.HBM) if isinstance(v, Far) else v

    made_arrays = pl.pallas_call(
        body,
        out_shape=tuple(
            pltpu.VMEM(v.value.shape, v.value.dtype) if isinstance(v, Keep) else v for v in outs
        ),
        in_specs=[away if i in far else near for i in range(len(ins))]
        + [pl.BlockSpec(memory_space=pl.ANY)] * len(after),
        out_specs=tuple(near for _ in outs),
        scratch_shapes=[*scratch, *room],
        compiler_params=pltpu.CompilerParams(vmem_limit_bytes=limit * 2**20),
        cost_estimate=pl.CostEstimate(flops=int(us * 10**9), bytes_accessed=0, transcendentals=0),
        name=kernel.__name__,
    )(*[placed(v) for v in ins], *after)
    STEPS.append(made_arrays[0])
    return made_arrays


def keep(*arrays):
    return [Keep(v) for v in arrays]


def sds(*shape, dtype=BF16):
    return jax.ShapeDtypeStruct(shape, dtype)


def pick_pieces(w_qkv, w_up, gains, patches, cots, own, near, far, rows, held):
    place = here()[0]
    held[...] = jnp.zeros_like(held)
    up = w_up.ready()[...].astype(F32)
    qkv = w_qkv.ready()[...].astype(F32)
    gain = gains.ready()[...].astype(F32)
    for b in range(4):
        for d in range(8):
            held[b, 0:24, d * 96 : d * 96 + 96] = up[:, d * 384 + b * 96 : d * 384 + b * 96 + 96]
        for part in range(3):
            held[b, 24:48, part * 192 : part * 192 + 192] = qkv[
                :, part * 768 + b * 192 : part * 768 + b * 192 + 192
            ]
        held[b, 24:28, 576:600] = gain
    own[...] = held[place].astype(BF16)
    near[...] = held[place ^ 1].astype(BF16)
    far[0:48, :] = held[place ^ 2].astype(BF16)
    far[48:96, :] = held[place ^ 3].astype(BF16)
    rows[0:176, :] = patches.ready()[...]
    rows[176:352, :] = cots.ready()[...]


def join_pieces(own, near, far, near_far, w_out, w_down, pack, both, wide, pack_f, up_f):
    place = here()[0]
    pack_f[96:112, :] = jnp.zeros((16, 768), F32)
    pieces = (
        own[...].astype(F32),
        near[...].astype(F32),
        far[0:48, :].astype(F32),
        near_far[48:96, :].astype(F32),
    )
    for k, piece in enumerate(pieces):
        source = place ^ k
        at = pl.ds(pl.multiple_of(source * 24, 8), 24)
        up_f[at, :] = piece[0:24]
        pack_f[at, 0:576] = piece[24:48, 0:576]
        lanes = pl.ds(pl.multiple_of(source * 128, 128), 128)
        pack_f[96:104, lanes] = piece[24:32, 576:704]
    out = w_out[...].astype(F32)
    for i in range(4):
        pack_f[i * 24 : i * 24 + 24, 576:768] = out[:, i * 192 : i * 192 + 192]
    pack[...] = pack_f[...].astype(BF16)
    both[0:96, :] = up_f[...].astype(BF16)
    both[96:192, :] = w_down[...]
    wide[0:112, :] = pack[...]
    wide[112:304, :] = both[...]


def open_pack(*refs):
    chunks, (w_qkv, w_out, gain_rows, out_f, gain_f) = refs[:8], refs[8:]
    _, _, _, z, y = here()
    for slot, chunk in enumerate(chunks):
        d = chunk_index(slot, z, y)
        w_qkv[pl.ds(pl.multiple_of(d * 96, 96), 96), :] = chunk[0:96, 0:576]
        tail = chunk[0:96, 576:768].astype(F32)
        for i in range(4):
            out_f[pl.ds(pl.multiple_of(d * 24, 8), 24), i * 192 : i * 192 + 192] = tail[
                i * 24 : i * 24 + 24
            ]
        gain_f[d] = chunk[96:112, :].astype(F32)
    w_out[...] = out_f[...].astype(BF16)
    gain_rows[...] = jnp.zeros_like(gain_rows)
    for d in range(8):
        for b in range(4):
            at = (d * 4 + b) * 24
            gain_rows[0:4, at : at + 24] = gain_f[d, 0:4, b * 128 : b * 128 + 24]


def normalise(rows):
    centre = rows - jnp.mean(rows, -1, keepdims=True)
    spread = jnp.mean(centre * centre, -1, keepdims=True)
    scale = lax.rsqrt(spread + EPSILON)
    return centre * scale, scale


def place_rows(scratch, blocks, tail, first):
    place = here()[0]
    for k, block in enumerate(blocks):
        rows = block[first : first + 176, :].astype(F32)
        source = place ^ k
        for m in range(MICRO):
            scratch[pl.ds(pl.multiple_of(m * 368 + source * 88, 8), 88), :] = rows[m * 88 : m * 88 + 88]
    rows = tail[...].astype(F32)
    for m in range(MICRO):
        scratch[m * 368 + 352 : m * 368 + 368, :] = jnp.zeros((16, 768), F32)
        scratch[m * 368 + 352 : m * 368 + 362, :] = rows[m * 10 : m * 10 + 10]


def turned(line):
    count = max(line.shape)
    down = lax.broadcasted_iota(jnp.int32, (count, count), 0)
    across = lax.broadcasted_iota(jnp.int32, (count, count), 1)
    return jnp.sum(jnp.where(down == across, line, 0.0), line.shape.index(count), keepdims=True)


def attend(
    rows_0, rows_1, rows_2, rows_3, tail, ids, w_qkv, gain_rows,
    attended, projected, probs, tokens, unit_low, rows_f,
):
    place_rows(rows_f, (rows_0, rows_1, rows_2, rows_3), tail, 0)
    gain = gain_rows[0:1, :]
    slot = lax.broadcasted_iota(jnp.int32, (1, 16), 1)
    tail_ids = jnp.where(slot < 2 * SPECIAL, (slot >= SPECIAL).astype(jnp.int32), PAD_ID)
    for m in range(MICRO):
        at = slice(m * 368, m * 368 + 368)
        row = jnp.concatenate([ids[b * 2 + m : b * 2 + m + 1, :] for b in range(4)] + [tail_ids], 1)
        row = row.astype(F32)
        bias = jnp.where(turned(row) == row, 0.0, MASKED)
        normed = []
        for block in row_blocks(16, at):
            rows = rows_f[block, :]
            tokens[block, :] = rows.astype(BF16)
            unit = normalise(rows)[0]
            unit_low[block, :] = unit.astype(BF16)
            normed.append((unit * gain).astype(BF16))
        qkv = mm(jnp.concatenate(normed, 0), w_qkv[...])
        qkv = jnp.concatenate([qkv[:, 0:192] * SCORE_SCALE, qkv[:, 192:576]], -1).astype(BF16)
        projected[at, :] = qkv
        heads = []
        for h in range(3):
            q = qkv[:, h * 64 : h * 64 + 64]
            k = qkv[:, 192 + h * 64 : 192 + h * 64 + 64]
            v = qkv[:, 384 + h * 64 : 384 + h * 64 + 64]
            scores = mm_nt(q, k) + bias
            weights = jnp.exp(scores - jnp.max(scores, -1, keepdims=True))
            weights = weights * (1.0 / jnp.sum(weights, -1, keepdims=True))
            weights = weights.astype(BF16)
            probs[m * 3 + h] = weights
            heads.append(mm(weights, v))
        attended[at, :] = jnp.concatenate(heads, -1).astype(BF16)


def order_out(
    out_0, out_1, out_2, out_3, rows_0, rows_1, rows_2, rows_3, cot_tail, gain_rows,
    ordered, mine, grad_mlp, cots, out_f,
):
    place = here()[0]
    for k, part in enumerate((out_0, out_1, out_2, out_3)):
        source = place ^ k
        rows = part[...].astype(F32)
        for d in range(8):
            at = pl.multiple_of((d * 4 + source) * 24, 8)
            out_f[pl.ds(at, 24), :] = rows[d * 24 : d * 24 + 24]
    ordered[...] = out_f[...].astype(BF16)
    mine[...] = out_f[pl.ds(pl.multiple_of(place * 192, 8), 192), :].astype(BF16)
    place_rows(out_f, (rows_0, rows_1, rows_2, rows_3), cot_tail, 176)
    gain = gain_rows[3:4, :]
    for at in row_blocks(32):
        rows = out_f[at, :]
        cots[at, :] = rows.astype(BF16)
        grad_mlp[at, :] = (gain * rows).astype(BF16)


def branch_rows(
    head_0, head_1, head_2, head_3, w_out, tokens, gain_rows, normed, branch, own_rows, rows_f
):
    place = here()[0]
    gain_s, gain_n = gain_rows[1:2, :], gain_rows[2:3, :]
    for m in range(MICRO):
        group = slice(m * 368, m * 368 + 368)
        total = None
        for k, part in enumerate((head_0, head_1, head_2, head_3)):
            rows = w_out[pl.ds(pl.multiple_of((place ^ k) * 192, 16), 192), :]
            term = mm(part[group, :], rows)
            total = term if total is None else total + term
        rows_f[group, :] = total
        for at in row_blocks(16, group):
            a = rows_f[at, :]
            branch[at, :] = a.astype(BF16)
            rows = tokens[at, :].astype(F32) + gain_s * a
            rows_f[at, :] = rows
            normed[at, :] = (normalise(rows)[0] * gain_n).astype(BF16)
        for part, first in ((0, place * 88), (88, 352)):
            rows = 88 if part == 0 else 16
            own_rows[m * 104 + part : m * 104 + part + rows, :] = rows_f[
                pl.ds(pl.multiple_of(m * 368 + first, 8), rows), :
            ]


def raise_rows(*refs):
    normed, chunks = refs[0], refs[1:9]
    active, slope, w_up, w_down, rows_f = refs[9:]
    _, _, _, z, y = here()
    for slot, chunk in enumerate(chunks):
        d = chunk_index(slot, z, y)
        skip = chunk.shape[0] - 192
        w_up[pl.ds(pl.multiple_of(d * 96, 96), 96), :] = chunk[skip : skip + 96, :]
        w_down[pl.ds(pl.multiple_of(d * 96, 96), 96), :] = chunk[skip + 96 : skip + 192, :]
    for m in range(MICRO):
        at = slice(m * 368, m * 368 + 368)
        rows_f[at, :] = mm(normed[at, :], w_up[...])
    for at in row_blocks(32):
        u = rows_f[at, :]
        half = 0.5 + 0.5 * lax.erf(u * 0.7071067811865476)
        active[at, :] = (u * half).astype(BF16)
        slope[at, :] = half + u * (0.3989422804014327 * jnp.exp(-0.5 * u * u))


def down_grads(active, grad_mlp, away, kept, work):
    _, _, _, z, _ = here()
    work[...] = mm_tn(active[...], grad_mlp[...])
    for pair in range(2):
        for side in range(2):
            ours = pl.multiple_of(((z ^ (2 * pair)) * 2 + side) * 96, 8)
            theirs = pl.multiple_of(((z ^ (2 * pair + 1)) * 2 + side) * 96, 8)
            kept[pair * 2 + side] = work[pl.ds(ours, 96), :]
            away[pair * 2 + side] = work[pl.ds(theirs, 96), :].astype(BF16)


def sum_fours(kept, came, own, away):
    own[...] = kept[0:2] + came[0:2].astype(F32)
    away[...] = (kept[2:4] + came[2:4].astype(F32)).astype(BF16)


def sum_sides(kept, came, own, away):
    y = here()[4]
    own[...] = kept[y] + came[y].astype(F32)
    away[...] = (kept[1 - y] + came[1 - y].astype(F32)).astype(BF16)


def lower_rows(slope, grad_mlp, w_up, w_down, away, kept, grad_hidden, work):
    core = here()[2]
    for m in range(MICRO):
        at = slice(m * 368, m * 368 + 368)
        grad = mm_nt(grad_mlp[at, :], w_down[...])
        grad_hidden[at, :] = (slope[at, :] * grad).astype(BF16)
        work[m] = mm_nt(grad_hidden[at, :], w_up[...])
    away[...] = work[1 - core].astype(BF16)
    kept[...] = work[core]


def split_rows(pieces, place, away, kept):
    away[0:208, :] = pieces[place ^ 1].astype(BF16)
    away[208:416, :] = pieces[place ^ 3].astype(BF16)
    kept[0:208, :] = pieces[place]
    kept[208:416, :] = pieces[place ^ 2]


def cut_rows(rows_f, pieces):
    for b in range(4):
        for m in range(MICRO):
            pieces[b, m * 104 : m * 104 + 88, :] = rows_f[m * 368 + b * 88 : m * 368 + b * 88 + 88, :]
            pieces[b, m * 104 + 88 : m * 104 + 104, :] = rows_f[m * 368 + 352 : m * 368 + 368, :]


def halve(grad_f, y, away, kept, rows):
    for zz in range(4):
        other = pl.ds(pl.multiple_of((zz * 2 + 1 - y) * rows, 8), rows)
        ours = pl.ds(pl.multiple_of((zz * 2 + y) * rows, 8), rows)
        away[zz] = grad_f[other, 0 : away.shape[2]].astype(BF16)
        kept[zz] = grad_f[ours, 0 : away.shape[2]]


def up_grads(normed, grad_hidden, away, kept, work):
    y = here()[4]
    work[...] = mm_tn(normed[...], grad_hidden[...])
    halve(work, y, away, kept, 96)


def mlp_rows(
    active, w_down, cots, head_0, head_1, head_2, head_3,
    rows_away, rows_kept, scale_grad, chosen, work, pieces,
):
    place = here()[0]
    for m in range(MICRO):
        at = slice(m * 368, m * 368 + 368)
        work[at, :] = mm(active[at, :], w_down[...])
    total = jnp.zeros((8, 768), F32)
    for at in row_blocks(32):
        total = total + fold(cots[at, :].astype(F32) * work[at, :])
    scale_grad[...] = total
    cut_rows(work, pieces)
    split_rows(pieces, place, rows_away, rows_kept)
    picked = None
    column = lax.broadcasted_iota(jnp.int32, (192, 192), 1)
    chunk = sum((column >= 24 * d).astype(jnp.int32) for d in range(1, 8))
    targets = column + chunk * 72 + place * 24
    for k, part in enumerate((head_0, head_1, head_2, head_3)):
        index = lax.broadcasted_iota(jnp.int32, (192, 192), 0) + (place ^ k) * 192
        pick = jnp.where(index == targets, 1.0, 0.0).astype(BF16)
        term = mm(part[...], pick)
        picked = term if picked is None else picked + term
    chosen[...] = picked.astype(BF16)


def add_rows(kept, came, total):
    total[...] = (kept[...] + came[...].astype(F32)).astype(BF16)


def add_pair(here_rows, came, total):
    total[...] = (here_rows[...].astype(F32) + came[...].astype(F32)).astype(BF16)


def branch_back(
    sum_own, sum_near, tokens, cots, branch, gain_rows, w_mine, probs, normed, scale_grad_mlp, chosen,
    grad_rows, grad_heads, grad_v, away, kept,
    work, grad_branch, grad_mid, extra, early,
):
    place, _, core, _, y = here()
    for m in range(MICRO):
        at = slice(m * 368, m * 368 + 368)

        @pl.when(core == m)
        def _():
            work[at, :] = sum_own[...].astype(F32)

        @pl.when(core != m)
        def _():
            work[at, :] = sum_near[...].astype(F32)

    gain_s, gain_n = gain_rows[1:2, :], gain_rows[2:3, :]
    scale_sum = jnp.zeros((8, 768), F32)
    for at in row_blocks(32):
        grown = branch[at, :].astype(F32)
        unit, scale = normalise(tokens[at, :].astype(F32) + gain_s * grown)
        pulled = work[at, :] * gain_n
        pulled = pulled - jnp.mean(pulled, -1, keepdims=True) - unit * jnp.mean(
            pulled * unit, -1, keepdims=True
        )
        through = cots[at, :].astype(F32) + scale * pulled
        grad_mid[at, :] = through
        grad_branch[at, :] = (gain_s * through).astype(BF16)
        scale_sum = scale_sum + fold(through * grown)
    for m in range(MICRO):
        for part, first in ((0, place * 88), (88, 352)):
            rows = 88 if part == 0 else 16
            grad_rows[m * 104 + part : m * 104 + part + rows, :] = grad_mid[
                pl.ds(pl.multiple_of(m * 368 + first, 8), rows), :
            ]
    for m in range(MICRO):
        at = slice(m * 368, m * 368 + 368)
        heads = mm_nt(grad_branch[at, :], w_mine[...]).astype(BF16)
        grad_heads[at, :] = heads
        terms = [mm_tn(probs[m * 3 + h], heads[:, h * 64 : h * 64 + 64]) for h in range(3)]
        grad_v[at, :] = jnp.concatenate(terms, -1).astype(BF16)
    grad_mid[0:768, 0:192] = mm_tn(normed[...], grad_v[...])
    extra[...] = mm_tn(chosen[...], grad_branch[...])
    scale_rows = (
        0.25 * jnp.sum(scale_sum, 0, keepdims=True),
        jnp.sum(scale_grad_mlp[...], 0, keepdims=True),
    )
    for d in range(8):
        base = d * 112
        early[base : base + 96, 0:192] = grad_mid[d * 96 : d * 96 + 96, 0:192]
        for i in range(4):
            early[base + i * 24 : base + i * 24 + 24, 192:384] = extra[
                d * 24 : d * 24 + 24, i * 192 : i * 192 + 192
            ]
        early[base + 96 : base + 112, :] = jnp.zeros((16, 384), F32)
        for i in range(2):
            early[base + 96 + i : base + 97 + i, 0:96] = scale_rows[i][:, d * 96 : d * 96 + 96]
    halve(early, y, away, kept, 112)


def score_back(probs, projected, grad_heads, normed, grad_qk, away, kept, work):
    _, _, _, _, y = here()
    for m in range(MICRO):
        at = slice(m * 368, m * 368 + 368)
        qkv = projected[at, :]
        g_heads = grad_heads[at, :]
        grads = [[], []]
        for h in range(3):
            q = qkv[:, h * 64 : h * 64 + 64]
            k = qkv[:, 192 + h * 64 : 192 + h * 64 + 64]
            v = qkv[:, 384 + h * 64 : 384 + h * 64 + 64]
            grad_prob = mm_nt(g_heads[:, h * 64 : h * 64 + 64], v)
            wide = probs[m * 3 + h].astype(F32)
            moved = wide * grad_prob
            delta = jnp.sum(moved, -1, keepdims=True)
            grad_score = (moved - wide * delta).astype(BF16)
            grads[0].append(mm(grad_score, k) * SCORE_SCALE)
            grads[1].append(mm_tn(q, grad_score))
        grad_qk[at, 0:192] = jnp.concatenate(grads[0], -1).astype(BF16)
        grad_qk[at, 192:384] = jnp.concatenate(grads[1], 0).T.astype(BF16)
    work[...] = mm_tn(normed[...], grad_qk[...])
    halve(work, y, away, kept, 96)


def project_back(grad_qk, grad_v, w_qkv, rows_away, rows_kept, work, pieces):
    place = here()[0]
    for m in range(MICRO):
        at = slice(m * 368, m * 368 + 368)
        work[at, :] = mm_nt(grad_qk[at, :], w_qkv[:, 0:384]) + mm_nt(grad_v[at, :], w_qkv[:, 384:576])
    cut_rows(work, pieces)
    split_rows(pieces, place, rows_away, rows_kept)


def sum_y(kept, came, own, send_1, send_2, send_3):
    _, _, _, z, _ = here()
    own[...] = kept[z] + came[z].astype(F32)
    for k, send in ((1, send_1), (2, send_2), (3, send_3)):
        send[...] = (kept[z ^ k] + came[z ^ k].astype(F32)).astype(BF16)


def sum_y_pairs(kept, came, own, away):
    _, _, _, z, _ = here()
    for k in range(2):
        own[k] = kept[z ^ (2 * k)] + came[z ^ (2 * k)].astype(F32)
        there = z ^ (2 * k + 1)
        away[k] = (kept[there] + came[there].astype(F32)).astype(BF16)


def sum_pairs(kept, came, own, away):
    own[...] = kept[0] + came[0].astype(F32)
    away[...] = (kept[1] + came[1].astype(F32)).astype(BF16)


def sum_last(own, came, total):
    total[...] = own[...] + came[...].astype(F32)


def add_pieces(kept_m, came_m, kept_h, came_h, stay, go):
    for i, (kept, came) in enumerate(((kept_m, came_m), (kept_h, came_h))):
        stay[i * 208 : i * 208 + 208, :] = kept[0:208, :] + came[0:208, :].astype(F32)
        go[i * 208 : i * 208 + 208, :] = (kept[208:416, :] + came[208:416, :].astype(F32)).astype(BF16)


def finish_rows(
    stay, came, own_rows, grad_rows, patches, tail, gain_rows,
    out_patches, out_special, grad_patches, grad_special,
):
    own = patches[...].astype(F32)
    rest = tail[...].astype(F32)
    outs, out_tails = [], []
    for m in range(MICRO):
        for part, count in ((0, 88), (88, 10)):
            at = slice(m * 104 + part, m * 104 + part + count)
            far_at = slice(208 + m * 104 + part, 208 + m * 104 + part + count)
            final = own_rows[at, :] + gain_rows[3:4, :] * (stay[at, :] + came[at, :].astype(F32))
            (outs if part == 0 else out_tails).append(final)
            rows = own[m * 88 : m * 88 + 88] if part == 0 else rest[m * 10 : m * 10 + 10]
            unit, scale = normalise(rows)
            pulled = gain_rows[0:1, :] * (stay[far_at, :] + came[far_at, :].astype(F32))
            pulled = pulled - jnp.mean(pulled, -1, keepdims=True) - unit * jnp.mean(
                pulled * unit, -1, keepdims=True
            )
            grad = grad_rows[at, :] + scale * pulled
            if part == 0:
                grad_patches[m * 88 : m * 88 + 88, :] = grad
            else:
                grad_special[m * 10 : m * 10 + 10, :] = grad
    out_patches[...] = jnp.concatenate(outs, 0).astype(BF16)
    out_special[...] = jnp.concatenate(out_tails, 0).astype(BF16)


def hand_out(held, own, near, far):
    place = here()[0]
    own[...] = held[place]
    near[...] = held[place ^ 1].astype(BF16)
    far[0:32, :] = held[place ^ 2].astype(BF16)
    far[32:64, :] = held[place ^ 3].astype(BF16)


def take_in(held, own, near, far, near_far):
    place = here()[0]
    held[place] = own[...]
    held[place ^ 1] = near[...].astype(F32)
    held[place ^ 2] = far[0:32, :].astype(F32)
    held[place ^ 3] = near_far[32:64, :].astype(F32)


def pick_up(kept, came, own, near, far, held):
    held[...] = jnp.zeros_like(held)
    for b in range(4):
        at = slice(b * 24, b * 24 + 24)
        held[b, 0:24, :] = kept[at, :] + came[at, :].astype(F32)
    hand_out(held, own, near, far)


def pick_attention(kept_a, came_a, kept_b, came_1, came_2, came_3, own, near, far, grad_out, held, sums):
    held[...] = jnp.zeros_like(held)
    sums[:, 0:384] = kept_a[...] + came_a[...].astype(F32)
    sums[0:96, 384:768] = (
        kept_b[...] + came_1[...].astype(F32) + came_2[...].astype(F32) + came_3[...].astype(F32)
    )
    for b in range(4):
        at = slice(b * 24, b * 24 + 24)
        held[b, 0:24, 0:384] = sums[at, 384:768]
        held[b, 0:24, 384:576] = sums[at, 0:192]
        held[b, 0:2, 576:600] = sums[96:98, at]
        grad_out[:, b * 192 : b * 192 + 192] = sums[at, 192:384]
    hand_out(held, own, near, far)


def join_up(own, near, far, near_far, w_up, gains, grad_up, norm_grad, held):
    take_in(held, own, near, far, near_far)
    for b in range(4):
        for d in range(8):
            at = d * 384 + b * 96
            grad_up[:, at : at + 96] = held[b, 0:24, d * 96 : d * 96 + 96]
    total = turned(jnp.sum(w_up[...].astype(F32) * grad_up[...], -1, keepdims=True))
    norm_grad[...] = total / gains[2:3, :].astype(F32)


def join_attention(
    own, near, far, near_far, w_qkv, gains, norm_grad, grad_qkv, grad_gains, held
):
    take_in(held, own, near, far, near_far)
    scales = None
    for b in range(4):
        for part in range(3):
            at = slice(part * 768 + b * 192, part * 768 + b * 192 + 192)
            grad_qkv[:, at] = held[b, 0:24, part * 192 : part * 192 + 192]
        term = held[b, 0:2, 576:600]
        scales = term if scales is None else scales + term
    plain = grad_qkv[...]
    grad_gains[0:1, :] = turned(jnp.sum(w_qkv[...].astype(F32) * plain, -1, keepdims=True))
    grad_gains[1:2, :] = scales[0:1, :]
    grad_gains[2:3, :] = norm_grad[...]
    grad_gains[3:4, :] = scales[1:2, :]
    grad_qkv[...] = plain * turned(gains[0:1, :].astype(F32))


def send(rows, axis, step):
    pairs = []
    for group in range(8):
        z, y = group // 2, group % 2
        for place in range(4):
            target = {
                "core": (group, place ^ 1),
                "x": (group, place ^ 2),
                "y": (z * 2 + 1 - y, place),
                "z": ((z ^ step) * 2 + y, place),
            }[axis]
            pairs.append((group * 4 + place, target[0] * 4 + target[1]))
    _, ready = plan()
    if ready:
        rows = lax.optimization_barrier((rows, *ready))[0]
    STEPS.append(lax.ppermute(rows, ("dp", "blk"), pairs))
    return STEPS[-1]


def add_y(kept, came):
    rows, width = kept.shape[1:]
    own, *parts = call(
        sum_y,
        [Keep(sds(rows, width, dtype=F32))] + [sds(rows, width)] * 3,
        [Keep(kept), came],
    )
    return [own, *[send(part, "z", k) for k, part in zip((1, 2, 3), parts)]]


def halve_y(kept, came):
    rows, width = kept.shape[1:]
    own, away = call(
        sum_y_pairs,
        [Keep(sds(2, rows, width, dtype=F32)), sds(2, rows, width)],
        [Keep(kept), came],
    )
    return own, send(away, "z", 1)


def halve_z(pair):
    kept, came = pair
    rows, width = kept.shape[1:]
    own, away = call(
        sum_pairs,
        [Keep(sds(rows, width, dtype=F32)), sds(rows, width)],
        [Keep(kept), came],
    )
    return own, send(away, "z", 2)


def side_y(kept, came):
    own, away = call(
        sum_sides,
        [Keep(sds(96, 768, dtype=F32)), sds(96, 768)],
        [Keep(kept), came],
    )
    return own, send(away, "y", 1)


def add_last(last):
    own, came = last
    return call(
        sum_last, [sds(*own.shape, dtype=F32)], [Keep(own), came]
    )[0]


def on_device_split(
    patches, special, image_ids, w_qkv, w_out, w_up, w_down, gains, cot_patches, cot_special
):
    STEPS.clear()
    own, near, far, rows = call(
        pick_pieces,
        [sds(48, 768), sds(48, 768), sds(96, 768), sds(352, 768)],
        [Far(w_qkv), Far(w_up), Far(gains), Far(patches), Far(cot_patches)],
        [pltpu.VMEM((4, 48, 768), F32)],
    )
    came_far = send(far, "x", 1)
    came_near, came_near_far = send(near, "core", 1), send(came_far, "core", 1)
    pack, both, wide = call(
        join_pieces,
        [sds(112, 768), sds(192, 768), sds(304, 768)],
        [own, came_near, came_far, came_near_far, w_out, w_down],
        [pltpu.VMEM((112, 768), F32), pltpu.VMEM((96, 768), F32)],
    )
    pack_2 = send(pack, "z", 2)
    pack_1 = send(pack, "z", 1)
    wide_y0 = send(wide, "y", 1)
    far_rows = send(rows, "x", 1)
    pack_y1 = send(pack_1, "y", 1)
    pack_3 = send(pack_2, "z", 1)
    pack_y2 = send(pack_2, "y", 1)
    both_2 = send(both, "z", 2)
    both_1 = send(both, "z", 1)
    near_rows = send(rows, "core", 1)
    row_parts = [rows, near_rows, far_rows, send(far_rows, "core", 1)]
    pack_y3 = send(pack_3, "y", 1)
    both_y1 = send(both_1, "y", 1)
    both_3 = send(both_2, "z", 1)
    qkv_full, out_part, gain_rows = call(
        open_pack,
        [Keep(sds(768, 576)), sds(192, 768), Keep(sds(8, 768, dtype=F32))],
        [pack, pack_1, pack_2, pack_3, wide_y0, pack_y1, pack_y2, pack_y3],
        [pltpu.VMEM((192, 768), F32), pltpu.VMEM((8, 16, 768), F32)],
    )
    far_out = send(out_part, "x", 1)
    attended, projected, probs, tokens, unit_low = call(
        attend,
        [sds(736, 192), *keep(sds(736, 576), sds(6, 368, 368), sds(736, 768), sds(736, 768))],
        [*keep(*row_parts), special, image_ids.reshape(8, 88), *keep(qkv_full, gain_rows)],
        [pltpu.VMEM((736, 768), F32)],
    )
    far_heads = send(attended, "x", 1)
    both_y2 = send(both_2, "y", 1)
    out_parts = [
        out_part, send(out_part, "core", 1),
        far_out, send(far_out, "core", 1),
    ]
    both_y3 = send(both_3, "y", 1)
    out_full, out_mine, grad_mlp, cots = call(
        order_out,
        keep(sds(768, 768), sds(192, 768), sds(736, 768), sds(736, 768)),
        [*out_parts, *keep(*row_parts), cot_special, Keep(gain_rows)],
        [pltpu.VMEM((768, 768), F32)],
    )
    heads = [
        attended, send(attended, "core", 1),
        far_heads, send(far_heads, "core", 1),
    ]
    both_chunks = [both, both_1, both_2, both_3, wide_y0, both_y1, both_y2, both_y3]
    normed_mlp, branch, own_rows = call(
        branch_rows,
        keep(sds(736, 768), sds(736, 768), sds(208, 768, dtype=F32)),
        [*heads, *keep(out_full, tokens, gain_rows)],
        [pltpu.VMEM((736, 768), F32)],
    )
    active, slope, up_full, down_full = call(
        raise_rows,
        keep(sds(736, 768), sds(736, 768, dtype=F32), sds(768, 768), sds(768, 768)),
        [Keep(normed_mlp), *both_chunks],
        [pltpu.VMEM((736, 768), F32)],
    )
    half = [sds(4, 96, 768), Keep(sds(4, 96, 768, dtype=F32))]
    rows_split = [sds(416, 768), Keep(sds(416, 768, dtype=F32))]

    def make_down(active):
        return call(
            down_grads,
            half,
            keep(active, grad_mlp),
            [pltpu.VMEM((768, 768), F32)],
        )

    sum_away, sum_kept, grad_hidden = call(
        lower_rows,
        [sds(368, 768), *keep(sds(368, 768, dtype=F32), sds(736, 768))],
        keep(slope, grad_mlp, up_full, down_full),
        [pltpu.VMEM((2, 368, 768), F32)],
    )
    sum_came = send(sum_away, "core", 1)
    chip_sum = call(add_rows, [sds(368, 768)], [Keep(sum_kept), sum_came])[0]
    chip_came = send(chip_sum, "x", 1)
    down_away, down_kept = make_down(active)
    down_came = send(down_away, "z", 1)
    up_away, up_kept = call(
        up_grads,
        half,
        keep(normed_mlp, grad_hidden),
        [pltpu.VMEM((768, 768), F32)],
    )
    up_came = send(up_away, "y", 1)
    m_away, m_kept, scale_mlp, chosen = call(
        mlp_rows,
        [*rows_split, *keep(sds(8, 768, dtype=F32), sds(736, 192))],
        [*keep(active, down_full, cots), *heads],
        [pltpu.VMEM((736, 768), F32), pltpu.VMEM((4, 208, 768), F32)],
    )
    m_came = send(m_away, "core", 1)
    down_two, down_away = call(
        sum_fours,
        [Keep(sds(2, 96, 768, dtype=F32)), sds(2, 96, 768)],
        [Keep(down_kept), down_came],
    )
    down_came = send(down_away, "z", 2)
    sum_own = call(add_pair, [sds(368, 768)], [chip_sum, chip_came])[0]
    sum_near = send(sum_own, "core", 1)
    grad_rows, grad_heads, grad_v, a_away, a_kept = call(
        branch_back,
        [
            *keep(sds(208, 768, dtype=F32), sds(736, 192), sds(736, 192)),
            sds(4, 112, 384), Keep(sds(4, 112, 384, dtype=F32)),
        ],
        [
            sum_own, sum_near, *keep(tokens, cots, branch, gain_rows, out_mine, probs, unit_low), *keep(scale_mlp, chosen),
        ],
        [
            pltpu.VMEM((736, 768), F32), pltpu.VMEM((736, 768), BF16),
            pltpu.VMEM((768, 768), F32), pltpu.VMEM((192, 768), F32), pltpu.VMEM((896, 384), F32),
        ],
    )
    a_came = send(a_away, "y", 1)
    up_steps = halve_y(up_kept, up_came)
    down_last = side_y(down_two, down_came)
    grad_qk, b_away, b_kept = call(
        score_back,
        [Keep(sds(736, 384)), sds(4, 96, 384), Keep(sds(4, 96, 384, dtype=F32))],
        keep(probs, projected, grad_heads, unit_low),
        [pltpu.VMEM((768, 384), F32)],
    )
    b_came = send(b_away, "y", 1)
    a_pair = halve_y(a_kept, a_came)
    h_away, h_kept = call(
        project_back,
        rows_split,
        keep(grad_qk, grad_v, qkv_full),
        [pltpu.VMEM((736, 768), F32), pltpu.VMEM((4, 208, 768), F32)],
    )
    h_came = send(h_away, "core", 1)
    stay, go = call(
        add_pieces,
        [Keep(sds(416, 768, dtype=F32)), sds(416, 768)],
        [Keep(m_kept), m_came, Keep(h_kept), h_came],
    )
    far_rows = send(go, "x", 1)
    b_steps = add_y(b_kept, b_came)
    a_last = halve_z(a_pair)
    up_last = halve_z(up_steps)
    grad_down = add_last(down_last)
    pieces = [Keep(sds(32, 768, dtype=F32)), sds(32, 768), sds(64, 768)]
    held = pltpu.VMEM((4, 32, 768), F32)
    own, near, far = call(pick_up, pieces, [Keep(up_last[0]), up_last[1]], [held])
    came_far = send(far, "x", 1)
    came_near, came_near_far = send(near, "core", 1), send(came_far, "core", 1)
    grad_up, norm_grad = call(
        join_up,
        [sds(24, 3072, dtype=F32), Keep(sds(1, 24, dtype=F32))],
        [Keep(own), came_near, came_far, came_near_far, w_up, gains],
        [held],
    )
    own, near, far, grad_out = call(
        pick_attention,
        [*pieces, sds(24, 768, dtype=F32)],
        [Keep(a_last[0]), a_last[1], Keep(b_steps[0]), *b_steps[1:]],
        [held, pltpu.VMEM((112, 768), F32)],
    )
    came_far = send(far, "x", 1)
    came_near, came_near_far = send(near, "core", 1), send(came_far, "core", 1)
    out_patches, out_special, grad_patches, grad_special = call(
        finish_rows,
        [
            sds(176, 768), sds(20, 768), sds(176, 768, dtype=F32), sds(20, 768, dtype=F32),
        ],
        [Keep(stay), far_rows, *keep(own_rows, grad_rows), patches, special, Keep(gain_rows)],
    )
    grad_qkv, grad_gains = call(
        join_attention,
        [sds(24, 2304, dtype=F32), sds(4, 24, dtype=F32)],
        [Keep(own), came_near, came_far, came_near_far, w_qkv, gains, Keep(norm_grad)],
        [held],
    )
    return (
        out_patches, out_special, grad_patches, grad_special,
        grad_qkv, grad_out, grad_up, grad_down, grad_gains,
    )


def solution(mesh):
    placed = (
        P(("dp", "blk"), None),
        P("dp", None),
        P("dp"),
        P(("dp", "blk"), None),
        P(("dp", "blk"), None),
        P(("dp", "blk"), None),
        P(("dp", "blk"), None),
        P(None, ("dp", "blk")),
        P(("dp", "blk"), None),
        P("dp", None),
    )
    whole = dict(mesh.shape) != {"dp": 8, "blk": 4}
    return jax.shard_map(
        on_device if whole else on_device_split,
        mesh=mesh,
        in_specs=placed,
        out_specs=(
            P(("dp", "blk"), None),
            P("dp", None),
            P(("dp", "blk"), None),
            P("dp", None),
            P(("dp", "blk"), None),
            P(("dp", "blk"), None),
            P(("dp", "blk"), None),
            P(("dp", "blk"), None),
            P(None, ("dp", "blk")),
        ),
        check_vma=False,
    )
```

```python
import jax
import jax.numpy as jnp
from jax import lax
from jax.experimental import pallas as pl
from jax.experimental.pallas import tpu as pltpu
from jax.sharding import PartitionSpec as P

HEAD_DIM = 64
SPECIAL = 5
MICRO = 2
TOK_MB = 88

SCORE_SCALE = 0.125
MASKED = -1e30
EPSILON = 1e-06

BF16 = jnp.bfloat16
F32 = jnp.float32


def merged(shard, axis, combine):
    everything = jax.tree.map(
        lambda part, kind: lax.all_gather(part.astype(kind), axis),
        shard,
        (jnp.bfloat16, jnp.bfloat16, jnp.bfloat16),
    )

    def take(k):
        return jax.tree.map(lambda part, own: part[k].astype(own.dtype), everything, shard)

    return lax.fori_loop(
        1, lax.axis_size(axis), lambda k, so_far: combine(so_far, take(k)), take(0)
    )


def from_behind(shard, axis, by):
    peers = lax.axis_size(axis)
    return lax.ppermute(shard, axis, [(i, (i + by) % peers) for i in range(peers)])


def norm_rows(values, gain_row):
    centre = values - jnp.mean(values, -1, keepdims=True)
    spread = jnp.mean(centre * centre, -1, keepdims=True)
    return centre * lax.rsqrt(spread + EPSILON) * gain_row


def split_heads(matrix):
    return matrix.reshape(matrix.shape[0], -1, HEAD_DIM)


def widen(per_head):
    return jnp.repeat(per_head.T, HEAD_DIM, axis=1)


def empty_state(length, head_count, feature_width):
    return (
        jnp.full((head_count, length), MASKED, jnp.float32),
        jnp.zeros((head_count, length), jnp.float32),
        jnp.zeros((length, feature_width), jnp.float32),
    )


def online(carried, queries, query_ids, key_rows, value_rows, key_ids):
    top_score, totals, accumulated = carried
    same_image = (query_ids[:, None] == key_ids[None, :])[None]
    scores = (
        jnp.einsum(
            "qhd,khd->hqk",
            split_heads(queries),
            split_heads(key_rows),
            preferred_element_type=jnp.float32,
        )
        * SCORE_SCALE
    )
    scores = jnp.where(same_image, scores, MASKED)
    new_top = jnp.maximum(top_score, jnp.max(scores, -1))
    weights = jnp.where(same_image, jnp.exp(scores - new_top[..., None]), 0.0)
    factor = jnp.exp(top_score - new_top)
    totals = totals * factor + jnp.sum(weights, -1)
    mixture = jnp.einsum(
        "hqk,khd->qhd",
        weights.astype(jnp.bfloat16),
        split_heads(value_rows),
        preferred_element_type=jnp.float32,
    )
    accumulated = accumulated * widen(factor) + mixture.reshape(accumulated.shape)
    return (new_top, totals, accumulated)


def combine(former, latter):
    highest = jnp.maximum(former[0], latter[0])
    scale_former = jnp.exp(former[0] - highest)
    scale_latter = jnp.exp(latter[0] - highest)
    return (
        highest,
        former[1] * scale_former + latter[1] * scale_latter,
        former[2] * widen(scale_former) + latter[2] * widen(scale_latter),
    )


def finish(carried):
    top_score, totals, accumulated = carried
    return (accumulated / widen(totals), top_score + jnp.log(totals))


def block_grads(queries, grad_attn, log_total, row_delta, query_ids, key_rows, value_rows, key_ids):
    same_image = (query_ids[:, None] == key_ids[None, :])[None]
    q_heads = split_heads(queries)
    g_heads = split_heads(grad_attn)
    scores = (
        jnp.einsum(
            "qhd,khd->hqk", q_heads, split_heads(key_rows), preferred_element_type=jnp.float32
        )
        * SCORE_SCALE
    )
    probabilities = jnp.where(same_image, jnp.exp(scores - log_total[..., None]), 0.0)
    grad_prob = jnp.einsum(
        "qhd,khd->hqk", g_heads, split_heads(value_rows), preferred_element_type=jnp.float32
    )
    dscore = (probabilities * (grad_prob - row_delta[..., None])).astype(jnp.bfloat16)
    grad_query = (
        jnp.einsum(
            "hqk,khd->qhd", dscore, split_heads(key_rows), preferred_element_type=jnp.float32
        ).reshape(queries.shape[0], -1)
        * SCORE_SCALE
    )
    grad_key = (
        jnp.einsum("hqk,qhd->khd", dscore, q_heads, preferred_element_type=jnp.float32).reshape(
            key_rows.shape[0], -1
        )
        * SCORE_SCALE
    )
    grad_value = jnp.einsum(
        "hqk,qhd->khd",
        probabilities.astype(jnp.bfloat16),
        g_heads,
        preferred_element_type=jnp.float32,
    ).reshape(key_rows.shape[0], -1)
    return (grad_query, grad_key, grad_value)


def fetch_weights(w_qkv, w_out, w_up, w_down, gains):
    return (
        lax.all_gather(w_qkv, ("dp", "blk"), axis=0, tiled=True),
        lax.all_gather(w_out, ("dp", "blk"), axis=0, tiled=True),
        lax.all_gather(w_up, ("dp", "blk"), axis=0, tiled=True),
        lax.all_gather(w_down, ("dp", "blk"), axis=0, tiled=True),
        lax.all_gather(gains, ("dp", "blk"), axis=1, tiled=True),
    )


def reduce_grads(grad_terms):
    g_qkv, g_out, g_up, g_down, g_gains = grad_terms
    return (
        lax.psum_scatter(g_qkv, ("dp", "blk"), scatter_dimension=0, tiled=True),
        lax.psum_scatter(g_out, ("dp", "blk"), scatter_dimension=0, tiled=True),
        lax.psum_scatter(g_up, ("dp", "blk"), scatter_dimension=0, tiled=True),
        lax.psum_scatter(g_down, ("dp", "blk"), scatter_dimension=0, tiled=True),
        lax.psum_scatter(g_gains, ("dp", "blk"), scatter_dimension=1, tiled=True),
    )


def contract_rows(left_rows, right_rows):
    return jnp.einsum("ra,rb->ab", left_rows, right_rows, preferred_element_type=jnp.float32)


def row_delta_of(grad_attn, attended):
    product = grad_attn.astype(jnp.float32) * attended
    return product.reshape(product.shape[0], -1, HEAD_DIM).sum(-1).T


def on_device(
    patches, special, image_ids, w_qkv, w_out, w_up, w_down, gains, cot_patches, cot_special
):
    cycle_size = lax.axis_size("blk")
    cycle_index = lax.axis_index("blk")
    width = w_out.shape[1]
    head_count = width // HEAD_DIM
    tok_rows = TOK_MB
    spec_rows = special.shape[0] // MICRO
    ids_group = image_ids.reshape(cycle_size, MICRO, tok_rows)
    spec_ids = jnp.arange(spec_rows, dtype=jnp.int32) // SPECIAL
    row_weight = jnp.concatenate(
        [jnp.ones((tok_rows,), jnp.float32), jnp.full((spec_rows,), 1.0 / cycle_size, jnp.float32)]
    )
    row_weight_low = row_weight.astype(jnp.bfloat16)[:, None]
    summed_terms = None
    shard_terms = None
    out_parts = []
    spec_parts = []
    grad_parts = []
    grad_spec_parts = []
    for micro_index in range(MICRO):
        full_weights = fetch_weights(w_qkv, w_out, w_up, w_down, gains)
        qkv_full, out_full, up_full, down_full, gains_full = full_weights
        gain_rows = gains_full.astype(jnp.float32)
        tokens = jnp.concatenate(
            [
                patches[micro_index * tok_rows : (micro_index + 1) * tok_rows],
                special[micro_index * spec_rows : (micro_index + 1) * spec_rows],
            ],
            0,
        ).astype(jnp.float32)
        ids_flat = ids_group[:, micro_index].reshape(-1)
        patch_ids = lax.dynamic_slice_in_dim(ids_flat, cycle_index * tok_rows, tok_rows)
        normed = norm_rows(tokens, gain_rows[0]).astype(jnp.bfloat16)
        projected = jnp.dot(normed, qkv_full, preferred_element_type=jnp.float32).astype(
            jnp.bfloat16
        )
        patch_q = projected[:tok_rows, :width]
        patch_k = projected[:tok_rows, width : 2 * width]
        patch_v = projected[:tok_rows, 2 * width :]
        spec_q = projected[tok_rows:, :width]
        spec_k = projected[tok_rows:, width : 2 * width]
        spec_v = projected[tok_rows:, 2 * width :]
        start_state = online(
            empty_state(tok_rows, head_count, width), patch_q, patch_ids, spec_k, spec_v, spec_ids
        )
        partial_value = start_state
        key_rows = lax.all_gather(patch_k, "blk", axis=0, tiled=True)
        value_rows = lax.all_gather(patch_v, "blk", axis=0, tiled=True)
        length = key_rows.shape[0]
        key_ids = ids_flat
        blocks = length // tok_rows

        def visit_block(running, block_item):
            return (
                online(running, patch_q, patch_ids, block_item[0], block_item[1], block_item[2]),
                None,
            )

        partial_value, unused = lax.scan(
            visit_block,
            partial_value,
            (
                key_rows.reshape(blocks, tok_rows, -1),
                value_rows.reshape(blocks, tok_rows, -1),
                key_ids.reshape(blocks, tok_rows),
            ),
        )
        spec_top, spec_total, spec_accum = online(
            empty_state(spec_rows, head_count, width), spec_q, spec_ids, patch_k, patch_v, patch_ids
        )
        spec_state = merged((spec_top, spec_total, spec_accum), "blk", combine)
        spec_state = online(spec_state, spec_q, spec_ids, spec_k, spec_v, spec_ids)
        patch_attn, patch_lse = finish(partial_value)
        spec_attn, spec_lse = finish(spec_state)
        attended = jnp.concatenate([patch_attn, spec_attn], 0)
        attended_low = attended.astype(jnp.bfloat16)
        branch = jnp.dot(attended_low, out_full, preferred_element_type=jnp.float32)
        middle = tokens + gain_rows[1] * branch
        normed_mlp = norm_rows(middle, gain_rows[2]).astype(jnp.bfloat16)
        hidden = jnp.dot(normed_mlp, up_full, preferred_element_type=jnp.float32)
        active = jax.nn.gelu(hidden, approximate=False).astype(jnp.bfloat16)
        mlp_out = jnp.dot(active, down_full, preferred_element_type=jnp.float32)
        final = middle + gain_rows[3] * mlp_out
        out_parts.append(final[:tok_rows].astype(jnp.bfloat16))
        spec_parts.append(final[tok_rows:].astype(jnp.bfloat16))
        upstream = jnp.concatenate(
            [
                cot_patches[micro_index * tok_rows : (micro_index + 1) * tok_rows],
                cot_special[micro_index * spec_rows : (micro_index + 1) * spec_rows],
            ],
            0,
        ).astype(jnp.float32)
        grad_mlp = (gain_rows[3] * upstream).astype(jnp.bfloat16)
        g_down = contract_rows(active, grad_mlp * row_weight_low)
        grad_active = jnp.einsum(
            "rd,fd->rf", grad_mlp, down_full, preferred_element_type=jnp.float32
        )
        unused_value, gelu_pull = jax.vjp(
            lambda pre_act: jax.nn.gelu(pre_act, approximate=False), hidden
        )
        grad_hidden = gelu_pull(grad_active)[0].astype(jnp.bfloat16)
        g_up = contract_rows(normed_mlp, grad_hidden * row_weight_low)
        grad_normed_mlp = jnp.einsum(
            "rf,df->rd", grad_hidden, up_full, preferred_element_type=jnp.float32
        )
        unused_value, norm_pull_mlp = jax.vjp(
            lambda rows_in: norm_rows(rows_in, gain_rows[2]), middle
        )
        grad_middle = upstream + norm_pull_mlp(grad_normed_mlp)[0]
        g_ln2 = jnp.sum(row_weight[:, None] * grad_normed_mlp * norm_rows(middle, 1.0), 0)
        g_ls2 = jnp.sum(row_weight[:, None] * upstream * mlp_out, 0)
        g_ls1 = jnp.sum(row_weight[:, None] * grad_middle * branch, 0)
        grad_branch = (gain_rows[1] * grad_middle).astype(jnp.bfloat16)
        g_out = contract_rows(attended_low, grad_branch * row_weight_low)
        grad_attended = jnp.einsum(
            "re,de->rd", grad_branch, out_full, preferred_element_type=jnp.float32
        ).astype(jnp.bfloat16)
        all_delta = row_delta_of(grad_attended, attended)
        patch_delta = all_delta[:, :tok_rows]
        spec_delta = all_delta[:, tok_rows:]
        patch_grad_attn = grad_attended[:tok_rows]
        spec_grad_attn = grad_attended[tok_rows:]
        grad_pq_first, grad_sk_part, grad_sv_part = block_grads(
            patch_q, patch_grad_attn, patch_lse, patch_delta, patch_ids, spec_k, spec_v, spec_ids
        )
        grad_sq_part, grad_pk_local, grad_pv_local = block_grads(
            spec_q, spec_grad_attn, spec_lse, spec_delta, spec_ids, patch_k, patch_v, patch_ids
        )
        sum_sq, sum_sk, sum_sv = (
            lax.psum(grad_sq_part.astype(jnp.bfloat16), "blk").astype(jnp.float32),
            lax.psum(grad_sk_part.astype(jnp.bfloat16), "blk").astype(jnp.float32),
            lax.psum(grad_sv_part.astype(jnp.bfloat16), "blk").astype(jnp.float32),
        )
        grad_sq_own, grad_sk_own, grad_sv_own = block_grads(
            spec_q, spec_grad_attn, spec_lse, spec_delta, spec_ids, spec_k, spec_v, spec_ids
        )

        def cycle_step(hop_index, carried):
            keys_now, values_now, grad_keys, grad_values, grad_queries = carried
            source = (cycle_index - hop_index) % cycle_size
            key_ids = lax.dynamic_slice_in_dim(ids_flat, source * tok_rows, tok_rows)
            term_q, term_k, term_v = block_grads(
                patch_q,
                patch_grad_attn,
                patch_lse,
                patch_delta,
                patch_ids,
                keys_now,
                values_now,
                key_ids,
            )
            keys_now, values_now = from_behind((keys_now, values_now), "blk", 1)
            grad_keys, grad_values = (
                from_behind((grad_keys + term_k).astype(jnp.bfloat16), "blk", 1).astype(
                    jnp.float32
                ),
                from_behind((grad_values + term_v).astype(jnp.bfloat16), "blk", 1).astype(
                    jnp.float32
                ),
            )
            return (keys_now, values_now, grad_keys, grad_values, grad_queries + term_q)

        zero_rows = jnp.zeros((tok_rows, width), jnp.float32)
        unused_keys, unused_values, grad_pk, grad_pv, grad_pq = lax.fori_loop(
            0, cycle_size, cycle_step, (patch_k, patch_v, zero_rows, zero_rows, grad_pq_first)
        )
        grad_pk = grad_pk + grad_pk_local
        grad_pv = grad_pv + grad_pv_local
        grad_patch_qkv = jnp.concatenate([grad_pq, grad_pk, grad_pv], 1)
        grad_spec_qkv = jnp.concatenate(
            [sum_sq + grad_sq_own, sum_sk + grad_sk_own, sum_sv + grad_sv_own], 1
        )
        grad_projected = jnp.concatenate([grad_patch_qkv, grad_spec_qkv], 0).astype(jnp.bfloat16)
        g_qkv = contract_rows(normed, grad_projected * row_weight_low)
        grad_normed = jnp.einsum(
            "re,de->rd", grad_projected, qkv_full, preferred_element_type=jnp.float32
        )
        unused_value, norm_pull_attn = jax.vjp(
            lambda rows_in: norm_rows(rows_in, gain_rows[0]), tokens
        )
        grad_tokens = grad_middle + norm_pull_attn(grad_normed)[0]
        g_ln1 = jnp.sum(row_weight[:, None] * grad_normed * norm_rows(tokens, 1.0), 0)
        grad_parts.append(grad_tokens[:tok_rows])
        grad_spec_parts.append(grad_tokens[tok_rows:])
        grad_terms = (g_qkv, g_out, g_up, g_down, jnp.stack([g_ln1, g_ls1, g_ln2, g_ls2], 0))
        summed_terms = (
            grad_terms
            if summed_terms is None
            else tuple((held + extra for held, extra in zip(summed_terms, grad_terms)))
        )
    shard_terms = reduce_grads(summed_terms)
    return (
        jnp.concatenate(out_parts, 0),
        jnp.concatenate(spec_parts, 0),
        jnp.concatenate(grad_parts, 0),
        jnp.concatenate(grad_spec_parts, 0),
        shard_terms[0],
        shard_terms[1],
        shard_terms[2],
        shard_terms[3],
        shard_terms[4],
    )


PAD_ID = 99
PLAN = (
    (9.0, ()), (0, (0,)), (0, (0,)), (0, (2,)), (21.0, (2,)), (0, ()), (0, ()), (0, ()), (0, (0,)),
    (0, (2, 4, 5)), (0, ()), (0, (8,)), (0, ()), (0, ()), (0, (9, 11)), (0, (7,)), (0, ()),
    (0, (10, 15, 16)), (0, ()), (36.0, (12,)), (0, ()), (2.4, ()), (0, (9,)), (0, (17,)), (0, (21,)),
    (0, (21,)), (0, (21, 6, 18)), (4.8, ()), (0, (27,)), (0, (27,)), (0.001, (26, 28, 21)), (0.001, ()),
    (1.11, ()), (0, ()), (2.7, ()), (0, ()), (0.002, ()), (0, (30,)), (0.6, (29,)), (0, (34,)), (0.6, ()),
    (0, ()), (0.07, ()), (0, ()), (0.27, ()), (0, ()), (0.4, ()), (0, ()), (21.0, ()), (0, ()),
    (7.0, (32,)), (0, (45,)), (0.42, ()), (0, ()), (1.05, ()), (0, ()), (0.0325, ()), (0, ()), (0.18, ()),
    (0, (56,)), (0.105, (58,)), (0, ()), (0, ()), (0, ()), (2.1, ()), (0, (47,)), (2.1, ()), (0, ()),
    (2.1, ()), (0.35, (59,)), (0, ()), (0, (69,)), (0, (55, 65)), (1.5, ()), (9.0, (68,)), (0, (68,)),
    (0, ()), (0, (70,)), (0.001, ()), (30, ()),
)
STEPS = []


def plan():
    us, steps = PLAN[len(STEPS)]
    return us, [STEPS[i] for i in steps]


def mm(a, b):
    return jnp.dot(a, b, preferred_element_type=F32)


def mm_nt(a, b):
    return lax.dot_general(a, b, (((1,), (1,)), ((), ())), preferred_element_type=F32)


def mm_tn(a, b):
    return lax.dot_general(a, b, (((0,), (0,)), ((), ())), preferred_element_type=F32)


def here():
    place = lax.axis_index("blk")
    group = lax.axis_index("dp")
    return place, place // 2, place % 2, group // 2, group % 2


def chunk_index(slot, z, y):
    return (z ^ (slot % 4)) * 2 + (y ^ (slot // 4))


def row_blocks(block, among=slice(0, 736)):
    return [slice(first, first + block) for first in range(among.start, among.stop, block)]


def fold(rows):
    return rows.reshape(rows.shape[0] // 8, 8, rows.shape[1]).sum(0)


class Keep:
    def __init__(self, value):
        self.value = value


class Far:
    def __init__(self, value):
        self.value = value


class Load:
    def __init__(self, buffer, copy):
        self.buffer, self.copy, self.waited = buffer, copy, False

    def ready(self):
        if not self.waited:
            self.copy.wait()
            self.waited = True
        return self.buffer


def call(kernel, outs, ins, scratch=(), limit=20):
    us, after = plan()
    far = [i for i, v in enumerate(ins) if isinstance(v, Far)]
    plain = [v.value if isinstance(v, (Far, Keep)) else v for v in ins]
    near, away = pl.BlockSpec(memory_space=pltpu.VMEM), pl.BlockSpec(memory_space=pltpu.HBM)
    room = [pltpu.VMEM(plain[i].shape, plain[i].dtype) for i in far]
    if far:
        room.append(pltpu.SemaphoreType.DMA((len(far),)))

    def body(*refs):
        given = [*refs[: len(ins)], *refs[len(ins) + len(after) :]]
        own = given[len(ins) + len(outs) + len(scratch) :]
        given = given[: len(ins) + len(outs) + len(scratch)]
        for k, i in enumerate(far):
            copy = pltpu.make_async_copy(given[i], own[k], own[-1].at[k])
            copy.start()
            given[i] = Load(own[k], copy)
        kernel(*given)

    def placed(v):
        if isinstance(v, Keep):
            return pltpu.with_memory_space_constraint(v.value, pltpu.VMEM)
        return pltpu.with_memory_space_constraint(v.value, pltpu.HBM) if isinstance(v, Far) else v

    made_arrays = pl.pallas_call(
        body,
        out_shape=tuple(
            pltpu.VMEM(v.value.shape, v.value.dtype) if isinstance(v, Keep) else v for v in outs
        ),
        in_specs=[away if i in far else near for i in range(len(ins))]
        + [pl.BlockSpec(memory_space=pl.ANY)] * len(after),
        out_specs=tuple(near for _ in outs),
        scratch_shapes=[*scratch, *room],
        compiler_params=pltpu.CompilerParams(vmem_limit_bytes=limit * 2**20),
        cost_estimate=pl.CostEstimate(flops=int(us * 10**9), bytes_accessed=0, transcendentals=0),
        name=kernel.__name__,
    )(*[placed(v) for v in ins], *after)
    STEPS.append(made_arrays[0])
    return made_arrays


def keep(*arrays):
    return [Keep(v) for v in arrays]


def sds(*shape, dtype=BF16):
    return jax.ShapeDtypeStruct(shape, dtype)


def pick_pieces(w_qkv, w_up, gains, patches, cots, own, near, far, rows, held):
    place = here()[0]
    held[...] = jnp.zeros_like(held)
    up = w_up.ready()[...].astype(F32)
    qkv = w_qkv.ready()[...].astype(F32)
    gain = gains.ready()[...].astype(F32)
    for b in range(4):
        for d in range(8):
            held[b, 0:24, d * 96 : d * 96 + 96] = up[:, d * 384 + b * 96 : d * 384 + b * 96 + 96]
        for part in range(3):
            held[b, 24:48, part * 192 : part * 192 + 192] = qkv[
                :, part * 768 + b * 192 : part * 768 + b * 192 + 192
            ]
        held[b, 24:28, 576:600] = gain
    own[...] = held[place].astype(BF16)
    near[...] = held[place ^ 1].astype(BF16)
    far[0:48, :] = held[place ^ 2].astype(BF16)
    far[48:96, :] = held[place ^ 3].astype(BF16)
    rows[0:176, :] = patches.ready()[...]
    rows[176:352, :] = cots.ready()[...]


def join_pieces(own, near, far, near_far, w_out, w_down, pack, both, wide, pack_f, up_f):
    place = here()[0]
    pack_f[96:112, :] = jnp.zeros((16, 768), F32)
    pieces = (
        own[...].astype(F32),
        near[...].astype(F32),
        far[0:48, :].astype(F32),
        near_far[48:96, :].astype(F32),
    )
    for k, piece in enumerate(pieces):
        source = place ^ k
        at = pl.ds(pl.multiple_of(source * 24, 8), 24)
        up_f[at, :] = piece[0:24]
        pack_f[at, 0:576] = piece[24:48, 0:576]
        lanes = pl.ds(pl.multiple_of(source * 128, 128), 128)
        pack_f[96:104, lanes] = piece[24:32, 576:704]
    out = w_out[...].astype(F32)
    for i in range(4):
        pack_f[i * 24 : i * 24 + 24, 576:768] = out[:, i * 192 : i * 192 + 192]
    pack[...] = pack_f[...].astype(BF16)
    both[0:96, :] = up_f[...].astype(BF16)
    both[96:192, :] = w_down[...]
    wide[0:112, :] = pack[...]
    wide[112:304, :] = both[...]


def open_pack(*refs):
    chunks, (w_qkv, w_out, gain_rows, out_f, gain_f) = refs[:8], refs[8:]
    _, _, _, z, y = here()
    for slot, chunk in enumerate(chunks):
        d = chunk_index(slot, z, y)
        w_qkv[pl.ds(pl.multiple_of(d * 96, 96), 96), :] = chunk[0:96, 0:576]
        tail = chunk[0:96, 576:768].astype(F32)
        for i in range(4):
            out_f[pl.ds(pl.multiple_of(d * 24, 8), 24), i * 192 : i * 192 + 192] = tail[
                i * 24 : i * 24 + 24
            ]
        gain_f[d] = chunk[96:112, :].astype(F32)
    w_out[...] = out_f[...].astype(BF16)
    gain_rows[...] = jnp.zeros_like(gain_rows)
    for d in range(8):
        for b in range(4):
            at = (d * 4 + b) * 24
            gain_rows[0:4, at : at + 24] = gain_f[d, 0:4, b * 128 : b * 128 + 24]


def normalise(rows):
    centre = rows - jnp.mean(rows, -1, keepdims=True)
    spread = jnp.mean(centre * centre, -1, keepdims=True)
    scale = lax.rsqrt(spread + EPSILON)
    return centre * scale, scale


def place_rows(scratch, blocks, tail, first):
    place = here()[0]
    for k, block in enumerate(blocks):
        rows = block[first : first + 176, :].astype(F32)
        source = place ^ k
        for m in range(MICRO):
            scratch[pl.ds(pl.multiple_of(m * 368 + source * 88, 8), 88), :] = rows[m * 88 : m * 88 + 88]
    rows = tail[...].astype(F32)
    for m in range(MICRO):
        scratch[m * 368 + 352 : m * 368 + 368, :] = jnp.zeros((16, 768), F32)
        scratch[m * 368 + 352 : m * 368 + 362, :] = rows[m * 10 : m * 10 + 10]


def turned(line):
    count = max(line.shape)
    down = lax.broadcasted_iota(jnp.int32, (count, count), 0)
    across = lax.broadcasted_iota(jnp.int32, (count, count), 1)
    return jnp.sum(jnp.where(down == across, line, 0.0), line.shape.index(count), keepdims=True)


def attend(
    rows_0, rows_1, rows_2, rows_3, tail, ids, w_qkv, gain_rows,
    attended, projected, probs, tokens, unit_low, rows_f, normed,
):
    place_rows(rows_f, (rows_0, rows_1, rows_2, rows_3), tail, 0)
    gain = gain_rows[0:1, :]
    slot = lax.broadcasted_iota(jnp.int32, (1, 16), 1)
    tail_ids = jnp.where(slot < 2 * SPECIAL, (slot >= SPECIAL).astype(jnp.int32), PAD_ID)
    for m in range(MICRO):
        at = slice(m * 368, m * 368 + 368)
        row = jnp.concatenate([ids[b * 2 + m : b * 2 + m + 1, :] for b in range(4)] + [tail_ids], 1)
        row = row.astype(F32)
        bias = jnp.where(turned(row) == row, 0.0, MASKED)
        for block in row_blocks(16, at):
            rows = rows_f[block, :]
            tokens[block, :] = rows.astype(BF16)
            unit = normalise(rows)[0]
            unit_low[block, :] = unit.astype(BF16)
            normed[block, :] = (unit * gain).astype(BF16)
        qkv = mm(normed[at, :], w_qkv[...])
        qkv = jnp.concatenate([qkv[:, 0:192] * SCORE_SCALE, qkv[:, 192:576]], -1).astype(BF16)
        projected[at, :] = qkv
        heads = []
        for h in range(3):
            q = qkv[:, h * 64 : h * 64 + 64]
            k = qkv[:, 192 + h * 64 : 192 + h * 64 + 64]
            v = qkv[:, 384 + h * 64 : 384 + h * 64 + 64]
            scores = mm_nt(q, k) + bias
            weights = jnp.exp(scores - jnp.max(scores, -1, keepdims=True))
            weights = weights * (1.0 / jnp.sum(weights, -1, keepdims=True))
            weights = weights.astype(BF16)
            probs[m * 3 + h] = weights
            heads.append(mm(weights, v))
        attended[at, :] = jnp.concatenate(heads, -1).astype(BF16)


def order_out(
    out_0, out_1, out_2, out_3, rows_0, rows_1, rows_2, rows_3, cot_tail, gain_rows,
    ordered, mine, grad_mlp, cots, out_f,
):
    place = here()[0]
    for k, part in enumerate((out_0, out_1, out_2, out_3)):
        source = place ^ k
        rows = part[...].astype(F32)
        for d in range(8):
            at = pl.multiple_of((d * 4 + source) * 24, 8)
            out_f[pl.ds(at, 24), :] = rows[d * 24 : d * 24 + 24]
    ordered[...] = out_f[...].astype(BF16)
    mine[...] = out_f[pl.ds(pl.multiple_of(place * 192, 8), 192), :].astype(BF16)
    place_rows(out_f, (rows_0, rows_1, rows_2, rows_3), cot_tail, 176)
    gain = gain_rows[3:4, :]
    for at in row_blocks(32):
        rows = out_f[at, :]
        cots[at, :] = rows.astype(BF16)
        grad_mlp[at, :] = (gain * rows).astype(BF16)


def branch_rows(
    head_0, head_1, head_2, head_3, w_out, tokens, gain_rows, normed, branch, own_rows, rows_f
):
    place = here()[0]
    gain_s, gain_n = gain_rows[1:2, :], gain_rows[2:3, :]
    for m in range(MICRO):
        group = slice(m * 368, m * 368 + 368)
        total = None
        for k, part in enumerate((head_0, head_1, head_2, head_3)):
            rows = w_out[pl.ds(pl.multiple_of((place ^ k) * 192, 16), 192), :]
            term = mm(part[group, :], rows)
            total = term if total is None else total + term
        rows_f[group, :] = total
        for at in row_blocks(16, group):
            a = rows_f[at, :]
            branch[at, :] = a.astype(BF16)
            rows = tokens[at, :].astype(F32) + gain_s * a
            rows_f[at, :] = rows
            normed[at, :] = (normalise(rows)[0] * gain_n).astype(BF16)
        for part, first in ((0, place * 88), (88, 352)):
            rows = 88 if part == 0 else 16
            own_rows[m * 104 + part : m * 104 + part + rows, :] = rows_f[
                pl.ds(pl.multiple_of(m * 368 + first, 8), rows), :
            ]


def raise_rows(*refs):
    normed, chunks = refs[0], refs[1:9]
    active, slope, w_up, w_down, rows_f = refs[9:]
    _, _, _, z, y = here()
    for slot, chunk in enumerate(chunks):
        d = chunk_index(slot, z, y)
        skip = chunk.shape[0] - 192
        w_up[pl.ds(pl.multiple_of(d * 96, 96), 96), :] = chunk[skip : skip + 96, :]
        w_down[pl.ds(pl.multiple_of(d * 96, 96), 96), :] = chunk[skip + 96 : skip + 192, :]
    for m in range(MICRO):
        at = slice(m * 368, m * 368 + 368)
        rows_f[at, :] = mm(normed[at, :], w_up[...])
    for at in row_blocks(32):
        u = rows_f[at, :]
        half = 0.5 + 0.5 * lax.erf(u * 0.7071067811865476)
        active[at, :] = (u * half).astype(BF16)
        slope[at, :] = half + u * (0.3989422804014327 * jnp.exp(-0.5 * u * u))


def down_grads(active, grad_mlp, away, kept, work):
    _, _, _, z, _ = here()
    work[...] = mm_tn(active[...], grad_mlp[...])
    for pair in range(2):
        for side in range(2):
            ours = pl.multiple_of(((z ^ (2 * pair)) * 2 + side) * 96, 8)
            theirs = pl.multiple_of(((z ^ (2 * pair + 1)) * 2 + side) * 96, 8)
            kept[pair * 2 + side] = work[pl.ds(ours, 96), :]
            away[pair * 2 + side] = work[pl.ds(theirs, 96), :].astype(BF16)


def sum_fours(kept, came, own, away):
    own[...] = kept[0:2] + came[0:2].astype(F32)
    away[...] = (kept[2:4] + came[2:4].astype(F32)).astype(BF16)


def sum_sides(kept, came, own, away):
    y = here()[4]
    own[...] = kept[y] + came[y].astype(F32)
    away[...] = (kept[1 - y] + came[1 - y].astype(F32)).astype(BF16)


def lower_rows(slope, grad_mlp, w_up, w_down, away, kept, grad_hidden, work):
    core = here()[2]
    for m in range(MICRO):
        at = slice(m * 368, m * 368 + 368)
        grad = mm_nt(grad_mlp[at, :], w_down[...])
        grad_hidden[at, :] = (slope[at, :] * grad).astype(BF16)
        work[m] = mm_nt(grad_hidden[at, :], w_up[...])
    away[...] = work[1 - core].astype(BF16)
    kept[...] = work[core]


def split_rows(pieces, place, away, kept):
    away[0:208, :] = pieces[place ^ 1].astype(BF16)
    away[208:416, :] = pieces[place ^ 3].astype(BF16)
    kept[0:208, :] = pieces[place]
    kept[208:416, :] = pieces[place ^ 2]


def cut_rows(rows_f, pieces):
    for b in range(4):
        for m in range(MICRO):
            pieces[b, m * 104 : m * 104 + 88, :] = rows_f[m * 368 + b * 88 : m * 368 + b * 88 + 88, :]
            pieces[b, m * 104 + 88 : m * 104 + 104, :] = rows_f[m * 368 + 352 : m * 368 + 368, :]


def halve(grad_f, y, away, kept, rows):
    for zz in range(4):
        other = pl.ds(pl.multiple_of((zz * 2 + 1 - y) * rows, 8), rows)
        ours = pl.ds(pl.multiple_of((zz * 2 + y) * rows, 8), rows)
        away[zz] = grad_f[other, 0 : away.shape[2]].astype(BF16)
        kept[zz] = grad_f[ours, 0 : away.shape[2]]


def up_grads(normed, grad_hidden, away, kept, work):
    y = here()[4]
    work[...] = mm_tn(normed[...], grad_hidden[...])
    halve(work, y, away, kept, 96)


def mlp_rows(
    active, w_down, cots, head_0, head_1, head_2, head_3,
    rows_away, rows_kept, scale_grad, chosen, work, pieces,
):
    place = here()[0]
    for m in range(MICRO):
        at = slice(m * 368, m * 368 + 368)
        work[at, :] = mm(active[at, :], w_down[...])
    total = jnp.zeros((8, 768), F32)
    for at in row_blocks(32):
        total = total + fold(cots[at, :].astype(F32) * work[at, :])
    scale_grad[...] = total
    cut_rows(work, pieces)
    split_rows(pieces, place, rows_away, rows_kept)
    picked = None
    column = lax.broadcasted_iota(jnp.int32, (192, 192), 1)
    chunk = sum((column >= 24 * d).astype(jnp.int32) for d in range(1, 8))
    targets = column + chunk * 72 + place * 24
    for k, part in enumerate((head_0, head_1, head_2, head_3)):
        index = lax.broadcasted_iota(jnp.int32, (192, 192), 0) + (place ^ k) * 192
        pick = jnp.where(index == targets, 1.0, 0.0).astype(BF16)
        term = mm(part[...], pick)
        picked = term if picked is None else picked + term
    chosen[...] = picked.astype(BF16)


def add_rows(kept, came, total):
    total[...] = (kept[...] + came[...].astype(F32)).astype(BF16)


def add_pair(here_rows, came, total):
    total[...] = (here_rows[...].astype(F32) + came[...].astype(F32)).astype(BF16)


def branch_back(
    sum_own, sum_near, tokens, cots, branch, gain_rows, w_mine, probs, normed, scale_grad_mlp, chosen,
    grad_rows, grad_heads, grad_v, away, kept,
    work, grad_branch, grad_mid, extra, early,
):
    place, _, core, _, y = here()
    for m in range(MICRO):
        at = slice(m * 368, m * 368 + 368)

        @pl.when(core == m)
        def _():
            work[at, :] = sum_own[...].astype(F32)

        @pl.when(core != m)
        def _():
            work[at, :] = sum_near[...].astype(F32)

    gain_s, gain_n = gain_rows[1:2, :], gain_rows[2:3, :]
    scale_sum = jnp.zeros((8, 768), F32)
    for at in row_blocks(16):
        grown = branch[at, :].astype(F32)
        unit, scale = normalise(tokens[at, :].astype(F32) + gain_s * grown)
        pulled = work[at, :] * gain_n
        pulled = pulled - jnp.mean(pulled, -1, keepdims=True) - unit * jnp.mean(
            pulled * unit, -1, keepdims=True
        )
        through = cots[at, :].astype(F32) + scale * pulled
        grad_mid[at, :] = through
        grad_branch[at, :] = (gain_s * through).astype(BF16)
        scale_sum = scale_sum + fold(through * grown)
    for m in range(MICRO):
        for part, first in ((0, place * 88), (88, 352)):
            rows = 88 if part == 0 else 16
            grad_rows[m * 104 + part : m * 104 + part + rows, :] = grad_mid[
                pl.ds(pl.multiple_of(m * 368 + first, 8), rows), :
            ]
    for m in range(MICRO):
        at = slice(m * 368, m * 368 + 368)
        heads = mm_nt(grad_branch[at, :], w_mine[...]).astype(BF16)
        grad_heads[at, :] = heads
        terms = [mm_tn(probs[m * 3 + h], heads[:, h * 64 : h * 64 + 64]) for h in range(3)]
        grad_v[at, :] = jnp.concatenate(terms, -1).astype(BF16)
    grad_mid[0:768, 0:192] = mm_tn(normed[...], grad_v[...])
    extra[...] = mm_tn(chosen[...], grad_branch[...])
    scale_rows = (
        0.25 * jnp.sum(scale_sum, 0, keepdims=True),
        jnp.sum(scale_grad_mlp[...], 0, keepdims=True),
    )
    for d in range(8):
        base = d * 112
        early[base : base + 96, 0:192] = grad_mid[d * 96 : d * 96 + 96, 0:192]
        for i in range(4):
            early[base + i * 24 : base + i * 24 + 24, 192:384] = extra[
                d * 24 : d * 24 + 24, i * 192 : i * 192 + 192
            ]
        early[base + 96 : base + 112, :] = jnp.zeros((16, 384), F32)
        for i in range(2):
            early[base + 96 + i : base + 97 + i, 0:96] = scale_rows[i][:, d * 96 : d * 96 + 96]
    halve(early, y, away, kept, 112)


def score_back(probs, projected, grad_heads, normed, grad_qk, away, kept, work):
    _, _, _, _, y = here()
    for m in range(MICRO):
        at = slice(m * 368, m * 368 + 368)
        qkv = projected[at, :]
        g_heads = grad_heads[at, :]
        grads = [[], []]
        for h in range(3):
            q = qkv[:, h * 64 : h * 64 + 64]
            k = qkv[:, 192 + h * 64 : 192 + h * 64 + 64]
            v = qkv[:, 384 + h * 64 : 384 + h * 64 + 64]
            grad_prob = mm_nt(g_heads[:, h * 64 : h * 64 + 64], v)
            wide = probs[m * 3 + h].astype(F32)
            moved = wide * grad_prob
            delta = jnp.sum(moved, -1, keepdims=True)
            grad_score = (moved - wide * delta).astype(BF16)
            grads[0].append(mm(grad_score, k) * SCORE_SCALE)
            grads[1].append(mm_tn(q, grad_score))
        grad_qk[at, 0:192] = jnp.concatenate(grads[0], -1).astype(BF16)
        grad_qk[at, 192:384] = jnp.concatenate(grads[1], 0).T.astype(BF16)
    work[...] = mm_tn(normed[...], grad_qk[...])
    halve(work, y, away, kept, 96)


def project_back(grad_qk, grad_v, w_qkv, rows_away, rows_kept, work, pieces):
    place = here()[0]
    for m in range(MICRO):
        at = slice(m * 368, m * 368 + 368)
        work[at, :] = mm_nt(grad_qk[at, :], w_qkv[:, 0:384]) + mm_nt(grad_v[at, :], w_qkv[:, 384:576])
    cut_rows(work, pieces)
    split_rows(pieces, place, rows_away, rows_kept)


def sum_y(kept, came, own, send_1, send_2, send_3):
    _, _, _, z, _ = here()
    own[...] = kept[z] + came[z].astype(F32)
    for k, send in ((1, send_1), (2, send_2), (3, send_3)):
        send[...] = (kept[z ^ k] + came[z ^ k].astype(F32)).astype(BF16)


def sum_y_pairs(kept, came, own, away):
    _, _, _, z, _ = here()
    for k in range(2):
        own[k] = kept[z ^ (2 * k)] + came[z ^ (2 * k)].astype(F32)
        there = z ^ (2 * k + 1)
        away[k] = (kept[there] + came[there].astype(F32)).astype(BF16)


def sum_pairs(kept, came, own, away):
    own[...] = kept[0] + came[0].astype(F32)
    away[...] = (kept[1] + came[1].astype(F32)).astype(BF16)


def sum_last(own, came, total):
    total[...] = own[...] + came[...].astype(F32)


def add_pieces(kept_m, came_m, kept_h, came_h, stay, go):
    for i, (kept, came) in enumerate(((kept_m, came_m), (kept_h, came_h))):
        stay[i * 208 : i * 208 + 208, :] = kept[0:208, :] + came[0:208, :].astype(F32)
        go[i * 208 : i * 208 + 208, :] = (kept[208:416, :] + came[208:416, :].astype(F32)).astype(BF16)


def finish_rows(
    stay, came, own_rows, grad_rows, patches, tail, gain_rows,
    out_patches, out_special, grad_patches, grad_special,
):
    own = patches[...].astype(F32)
    rest = tail[...].astype(F32)
    outs, out_tails = [], []
    for m in range(MICRO):
        for part, count in ((0, 88), (88, 10)):
            at = slice(m * 104 + part, m * 104 + part + count)
            far_at = slice(208 + m * 104 + part, 208 + m * 104 + part + count)
            final = own_rows[at, :] + gain_rows[3:4, :] * (stay[at, :] + came[at, :].astype(F32))
            (outs if part == 0 else out_tails).append(final)
            rows = own[m * 88 : m * 88 + 88] if part == 0 else rest[m * 10 : m * 10 + 10]
            unit, scale = normalise(rows)
            pulled = gain_rows[0:1, :] * (stay[far_at, :] + came[far_at, :].astype(F32))
            pulled = pulled - jnp.mean(pulled, -1, keepdims=True) - unit * jnp.mean(
                pulled * unit, -1, keepdims=True
            )
            grad = grad_rows[at, :] + scale * pulled
            if part == 0:
                grad_patches[m * 88 : m * 88 + 88, :] = grad
            else:
                grad_special[m * 10 : m * 10 + 10, :] = grad
    out_patches[...] = jnp.concatenate(outs, 0).astype(BF16)
    out_special[...] = jnp.concatenate(out_tails, 0).astype(BF16)


def hand_out(held, own, near, far):
    place = here()[0]
    own[...] = held[place]
    near[...] = held[place ^ 1].astype(BF16)
    far[0:32, :] = held[place ^ 2].astype(BF16)
    far[32:64, :] = held[place ^ 3].astype(BF16)


def take_in(held, own, near, far, near_far):
    place = here()[0]
    held[place] = own[...]
    held[place ^ 1] = near[...].astype(F32)
    held[place ^ 2] = far[0:32, :].astype(F32)
    held[place ^ 3] = near_far[32:64, :].astype(F32)


def pick_up(kept, came, own, near, far, held):
    held[...] = jnp.zeros_like(held)
    for b in range(4):
        at = slice(b * 24, b * 24 + 24)
        held[b, 0:24, :] = kept[at, :] + came[at, :].astype(F32)
    hand_out(held, own, near, far)


def pick_attention(kept_a, came_a, kept_b, came_1, came_2, came_3, own, near, far, grad_out, held, sums):
    held[...] = jnp.zeros_like(held)
    sums[:, 0:384] = kept_a[...] + came_a[...].astype(F32)
    sums[0:96, 384:768] = (
        kept_b[...] + came_1[...].astype(F32) + came_2[...].astype(F32) + came_3[...].astype(F32)
    )
    for b in range(4):
        at = slice(b * 24, b * 24 + 24)
        held[b, 0:24, 0:384] = sums[at, 384:768]
        held[b, 0:24, 384:576] = sums[at, 0:192]
        held[b, 0:2, 576:600] = sums[96:98, at]
        grad_out[:, b * 192 : b * 192 + 192] = sums[at, 192:384]
    hand_out(held, own, near, far)


def join_up(own, near, far, near_far, w_up, gains, grad_up, norm_grad, held):
    take_in(held, own, near, far, near_far)
    for b in range(4):
        for d in range(8):
            at = d * 384 + b * 96
            grad_up[:, at : at + 96] = held[b, 0:24, d * 96 : d * 96 + 96]
    total = turned(jnp.sum(w_up[...].astype(F32) * grad_up[...], -1, keepdims=True))
    norm_grad[...] = total / gains[2:3, :].astype(F32)


def join_attention(
    own, near, far, near_far, w_qkv, gains, norm_grad, grad_qkv, grad_gains, held
):
    take_in(held, own, near, far, near_far)
    scales = None
    for b in range(4):
        for part in range(3):
            at = slice(part * 768 + b * 192, part * 768 + b * 192 + 192)
            grad_qkv[:, at] = held[b, 0:24, part * 192 : part * 192 + 192]
        term = held[b, 0:2, 576:600]
        scales = term if scales is None else scales + term
    plain = grad_qkv[...]
    grad_gains[0:1, :] = turned(jnp.sum(w_qkv[...].astype(F32) * plain, -1, keepdims=True))
    grad_gains[1:2, :] = scales[0:1, :]
    grad_gains[2:3, :] = norm_grad[...]
    grad_gains[3:4, :] = scales[1:2, :]
    grad_qkv[...] = plain * turned(gains[0:1, :].astype(F32))


def send(rows, axis, step):
    pairs = []
    for group in range(8):
        z, y = group // 2, group % 2
        for place in range(4):
            target = {
                "core": (group, place ^ 1),
                "x": (group, place ^ 2),
                "y": (z * 2 + 1 - y, place),
                "z": ((z ^ step) * 2 + y, place),
            }[axis]
            pairs.append((group * 4 + place, target[0] * 4 + target[1]))
    _, ready = plan()
    if ready:
        rows = lax.optimization_barrier((rows, *ready))[0]
    STEPS.append(lax.ppermute(rows, ("dp", "blk"), pairs))
    return STEPS[-1]


def add_y(kept, came):
    rows, width = kept.shape[1:]
    own, *parts = call(
        sum_y,
        [Keep(sds(rows, width, dtype=F32))] + [sds(rows, width)] * 3,
        [Keep(kept), came],
    )
    return [own, *[send(part, "z", k) for k, part in zip((1, 2, 3), parts)]]


def halve_y(kept, came):
    rows, width = kept.shape[1:]
    own, away = call(
        sum_y_pairs,
        [Keep(sds(2, rows, width, dtype=F32)), sds(2, rows, width)],
        [Keep(kept), came],
    )
    return own, send(away, "z", 1)


def halve_z(pair):
    kept, came = pair
    rows, width = kept.shape[1:]
    own, away = call(
        sum_pairs,
        [Keep(sds(rows, width, dtype=F32)), sds(rows, width)],
        [Keep(kept), came],
    )
    return own, send(away, "z", 2)


def side_y(kept, came):
    own, away = call(
        sum_sides,
        [Keep(sds(96, 768, dtype=F32)), sds(96, 768)],
        [Keep(kept), came],
    )
    return own, send(away, "y", 1)


def add_last(last):
    own, came = last
    return call(
        sum_last, [sds(*own.shape, dtype=F32)], [Keep(own), came]
    )[0]


def on_device_split(
    patches, special, image_ids, w_qkv, w_out, w_up, w_down, gains, cot_patches, cot_special
):
    STEPS.clear()
    own, near, far, rows = call(
        pick_pieces,
        [sds(48, 768), sds(48, 768), sds(96, 768), sds(352, 768)],
        [Far(w_qkv), Far(w_up), Far(gains), Far(patches), Far(cot_patches)],
        [pltpu.VMEM((4, 48, 768), F32)],
    )
    came_far = send(far, "x", 1)
    came_near, came_near_far = send(near, "core", 1), send(came_far, "core", 1)
    pack, both, wide = call(
        join_pieces,
        [sds(112, 768), sds(192, 768), sds(304, 768)],
        [own, came_near, came_far, came_near_far, w_out, w_down],
        [pltpu.VMEM((112, 768), F32), pltpu.VMEM((96, 768), F32)],
    )
    pack_2 = send(pack, "z", 2)
    pack_1 = send(pack, "z", 1)
    wide_y0 = send(wide, "y", 1)
    far_rows = send(rows, "x", 1)
    pack_y1 = send(pack_1, "y", 1)
    pack_3 = send(pack_2, "z", 1)
    pack_y2 = send(pack_2, "y", 1)
    both_2 = send(both, "z", 2)
    both_1 = send(both, "z", 1)
    near_rows = send(rows, "core", 1)
    row_parts = [rows, near_rows, far_rows, send(far_rows, "core", 1)]
    pack_y3 = send(pack_3, "y", 1)
    both_y1 = send(both_1, "y", 1)
    both_3 = send(both_2, "z", 1)
    qkv_full, out_part, gain_rows = call(
        open_pack,
        [Keep(sds(768, 576)), sds(192, 768), Keep(sds(8, 768, dtype=F32))],
        [pack, pack_1, pack_2, pack_3, wide_y0, pack_y1, pack_y2, pack_y3],
        [pltpu.VMEM((192, 768), F32), pltpu.VMEM((8, 16, 768), F32)],
    )
    far_out = send(out_part, "x", 1)
    attended, projected, probs, tokens, unit_low = call(
        attend,
        [sds(736, 192), *keep(sds(736, 576), sds(6, 368, 368), sds(736, 768), sds(736, 768))],
        [*keep(*row_parts), special, image_ids.reshape(8, 88), *keep(qkv_full, gain_rows)],
        [pltpu.VMEM((736, 768), F32), pltpu.VMEM((736, 768), BF16)],
    )
    far_heads = send(attended, "x", 1)
    both_y2 = send(both_2, "y", 1)
    out_parts = [
        out_part, send(out_part, "core", 1),
        far_out, send(far_out, "core", 1),
    ]
    both_y3 = send(both_3, "y", 1)
    out_full, out_mine, grad_mlp, cots = call(
        order_out,
        keep(sds(768, 768), sds(192, 768), sds(736, 768), sds(736, 768)),
        [*out_parts, *keep(*row_parts), cot_special, Keep(gain_rows)],
        [pltpu.VMEM((768, 768), F32)],
    )
    heads = [
        attended, send(attended, "core", 1),
        far_heads, send(far_heads, "core", 1),
    ]
    both_chunks = [both, both_1, both_2, both_3, wide_y0, both_y1, both_y2, both_y3]
    normed_mlp, branch, own_rows = call(
        branch_rows,
        keep(sds(736, 768), sds(736, 768), sds(208, 768, dtype=F32)),
        [*heads, *keep(out_full, tokens, gain_rows)],
        [pltpu.VMEM((736, 768), F32)],
    )
    active, slope, up_full, down_full = call(
        raise_rows,
        keep(sds(736, 768), sds(736, 768, dtype=F32), sds(768, 768), sds(768, 768)),
        [Keep(normed_mlp), *both_chunks],
        [pltpu.VMEM((736, 768), F32)],
    )
    half = [sds(4, 96, 768), Keep(sds(4, 96, 768, dtype=F32))]
    rows_split = [sds(416, 768), Keep(sds(416, 768, dtype=F32))]

    def make_down(active):
        return call(
            down_grads,
            half,
            keep(active, grad_mlp),
            [pltpu.VMEM((768, 768), F32)],
        )

    sum_away, sum_kept, grad_hidden = call(
        lower_rows,
        [sds(368, 768), *keep(sds(368, 768, dtype=F32), sds(736, 768))],
        keep(slope, grad_mlp, up_full, down_full),
        [pltpu.VMEM((2, 368, 768), F32)],
    )
    sum_came = send(sum_away, "core", 1)
    chip_sum = call(add_rows, [sds(368, 768)], [Keep(sum_kept), sum_came])[0]
    chip_came = send(chip_sum, "x", 1)
    down_away, down_kept = make_down(active)
    down_came = send(down_away, "z", 1)
    up_away, up_kept = call(
        up_grads,
        half,
        keep(normed_mlp, grad_hidden),
        [pltpu.VMEM((768, 768), F32)],
    )
    up_came = send(up_away, "y", 1)
    m_away, m_kept, scale_mlp, chosen = call(
        mlp_rows,
        [*rows_split, *keep(sds(8, 768, dtype=F32), sds(736, 192))],
        [*keep(active, down_full, cots), *heads],
        [pltpu.VMEM((736, 768), F32), pltpu.VMEM((4, 208, 768), F32)],
    )
    m_came = send(m_away, "core", 1)
    down_two, down_away = call(
        sum_fours,
        [Keep(sds(2, 96, 768, dtype=F32)), sds(2, 96, 768)],
        [Keep(down_kept), down_came],
    )
    down_came = send(down_away, "z", 2)
    sum_own = call(add_pair, [sds(368, 768)], [chip_sum, chip_came])[0]
    sum_near = send(sum_own, "core", 1)
    grad_rows, grad_heads, grad_v, a_away, a_kept = call(
        branch_back,
        [
            *keep(sds(208, 768, dtype=F32), sds(736, 192), sds(736, 192)),
            sds(4, 112, 384), Keep(sds(4, 112, 384, dtype=F32)),
        ],
        [
            sum_own, sum_near, *keep(tokens, cots, branch, gain_rows, out_mine, probs, unit_low), *keep(scale_mlp, chosen),
        ],
        [
            pltpu.VMEM((736, 768), F32), pltpu.VMEM((736, 768), BF16),
            pltpu.VMEM((768, 768), F32), pltpu.VMEM((192, 768), F32), pltpu.VMEM((896, 384), F32),
        ],
    )
    a_came = send(a_away, "y", 1)
    up_steps = halve_y(up_kept, up_came)
    down_last = side_y(down_two, down_came)
    grad_qk, b_away, b_kept = call(
        score_back,
        [Keep(sds(736, 384)), sds(4, 96, 384), Keep(sds(4, 96, 384, dtype=F32))],
        keep(probs, projected, grad_heads, unit_low),
        [pltpu.VMEM((768, 384), F32)],
    )
    b_came = send(b_away, "y", 1)
    a_pair = halve_y(a_kept, a_came)
    h_away, h_kept = call(
        project_back,
        rows_split,
        keep(grad_qk, grad_v, qkv_full),
        [pltpu.VMEM((736, 768), F32), pltpu.VMEM((4, 208, 768), F32)],
    )
    h_came = send(h_away, "core", 1)
    stay, go = call(
        add_pieces,
        [Keep(sds(416, 768, dtype=F32)), sds(416, 768)],
        [Keep(m_kept), m_came, Keep(h_kept), h_came],
    )
    far_rows = send(go, "x", 1)
    b_steps = add_y(b_kept, b_came)
    a_last = halve_z(a_pair)
    up_last = halve_z(up_steps)
    grad_down = add_last(down_last)
    pieces = [Keep(sds(32, 768, dtype=F32)), sds(32, 768), sds(64, 768)]
    held = pltpu.VMEM((4, 32, 768), F32)
    own, near, far = call(pick_up, pieces, [Keep(up_last[0]), up_last[1]], [held])
    came_far = send(far, "x", 1)
    came_near, came_near_far = send(near, "core", 1), send(came_far, "core", 1)
    grad_up, norm_grad = call(
        join_up,
        [sds(24, 3072, dtype=F32), Keep(sds(1, 24, dtype=F32))],
        [Keep(own), came_near, came_far, came_near_far, w_up, gains],
        [held],
    )
    own, near, far, grad_out = call(
        pick_attention,
        [*pieces, sds(24, 768, dtype=F32)],
        [Keep(a_last[0]), a_last[1], Keep(b_steps[0]), *b_steps[1:]],
        [held, pltpu.VMEM((112, 768), F32)],
    )
    came_far = send(far, "x", 1)
    came_near, came_near_far = send(near, "core", 1), send(came_far, "core", 1)
    out_patches, out_special, grad_patches, grad_special = call(
        finish_rows,
        [
            sds(176, 768), sds(20, 768), sds(176, 768, dtype=F32), sds(20, 768, dtype=F32),
        ],
        [Keep(stay), far_rows, *keep(own_rows, grad_rows), patches, special, Keep(gain_rows)],
    )
    grad_qkv, grad_gains = call(
        join_attention,
        [sds(24, 2304, dtype=F32), sds(4, 24, dtype=F32)],
        [Keep(own), came_near, came_far, came_near_far, w_qkv, gains, Keep(norm_grad)],
        [held],
    )
    return (
        out_patches, out_special, grad_patches, grad_special,
        grad_qkv, grad_out, grad_up, grad_down, grad_gains,
    )


def solution(mesh):
    placed = (
        P(("dp", "blk"), None),
        P("dp", None),
        P("dp"),
        P(("dp", "blk"), None),
        P(("dp", "blk"), None),
        P(("dp", "blk"), None),
        P(("dp", "blk"), None),
        P(None, ("dp", "blk")),
        P(("dp", "blk"), None),
        P("dp", None),
    )
    whole = dict(mesh.shape) != {"dp": 8, "blk": 4}
    return jax.shard_map(
        on_device if whole else on_device_split,
        mesh=mesh,
        in_specs=placed,
        out_specs=(
            P(("dp", "blk"), None),
            P("dp", None),
            P(("dp", "blk"), None),
            P("dp", None),
            P(("dp", "blk"), None),
            P(("dp", "blk"), None),
            P(("dp", "blk"), None),
            P(("dp", "blk"), None),
            P(None, ("dp", "blk")),
        ),
        check_vma=False,
    )
```
